32 devices in a mesh: batch: 4 (over y, x), strip: 8 (over z, core).
Axes of the slice: x: 2, y: 2, z: 4, core: 2. Of those that a mesh axis runs over, the one named last changes fastest.
Arguments:
- tokens: bfloat16 [4, 64, 32, 768], P('batch', 'strip'), may hold values from -6 to 6
- tile_owner: int32 [4, 4, 2], P('batch'), may hold values from 0 to 7, as said below
- time_steps: int32 [4, 8], P('batch'), may hold values from 0 to 999
- class_labels: int32 [4, 8], P('batch'), may hold values from 0 to 999
- class_embedding_matrix: bfloat16 [768, 1000], replicated, may hold values from -6 to 6
- adaptive_weight: bfloat16 [768, 4608], replicated, may hold values from -0.21875 to 0.21875
- adaptive_bias: bfloat16 [4608], replicated, may hold values from -3 to 3
- mixer_kernel: bfloat16 [768, 9], replicated, may hold values from -2 to 2
- joint_weight: bfloat16 [768, 2304], replicated, may hold values from -0.21875 to 0.21875
- output_weight: bfloat16 [768, 768], replicated, may hold values from -2.5 to 2.5
- output_bias: bfloat16 [768], replicated, may hold values from -2 to 2
- expand_weight: bfloat16 [768, 3072], replicated, may hold values from -0.21875 to 0.21875
- expand_bias: bfloat16 [3072], replicated, may hold values from -2 to 2
- hidden_kernel: bfloat16 [3072, 9], replicated, may hold values from -2 to 2
- reduce_weight: bfloat16 [3072, 768], replicated, may hold values from -0.109375 to 0.109375
- reduce_bias: bfloat16 [768], replicated, may hold values from -2 to 2
- output_cotangent: bfloat16 [4, 64, 32, 768], P('batch', 'strip'), may hold values from -6 to 6
Outputs:
- outputs: bfloat16 [4, 64, 32, 768], P('batch', 'strip')
- tokens_grad: float32 [4, 64, 32, 768], P('batch', 'strip')
- class_table_grad: float32 [768, 1000], P('strip')
- adaptive_weight_grad: float32 [768, 4608], P('strip')
- adaptive_bias_grad: float32 [4608], P('strip')
- mixer_kernel_grad: float32 [768, 9], P('strip')
- joint_weight_grad: float32 [768, 2304], P('strip')
- output_weight_grad: float32 [768, 768], P('strip')
- output_bias_grad: float32 [768], P('strip')
- expand_weight_grad: float32 [768, 3072], P('strip')
- expand_bias_grad: float32 [3072], P('strip')
- hidden_kernel_grad: float32 [3072, 9], P('strip')
- reduce_weight_grad: float32 [3072, 768], P('strip')
- reduce_bias_grad: float32 [768], P('strip')
The draws below stay inside these ranges and needn't reach their ends.
Inputs may be any that keep to these rules, and one draw needn't show every extreme that they name: `tile_owner`: A canvas is cut into 4 x 2 tiles of 16 rows and 16 columns; the tiles of one slot form one latent, a rectangle of whole tiles; among the canvases of each index of batch, some canvas has a latent that spans all 64 rows.
All inputs are finite; a program needn't handle non-finite values.
Results may differ from the reference program's by a relative error of at most 0.023.
Values may be sent and summed in bfloat16 or wider, within the bound.
A program may use at most 320 MiB of HBM per device.

```python
import math
import jax
import jax.numpy as jnp
import numpy as np
from jax import lax

D = 768
HEADS = 12
HEAD_DIM = 64
FF = 3072
NCLASS = 1000
NSTEPS = 1000
LATENTS = 8
COLS = 32
CANVAS_ROWS = 64
CANV_DEV = 1
CANVASES = 4


LAYOUT_TABLE = np.array([[[0, 0], [0, 0], [0, 0], [0, 0]], [[0, 0], [0, 0], [1, 1], [1, 1]], [[0, 0], [0, 0], [1, 2], [3, 4]], [[0, 1], [2, 3], [4, 5], [6, 7]], [[0, 1], [0, 2], [0, 3], [0, 4]], [[0, 1], [0, 1], [0, 1], [0, 1]]], dtype=np.int32)


def slot_order(subkey):
    return jax.random.permutation(subkey, LATENTS).astype(jnp.int32)


def draw_tile_owner(key, part):
    key = jax.random.fold_in(key, 11)
    kind_key, pick_key, span_key, order_key = jax.random.split(key, 4)
    groups = CANVASES // CANV_DEV
    kinds = jax.random.randint(kind_key, (CANVASES,), 0, 6)
    picked = jax.random.randint(pick_key, (groups,), 0, CANV_DEV)
    spanning = jnp.array([0, 4, 5], jnp.int32)[jax.random.randint(span_key, (groups,), 0, 3)]
    position = jnp.arange(CANVASES, dtype=jnp.int32)
    forced = position % CANV_DEV == jnp.repeat(picked, CANV_DEV, total_repeat_length=CANVASES)
    kinds = jnp.where(forced, jnp.repeat(spanning, CANV_DEV, total_repeat_length=CANVASES), kinds)
    base = jnp.asarray(LAYOUT_TABLE)[kinds].reshape(CANVASES, 8)
    orders = jax.vmap(slot_order)(jax.random.split(order_key, CANVASES))
    shuffled = jnp.take_along_axis(orders, base, axis=1)
    owner = jnp.where(forced[:, None], LATENTS - 1 - base, shuffled)
    return owner.reshape(CANVASES, 4, 2).astype(jnp.int32)


def set_ends(values, stream_key, low, top_value):
    spot = [jax.random.randint(jax.random.fold_in(stream_key, axis), (), 0, length) for axis, length in enumerate(values.shape)]
    widest = values.shape.index(max(values.shape))
    next_to = spot[:widest] + [(spot[widest] + 1) % values.shape[widest]] + spot[widest + 1:]
    return values.at[tuple(spot)].set(low).at[tuple(next_to)].set(top_value)


def shard_levels(rng, shape, pieces, low, largest):
    loudness = 1.0
    for dim, shards_of in pieces:
        draws = jax.random.uniform(jax.random.fold_in(jax.random.fold_in(rng, 6), dim), (shards_of,), jnp.float32, low / len(pieces), largest / len(pieces))
        loudness = loudness * jnp.repeat(jnp.exp(draws), shape[dim] // shards_of).reshape((-1,) + (1,) * (len(shape) - 1 - dim))
    return loudness


def normal_values(own_key, extent, scale, limit, cuts=(), held_as=jnp.bfloat16):
    gain = shard_levels(own_key, extent, cuts, -0.22, 0.18) if cuts else 1.0
    values = jax.random.normal(own_key, extent, jnp.float32) * scale * gain
    return jnp.minimum(jnp.maximum(values, -limit), limit).astype(held_as)


def setup_inputs(seed: int = 0) -> dict:
    seeds = jax.random.split(jax.random.key(seed), 18)
    tokens = normal_values(seeds[0], (CANVASES, CANVAS_ROWS, COLS, D), 1.0, 6.0, ((0, 4), (1, 8)))
    tile_owner = draw_tile_owner(jax.random.fold_in(seeds[17], 71), 0)
    time_steps = set_ends(jax.random.randint(seeds[2], (CANVASES, LATENTS), 0, NSTEPS), jax.random.fold_in(seeds[2], 1), 0, NSTEPS - 1).astype(jnp.int32)
    class_labels = set_ends(jax.random.randint(seeds[3], (CANVASES, LATENTS), 0, NCLASS), jax.random.fold_in(seeds[3], 1), 0, NCLASS - 1).astype(jnp.int32)
    class_embedding_matrix = normal_values(seeds[4], (D, NCLASS), 1.0, 6.0)
    adaptive_weight = normal_values(seeds[5], (D, 6 * D), D ** -0.5, 0.21875)
    adaptive_bias = normal_values(seeds[6], (6 * D,), 0.5, 3.0)
    mixer_kernel = normal_values(seeds[7], (D, 9), 9 ** -0.5, 2.0)
    joint_weight = normal_values(seeds[8], (D, 3 * D), D ** -0.5, 0.21875)
    output_weight = normal_values(seeds[9], (D, D), (max(D * 16 // (CANVAS_ROWS * COLS), 1)) ** -0.5, 2.5)
    output_bias = normal_values(seeds[10], (D,), 0.3, 2.0)
    expand_weight = normal_values(seeds[11], (D, FF), D ** -0.5, 0.21875)
    expand_bias = normal_values(seeds[12], (FF,), 0.3, 2.0)
    hidden_kernel = normal_values(seeds[13], (FF, 9), 9 ** -0.5, 2.0)
    reduce_weight = normal_values(seeds[14], (FF, D), FF ** -0.5, 0.109375)
    reduce_bias = normal_values(seeds[15], (D,), 0.3, 2.0)
    output_cotangent = normal_values(seeds[16], (CANVASES, CANVAS_ROWS, COLS, D), 1.0, 6.0, ((0, 4), (1, 8)))
    return dict(tokens=tokens, tile_owner=tile_owner, time_steps=time_steps, class_labels=class_labels, class_embedding_matrix=class_embedding_matrix, adaptive_weight=adaptive_weight, adaptive_bias=adaptive_bias, mixer_kernel=mixer_kernel, joint_weight=joint_weight, output_weight=output_weight, output_bias=output_bias, expand_weight=expand_weight, expand_bias=expand_bias, hidden_kernel=hidden_kernel, reduce_weight=reduce_weight, reduce_bias=reduce_bias, output_cotangent=output_cotangent)


@jax.custom_vjp
def low(v):
    return lax.optimization_barrier(v.astype(jnp.bfloat16)).astype(jnp.float32)

@jax.custom_vjp
def low_back(v):
    return v

def low_keep(v):
    return (low(v), None)

def low_pass(kept, grad):
    return (grad,)

def back_keep(v):
    return (v, None)

def back_low(kept, grad):
    return (low(grad),)
low.defvjp(low_keep, low_pass)
low_back.defvjp(back_keep, back_low)
EPSILON = 1e-06
MASKED = -1e+30
EXACT_PRECISION = lax.Precision.HIGHEST

def owner_table(tile_owner):
    rows = jnp.repeat(tile_owner, CANVAS_ROWS // 4, axis=1)
    owners = jnp.repeat(rows, COLS // 2, axis=2).astype(jnp.int32)
    token_hot = (owners[..., None] == jnp.arange(LATENTS, dtype=jnp.int32)).astype(jnp.float32)
    return (owners, token_hot)

def timestep_features(time_steps):
    half_width = D // 2
    frequencies = jnp.exp(-math.log(10000.0) * jnp.arange(half_width, dtype=jnp.float32) / half_width)
    angles = time_steps.astype(jnp.float32)[..., None] * frequencies
    return jnp.concatenate([jnp.cos(angles), jnp.sin(angles)], axis=-1)

def normalize(values):
    centre = lax.optimization_barrier(jnp.mean(values, axis=-1, keepdims=True))
    centred = values - centre
    spread = lax.optimization_barrier(jnp.mean(centred * centred, axis=-1, keepdims=True))
    return centred * lax.rsqrt(spread + EPSILON)

def depthwise(padded, kernel):
    row_count = padded.shape[-3] - 2
    column_total = padded.shape[-2]
    widened = jnp.pad(padded, [(0, 0)] * (padded.ndim - 2) + [(1, 1), (0, 0)])
    result = jnp.zeros(padded.shape[:-3] + (row_count, column_total, padded.shape[-1]), padded.dtype)
    for tapping in range(9):
        row_shift = tapping // 3
        col_shift = tapping % 3
        window = lax.slice_in_dim(widened, row_shift, row_shift + row_count, axis=widened.ndim - 3)
        window = lax.slice_in_dim(window, col_shift, col_shift + column_total, axis=widened.ndim - 2)
        result = result + kernel[:, tapping] * window
    return result

def reference_groups(tensor):
    row_count, column_total, features = tensor.shape
    head_size = features // HEADS
    shaped = tensor.reshape(row_count // 2, 2, column_total // 2, 2, HEADS, head_size)
    shaped = shaped.transpose(1, 3, 4, 0, 2, 5)
    return shaped.reshape(2, 2, HEADS, row_count // 2 * (column_total // 2), head_size)

def reference_merge(tensor, row_count, column_total):
    head_size = tensor.shape[-1]
    shaped = tensor.reshape(2, 2, HEADS, row_count // 2, column_total // 2, head_size)
    shaped = shaped.transpose(3, 0, 4, 1, 2, 5)
    return shaped.reshape(row_count, column_total, HEADS * head_size)

def owner_groups(owner):
    row_count, column_total = owner.shape
    shaped = owner.reshape(row_count // 2, 2, column_total // 2, 2).transpose(1, 3, 0, 2)
    return shaped.reshape(2, 2, row_count // 2 * (column_total // 2))

def grouped_attention(query_rows, keys, values, owner):
    row_count, column_total = (query_rows.shape[0], query_rows.shape[1])
    grouped_owner = owner_groups(owner)
    allowed = grouped_owner[:, :, :, None] == grouped_owner[:, :, None, :]
    query_groups = reference_groups(query_rows)
    key_groups = reference_groups(keys)
    value_groups = reference_groups(values)
    factor = HEAD_DIM ** (-0.5)
    scores = low_back(jnp.einsum('abhnd,abhmd->abhnm', query_groups, key_groups, precision=EXACT_PRECISION) * factor)
    scores = jnp.where(allowed[:, :, None], scores, MASKED)
    softened = low(jax.nn.softmax(scores, axis=-1))
    attended = jnp.einsum('abhnm,abhmd->abhnd', softened, value_groups, precision=EXACT_PRECISION)
    return reference_merge(attended, row_count, column_total)

def canvas_forward(params, canvas, owner, token_hot, canvas_steps, labels):
    class_embedding_matrix, adaptive_weight, adaptive_bias, mixer_kernel, joint_weight, output_weight, output_bias, expand_weight, expand_bias, hidden_kernel, reduce_weight, reduce_bias = params
    condition = timestep_features(canvas_steps) + jnp.take(class_embedding_matrix, labels, axis=1).T
    modulation = jnp.dot(low(jax.nn.silu(condition)), adaptive_weight, precision=EXACT_PRECISION) + adaptive_bias
    token_mod = jnp.dot(token_hot, modulation, precision=EXACT_PRECISION)
    shift_one, scale_one, gate_one, shift_two, scale_two, gate_two = jnp.split(token_mod, 6, axis=-1)
    first = low(normalize(canvas) * (1.0 + scale_one) + shift_one)
    mixed = low_back(low(depthwise(jnp.pad(first, ((1, 1), (0, 0), (0, 0))), mixer_kernel)))
    joint = jnp.dot(mixed, joint_weight, precision=EXACT_PRECISION)
    query_rows = low_back(low(joint[..., :D]))
    keys = low_back(low(joint[..., D:2 * D]))
    values = low_back(low(joint[..., 2 * D:]))
    attended = low_back(low(grouped_attention(query_rows, keys, values, owner)))
    branch_one = low_back(jnp.dot(attended, output_weight, precision=EXACT_PRECISION) + output_bias)
    residual = canvas + gate_one * branch_one
    second = low(normalize(residual) * (1.0 + scale_two) + shift_two)
    expanded = low_back(low(jnp.dot(second, expand_weight, precision=EXACT_PRECISION) + expand_bias))
    conv_out = low_back(depthwise(jnp.pad(expanded, ((1, 1), (0, 0), (0, 0))), hidden_kernel))
    activated = low(jax.nn.gelu(conv_out))
    branch_two = low_back(jnp.dot(activated, reduce_weight, precision=EXACT_PRECISION) + reduce_bias)
    return residual + gate_two * branch_two

def reference(tokens, tile_owner, time_steps, class_labels, class_embedding_matrix, adaptive_weight, adaptive_bias, mixer_kernel, joint_weight, output_weight, output_bias, expand_weight, expand_bias, hidden_kernel, reduce_weight, reduce_bias, output_cotangent):
    params = tuple((item.astype(jnp.float32) for item in (class_embedding_matrix, adaptive_weight, adaptive_bias, mixer_kernel, joint_weight, output_weight, output_bias, expand_weight, expand_bias, hidden_kernel, reduce_weight, reduce_bias)))
    owners, token_hot = owner_table(tile_owner)

    def canvas_step(totals, items):
        canvas, cotangent, canvas_owner, canvas_hot, canvas_steps, labels = items

        def forward(weights, inputs):
            return canvas_forward(weights, inputs, canvas_owner, canvas_hot, canvas_steps, labels)
        result, pullback = jax.vjp(forward, params, canvas)
        weight_grads, input_grad = pullback(cotangent)
        totals = jax.tree.map(jnp.add, totals, weight_grads)
        return (totals, (result.astype(jnp.bfloat16), input_grad))
    starting = tuple((jnp.zeros_like(item) for item in params))
    totals, produced = lax.scan(canvas_step, starting, (tokens.astype(jnp.float32), output_cotangent.astype(jnp.float32), owners, token_hot, time_steps, class_labels))
    return (produced[0], produced[1], totals[0], totals[1], totals[2], totals[3], totals[4], totals[5], totals[6], totals[7], totals[8], totals[9], totals[10], totals[11])
```

```python
import functools
import math

import jax
import jax.numpy as jnp
from jax import lax
from jax.experimental import pallas as pl
from jax.experimental.pallas import tpu as pltpu
from jax.sharding import PartitionSpec as P

HEADS = 12
EPSILON = 1e-06
MASKED = -1e30
MESH = pl.DeviceIdType.MESH
F32 = jnp.float32
BF16 = jnp.bfloat16
VMEM_BYTES = 56 * 1024 * 1024
WHOLE = pl.BlockSpec(memory_space=pltpu.VMEM)
LEFT = pl.BlockSpec(memory_space=pl.ANY)
SCALARS = pl.BlockSpec(memory_space=pltpu.SMEM)
NT = (((1,), (1,)), ((), ()))
TN = (((0,), (0,)), ((), ()))


def rcopy(src, dst, send, recv, strip):
    return pltpu.make_async_remote_copy(
        src_ref=src,
        dst_ref=dst,
        send_sem=send,
        recv_sem=recv,
        device_id=(lax.axis_index("batch"), strip),
        device_id_type=MESH,
    )


def strip_barrier(strips):
    me = lax.axis_index("strip")
    barrier = pltpu.get_barrier_semaphore()
    for d in range(1, strips):
        pl.semaphore_signal(
            barrier,
            inc=1,
            device_id=(lax.axis_index("batch"), lax.rem(me + d, strips)),
            device_id_type=MESH,
        )
    pl.semaphore_wait(barrier, strips - 1)


def spread(mod, width):
    return jnp.concatenate(
        [jnp.broadcast_to(mod[0:1], (8, width)), jnp.broadcast_to(mod[1:2], (8, width))], axis=0
    )


def spread_columns(buffer, r, x):
    for k in range(x.shape[-1] // 128):
        buffer[r, k] = x[:, k * 128 : k * 128 + 128]


def every_second(buffer, r, p):
    return jnp.concatenate(
        [buffer[r, k, pl.ds(p, 16, stride=2), :] for k in range(buffer.shape[1])], axis=-1
    )


def ln_parts(x):
    centre = jnp.mean(x, axis=-1, keepdims=True)
    centred = x - centre
    var = jnp.mean(centred * centred, axis=-1, keepdims=True)
    inv = lax.rsqrt(var + EPSILON)
    return centred * inv, inv


def shifts(even, odd):
    j = lax.broadcasted_iota(jnp.int32, even.shape, 0)
    n = even.shape[0]
    odd_m = jnp.where(j == 0, 0.0, pltpu.roll(odd, 1, 0))
    even_p = jnp.where(j == n - 1, 0.0, pltpu.roll(even, n - 1, 0))
    return odd_m, even_p


def conv_row(load, weights, flip):
    out0 = out1 = None
    for i in range(3):
        even, odd = load(i)
        odd_m, even_p = shifts(even, odd)
        t = [weights[8 - (3 * i + k) if flip else 3 * i + k] for k in range(3)]
        a0 = t[0] * odd_m + t[1] * even + t[2] * odd
        a1 = t[0] * even + t[1] * odd + t[2] * even_p
        out0 = a0 if out0 is None else out0 + a0
        out1 = a1 if out1 is None else out1 + a1
    return out0, out1


def attend_kernel(
    tok_ref, mod_ref, mk_ref, owner_ref, wj_hbm,
    xd_ref, fp_ref, mg_ref, qkv_ref, p_ref, ag_ref, ai_ref,
    tokf, wj, ms, wsem, hs, hr, g_s, g_r, f_s, f_r, a_s, a_r, e_s, e_r,
):
    rows = tok_ref.shape[0]
    width = tok_ref.shape[2]
    half = width // 2
    strips = lax.axis_size("strip")
    chips = strips // 2
    s = lax.axis_index("strip")
    z = s // 2
    c = lax.rem(s, 2)
    sibling = 2 * z + 1 - c

    wcopies = []
    for part in range(3):
        off = pl.multiple_of(part * width + c * half, 128)
        cp = pltpu.make_async_copy(wj_hbm.at[:, pl.ds(off, half)], wj.at[part], wsem.at[part])
        cp.start()
        wcopies.append(cp)
    strip_barrier(strips)

    scale1 = spread(1.0 + mod_ref[:, width : 2 * width], width)
    shift1 = spread(mod_ref[:, 0:width], width)

    def first_row(r):
        spread_columns(tokf, r, tok_ref[r].astype(F32))
        for p in range(2):
            x = every_second(tokf, r, p)
            xd_ref[r, p] = x.astype(BF16)
            n, _ = ln_parts(x)
            fp_ref[r + 1, p] = (n * scale1 + shift1).astype(BF16)

    first_row(0)
    first_row(rows - 1)
    up = rcopy(fp_ref.at[1], fp_ref.at[rows + 1], hs.at[0], hr.at[0], s - 1)
    down = rcopy(fp_ref.at[rows], fp_ref.at[0], hs.at[1], hr.at[1], s + 1)

    @pl.when(s > 0)
    def _():
        up.start()

    @pl.when(s < strips - 1)
    def _():
        down.start()

    def body(r, _):
        first_row(r)
        return 0

    lax.fori_loop(1, rows - 1, body, 0)

    def mixed_row(r):
        for k in range(width // 128):
            lanes = pl.ds(k * 128, 128)
            weights = [mk_ref[t : t + 1, k * 128 : k * 128 + 128] for t in range(9)]
            out = conv_row(
                lambda i: (fp_ref[r + i, 0, :, lanes].astype(F32), fp_ref[r + i, 1, :, lanes].astype(F32)),
                weights,
                False,
            )
            for p in range(2):
                ms[lax.rem(r, 2) * 2 + p, r // 2, :, lanes] = out[p].astype(BF16)

    def body(r, _):
        mixed_row(r)
        return 0

    lax.fori_loop(1, rows - 1, body, 0)

    @pl.when(s > 0)
    def _():
        rcopy(fp_ref.at[1], fp_ref.at[0], hs.at[1], hr.at[1], s - 1).wait_recv()

    @pl.when(s == 0)
    def _():
        fp_ref[0] = jnp.zeros_like(fp_ref[0])

    mixed_row(0)

    @pl.when(s < strips - 1)
    def _():
        rcopy(fp_ref.at[1], fp_ref.at[rows + 1], hs.at[0], hr.at[0], s + 1).wait_recv()

    @pl.when(s == strips - 1)
    def _():
        fp_ref[rows + 1] = jnp.zeros_like(fp_ref[rows + 1])

    mixed_row(rows - 1)

    gathers = []
    for d in range(1, chips):
        g = lax.rem(z + d, chips)
        cp = rcopy(ms.at[g], mg_ref.at[s], g_s.at[d], g_r.at[d], 2 * g + c)
        cp.start()
        gathers.append(cp)
    mg_ref[s] = ms[z]
    forwards = []
    for d in range(chips):
        i = 2 * lax.rem(z - d + chips, chips) + c
        if d:
            rcopy(ms.at[z], mg_ref.at[i], g_s.at[d], g_r.at[d], i).wait_recv()
        cp = rcopy(mg_ref.at[i], mg_ref.at[i], f_s.at[d], f_r.at[d], sibling)
        cp.start()
        forwards.append(cp)
    for d in range(chips):
        i = 2 * lax.rem(z - d + chips, chips) + 1 - c
        rcopy(mg_ref.at[i], mg_ref.at[i], f_s.at[d], f_r.at[d], sibling).wait_recv()

    for part in range(3):
        wcopies[part].wait()

    def project(t, _):
        x = mg_ref[pl.ds(2 * t, 2)].reshape(128, width)
        for part in range(3):
            y = jnp.dot(x, wj[part], preferred_element_type=F32).astype(BF16)
            for n in range(3):
                qkv_ref[3 * part + n, pl.ds(pl.multiple_of(t * 128, 128), 128), :] = y[:, n * 128 : n * 128 + 128]
        return 0

    lax.fori_loop(0, chips, project, 0)

    total = strips * 64
    where = lax.broadcasted_iota(jnp.int32, (1, total), 1)
    lefts = lax.rem(where, 16) < 8
    key_owner = jnp.zeros((1, total), jnp.int32)
    for t in range(4):
        both = jnp.where(lefts, owner_ref[2 * t], owner_ref[2 * t + 1])
        key_owner = jnp.where(where // 128 == t, both, key_owner)
    qleft = lax.rem(lax.broadcasted_iota(jnp.int32, (128, 1), 0), 16) < 8
    lane = lax.broadcasted_iota(jnp.int32, (128, 128), 1) < 64
    factor = 64 ** -0.5
    sends = []
    for n in range(3):
        mine = c * 3 + n

        def attend(t, _):
            rws = pl.ds(pl.multiple_of(t * 128, 128), 128)
            owner = jnp.where(qleft, owner_ref[2 * t], owner_ref[2 * t + 1])
            allowed = owner == key_owner
            q2 = qkv_ref[n, rws, :]
            keys = qkv_ref[3 + n]
            values = qkv_ref[6 + n]
            outs = []
            for h in range(2):
                q = jnp.where(lane if h == 0 else jnp.logical_not(lane), q2, jnp.zeros_like(q2))
                scores = lax.dot_general(q, keys, NT, preferred_element_type=F32) * factor
                scores = jnp.where(allowed, scores, MASKED)
                peak = jnp.max(scores, axis=-1, keepdims=True)
                lifted = jnp.exp(scores - peak)
                inv = 1.0 / jnp.sum(lifted, axis=-1, keepdims=True)
                probs = (lifted * inv).astype(BF16)
                p_ref[n, h, rws, :] = probs
                outs.append(jnp.dot(probs, values, preferred_element_type=F32))
            ag_ref[mine, rws, :] = jnp.where(lane, outs[0], outs[1]).astype(BF16)
            return 0

        lax.fori_loop(0, 4, attend, 0)
        cp = rcopy(ag_ref.at[mine], ag_ref.at[mine], e_s.at[n], e_r.at[n], sibling)
        cp.start()
        sends.append(cp)
        for d in range(1, strips):
            t = lax.rem(s + d, strips)
            cp = rcopy(
                ag_ref.at[mine, pl.ds(pl.multiple_of(t * 64, 64), 64)],
                ai_ref.at[mine, z],
                a_s.at[n, d],
                a_r.at[n, d],
                t,
            )
            cp.start()
            sends.append(cp)
        ai_ref[mine, z] = ag_ref[mine, pl.ds(pl.multiple_of(s * 64, 64), 64), :]

    for n in range(3):
        other = (1 - c) * 3 + n
        rcopy(ag_ref.at[other], ag_ref.at[other], e_s.at[n], e_r.at[n], sibling).wait_recv()
        for d in range(1, strips):
            i = lax.rem(s - d + strips, strips)
            spot = lax.rem(i, 2) * 3 + n
            rcopy(
                ag_ref.at[spot, pl.ds(0, 64)], ai_ref.at[spot, i // 2], a_s.at[n, d], a_r.at[n, d], i
            ).wait_recv()
    for cp in gathers + forwards + sends:
        cp.wait_send()

    @pl.when(s > 0)
    def _():
        up.wait_send()

    @pl.when(s < strips - 1)
    def _():
        down.wait_send()


def attend(tokens, mod, mixer, owner, joint_weight, strips):
    rows, cols, width = tokens.shape
    chips = strips // 2
    dma = pltpu.SemaphoreType.DMA
    return pl.pallas_call(
        attend_kernel,
        name="attend_forward",
        out_shape=(
            jax.ShapeDtypeStruct((rows, 2, 16, width), BF16),
            jax.ShapeDtypeStruct((rows + 2, 2, 16, width), BF16),
            jax.ShapeDtypeStruct((strips, rows // 2, 16, width), BF16),
            jax.ShapeDtypeStruct((9, strips * 64, 128), BF16),
            jax.ShapeDtypeStruct((3, 2, strips * 64, strips * 64), BF16),
            jax.ShapeDtypeStruct((6, strips * 64, 128), BF16),
            jax.ShapeDtypeStruct((6, chips, 64, 128), BF16),
        ),
        in_specs=[WHOLE, WHOLE, WHOLE, SCALARS, LEFT],
        out_specs=(WHOLE,) * 7,
        scratch_shapes=[
            pltpu.VMEM((rows, width // 128, cols, 128), F32),
            pltpu.VMEM((3, width, width // 2), BF16),
            pltpu.VMEM((chips, rows // 2, 16, width), BF16),
            dma((3,)),
            dma((2,)),
            dma((2,)),
            dma((chips,)),
            dma((chips,)),
            dma((chips,)),
            dma((chips,)),
            dma((3, strips)),
            dma((3, strips)),
            dma((3,)),
            dma((3,)),
        ],
        compiler_params=pltpu.CompilerParams(
            collective_id=0, has_side_effects=True, vmem_limit_bytes=VMEM_BYTES
        ),
    )(tokens, mod, mixer, owner, joint_weight)


def gelu_both(x):
    k0 = math.sqrt(2.0 / math.pi)
    square = x * x
    t = jnp.tanh(k0 * x * (1.0 + 0.044715 * square))
    cdf = 0.5 + 0.5 * t
    slope = cdf + (0.5 * k0) * x * (1.0 - t * t) * (1.0 + (3.0 * 0.044715) * square)
    return x * cdf, slope


def fold(x):
    return x[0:8] + x[8:16]


def ffn_kernel(
    xd_ref, mod_ref, ai_ref, wo_ref, ob_ref, eb_ref, hk_ref, rb_ref, cot_ref, we_hbm, wr_hbm,
    out_ref, rg_ref, og_ref, rw_ref, ew_ref, hkg_ref, mg_ref, sb_ref,
    we, wr, tg, sc, ex, cg, act, agr, eg, b2, sg, b2_in, sg_in, res, b1, ctd, cotf, acc,
    wsem, x_s, x_r, h_s, h_r, k_s, k_r,
):
    rows, _, width = cot_ref.shape
    chip_rows = 2 * rows
    blocks = rows * 2
    piece = we.shape[2]
    strips = lax.axis_size("strip")
    chips = strips // 2
    s = lax.axis_index("strip")
    z = s // 2
    c = lax.rem(s, 2)
    sibling = 2 * z + 1 - c

    def weight_copies(n):
        off = pl.multiple_of((2 * n + c) * piece, 128)
        return (
            pltpu.make_async_copy(we_hbm.at[:, pl.ds(off, piece)], we.at[n], wsem.at[0, n]),
            pltpu.make_async_copy(wr_hbm.at[pl.ds(off, piece)], wr.at[n], wsem.at[1, n]),
        )

    for n in range(chips):
        for cp in weight_copies(n):
            cp.start()
    strip_barrier(strips)

    def block_mod(n):
        return spread(mod_ref[:, n * width : (n + 1) * width], width)

    acc[...] = jnp.zeros_like(acc)
    gate2 = block_mod(5)

    def upstream_row(r, _):
        spread_columns(cotf, r, cot_ref[r].astype(F32))
        for p in range(2):
            up = every_second(cotf, r, p)
            ctd[2 * r + p] = up.astype(BF16)
            two = (up * gate2).astype(BF16)
            tg[c, 2 * r + p] = two
            acc[0] += two.astype(F32)
        return 0

    lax.fori_loop(0, rows, upstream_row, 0)
    tg_copy = rcopy(tg.at[c], tg.at[c], x_s.at[0], x_r.at[0], sibling)
    tg_copy.start()

    gate1 = block_mod(2)
    shift2 = block_mod(3)
    scale2 = 1.0 + block_mod(4)
    bias1 = ob_ref[...]

    def project(g, _):
        x = jnp.concatenate([ai_ref[n, g] for n in range(6)], axis=-1)
        y = jnp.dot(x, wo_ref[...], preferred_element_type=F32) + bias1
        for r2 in range(rows // 2):
            rp = 4 * r2 + g
            branch = y[r2 * 16 : r2 * 16 + 16]
            b1[rp] = branch
            v = xd_ref[rp // 2, lax.rem(rp, 2)].astype(F32) + gate1 * branch
            res[rp] = v
            n, _ = ln_parts(v)
            sc[c, rp] = (n * scale2 + shift2).astype(BF16)
        return 0

    lax.fori_loop(0, 4, project, 0)
    sc_copy = rcopy(sc.at[c], sc.at[c], x_s.at[1], x_r.at[1], sibling)
    sc_copy.start()

    def up_copy(buffer, k, n):
        return rcopy(
            buffer.at[n, 1], buffer.at[n, chip_rows + 1], h_s.at[k, 0, n], h_r.at[k, 0, n], s - 2
        )

    def down_copy(buffer, k, n):
        return rcopy(
            buffer.at[n, chip_rows], buffer.at[n, 0], h_s.at[k, 1, n], h_r.at[k, 1, n], s + 2
        )

    def send_halo(buffer, k, n):
        @pl.when(z > 0)
        def _():
            up_copy(buffer, k, n).start()

        @pl.when(z < chips - 1)
        def _():
            down_copy(buffer, k, n).start()

    def take_halo(buffer, k, n):
        @pl.when(z > 0)
        def _():
            rcopy(
                buffer.at[n, 1], buffer.at[n, 0], h_s.at[k, 1, n], h_r.at[k, 1, n], s - 2
            ).wait_recv()

        @pl.when(z == 0)
        def _():
            buffer[n, 0] = jnp.zeros_like(buffer[n, 0])

        @pl.when(z < chips - 1)
        def _():
            rcopy(
                buffer.at[n, 1], buffer.at[n, chip_rows + 1], h_s.at[k, 0, n], h_r.at[k, 0, n], s + 2
            ).wait_recv()

        @pl.when(z == chips - 1)
        def _():
            buffer[n, chip_rows + 1] = jnp.zeros_like(buffer[n, 0])

    def drain_halo(buffer, k, n):
        @pl.when(z > 0)
        def _():
            up_copy(buffer, k, n).wait_send()

        @pl.when(z < chips - 1)
        def _():
            down_copy(buffer, k, n).wait_send()

    sc_copy.wait_recv()
    tiles = chip_rows // 4

    def chip_tile(buffer, t):
        return buffer[t // 2, pl.ds(lax.rem(t, 2) * 8, 8)].reshape(128, width)

    def expand(n, _):
        for cp in weight_copies(n):
            cp.wait()
        bias = eb_ref[2 * n + c]
        for t in range(tiles):
            y = jnp.dot(chip_tile(sc, t), we[n], preferred_element_type=F32) + bias
            ex[n, pl.ds(1 + 4 * t, 4)] = y.astype(BF16).reshape(4, 2, 16, piece)
        send_halo(ex, 0, n)
        return 0

    lax.fori_loop(0, chips, expand, 0)
    tg_copy.wait_recv()
    for cp in (tg_copy, sc_copy):
        cp.wait_send()

    def activate(n, _):
        take_halo(ex, 0, n)
        for t in range(tiles):
            agr[pl.ds(8 * t, 8)] = lax.dot_general(
                chip_tile(tg, t), wr[n], NT, preferred_element_type=F32
            ).reshape(8, 16, piece)

        def row(r, _):
            for k in range(piece // 128):
                lanes = pl.ds(k * 128, 128)
                weights = [hk_ref[2 * n + c, t : t + 1, lanes] for t in range(9)]
                out = conv_row(
                    lambda i: (ex[n, r + i, 0, :, lanes].astype(F32), ex[n, r + i, 1, :, lanes].astype(F32)),
                    weights,
                    False,
                )
                for p in range(2):
                    value, slope = gelu_both(out[p])
                    act[2 * r + p, :, lanes] = value.astype(BF16)
                    cg[n, r + 1, p, :, lanes] = (agr[2 * r + p, :, lanes] * slope).astype(BF16)
            return 0

        lax.fori_loop(0, chip_rows, row, 0)
        send_halo(cg, 1, n)
        full = act[...].reshape(chip_rows * 32, piece)
        for t in range(tiles):
            y = jnp.dot(full[t * 128 : t * 128 + 128], wr[n], preferred_element_type=F32)
            y = y.reshape(8, 16, width)
            spot = (t // 2, pl.ds((t % 2) * 8, 8))

            @pl.when(n == 0)
            def _():
                b2[spot] = y

            @pl.when(n > 0)
            def _():
                b2[spot] += y

        rw_ref[n] = lax.dot_general(
            full, tg[...].reshape(chip_rows * 32, width), TN, preferred_element_type=F32
        ).astype(BF16)
        return 0

    hkg_ref[...] = jnp.zeros_like(hkg_ref)
    lax.fori_loop(0, chips, activate, 0)
    b2_copy = rcopy(b2.at[1 - c], b2_in, x_s.at[2], x_r.at[2], sibling)
    b2_copy.start()

    def backward(n, _):
        take_halo(cg, 1, n)
        for k in range(piece // 128):
            lanes = pl.ds(k * 128, 128)
            weights = [hk_ref[2 * n + c, t : t + 1, lanes] for t in range(9)]

            def row(r, sums):
                out = conv_row(
                    lambda i: (cg[n, r + i, 0, :, lanes].astype(F32), cg[n, r + i, 1, :, lanes].astype(F32)),
                    weights,
                    True,
                )
                low = [out[p].astype(BF16) for p in range(2)]
                for p in range(2):
                    eg[2 * r + p, :, lanes] = low[p]
                g0 = cg[n, r + 1, 0, :, lanes].astype(F32)
                g1 = cg[n, r + 1, 1, :, lanes].astype(F32)
                new = []
                for i in range(3):
                    even = ex[n, r + i, 0, :, lanes].astype(F32)
                    odd = ex[n, r + i, 1, :, lanes].astype(F32)
                    odd_m, even_p = shifts(even, odd)
                    new.append(sums[3 * i] + fold(odd_m * g0 + even * g1))
                    new.append(sums[3 * i + 1] + fold(even * g0 + odd * g1))
                    new.append(sums[3 * i + 2] + fold(odd * g0 + even_p * g1))
                new.append(sums[9] + fold(low[0].astype(F32) + low[1].astype(F32)))
                return tuple(new)

            sums = lax.fori_loop(
                0, chip_rows, row, tuple(jnp.zeros((8, 128), F32) for _ in range(10))
            )
            for t in range(10):
                hkg_ref[n, t : t + 1, lanes] = jnp.sum(sums[t], axis=0, keepdims=True)
        full = eg[...].reshape(chip_rows * 32, piece)
        for t in range(tiles):
            y = lax.dot_general(
                full[t * 128 : t * 128 + 128], we[n], NT, preferred_element_type=F32
            )
            y = y.reshape(8, 16, width)
            spot = (t // 2, pl.ds((t % 2) * 8, 8))

            @pl.when(n == 0)
            def _():
                sg[spot] = y

            @pl.when(n > 0)
            def _():
                sg[spot] += y

        ew_ref[n] = lax.dot_general(
            sc[...].reshape(chip_rows * 32, width), full, TN, preferred_element_type=F32
        ).astype(BF16)
        return 0

    lax.fori_loop(0, chips, backward, 0)
    sg_copy = rcopy(sg.at[1 - c], sg_in, x_s.at[3], x_r.at[3], sibling)
    sg_copy.start()
    b2_copy.wait_recv()
    sg_copy.wait_recv()
    bias2 = rb_ref[...]

    def finish(r, _):
        for p in range(2):
            rp = 2 * r + p
            grad = sg[c, rp] + sg_in[rp]
            v = res[rp]
            n, inv = ln_parts(v)
            branch = b1[rp]
            up = ctd[rp].astype(F32)
            acc[1] += grad
            acc[2] += grad * n
            inner = grad * scale2
            mean0 = jnp.mean(inner, axis=-1, keepdims=True)
            mean1 = jnp.mean(inner * n, axis=-1, keepdims=True)
            total = up + inv * (inner - mean0 - n * mean1)
            rg_ref[rp] = total
            acc[3] += total * branch
            one = (total * gate1).astype(BF16)
            og_ref[lax.rem(rp, 4), rp // 4] = one
            acc[4] += one.astype(F32)
            branch2 = b2[c, rp] + b2_in[rp] + bias2
            acc[5] += up * branch2
            y = v + gate2 * branch2
            for k in range(width // 128):
                cotf[r, k, pl.ds(p, 16, stride=2), :] = y[:, k * 128 : k * 128 + 128]
        out_ref[r] = jnp.concatenate(
            [cotf[r, k] for k in range(width // 128)], axis=-1
        ).astype(BF16)
        return 0

    lax.fori_loop(0, rows, finish, 0)

    def halves(x):
        return jnp.concatenate(
            [jnp.sum(x[0:8], axis=0, keepdims=True), jnp.sum(x[8:16], axis=0, keepdims=True)], axis=0
        )

    mg_ref[0] = halves(acc[3])
    mg_ref[1] = halves(acc[1])
    mg_ref[2] = halves(acc[2])
    mg_ref[3] = halves(acc[5])
    sb_ref[0:1] = jnp.sum(acc[0], axis=0, keepdims=True)
    sb_ref[1:2] = jnp.sum(acc[4], axis=0, keepdims=True)

    def drain(n, _):
        drain_halo(ex, 0, n)
        drain_halo(cg, 1, n)
        return 0

    lax.fori_loop(0, chips, drain, 0)
    b2_copy.wait_send()
    sg_copy.wait_send()


def feed_forward(xd, mod, ai, wo, ob, eb, hk, rb, cot, we, wr, strips):
    rows, cols, width = cot.shape
    chips = strips // 2
    hidden = we.shape[1]
    piece = hidden // strips
    dma = pltpu.SemaphoreType.DMA
    chip_rows = 2 * rows
    blocks = 2 * rows
    shape = jax.ShapeDtypeStruct
    return pl.pallas_call(
        ffn_kernel,
        name="feed_forward",
        out_shape=(
            shape((rows, cols, width), BF16),
            shape((blocks, 16, width), F32),
            shape((4, rows // 2, 16, width), BF16),
            shape((chips, piece, width), BF16),
            shape((chips, width, piece), BF16),
            shape((chips, 16, piece), F32),
            shape((4, 2, width), F32),
            shape((2, width), F32),
        ),
        in_specs=[WHOLE] * 9 + [LEFT] * 2,
        out_specs=(WHOLE,) * 8,
        scratch_shapes=[
            pltpu.VMEM((chips, width, piece), BF16),
            pltpu.VMEM((chips, piece, width), BF16),
            pltpu.VMEM((2, blocks, 16, width), BF16),
            pltpu.VMEM((2, blocks, 16, width), BF16),
            pltpu.VMEM((chips, chip_rows + 2, 2, 16, piece), BF16),
            pltpu.VMEM((chips, chip_rows + 2, 2, 16, piece), BF16),
            pltpu.VMEM((2 * blocks, 16, piece), BF16),
            pltpu.VMEM((2 * blocks, 16, piece), F32),
            pltpu.VMEM((2 * blocks, 16, piece), BF16),
            pltpu.VMEM((2, blocks, 16, width), F32),
            pltpu.VMEM((2, blocks, 16, width), F32),
            pltpu.VMEM((blocks, 16, width), F32),
            pltpu.VMEM((blocks, 16, width), F32),
            pltpu.VMEM((blocks, 16, width), F32),
            pltpu.VMEM((blocks, 16, width), F32),
            pltpu.VMEM((blocks, 16, width), BF16),
            pltpu.VMEM((rows, width // 128, cols, 128), F32),
            pltpu.VMEM((6, 16, width), F32),
            dma((2, chips)),
            dma((4,)),
            dma((4,)),
            dma((2, 2, chips)),
            dma((2, 2, chips)),
            dma((2,)),
            dma((2,)),
        ],
        compiler_params=pltpu.CompilerParams(
            collective_id=1, has_side_effects=True, vmem_limit_bytes=VMEM_BYTES
        ),
    )(xd, mod, ai, wo, ob, eb, hk, rb, cot, we, wr)


def attend_back_kernel(
    og_ref, qkv_ref, p_ref, ag_ref, mg_ref, fp_ref, xd_ref, rg_ref, mod_ref, mk_ref, wo_ref, wj_hbm,
    tg_ref, jo_ref, mkg_ref, m1_ref,
    wj, gg, da, ds, dqkv, mp, mp_in, md, mr, mo, fg, tkf, acc,
    wsem, g_s, g_r, f_s, f_r, p_s, p_r, b_s, b_r, hs, hr,
):
    rows, cols, width = tg_ref.shape
    half = width // 2
    strips = lax.axis_size("strip")
    chips = strips // 2
    s = lax.axis_index("strip")
    z = s // 2
    c = lax.rem(s, 2)
    sibling = 2 * z + 1 - c
    total = strips * 64

    wcopies = []
    for part in range(3):
        off = pl.multiple_of(part * width + c * half, 128)
        cp = pltpu.make_async_copy(wj_hbm.at[:, pl.ds(off, half)], wj.at[part], wsem.at[part])
        cp.start()
        wcopies.append(cp)
    strip_barrier(strips)

    gathers = []
    for d in range(1, chips):
        g = lax.rem(z + d, chips)
        cp = rcopy(og_ref.at[g], gg.at[s], g_s.at[d], g_r.at[d], 2 * g + c)
        cp.start()
        gathers.append(cp)
    gg[s] = og_ref[z]
    forwards = []
    for d in range(chips):
        i = 2 * lax.rem(z - d + chips, chips) + c
        if d:
            rcopy(og_ref.at[z], gg.at[i], g_s.at[d], g_r.at[d], i).wait_recv()
        cp = rcopy(gg.at[i], gg.at[i], f_s.at[d], f_r.at[d], sibling)
        cp.start()
        forwards.append(cp)
    for d in range(chips):
        i = 2 * lax.rem(z - d + chips, chips) + 1 - c
        rcopy(gg.at[i], gg.at[i], f_s.at[d], f_r.at[d], sibling).wait_recv()

    wo_own = wo_ref[pl.ds(pl.multiple_of(c * half, 128), half), :]

    def attended_grad(t, _):
        x = gg[pl.ds(2 * t, 2)].reshape(128, width)
        y = lax.dot_general(x, wo_own, NT, preferred_element_type=F32).astype(BF16)
        for n in range(3):
            da[n, pl.ds(pl.multiple_of(t * 128, 128), 128), :] = y[:, n * 128 : n * 128 + 128]
        return 0

    lax.fori_loop(0, chips, attended_grad, 0)

    lane = lax.broadcasted_iota(jnp.int32, (128, 128), 1) < 64
    lanes_all = lax.broadcasted_iota(jnp.int32, (total, 128), 1) < 64
    factor = 64 ** -0.5
    for n in range(3):

        def tile(t, _):
            rws = pl.ds(pl.multiple_of(t * 128, 128), 128)
            d2 = da[n, rws, :]
            keys = qkv_ref[3 + n]
            values = qkv_ref[6 + n]
            outs = []
            for h in range(2):
                dh = jnp.where(lane if h == 0 else jnp.logical_not(lane), d2, jnp.zeros_like(d2))
                dp = lax.dot_general(dh, values, NT, preferred_element_type=F32)
                probs = p_ref[n, h, rws, :].astype(F32)
                inner = jnp.sum(probs * dp, axis=-1, keepdims=True)
                grad = (probs * (dp - inner)).astype(BF16)
                ds[h, rws, :] = grad
                outs.append(jnp.dot(grad, keys, preferred_element_type=F32))
            dqkv[n, rws, :] = (jnp.where(lane, outs[0], outs[1]) * factor).astype(BF16)
            return 0

        lax.fori_loop(0, 4, tile, 0)
        q2 = qkv_ref[n]
        d2 = da[n]
        dk = [lax.dot_general(ds[h], q2, TN, preferred_element_type=F32) for h in range(2)]
        dqkv[3 + n] = (jnp.where(lanes_all, dk[0], dk[1]) * factor).astype(BF16)
        dv = [lax.dot_general(p_ref[n, h], d2, TN, preferred_element_type=F32) for h in range(2)]
        dqkv[6 + n] = jnp.where(lanes_all, dv[0], dv[1]).astype(BF16)

    for part in range(3):
        wcopies[part].wait()

    def joined(part, rws):
        return jnp.concatenate([dqkv[3 * part + n, rws, :] for n in range(3)], axis=-1)

    def partial(core):
        def body(i, _):
            rws = pl.ds(pl.multiple_of((2 * i + core) * 64, 64), 64)
            y = None
            for part in range(3):
                w = lax.dot_general(joined(part, rws), wj[part], NT, preferred_element_type=F32)
                y = w if y is None else y + w
            mp[core, i] = y
            return 0

        lax.fori_loop(0, chips, body, 0)

    partial(1 - c)
    mp_copy = rcopy(mp.at[1 - c], mp_in, p_s.at[0], p_r.at[0], sibling)
    mp_copy.start()
    partial(c)
    mp_copy.wait_recv()
    backs = []
    for d in range(chips):
        i = lax.rem(z + d, chips)
        low = (mp[c, i] + mp_in[i]).astype(BF16).reshape(rows // 2, 16, width)
        if d:
            mo[i] = low
            cp = rcopy(mo.at[i], mr.at[z], b_s.at[d], b_r.at[d], 2 * i + c)
            cp.start()
            backs.append(cp)
        else:
            mr[z] = low

    def joint_grad(part, _):
        x = mg_ref[...].reshape(total, width)
        y = lax.dot_general(x, joined(part, slice(None)), TN, preferred_element_type=F32)
        jo_ref[part] = y.astype(BF16).reshape(jo_ref.shape[1:])
        return 0

    lax.fori_loop(0, 3, joint_grad, 0)
    own = gg[:, :, :, pl.ds(pl.multiple_of(c * half, 128), half)].reshape(total, half)
    full = jnp.concatenate([ag_ref[n] for n in range(6)], axis=-1)
    y = lax.dot_general(full, own, TN, preferred_element_type=F32)
    jo_ref[3] = y.astype(BF16).reshape(jo_ref.shape[1:])

    for d in range(1, chips):
        i = lax.rem(z - d + chips, chips)
        rcopy(mo.at[i], mr.at[i], b_s.at[d], b_r.at[d], 2 * i + c).wait_recv()
    for r in (0, rows - 1):
        for p in range(2):
            md[r + 1, p] = mr[(r % 2) * 2 + p, r // 2]
    up = rcopy(md.at[1], md.at[rows + 1], hs.at[0], hr.at[0], s - 1)
    down = rcopy(md.at[rows], md.at[0], hs.at[1], hr.at[1], s + 1)

    @pl.when(s > 0)
    def _():
        up.start()

    @pl.when(s < strips - 1)
    def _():
        down.start()

    for r in range(1, rows - 1):
        for p in range(2):
            md[r + 1, p] = mr[(r % 2) * 2 + p, r // 2]

    acc[...] = jnp.zeros_like(acc)
    scale1 = spread(1.0 + mod_ref[:, width : 2 * width], width)

    def finish_row(r):
        for k in range(width // 128):
            lanes = pl.ds(k * 128, 128)
            weights = [mk_ref[t : t + 1, k * 128 : k * 128 + 128] for t in range(9)]
            out = conv_row(
                lambda i: (md[r + i, 0, :, lanes].astype(F32), md[r + i, 1, :, lanes].astype(F32)),
                weights,
                True,
            )
            fg[0, :, lanes] = out[0]
            fg[1, :, lanes] = out[1]
            g0 = md[r + 1, 0, :, lanes].astype(F32)
            g1 = md[r + 1, 1, :, lanes].astype(F32)
            for i in range(3):
                even = fp_ref[r + i, 0, :, lanes].astype(F32)
                odd = fp_ref[r + i, 1, :, lanes].astype(F32)
                odd_m, even_p = shifts(even, odd)
                acc[3 * i, :, lanes] += odd_m * g0 + even * g1
                acc[3 * i + 1, :, lanes] += even * g0 + odd * g1
                acc[3 * i + 2, :, lanes] += odd * g0 + even_p * g1
        for p in range(2):
            rp = 2 * r + p
            grad = fg[p]
            n, inv = ln_parts(xd_ref[r, p].astype(F32))
            acc[9] += grad
            acc[10] += grad * n
            inner = grad * scale1
            mean0 = jnp.mean(inner, axis=-1, keepdims=True)
            mean1 = jnp.mean(inner * n, axis=-1, keepdims=True)
            y = rg_ref[rp] + inv * (inner - mean0 - n * mean1)
            for k in range(width // 128):
                tkf[r, k, pl.ds(p, 16, stride=2), :] = y[:, k * 128 : k * 128 + 128]
        tg_ref[r] = jnp.concatenate([tkf[r, k] for k in range(width // 128)], axis=-1)

    def body(r, _):
        finish_row(r)
        return 0

    lax.fori_loop(1, rows - 1, body, 0)

    @pl.when(s > 0)
    def _():
        rcopy(md.at[1], md.at[0], hs.at[1], hr.at[1], s - 1).wait_recv()

    @pl.when(s == 0)
    def _():
        md[0] = jnp.zeros_like(md[0])

    finish_row(0)

    @pl.when(s < strips - 1)
    def _():
        rcopy(md.at[1], md.at[rows + 1], hs.at[0], hr.at[0], s + 1).wait_recv()

    @pl.when(s == strips - 1)
    def _():
        md[rows + 1] = jnp.zeros_like(md[0])

    finish_row(rows - 1)

    mkg_ref[...] = jnp.zeros_like(mkg_ref)
    for t in range(9):
        mkg_ref[t : t + 1] = jnp.sum(acc[t], axis=0, keepdims=True)

    def halves(x):
        return jnp.concatenate(
            [jnp.sum(x[0:8], axis=0, keepdims=True), jnp.sum(x[8:16], axis=0, keepdims=True)], axis=0
        )

    m1_ref[0] = halves(acc[9])
    m1_ref[1] = halves(acc[10])
    for cp in gathers + forwards + backs + [mp_copy]:
        cp.wait_send()

    @pl.when(s > 0)
    def _():
        up.wait_send()

    @pl.when(s < strips - 1)
    def _():
        down.wait_send()


def attend_back(og, qkv, probs, ag, mg, fp, xd, rg, mod, mk, wo, wj, strips):
    rows, _, _, width = xd.shape
    chips = strips // 2
    total = strips * 64
    half = width // 2
    dma = pltpu.SemaphoreType.DMA
    shape = jax.ShapeDtypeStruct
    return pl.pallas_call(
        attend_back_kernel,
        name="attend_backward",
        out_shape=(
            shape((rows, 32, width), F32),
            shape((4, chips, 2, 2, width // chips // 4, half), BF16),
            shape((16, width), F32),
            shape((2, 2, width), F32),
        ),
        in_specs=[WHOLE] * 11 + [LEFT],
        out_specs=(WHOLE,) * 4,
        scratch_shapes=[
            pltpu.VMEM((3, width, half), BF16),
            pltpu.VMEM((strips, rows // 2, 16, width), BF16),
            pltpu.VMEM((3, total, 128), BF16),
            pltpu.VMEM((2, total, total), BF16),
            pltpu.VMEM((9, total, 128), BF16),
            pltpu.VMEM((2, chips, 64, width), F32),
            pltpu.VMEM((chips, 64, width), F32),
            pltpu.VMEM((rows + 2, 2, 16, width), BF16),
            pltpu.VMEM((4, rows // 2, 16, width), BF16),
            pltpu.VMEM((4, rows // 2, 16, width), BF16),
            pltpu.VMEM((2, 16, width), F32),
            pltpu.VMEM((rows, width // 128, 32, 128), F32),
            pltpu.VMEM((11, 16, width), F32),
            dma((3,)),
            dma((chips,)),
            dma((chips,)),
            dma((chips,)),
            dma((chips,)),
            dma((1,)),
            dma((1,)),
            dma((chips,)),
            dma((chips,)),
            dma((2,)),
            dma((2,)),
        ],
        compiler_params=pltpu.CompilerParams(
            collective_id=2, has_side_effects=True, vmem_limit_bytes=VMEM_BYTES
        ),
    )(og, qkv, probs, ag, mg, fp, xd, rg, mod, mk, wo, wj)


def bcopy(src, dst, send, recv, batch, strip):
    return pltpu.make_async_remote_copy(
        src_ref=src, dst_ref=dst, send_sem=send, recv_sem=recv,
        device_id=(batch, strip), device_id_type=MESH,
    )


def block_barrier(strips):
    s = lax.axis_index("strip")
    b = lax.axis_index("batch")
    z = s // 2
    barrier = pltpu.get_barrier_semaphore()
    count = 0
    for d in range(1, strips):
        pl.semaphore_signal(
            barrier, inc=1, device_id=(b, lax.rem(s + d, strips)), device_id_type=MESH
        )
        count += 1
    for e in range(1, 4):
        for core in range(2):
            pl.semaphore_signal(
                barrier, inc=1, device_id=(lax.rem(b + e, 4), 2 * z + core), device_id_type=MESH
            )
            count += 1
    pl.semaphore_wait(barrier, count)


def reduce_kernel(
    rw_ref, ew_ref, jo_ref,
    rout_ref, eout_ref, jout_ref, oout_ref,
    r_in1, r_s1, r_in2, r_s2, r_in3, r_all,
    e_in1, e_s1, e_in2, e_s2, e_in3, e_all,
    a_in1, a_s1, a_in2, a_s2, a_in3, a_all,
    b_in1, b_s1, b_in2, b_s2, b_in3, b_all,
    s1s, s1r, s2s, s2r, s3s, s3r, s4s, s4r,
):
    strips = lax.axis_size("strip")
    chips = strips // 2
    s = lax.axis_index("strip")
    b = lax.axis_index("batch")
    z = s // 2
    c = lax.rem(s, 2)
    y, x = b // 2, lax.rem(b, 2)
    x_mate = 2 * y + 1 - x
    y_mate = 2 * (1 - y) + x
    block_barrier(strips)

    parts = [
        (0, lambda t, q: rw_ref.at[t, :, q], r_in1, r_s1, r_in2, r_s2, r_in3),
        (1, lambda t, q: ew_ref.at[:, t, q], e_in1, e_s1, e_in2, e_s2, e_in3),
        (0, lambda t, q: jo_ref.at[pl.ds(0, 2), t, :, q], a_in1, a_s1, a_in2, a_s2, a_in3),
        (1, lambda t, q: jo_ref.at[pl.ds(2, 2), t, q], b_in1, b_s1, b_in2, b_s2, b_in3),
    ]
    order = [1, 2, 3, 0]

    def mates(first):
        return (x, x_mate, y, y_mate) if first == 0 else (y, y_mate, x, x_mate)

    def step1(k, d):
        first, pick, in1 = parts[k][:3]
        mine, mate, _, _ = mates(first)
        t = lax.rem(z + d, chips)
        return bcopy(pick(t, 1 - mine), in1.at[t], s1s.at[k, d], s1r.at[k, d], mate, s)

    def step2(k, d):
        first, _, _, s1, in2 = parts[k][:5]
        _, _, other, mate = mates(first)
        t = lax.rem(z + d, chips)
        lead = (lambda q: s1.at[t, q]) if k == 0 else (lambda q: s1.at[t, :, q])
        return bcopy(lead(1 - other), in2.at[t], s2s.at[k, d], s2r.at[k, d], mate, s), lead, other

    def step3(k, d):
        _, _, _, _, _, s2, in3 = parts[k]
        t = lax.rem(z + d, chips)
        return bcopy(s2.at[t], in3.at[d], s3s.at[k, d], s3r.at[k, d], b, 2 * t + c)

    for k in range(4):
        for d in order:
            step1(k, d).start()
    for d in order:
        t = lax.rem(z + d, chips)
        for k in range(4):
            first, pick, in1, s1 = parts[k][:4]
            mine = mates(first)[0]
            step1(k, d).wait_recv()
            own = pick(t, mine)
            for i in range(2 if k != 1 else 4):
                s1[t, i] = (own[i].astype(F32) + in1[t, i].astype(F32)).astype(BF16)
            step2(k, d)[0].start()
    for d in order:
        t = lax.rem(z + d, chips)
        for k in range(4):
            s2, in2 = parts[k][5], parts[k][4]
            cp, lead, other = step2(k, d)
            cp.wait_recv()
            s2[t] = (lead(other)[...].astype(F32) + in2[t].astype(F32)).astype(BF16)
            if d:
                step3(k, d).start()
    alls = [r_all, e_all, a_all, b_all]

    def step4(k, e):
        dest = lax.rem(b + e, 4)
        if k == 0:
            return bcopy(alls[0].at[b], alls[0].at[b], s4s.at[k, e], s4r.at[k, e, c], dest, s)
        return bcopy(
            alls[k].at[2, 0], alls[k].at[x, c], s4s.at[k, e], s4r.at[k, e, c], dest, 2 * z + y
        )

    for k in range(4):
        s2, in3 = parts[k][5], parts[k][6]
        v = s2[z].astype(F32)
        for d in range(1, chips):
            step3(k, d).wait_recv()
            v = v + in3[d].astype(F32)
        if k == 0:
            alls[k][b] = v.astype(BF16)
        else:
            alls[k][2, 0] = v.astype(BF16)

            @pl.when(c == y)
            def _():
                alls[k][x, c] = v.astype(BF16)

        for e in range(1, 4):
            step4(k, e).start()
        if k:

            @pl.when(c != y)
            def _():
                step4(k, 0).start()

    for e in range(1, 4):
        step4(0, e).wait_recv()
    for q in range(4):
        n = r_all.shape[1]
        rout_ref[q * n : q * n + n] = r_all[q].astype(F32)
    for k in range(1, 4):
        for xs in range(2):
            for cs in range(2):
                source = 2 * c + xs
                e = lax.rem(b - source + 4, 4)
                local = jnp.logical_and(source == b, cs == c)

                @pl.when(jnp.logical_not(local))
                def _():
                    bcopy(
                        alls[k].at[xs, cs], alls[k].at[xs, cs], s4s.at[k, e], s4r.at[k, e, cs],
                        source, 2 * z + cs,
                    ).wait_recv()

                rows = slice(xs * 48, xs * 48 + 48)
                half = alls[k].shape[-1]
                if k == 1:
                    for n in range(4):
                        at = pl.multiple_of((2 * n + cs) * half, 128)
                        eout_ref[rows, pl.ds(at, half)] = alls[1][xs, cs, n].astype(F32)
                elif k == 2:
                    for n in range(2):
                        at = (2 * n + cs) * half
                        jout_ref[rows, at : at + half] = alls[2][xs, cs, n].astype(F32)
                else:
                    at = (4 + cs) * half
                    jout_ref[rows, at : at + half] = alls[3][xs, cs, 0].astype(F32)
                    oout_ref[rows, cs * half : cs * half + half] = alls[3][xs, cs, 1].astype(F32)
    for k in range(4):
        for d in order:
            step1(k, d).wait_send()
            step2(k, d)[0].wait_send()
            if d:
                step3(k, d).wait_send()
        for e in range(1, 4):
            step4(k, e).wait_send()
        if k:

            @pl.when(c != y)
            def _():
                step4(k, 0).wait_send()


def reduce_weights(rw, ew, jo, strips):
    chips = strips // 2
    dma = pltpu.SemaphoreType.DMA
    shape = jax.ShapeDtypeStruct
    vm = pltpu.VMEM

    def buffers(n, m, lanes, lead):
        full = (chips,) + lead
        return full

    half = ew.shape[-1]
    hidden = 8 * half
    width = 2 * half
    r = [
        vm((chips, 2, 96, width), BF16),
        vm((chips, 2, 96, width), BF16),
        vm((chips, 96, width), BF16),
        vm((chips, 96, width), BF16),
        vm((chips, 96, width), BF16),
        vm((4, 96, width), BF16),
    ]

    def cols(n):
        return [
            vm((chips, n, 2, 48, half), BF16),
            vm((chips, n, 2, 48, half), BF16),
            vm((chips, n, 48, half), BF16),
            vm((chips, n, 48, half), BF16),
            vm((chips, n, 48, half), BF16),
            vm((3, 2, n, 48, half), BF16),
        ]

    return pl.pallas_call(
        reduce_kernel,
        name="reduce_weights",
        out_shape=(
            shape((384, width), F32),
            shape((96, hidden), F32),
            shape((96, 3 * width), F32),
            shape((96, width), F32),
        ),
        in_specs=[WHOLE] * 3,
        out_specs=(WHOLE,) * 4,
        scratch_shapes=r + cols(4) + cols(2) + cols(2) + [dma((4, 4))] * 7 + [dma((4, 4, 2))],
        compiler_params=pltpu.CompilerParams(
            collective_id=3, has_side_effects=True, vmem_limit_bytes=VMEM_BYTES
        ),
    )(rw, ew, jo)


def tail_kernel(
    hkg_ref, mkg_ref, sb_ref, m1_ref, m4_ref, silu_ref, slope_ref, label_ref, slot_ref, aw_hbm,
    ag_ref, tab_ref, ab_ref, sm_ref,
    pieces, arrived, summed, amod, aw,
    wsem, s1s, s1r, s2s, s2r, m1s, m1r, m2s, m2r, m3s, m3r,
):
    strips = lax.axis_size("strip")
    chips = strips // 2
    s = lax.axis_index("strip")
    b = lax.axis_index("batch")
    z = s // 2
    c = lax.rem(s, 2)
    sibling = 2 * z + 1 - c
    width = m1_ref.shape[-1]
    own = width // strips
    weights = pltpu.make_async_copy(
        aw_hbm.at[pl.ds(pl.multiple_of(s * own, 16), own)], aw, wsem.at[0]
    )
    weights.start()
    block_barrier(strips)

    rows = [m1_ref[0], m1_ref[1], m4_ref[0], m4_ref[1], m4_ref[2], m4_ref[3]]
    rows.append(jnp.zeros((4, width), F32))
    amod[b, s] = jnp.concatenate(rows, axis=0).astype(BF16)
    copies = []
    for e in range(1, 4):
        cp = bcopy(
            amod.at[b, s], amod.at[b, s], m1s.at[e], m1r.at[e], lax.rem(b + e, 4), s
        )
        cp.start()
        copies.append(cp)

    pad = jnp.zeros((16, 128 - own), F32)
    biases = jnp.concatenate([mkg_ref[0:9], sb_ref[1:2], sb_ref[0:1], mkg_ref[11:16]], axis=0)
    for t in range(strips):
        hidden = jnp.where(c == t % 2, hkg_ref[t // 2], 0.0)
        piece = jnp.concatenate([hidden, biases[:, t * own : t * own + own], pad], axis=1)
        pieces[t] = piece.astype(BF16)
    for d in range(1, strips):
        t = lax.rem(s + d, strips)
        cp = bcopy(pieces.at[t], arrived.at[d], s1s.at[d], s1r.at[d], b, t)
        cp.start()
        copies.append(cp)

    def batch_wait(e):
        i = lax.rem(b - e + 4, 4)
        bcopy(amod.at[i, s], amod.at[i, s], m1s.at[e], m1r.at[e], i, s).wait_recv()

    for e in range(1, 4):
        batch_wait(e)
    for d in range(1, chips):
        t = 2 * lax.rem(z + d, chips) + c
        cp = bcopy(amod.at[:, s], amod.at[:, s], m2s.at[d], m2r.at[d], b, t)
        cp.start()
        copies.append(cp)
    for d in range(chips):
        i = 2 * lax.rem(z - d + chips, chips) + c
        if d:
            bcopy(amod.at[:, i], amod.at[:, i], m2s.at[d], m2r.at[d], b, i).wait_recv()
        cp = bcopy(amod.at[:, i], amod.at[:, i], m3s.at[d], m3r.at[d], b, sibling)
        cp.start()
        copies.append(cp)

    total = pieces[s].astype(F32)
    for d in range(1, strips):
        bcopy(pieces.at[0], arrived.at[d], s1s.at[d], s1r.at[d], b, s).wait_recv()
        total = total + arrived[d].astype(F32)
    summed[b] = total.astype(BF16)
    for e in range(1, 4):
        cp = bcopy(summed.at[b], summed.at[b], s2s.at[e], s2r.at[e], lax.rem(b + e, 4), s)
        cp.start()
        copies.append(cp)

    for d in range(chips):
        i = 2 * lax.rem(z - d + chips, chips) + 1 - c
        bcopy(amod.at[:, i], amod.at[:, i], m3s.at[d], m3r.at[d], b, sibling).wait_recv()

    weights.wait()
    count = 4 * strips * 16
    slots = silu_ref.shape[0]
    flat = amod[...].reshape(count, width)
    column = lax.broadcasted_iota(jnp.int32, (slots, count), 1)
    hit = lax.broadcasted_iota(jnp.int32, (slots, count), 0) == slot_ref[...]
    silu_grad = jnp.zeros((slots, own), F32)
    for m in range(6):
        chosen = jnp.logical_and(hit, lax.rem(column, 16) // 2 == m)
        chosen = jnp.where(chosen, 1.0, 0.0).astype(BF16)
        grad = jnp.dot(chosen, flat, preferred_element_type=F32)
        ab_ref[m : m + 1] = jnp.sum(grad, axis=0, keepdims=True)
        low = grad.astype(BF16)
        lanes = slice(m * width, m * width + width)
        ag_ref[:, lanes] = lax.dot_general(silu_ref[...], low, TN, preferred_element_type=F32)
        silu_grad = silu_grad + lax.dot_general(low, aw[:, lanes], NT, preferred_element_type=F32)
    grad = silu_grad * slope_ref[...]
    classes = tab_ref.shape[1]
    onehot = lax.broadcasted_iota(jnp.int32, (slots, classes), 1) == label_ref[...]
    tab_ref[...] = lax.dot_general(
        grad, jnp.where(onehot, 1.0, 0.0), TN,
        precision=lax.Precision.HIGHEST, preferred_element_type=F32,
    )

    total = summed[b].astype(F32)
    for e in range(1, 4):
        i = lax.rem(b - e + 4, 4)
        bcopy(summed.at[i], summed.at[i], s2s.at[e], s2r.at[e], i, s).wait_recv()
        total = total + summed[i].astype(F32)
    sm_ref[...] = total
    for cp in copies:
        cp.wait_send()


def tail(hkg, mkg, sb, m1, m4, silu, slope, labels, slot, aw, classes, strips):
    width = m1.shape[-1]
    chips = strips // 2
    own = width // strips
    dma = pltpu.SemaphoreType.DMA
    shape = jax.ShapeDtypeStruct
    return pl.pallas_call(
        tail_kernel,
        name="tail",
        out_shape=(
            shape((own, 6 * width), F32),
            shape((own, classes), F32),
            shape((6, width), F32),
            shape((16, 512), F32),
        ),
        in_specs=[WHOLE] * 9 + [LEFT],
        out_specs=(WHOLE,) * 4,
        scratch_shapes=[
            pltpu.VMEM((strips, 16, 512), BF16),
            pltpu.VMEM((strips, 16, 512), BF16),
            pltpu.VMEM((4, 16, 512), BF16),
            pltpu.VMEM((4, strips, 16, width), BF16),
            pltpu.VMEM((own, 6 * width), BF16),
            dma((1,)),
            dma((strips,)),
            dma((strips,)),
            dma((4,)),
            dma((4,)),
            dma((4,)),
            dma((4,)),
            dma((chips,)),
            dma((chips,)),
            dma((chips,)),
            dma((chips,)),
        ],
        compiler_params=pltpu.CompilerParams(
            collective_id=4, has_side_effects=True, vmem_limit_bytes=VMEM_BYTES
        ),
    )(hkg, mkg, sb, m1, m4, silu, slope, labels, slot, aw)


def timestep_features(time_steps, model_width):
    half_width = model_width // 2
    frequencies = jnp.exp(
        -math.log(10000.0) * jnp.arange(half_width, dtype=F32) / half_width
    )
    angles = time_steps.astype(F32)[..., None] * frequencies
    return jnp.concatenate([jnp.cos(angles), jnp.sin(angles)], axis=-1)


def local_grouped(
    tokens, tile_owner, time_steps, class_labels, class_embedding_matrix, adaptive_weight,
    adaptive_bias, mixer_kernel, joint_weight, output_weight, output_bias, expand_weight,
    expand_bias, hidden_kernel, reduce_weight, reduce_bias, output_cotangent,
):
    _, rows, cols, width = tokens.shape
    strips = lax.axis_size("strip")
    s = lax.axis_index("strip")
    classes = class_embedding_matrix.shape[1]
    latents = time_steps.shape[1]
    own = width // strips
    piece = expand_weight.shape[1] // strips
    owner = tile_owner[0].reshape(-1)

    numbers = lax.all_gather(
        jnp.concatenate([time_steps[0], class_labels[0], owner]), "batch", axis=0
    )
    onehot = (class_labels[0][:, None] == jnp.arange(classes, dtype=jnp.int32)).astype(BF16)
    condition = timestep_features(time_steps[0], width) + jnp.einsum(
        "bn,dn->bd", onehot, class_embedding_matrix, preferred_element_type=F32
    )
    silu_cond = jax.nn.silu(condition).astype(BF16)
    modulation = jnp.dot(silu_cond, adaptive_weight, preferred_element_type=F32)
    modulation = modulation + adaptive_bias.astype(F32)
    pair = lax.dynamic_slice_in_dim(owner, 2 * (s * rows // (strips * rows // 4)), 2)
    mod = jnp.dot(
        (pair[:, None] == jnp.arange(latents, dtype=jnp.int32)).astype(F32),
        modulation,
        precision=lax.Precision.HIGHEST,
    )
    mixer = mixer_kernel.T.astype(F32)
    hidden = hidden_kernel.T.astype(F32).reshape(9, strips, piece).transpose(1, 0, 2)

    xd, fp, mg, qkv, probs, ag, ai = attend(tokens[0], mod, mixer, owner, joint_weight, strips)
    out, rg, og, rw, ew, hkg, m4, sb = feed_forward(
        xd, mod, ai, output_weight, output_bias.astype(F32)[None],
        expand_bias.astype(F32).reshape(strips, 1, piece), hidden,
        reduce_bias.astype(F32)[None], output_cotangent[0], expand_weight, reduce_weight, strips,
    )
    tg, jo, mkg, m1 = attend_back(
        og, qkv, probs, ag, mg, fp, xd, rg, mod, mixer, output_weight, joint_weight, strips
    )
    chips = strips // 2
    rout, eout, jout, oout = reduce_weights(
        rw.reshape(chips, 2, 2, piece // 4, width),
        ew.reshape(chips, chips, 2, 2, width // chips // 4, piece),
        jo,
        strips,
    )

    all_steps = numbers[:, :latents].reshape(-1)
    all_labels = numbers[:, latents : 2 * latents].reshape(-1)
    all_owner = numbers[:, 2 * latents :].reshape(4, 4, 2)
    features = lax.dynamic_slice_in_dim(timestep_features(all_steps, width), s * own, own, 1)
    all_hot = (all_labels[:, None] == jnp.arange(classes, dtype=jnp.int32)).astype(BF16)
    table = lax.dynamic_slice_in_dim(class_embedding_matrix, s * own, own, 0)
    all_condition = features + jnp.einsum("bn,dn->bd", all_hot, table, preferred_element_type=F32)
    sigmoid = jax.nn.sigmoid(all_condition)
    silu_own = (all_condition * sigmoid).astype(BF16)
    slope = sigmoid * (1.0 + all_condition * (1.0 - sigmoid))
    slot = all_owner + latents * jnp.arange(4, dtype=jnp.int32)[:, None, None]
    slot = jnp.broadcast_to(slot[:, :, None, None, :], (4, 4, strips // 4, 8, 2)).reshape(1, -1)
    adaptive, table_grad, bias, small = tail(
        hkg, mkg, sb, m1, m4, silu_own, slope, all_labels[:, None], slot, adaptive_weight,
        classes, strips,
    )
    bias = lax.dynamic_slice_in_dim(bias.reshape(-1), s * 6 * own, 6 * own)
    return (
        out[None],
        tg[None],
        table_grad,
        adaptive,
        bias,
        small[:9, piece : piece + own].T,
        jout,
        oout,
        small[9, piece : piece + own],
        eout,
        small[9, :piece],
        small[:9, :piece].T,
        rout,
        small[10, piece : piece + own],
    )


EXACT_PRECISION = lax.Precision.HIGHEST


def padded_2(block, sides, width):
    for axis, dim in sides:
        count = lax.axis_size(axis)
        forward = [(i, i + 1) for i in range(count - 1)]
        backward = [(target, source) for source, target in forward]
        low = lax.ppermute(
            lax.slice_in_dim(block, block.shape[dim] - width, None, axis=dim), axis, forward
        )
        high = lax.ppermute(lax.slice_in_dim(block, 0, width, axis=dim), axis, backward)
        block = jnp.concatenate([low, block, high], axis=dim)
    return block


def normalize(values):
    centre = jnp.mean(values, axis=-1, keepdims=True)
    centred = values - centre
    spread = jnp.mean(centred * centred, axis=-1, keepdims=True)
    return centred * lax.rsqrt(spread + EPSILON)


def modulate(values, shifting, scaling):
    return normalize(values) * (1.0 + scaling) + shifting


def depthwise(padded, kernel):
    row_count = padded.shape[-3] - 2
    column_total = padded.shape[-2]
    widened = jnp.pad(padded, [(0, 0)] * (padded.ndim - 2) + [(1, 1), (0, 0)])
    result = jnp.zeros(
        padded.shape[:-3] + (row_count, column_total, padded.shape[-1]), padded.dtype
    )
    for tapping in range(9):
        row_shift = tapping // 3
        col_shift = tapping % 3
        window = lax.slice_in_dim(widened, row_shift, row_shift + row_count, axis=widened.ndim - 3)
        window = lax.slice_in_dim(
            window, col_shift, col_shift + column_total, axis=widened.ndim - 2
        )
        result = result + kernel[:, tapping] * window
    return result


def kernel_grad(padded, gradient):
    row_count = gradient.shape[1]
    column_total = gradient.shape[2]
    widened = jnp.pad(padded, ((0, 0), (0, 0), (1, 1), (0, 0)))
    columns = []
    for tapping in range(9):
        row_shift = tapping // 3
        col_shift = tapping % 3
        window = widened[
            :, row_shift : row_shift + row_count, col_shift : col_shift + column_total, :
        ]
        columns.append(jnp.sum(window * gradient, axis=(0, 1, 2)))
    return jnp.stack(columns, axis=1)


def group_owner(owner):
    canvases, row_count, column_total = owner.shape
    shaped = owner.reshape(canvases, row_count // 2, 2, column_total // 2, 2).transpose(
        0, 2, 4, 1, 3
    )
    return shaped.reshape(canvases, 2, 2, row_count // 2 * (column_total // 2))


def to_groups(tensor, head_count):
    canvases, row_count, column_total, features = tensor.shape
    head_size = features // head_count
    shaped = tensor.reshape(
        canvases, row_count // 2, 2, column_total // 2, 2, head_count, head_size
    )
    shaped = shaped.transpose(0, 2, 4, 5, 1, 3, 6)
    return shaped.reshape(
        canvases, 2, 2, head_count, row_count // 2 * (column_total // 2), head_size
    )


def from_groups(tensor, row_count, column_total):
    canvases, head_count, head_size = (tensor.shape[0], tensor.shape[3], tensor.shape[-1])
    shaped = tensor.reshape(
        canvases, 2, 2, head_count, row_count // 2, column_total // 2, head_size
    )
    shaped = shaped.transpose(0, 4, 1, 5, 2, 3, 6)
    return shaped.reshape(canvases, row_count, column_total, head_count * head_size)


def local(
    tokens,
    tile_owner,
    time_steps,
    class_labels,
    class_embedding_matrix,
    adaptive_weight,
    adaptive_bias,
    mixer_kernel,
    joint_weight,
    output_weight,
    output_bias,
    expand_weight,
    expand_bias,
    hidden_kernel,
    reduce_weight,
    reduce_bias,
    output_cotangent,
):
    canvases, row_count, column_total, model_width = tokens.shape
    head_count = HEADS
    head_size = model_width // head_count
    factor = head_size ** (-0.5)
    half_cols = column_total // 2
    strips = lax.axis_size("strip")
    strip_index = lax.axis_index("strip")
    canvas_rows = row_count * strips
    class_count = class_embedding_matrix.shape[1]
    latent_count = time_steps.shape[1]
    tile_rows = canvas_rows // 4
    full_owner = jnp.broadcast_to(
        tile_owner[:, :, None, :, None], (canvases, 4, tile_rows, 2, half_cols)
    ).reshape(canvases, canvas_rows, column_total)
    local_owner = lax.dynamic_slice_in_dim(full_owner, strip_index * row_count, row_count, 1)
    token_hot = (local_owner[..., None] == jnp.arange(latent_count, dtype=jnp.int32)).astype(
        jnp.float32
    )
    class_onehot = (class_labels[..., None] == jnp.arange(class_count, dtype=jnp.int32)).astype(
        jnp.bfloat16
    )
    class_rows = jnp.einsum(
        "ywj,gj->ywg", class_onehot, class_embedding_matrix, preferred_element_type=jnp.float32
    )
    condition = timestep_features(time_steps, model_width) + class_rows
    silu_value, silu_pull = jax.vjp(jax.nn.silu, condition)
    silu_cond = silu_value.astype(jnp.bfloat16)
    modulation = jnp.einsum(
        "cbd,de->cbe", silu_cond, adaptive_weight, preferred_element_type=jnp.float32
    )
    modulation = modulation + adaptive_bias.astype(jnp.float32)
    token_mod = jnp.einsum("crkb,cbe->crke", token_hot, modulation, precision=EXACT_PRECISION)
    shift_one, scale_one, gate_one, shift_two, scale_two, gate_two = jnp.split(
        token_mod, 6, axis=-1
    )
    inputs = tokens.astype(jnp.float32)
    first_value, first_pull = jax.vjp(modulate, inputs, shift_one, scale_one)
    first = first_value.astype(jnp.bfloat16)
    first_padded = padded_2(first, (("strip", 1),), 1)
    mixer_single_float = mixer_kernel.astype(jnp.float32)
    mixed = depthwise(first_padded.astype(jnp.float32), mixer_single_float).astype(jnp.bfloat16)
    joint = jnp.einsum("crkd,de->crke", mixed, joint_weight, preferred_element_type=jnp.float32)
    query_rows = joint[..., :model_width].astype(jnp.bfloat16)
    keys_local = joint[..., model_width : 2 * model_width].astype(jnp.bfloat16)
    values_local = joint[..., 2 * model_width :].astype(jnp.bfloat16)
    keys_canvas, values_canvas = (
        lax.all_gather(keys_local, "strip", axis=1, tiled=True),
        lax.all_gather(values_local, "strip", axis=1, tiled=True),
    )
    query_groups = to_groups(query_rows, head_count)
    key_groups = to_groups(keys_canvas, head_count)
    value_groups = to_groups(values_canvas, head_count)
    query_owner = group_owner(local_owner)
    key_owner = group_owner(full_owner)
    allowed = (query_owner[..., :, None] == key_owner[..., None, :])[:, :, :, None]

    def attention_scores():
        raw = (
            jnp.einsum(
                "cabhnd,cabhmd->cabhnm",
                query_groups,
                key_groups,
                preferred_element_type=jnp.float32,
            )
            * factor
        )
        return jnp.where(allowed, raw, MASKED)

    scores = attention_scores()
    peak = jnp.max(scores, axis=-1, keepdims=True)
    lifted_float = jnp.exp(scores - peak)
    total = jnp.sum(lifted_float, axis=-1, keepdims=True)
    softened = (lifted_float / total).astype(jnp.bfloat16)
    log_total = peak + jnp.log(total)
    attended_groups = jnp.einsum(
        "cabhnm,cabhmd->cabhnd", softened, value_groups, preferred_element_type=jnp.float32
    )
    attended = from_groups(attended_groups, row_count, column_total).astype(jnp.bfloat16)
    branch_one = jnp.einsum(
        "crkd,de->crke", attended, output_weight, preferred_element_type=jnp.float32
    )
    branch_one = branch_one + output_bias.astype(jnp.float32)
    residual = inputs + gate_one * branch_one
    second_value, second_pull = jax.vjp(modulate, residual, shift_two, scale_two)
    second = second_value.astype(jnp.bfloat16)
    expanded = jnp.einsum(
        "crkd,df->crkf", second, expand_weight, preferred_element_type=jnp.float32
    )
    expanded = (expanded + expand_bias.astype(jnp.float32)).astype(jnp.bfloat16)
    expanded_padded = padded_2(expanded, (("strip", 1),), 1)
    hidden_float = hidden_kernel.astype(jnp.float32)
    conv_out = depthwise(expanded_padded.astype(jnp.float32), hidden_float)
    gelu_value, gelu_pull = jax.vjp(jax.nn.gelu, conv_out)
    activated = gelu_value.astype(jnp.bfloat16)
    branch_two = jnp.einsum(
        "crkf,fd->crkd", activated, reduce_weight, preferred_element_type=jnp.float32
    )
    branch_two = branch_two + reduce_bias.astype(jnp.float32)
    outputs = (residual + gate_two * branch_two).astype(jnp.bfloat16)
    upstream = output_cotangent.astype(jnp.float32)
    two_grad = (upstream * gate_two).astype(jnp.bfloat16)
    gate_two_grad = upstream * branch_two
    reduce_bias_grad = jnp.sum(two_grad.astype(jnp.float32), axis=(0, 1, 2))
    reduce_weight_grad = jnp.einsum(
        "crkf,crkd->fd", activated, two_grad, preferred_element_type=jnp.float32
    )
    activated_grad = jnp.einsum(
        "crkd,fd->crkf", two_grad, reduce_weight, preferred_element_type=jnp.float32
    )
    conv_grad = gelu_pull(activated_grad)[0].astype(jnp.bfloat16)
    conv_padded = padded_2(conv_grad, (("strip", 1),), 1)
    expanded_grad = depthwise(conv_padded.astype(jnp.float32), hidden_float[:, ::-1]).astype(
        jnp.bfloat16
    )
    hidden_kernel_grad = kernel_grad(
        expanded_padded.astype(jnp.float32), conv_grad.astype(jnp.float32)
    )
    expand_bias_grad = jnp.sum(expanded_grad.astype(jnp.float32), axis=(0, 1, 2))
    expand_weight_grad = jnp.einsum(
        "crkd,crkf->df", second, expanded_grad, preferred_element_type=jnp.float32
    )
    second_grad = jnp.einsum(
        "crkf,df->crkd", expanded_grad, expand_weight, preferred_element_type=jnp.float32
    )
    residual_part, shift_two_grad, scale_two_grad = second_pull(second_grad)
    residual_grad = upstream + residual_part
    gate_one_grad = residual_grad * branch_one
    one_grad = (residual_grad * gate_one).astype(jnp.bfloat16)
    output_bias_grad = jnp.sum(one_grad.astype(jnp.float32), axis=(0, 1, 2))
    output_weight_grad = jnp.einsum(
        "crkd,crke->de", attended, one_grad, preferred_element_type=jnp.float32
    )
    attended_grad = jnp.einsum(
        "crke,de->crkd", one_grad, output_weight, preferred_element_type=jnp.float32
    ).astype(jnp.bfloat16)
    attended_grad_groups = to_groups(attended_grad, head_count)
    probs = jnp.exp(attention_scores() - log_total)
    prob_grads = jnp.einsum(
        "cabhnd,cabhmd->cabhnm",
        attended_grad_groups,
        value_groups,
        preferred_element_type=jnp.float32,
    )
    spread_sum = jnp.sum(probs * prob_grads, axis=-1, keepdims=True)
    score_grads = (probs * (prob_grads - spread_sum)).astype(jnp.bfloat16)
    query_grad_groups = (
        jnp.einsum(
            "cabhnm,cabhmd->cabhnd", score_grads, key_groups, preferred_element_type=jnp.float32
        )
        * factor
    )
    query_grad = from_groups(query_grad_groups, row_count, column_total).astype(jnp.bfloat16)
    all_queries, all_attended = (
        lax.all_gather(query_groups, "strip", axis=4, tiled=True),
        lax.all_gather(attended_grad_groups, "strip", axis=4, tiled=True),
    )
    all_logs, all_spreads = (
        lax.all_gather(log_total[..., 0], "strip", axis=4, tiled=True),
        lax.all_gather(spread_sum[..., 0], "strip", axis=4, tiled=True),
    )
    own_keys = to_groups(keys_local, head_count)
    own_values = to_groups(values_local, head_count)
    own_allowed = (key_owner[..., :, None] == query_owner[..., None, :])[:, :, :, None]
    own_scores = (
        jnp.einsum(
            "cabhnd,cabhmd->cabhnm", all_queries, own_keys, preferred_element_type=jnp.float32
        )
        * factor
    )
    own_scores = jnp.where(own_allowed, own_scores, MASKED)
    own_probs = jnp.exp(own_scores - all_logs[..., None])
    own_prob_grads = jnp.einsum(
        "cabhnd,cabhmd->cabhnm", all_attended, own_values, preferred_element_type=jnp.float32
    )
    own_score_grads = (own_probs * (own_prob_grads - all_spreads[..., None])).astype(jnp.bfloat16)
    key_grad_groups = (
        jnp.einsum(
            "cabhnm,cabhnd->cabhmd",
            own_score_grads,
            all_queries,
            preferred_element_type=jnp.float32,
        )
        * factor
    )
    value_grad_groups = jnp.einsum(
        "cabhnm,cabhnd->cabhmd",
        own_probs.astype(jnp.bfloat16),
        all_attended,
        preferred_element_type=jnp.float32,
    )
    key_grad = from_groups(key_grad_groups, row_count, column_total).astype(jnp.bfloat16)
    value_grad = from_groups(value_grad_groups, row_count, column_total).astype(jnp.bfloat16)
    joint_grad = jnp.concatenate([query_grad, key_grad, value_grad], axis=-1)
    joint_weight_grad = jnp.einsum(
        "crkd,crke->de", mixed, joint_grad, preferred_element_type=jnp.float32
    )
    mixed_grad = jnp.einsum(
        "crke,de->crkd", joint_grad, joint_weight, preferred_element_type=jnp.float32
    ).astype(jnp.bfloat16)
    mixed_padded = padded_2(mixed_grad, (("strip", 1),), 1)
    first_grad = depthwise(mixed_padded.astype(jnp.float32), mixer_single_float[:, ::-1])
    mixer_kernel_grad = kernel_grad(
        first_padded.astype(jnp.float32), mixed_grad.astype(jnp.float32)
    )
    input_part, shift_one_grad, scale_one_grad = first_pull(first_grad)
    tokens_grad = residual_grad + input_part
    token_grad = jnp.concatenate(
        [
            shift_one_grad,
            scale_one_grad,
            gate_one_grad,
            shift_two_grad,
            scale_two_grad,
            gate_two_grad,
        ],
        axis=-1,
    )
    modulation_grad = jnp.einsum("crkb,crke->cbe", token_hot, token_grad, precision=EXACT_PRECISION)
    silu_grad = jnp.einsum(
        "cbe,de->cbd",
        modulation_grad,
        adaptive_weight.astype(jnp.float32),
        precision=EXACT_PRECISION,
    )
    conditioning_grad = silu_pull(silu_grad)[0]
    table_grad = jnp.einsum(
        "soy,sok->yk",
        conditioning_grad,
        class_onehot.astype(jnp.float32),
        precision=EXACT_PRECISION,
    )
    adaptive_grad = jnp.einsum(
        "cbd,cbe->de", silu_cond.astype(jnp.float32), modulation_grad, precision=EXACT_PRECISION
    )
    adaptive_bias_grad = jnp.sum(modulation_grad, axis=(0, 1))
    (
        table_shard,
        adaptive_shard,
        adaptive_bias_shard,
        mixer_shard,
        joint_shard,
        output_shard,
        output_bias_shard,
        expand_shard,
        expand_bias_shard,
        hidden_shard,
        reduce_shard,
        reduce_bias_shard,
    ) = (
        lax.psum_scatter(
            table_grad.astype(jnp.bfloat16), "strip", scatter_dimension=0, tiled=True
        ).astype(jnp.float32),
        lax.psum_scatter(
            adaptive_grad.astype(jnp.bfloat16), "strip", scatter_dimension=0, tiled=True
        ).astype(jnp.float32),
        lax.psum_scatter(
            adaptive_bias_grad.astype(jnp.bfloat16), "strip", scatter_dimension=0, tiled=True
        ).astype(jnp.float32),
        lax.psum_scatter(
            mixer_kernel_grad.astype(jnp.bfloat16), "strip", scatter_dimension=0, tiled=True
        ).astype(jnp.float32),
        lax.psum_scatter(
            joint_weight_grad.astype(jnp.bfloat16), "strip", scatter_dimension=0, tiled=True
        ).astype(jnp.float32),
        lax.psum_scatter(
            output_weight_grad.astype(jnp.bfloat16), "strip", scatter_dimension=0, tiled=True
        ).astype(jnp.float32),
        lax.psum_scatter(
            output_bias_grad.astype(jnp.bfloat16), "strip", scatter_dimension=0, tiled=True
        ).astype(jnp.float32),
        lax.psum_scatter(
            expand_weight_grad.astype(jnp.bfloat16), "strip", scatter_dimension=0, tiled=True
        ).astype(jnp.float32),
        lax.psum_scatter(
            expand_bias_grad.astype(jnp.bfloat16), "strip", scatter_dimension=0, tiled=True
        ).astype(jnp.float32),
        lax.psum_scatter(
            hidden_kernel_grad.astype(jnp.bfloat16), "strip", scatter_dimension=0, tiled=True
        ).astype(jnp.float32),
        lax.psum_scatter(
            reduce_weight_grad.astype(jnp.bfloat16), "strip", scatter_dimension=0, tiled=True
        ).astype(jnp.float32),
        lax.psum_scatter(
            reduce_bias_grad.astype(jnp.bfloat16), "strip", scatter_dimension=0, tiled=True
        ).astype(jnp.float32),
    )
    summed = (
        lax.psum(table_shard.astype(jnp.bfloat16), "batch").astype(jnp.float32),
        lax.psum(adaptive_shard.astype(jnp.bfloat16), "batch").astype(jnp.float32),
        lax.psum(adaptive_bias_shard.astype(jnp.bfloat16), "batch").astype(jnp.float32),
        lax.psum(mixer_shard.astype(jnp.bfloat16), "batch").astype(jnp.float32),
        lax.psum(joint_shard.astype(jnp.bfloat16), "batch").astype(jnp.float32),
        lax.psum(output_shard.astype(jnp.bfloat16), "batch").astype(jnp.float32),
        lax.psum(output_bias_shard.astype(jnp.bfloat16), "batch").astype(jnp.float32),
        lax.psum(expand_shard.astype(jnp.bfloat16), "batch").astype(jnp.float32),
        lax.psum(expand_bias_shard.astype(jnp.bfloat16), "batch").astype(jnp.float32),
        lax.psum(hidden_shard.astype(jnp.bfloat16), "batch").astype(jnp.float32),
        lax.psum(reduce_shard.astype(jnp.bfloat16), "batch").astype(jnp.float32),
        lax.psum(reduce_bias_shard.astype(jnp.bfloat16), "batch").astype(jnp.float32),
    )
    return (
        outputs,
        tokens_grad,
        summed[0],
        summed[1],
        summed[2],
        summed[3],
        summed[4],
        summed[5],
        summed[6],
        summed[7],
        summed[8],
        summed[9],
        summed[10],
        summed[11],
    )


def solution(mesh):
    grouped = (mesh.shape["batch"], mesh.shape["strip"]) == (4, 8)
    return jax.shard_map(
        local_grouped if grouped else local,
        mesh=mesh,
        in_specs=(
            P("batch", "strip", None, None),
            P("batch", None, None),
            P("batch", None),
            P("batch", None),
            P(),
            P(),
            P(),
            P(),
            P(),
            P(),
            P(),
            P(),
            P(),
            P(),
            P(),
            P(),
            P("batch", "strip", None, None),
        ),
        out_specs=(
            P("batch", "strip", None, None),
            P("batch", "strip", None, None),
            P("strip", None),
            P("strip", None),
            P("strip"),
            P("strip", None),
            P("strip", None),
            P("strip", None),
            P("strip"),
            P("strip", None),
            P("strip"),
            P("strip", None),
            P("strip", None),
            P("strip"),
        ),
        check_vma=False,
    )
```

```python
import math
from types import SimpleNamespace

import jax
import jax.numpy as jnp
from jax import lax
from jax.experimental import pallas as pl
from jax.experimental.pallas import tpu as pltpu
from jax.sharding import PartitionSpec as P

HEADS = 12
EPSILON = 1e-06
MASKED = -1e30
MESH = pl.DeviceIdType.MESH
F32 = jnp.float32
BF16 = jnp.bfloat16
VMEM_BYTES = 62 * 1024 * 1024
WHOLE = pl.BlockSpec(memory_space=pltpu.VMEM)
LEFT = pl.BlockSpec(memory_space=pl.ANY)
SCALARS = pl.BlockSpec(memory_space=pltpu.SMEM)
NT = (((1,), (1,)), ((), ()))
TN = (((0,), (0,)), ((), ()))


def dot(a, b):
    return jnp.dot(a, b, preferred_element_type=F32)


def dot_nt(a, b):
    return lax.dot_general(a, b, NT, preferred_element_type=F32)


def dot_tn(a, b):
    return lax.dot_general(a, b, TN, preferred_element_type=F32)


def send_to(src, dst, sems, index, batch, strip):
    return pltpu.make_async_remote_copy(
        src_ref=src,
        dst_ref=dst,
        send_sem=sems[0].at[index],
        recv_sem=sems[1].at[index],
        device_id=(batch, strip),
        device_id_type=MESH,
    )


def entry_barrier(strips):
    s = lax.axis_index("strip")
    b = lax.axis_index("batch")
    z = s // 2
    barrier = pltpu.get_barrier_semaphore()
    count = 0
    for d in range(1, strips):
        pl.semaphore_signal(
            barrier, inc=1, device_id=(b, lax.rem(s + d, strips)), device_id_type=MESH
        )
        count += 1
    for e in range(1, 4):
        for core in range(2):
            pl.semaphore_signal(
                barrier, inc=1, device_id=(lax.rem(b + e, 4), 2 * z + core), device_id_type=MESH
            )
            count += 1
    pl.semaphore_wait(barrier, count)


def spread(mod, width):
    return jnp.concatenate(
        [jnp.broadcast_to(mod[0:1], (8, width)), jnp.broadcast_to(mod[1:2], (8, width))], axis=0
    )


def spread_columns(buffer, r, x):
    for k in range(x.shape[-1] // 128):
        buffer[r, k] = x[:, k * 128 : k * 128 + 128]


def every_second(buffer, r, p):
    return jnp.concatenate(
        [buffer[r, k, pl.ds(p, 16, stride=2), :] for k in range(buffer.shape[1])], axis=-1
    )


def interleave(buffer, r, p, x):
    for k in range(x.shape[-1] // 128):
        buffer[r, k, pl.ds(p, 16, stride=2), :] = x[:, k * 128 : k * 128 + 128]


def joined(buffer, r):
    return jnp.concatenate([buffer[r, k] for k in range(buffer.shape[1])], axis=-1)


def ln_parts(x):
    centre = jnp.mean(x, axis=-1, keepdims=True)
    centred = x - centre
    var = jnp.mean(centred * centred, axis=-1, keepdims=True)
    inv = lax.rsqrt(var + EPSILON)
    return centred * inv, inv


def ln_back(grad, n, inv):
    mean0 = jnp.mean(grad, axis=-1, keepdims=True)
    mean1 = jnp.mean(grad * n, axis=-1, keepdims=True)
    return inv * (grad - mean0 - n * mean1)


def window(load, r):
    even = load(r, 0).astype(F32)
    odd = load(r, 1).astype(F32)
    n = even.shape[0]
    j = lax.broadcasted_iota(jnp.int32, even.shape, 0)
    odd_m = jnp.where(j == 0, 0.0, pltpu.roll(odd, 1, 0))
    even_p = jnp.where(j == n - 1, 0.0, pltpu.roll(even, n - 1, 0))
    return odd_m, even, odd, even_p


def conv(rows, weights, flip):
    out = []
    for p in range(2):
        total = None
        for i in range(3):
            for j in range(3):
                t = 3 * i + j
                a = weights[8 - t if flip else t] * rows[i][p + j]
                total = a if total is None else total + a
        out.append(total)
    return out


def taps(rows, centre, sums):
    new = list(sums)
    for i in range(3):
        for j in range(3):
            a = rows[i][j] * centre[0] + rows[i][1 + j] * centre[1]
            t = 8 - (3 * i + j)
            new[t] = sums[t] + (a[0:8] + a[8:16])
    return new


def halves(x):
    return jnp.concatenate(
        [jnp.sum(x[0:8], axis=0, keepdims=True), jnp.sum(x[8:16], axis=0, keepdims=True)], axis=0
    )


def gelu_both(x):
    k0 = math.sqrt(2.0 / math.pi)
    square = x * x
    t = jnp.tanh(k0 * x * (1.0 + 0.044715 * square))
    cdf = 0.5 + 0.5 * t
    slope = cdf + (0.5 * k0) * x * (1.0 - t * t) * (1.0 + (3.0 * 0.044715) * square)
    return x * cdf, slope


def block_kernel(names, *refs):
    m = SimpleNamespace(**dict(zip(names, refs)))
    rows, cols, width = m.tok.shape
    half = width // 2
    strips = lax.axis_size("strip")
    chips = strips // 2
    chip_rows = 2 * rows
    total = strips * 64
    own = width // strips
    s = lax.axis_index("strip")
    b = lax.axis_index("batch")
    z = s // 2
    c = lax.rem(s, 2)
    sibling = 2 * z + 1 - c
    y, x = b // 2, lax.rem(b, 2)
    x_mate = 2 * y + 1 - x
    y_mate = 2 * (1 - y) + x
    sent = []

    def chip(d):
        return lax.rem(z + d, chips)

    def start(copy):
        copy.start()
        sent.append(copy)

    loads = {}

    def load(name, src, dst, index):
        loads[name] = pltpu.make_async_copy(src, dst, m.load_sem.at[index])
        loads[name].start()

    for part in range(3):
        off = pl.multiple_of(part * width + c * half, 128)
        load(f"wj{part}", m.wj_hbm.at[:, pl.ds(off, half)], m.wj.at[part], part)
    load("cot", m.cot_hbm, m.cot, 3)
    load("wo", m.wo_hbm, m.wo, 4)
    for n in range(chips):
        off = pl.multiple_of((2 * n + c) * half, 128)
        load(f"we{n}", m.we_hbm.at[:, pl.ds(off, half)], m.we.at[n], 5 + n)
        load(f"wr{n}", m.wr_hbm.at[pl.ds(off, half)], m.wr.at[n], 5 + chips + n)
    entry_barrier(strips)

    m.cond_all[b] = m.cond[...]
    for e in range(1, 4):
        start(
            send_to(m.cond_all.at[b], m.cond_all.at[b], m.cond_sem, e, lax.rem(b + e, 4), s)
        )

    def block_mod(n):
        return spread(m.mod[:, n * width : (n + 1) * width], width)

    scale1 = 1.0 + block_mod(1)
    shift1 = block_mod(0)

    def first_row(r):
        spread_columns(m.rowf, r, m.tok[r].astype(F32))
        for p in range(2):
            v = every_second(m.rowf, r, p)
            m.xd[r, p] = v.astype(BF16)
            n, _ = ln_parts(v)
            m.fp[r + 1, p] = (n * scale1 + shift1).astype(BF16)

    def edge_sends(buffer, sems):
        up = send_to(buffer.at[1], buffer.at[rows + 1], sems, 0, b, s - 1)
        down = send_to(buffer.at[rows], buffer.at[0], sems, 1, b, s + 1)
        return up, down

    def start_edges(buffer, sems):
        up, down = edge_sends(buffer, sems)

        @pl.when(s > 0)
        def _():
            up.start()

        @pl.when(s < strips - 1)
        def _():
            down.start()

    def edges_sent(buffer, sems):
        up, down = edge_sends(buffer, sems)

        @pl.when(s > 0)
        def _():
            up.wait_send()

        @pl.when(s < strips - 1)
        def _():
            down.wait_send()

    def top_edge(buffer, sems):
        @pl.when(s > 0)
        def _():
            send_to(buffer.at[1], buffer.at[0], sems, 1, b, s - 1).wait_recv()

        @pl.when(s == 0)
        def _():
            buffer[0] = jnp.zeros_like(buffer[0])

    def bottom_edge(buffer, sems):
        @pl.when(s < strips - 1)
        def _():
            send_to(buffer.at[1], buffer.at[rows + 1], sems, 0, b, s + 1).wait_recv()

        @pl.when(s == strips - 1)
        def _():
            buffer[rows + 1] = jnp.zeros_like(buffer[0])

    first_row(0)
    first_row(rows - 1)
    start_edges(m.fp, m.fp_sem)

    def body(r, _):
        first_row(r)
        return 0

    lax.fori_loop(1, rows - 1, body, 0)

    def mixed_rows(low, high):
        for k in range(width // 128):
            lanes = pl.ds(k * 128, 128)
            weights = [m.mk[t : t + 1, k * 128 : k * 128 + 128] for t in range(9)]

            def line(r, p):
                return m.fp[r, p, :, lanes]

            def step(r, carry):
                new = window(line, r + 2)
                out = conv((carry[0], carry[1], new), weights, False)
                for p in range(2):
                    m.ms[lax.rem(r, 2) * 2 + p, r // 2, :, lanes] = out[p].astype(BF16)
                return carry[1], new

            lax.fori_loop(low, high, step, (window(line, low), window(line, low + 1)))

    mixed_rows(1, rows - 1)
    top_edge(m.fp, m.fp_sem)
    mixed_rows(0, 1)
    bottom_edge(m.fp, m.fp_sem)
    mixed_rows(rows - 1, rows)

    def to_groups(source, target, sems, sems2):
        for d in range(1, chips):
            g = chip(d)
            start(send_to(source.at[g], target.at[s], sems, d, b, 2 * g + c))
        target[s] = source[z]

    def pass_on(target, sems, sems2):
        for d in range(chips):
            i = 2 * chip(chips - d) + c
            if d:
                send_to(target.at[i], target.at[i], sems, d, b, i).wait_recv()
            start(send_to(target.at[i], target.at[i], sems2, d, b, sibling))

    def groups_ready(target, sems2):
        for d in range(chips):
            i = 2 * chip(chips - d) + 1 - c
            send_to(target.at[i], target.at[i], sems2, d, b, sibling).wait_recv()

    to_groups(m.ms, m.mg, m.mg_sem, m.mg_sem2)

    m.acc[...] = jnp.zeros_like(m.acc)
    gate2 = block_mod(5)
    loads["cot"].wait()

    def upstream_row(r, _):
        spread_columns(m.rowf, r, m.cot[r].astype(F32))
        for p in range(2):
            up = every_second(m.rowf, r, p)
            m.ctd[2 * r + p] = up.astype(BF16)
            two = (up * gate2).astype(BF16)
            m.tg[c, 2 * r + p] = two
            m.acc[0] += two.astype(F32)
        return 0

    lax.fori_loop(0, rows, upstream_row, 0)
    start(send_to(m.tg.at[c], m.tg.at[c], m.pair_sem, 0, b, sibling))

    pass_on(m.mg, m.mg_sem, m.mg_sem2)
    groups_ready(m.mg, m.mg_sem2)
    for part in range(3):
        loads[f"wj{part}"].wait()

    def qkv_tile(t, _):
        v = m.mg[pl.ds(2 * t, 2)].reshape(128, width)
        for part in range(3):
            w = dot(v, m.wj[part]).astype(BF16)
            for n in range(3):
                m.qkv[3 * part + n, pl.ds(pl.multiple_of(t * 128, 128), 128), :] = w[
                    :, n * 128 : n * 128 + 128
                ]
        return 0

    lax.fori_loop(0, chips, qkv_tile, 0)

    where = lax.broadcasted_iota(jnp.int32, (1, total), 1)
    lefts = lax.rem(where, 16) < 8
    key_owner = jnp.zeros((1, total), jnp.int32)
    for t in range(4):
        both = jnp.where(lefts, m.owner[2 * t], m.owner[2 * t + 1])
        key_owner = jnp.where(where // 128 == t, both, key_owner)
    qleft = lax.rem(lax.broadcasted_iota(jnp.int32, (128, 1), 0), 16) < 8
    lane = lax.broadcasted_iota(jnp.int32, (128, 128), 1) < 64
    factor = 64 ** -0.5

    def head(v, h):
        return jnp.where(lane if h == 0 else jnp.logical_not(lane), v, jnp.zeros_like(v))

    for n in range(3):
        mine = c * 3 + n

        def attend(t, _):
            rws = pl.ds(pl.multiple_of(t * 128, 128), 128)
            owner = jnp.where(qleft, m.owner[2 * t], m.owner[2 * t + 1])
            allowed = owner == key_owner
            q2 = m.qkv[n, rws, :]
            keys = m.qkv[3 + n]
            values = m.qkv[6 + n]
            outs = []
            for h in range(2):
                scores = dot_nt(head(q2, h), keys) * factor
                scores = jnp.where(allowed, scores, MASKED)
                peak = jnp.max(scores, axis=-1, keepdims=True)
                lifted = jnp.exp(scores - peak)
                inv = 1.0 / jnp.sum(lifted, axis=-1, keepdims=True)
                probs = (lifted * inv).astype(BF16)
                m.probs[n, h, rws, :] = probs
                outs.append(dot(probs, values))
            m.ag[mine, rws, :] = jnp.where(lane, outs[0], outs[1]).astype(BF16)
            return 0

        lax.fori_loop(0, 4, attend, 0)
        for d in range(1, strips):
            t = lax.rem(s + d, strips)
            start(
                send_to(
                    m.ag.at[mine, pl.ds(pl.multiple_of(t * 64, 64), 64)],
                    m.ai.at[mine, z],
                    m.ai_sem,
                    (n, d),
                    b,
                    t,
                )
            )
        start(send_to(m.ag.at[mine], m.ag.at[mine], m.ag_sem, n, b, sibling))
        m.ai[mine, z] = m.ag[mine, pl.ds(pl.multiple_of(s * 64, 64), 64), :]

    def chip_tile(buffer, t):
        return buffer[t // 2, pl.ds((t % 2) * 8, 8)].reshape(128, width)

    send_to(m.tg.at[c], m.tg.at[1 - c], m.pair_sem, 0, b, sibling).wait_recv()
    for t in range(4):
        m.tg_t[:, t * 128 : t * 128 + 128] = chip_tile(m.tg, t).T

    for n in range(3):
        for d in range(1, strips):
            i = lax.rem(s - d + strips, strips)
            spot = lax.rem(i, 2) * 3 + n
            send_to(
                m.ag.at[spot, pl.ds(0, 64)], m.ai.at[spot, i // 2], m.ai_sem, (n, d), b, i
            ).wait_recv()

    gate1 = block_mod(2)
    shift2 = block_mod(3)
    scale2 = 1.0 + block_mod(4)
    loads["wo"].wait()

    def project(g, _):
        v = jnp.concatenate([m.ai[n, g] for n in range(6)], axis=-1)
        w = dot(v, m.wo[...]) + m.ob[...]
        for r2 in range(rows // 2):
            rp = 4 * r2 + g
            branch = w[r2 * 16 : r2 * 16 + 16]
            m.b1[rp] = branch
            u = m.xd[rp // 2, lax.rem(rp, 2)].astype(F32) + gate1 * branch
            m.res[rp] = u
            n, _ = ln_parts(u)
            m.sc[c, rp] = (n * scale2 + shift2).astype(BF16)
        return 0

    lax.fori_loop(0, 4, project, 0)
    start(send_to(m.sc.at[c], m.sc.at[c], m.pair_sem, 1, b, sibling))

    def halo_sends(buffer, sems, n):
        up = send_to(buffer.at[n, 1], buffer.at[n, chip_rows + 1], sems, (0, n), b, s - 2)
        down = send_to(buffer.at[n, chip_rows], buffer.at[n, 0], sems, (1, n), b, s + 2)
        return up, down

    def start_halo(buffer, sems, n):
        up, down = halo_sends(buffer, sems, n)

        @pl.when(z > 0)
        def _():
            up.start()

        @pl.when(z < chips - 1)
        def _():
            down.start()

    def halo_sent(buffer, sems, n):
        up, down = halo_sends(buffer, sems, n)

        @pl.when(z > 0)
        def _():
            up.wait_send()

        @pl.when(z < chips - 1)
        def _():
            down.wait_send()

    def take_halo(buffer, sems, n):
        @pl.when(z > 0)
        def _():
            send_to(buffer.at[n, 1], buffer.at[n, 0], sems, (1, n), b, s - 2).wait_recv()

        @pl.when(z == 0)
        def _():
            buffer[n, 0] = jnp.zeros_like(buffer[n, 0])

        @pl.when(z < chips - 1)
        def _():
            send_to(buffer.at[n, 1], buffer.at[n, chip_rows + 1], sems, (0, n), b, s + 2).wait_recv()

        @pl.when(z == chips - 1)
        def _():
            buffer[n, chip_rows + 1] = jnp.zeros_like(buffer[n, 0])

    send_to(m.sc.at[c], m.sc.at[1 - c], m.pair_sem, 1, b, sibling).wait_recv()
    for n in range(chips):
        loads[f"we{n}"].wait()
        loads[f"wr{n}"].wait()

    def expand(n, _):
        bias = m.eb[2 * n + c]
        for t in range(4):
            w = dot(chip_tile(m.sc, t), m.we[n]) + bias
            m.ex[n, pl.ds(1 + 4 * t, 4)] = w.astype(BF16).reshape(4, 2, 16, half)
        start_halo(m.ex, m.ex_sem, n)
        return 0

    lax.fori_loop(0, chips, expand, 0)
    for t in range(4):
        m.sc_t[:, t * 128 : t * 128 + 128] = chip_tile(m.sc, t).T

    def r_one(n):
        return send_to(m.rw.at[n, :, 1 - x], m.r1.at[n], m.r1_sem, n, x_mate, s)

    def r_two(n):
        return send_to(m.r1.at[n, 1 - y], m.r2.at[n], m.r2_sem, n, y_mate, s)

    def r_three(d):
        n = chip(d)
        return send_to(m.r2.at[n], m.r3.at[d], m.r3_sem, d, b, 2 * n + c)

    def r_four(e):
        return send_to(m.r_all.at[b], m.r_all.at[b], m.r4_sem, e, lax.rem(b + e, 4), s)

    def r_half(n):
        r_one(n).wait_recv()
        for i in range(2):
            m.r1[n, i] = (m.r1[n, i].astype(F32) + m.rw[n, i, x].astype(F32)).astype(BF16)
        r_two(n).start()

    def r_quarter():
        for d in (1, 2, 3, 0):
            n = chip(d)
            r_two(n).wait_recv()
            m.r2[n] = (m.r2[n].astype(F32) + m.r1[n, y].astype(F32)).astype(BF16)
            if d:
                r_three(d).start()

    def r_sum():
        v = m.r2[z].astype(F32)
        for d in range(1, chips):
            r_three(d).wait_recv()
            v = v + m.r3[d].astype(F32)
        m.r_all[b] = v.astype(BF16)
        for e in range(1, 4):
            r_four(e).start()

    def by_x(j):
        return isinstance(j, int) and j in (4, 6)

    def c_source(j):
        return m.ew.at[j] if not isinstance(j, int) or j < 4 else m.jo.at[j - 4]

    def c_one(j):
        if by_x(j):
            return send_to(c_source(j).at[:, :, 1 - x], m.c1.at[j], m.c1_sem, j, x_mate, s)
        return send_to(c_source(j).at[:, 1 - y], m.c1.at[j], m.c1_sem, j, y_mate, s)

    def c_two(j):
        if by_x(j):
            return send_to(m.c1.at[j, :, 1 - y], m.c2.at[j], m.c2_sem, j, y_mate, s)
        return send_to(m.c1.at[j, :, 1 - x], m.c2.at[j], m.c2_sem, j, x_mate, s)

    def c_three(g, d):
        t = chip(d)
        return send_to(
            m.c2.at[pl.ds(4 * g, 4), t], m.c3.at[g, d], m.c3_sem, (g, d), b, 2 * t + c
        )

    def c_four(g, e):
        return pltpu.make_async_remote_copy(
            src_ref=m.c_out.at[g],
            dst_ref=m.c_all.at[g, x, c],
            send_sem=m.c4_sem[0].at[g, e],
            recv_sem=m.c4_sem[1].at[g, e, c],
            device_id=(lax.rem(b + e, 4), 2 * z + y),
            device_id_type=MESH,
        )

    def c_half(j):
        c_one(j).wait_recv()
        kept = c_source(j)[:, :, x] if by_x(j) else c_source(j)[:, y]
        m.c1[j] = (m.c1[j].astype(F32) + kept.astype(F32)).astype(BF16)
        c_two(j).start()

    def c_quarter(g):
        for j in range(4 * g, 4 * g + 4):
            c_two(j).wait_recv()
            kept = m.c1[j, :, y] if by_x(j) else m.c1[j, :, x]
            m.c2[j] = (m.c2[j].astype(F32) + kept.astype(F32)).astype(BF16)
        for d in range(1, chips):
            c_three(g, d).start()

    def c_sum(g):
        v = [m.c2[4 * g + i, z].astype(F32) for i in range(4)]
        for d in range(1, chips):
            c_three(g, d).wait_recv()
            for i in range(4):
                v[i] = v[i] + m.c3[g, d, i].astype(F32)
        for i in range(4):
            m.c_out[g, i] = v[i].astype(BF16)

        @pl.when(c == y)
        def _():
            m.c_all[g, x, c] = m.c_out[g]

        for e in range(1, 4):
            c_four(g, e).start()

        @pl.when(c != y)
        def _():
            c_four(g, 0).start()

    def activate(n, _):
        take_halo(m.ex, m.ex_sem, n)
        for t in range(4):
            m.agr[pl.ds(8 * t, 8)] = dot_nt(chip_tile(m.tg, t), m.wr[n]).reshape(8, 16, half)
        for k in range(half // 128):
            lanes = pl.ds(k * 128, 128)
            weights = [m.hk[2 * n + c, t : t + 1, lanes] for t in range(9)]

            def line(r, p):
                return m.ex[n, r, p, :, lanes]

            def step(r, carry):
                new = window(line, r + 2)
                out = conv((carry[0], carry[1], new), weights, False)
                for p in range(2):
                    value, slope = gelu_both(out[p])
                    m.act[2 * r + p, :, lanes] = value.astype(BF16)
                    m.cg[n, r + 1, p, :, lanes] = (m.agr[2 * r + p, :, lanes] * slope).astype(BF16)
                return carry[1], new

            lax.fori_loop(0, chip_rows, step, (window(line, 0), window(line, 1)))
        start_halo(m.cg, m.cg_sem, n)
        full = m.act[...].reshape(total, half)
        m.rw[n] = dot(m.tg_t[...], full).astype(BF16).reshape(m.rw.shape[1:])
        r_one(n).start()
        for t in range(4):
            w = dot(full[t * 128 : t * 128 + 128], m.wr[n]).reshape(8, 16, width)
            spot = (t // 2, pl.ds((t % 2) * 8, 8))

            @pl.when(n == 0)
            def _():
                m.b2[spot] = w

            @pl.when(n > 0)
            def _():
                m.b2[spot] += w

        return 0

    m.hkg[...] = jnp.zeros_like(m.hkg)
    lax.fori_loop(0, chips, activate, 0)
    start(send_to(m.b2.at[1 - c], m.b2_in, m.pair_sem, 2, b, sibling))

    def backward(n, _):
        take_halo(m.cg, m.cg_sem, n)
        for k in range(half // 128):
            lanes = pl.ds(k * 128, 128)
            weights = [m.hk[2 * n + c, t : t + 1, lanes] for t in range(9)]

            def line(r, p):
                return m.cg[n, r, p, :, lanes]

            def step(r, carry):
                new = window(line, r + 2)
                three = (carry[0], carry[1], new)
                low = [v.astype(BF16) for v in conv(three, weights, True)]
                for p in range(2):
                    m.eg[2 * r + p, :, lanes] = low[p]
                centre = [m.ex[n, r + 1, p, :, lanes].astype(F32) for p in range(2)]
                sums = taps(three, centre, carry[2][:9])
                both = low[0].astype(F32) + low[1].astype(F32)
                sums.append(carry[2][9] + (both[0:8] + both[8:16]))
                return carry[1], new, tuple(sums)

            zeros = tuple(jnp.zeros((8, 128), F32) for _ in range(10))
            _, _, sums = lax.fori_loop(
                0, chip_rows, step, (window(line, 0), window(line, 1), zeros)
            )
            for t in range(10):
                m.hkg[n, t : t + 1, lanes] = jnp.sum(sums[t], axis=0, keepdims=True)
        full = m.eg[...].reshape(total, half)
        for t in range(4):
            w = dot_nt(full[t * 128 : t * 128 + 128], m.we[n]).reshape(8, 16, width)
            spot = (t // 2, pl.ds((t % 2) * 8, 8))

            @pl.when(n == 0)
            def _():
                m.sg[spot] = w

            @pl.when(n > 0)
            def _():
                m.sg[spot] += w

        m.ew[n] = dot(m.sc_t[...], full).astype(BF16).reshape(m.ew.shape[1:])
        c_one(n).start()
        r_half(n)
        return 0

    lax.fori_loop(0, chips, backward, 0)
    start(send_to(m.sg.at[1 - c], m.sg_in, m.pair_sem, 3, b, sibling))
    send_to(m.b2.at[c], m.b2_in, m.pair_sem, 2, b, sibling).wait_recv()
    send_to(m.sg.at[c], m.sg_in, m.pair_sem, 3, b, sibling).wait_recv()

    def finish(r, _):
        for p in range(2):
            rp = 2 * r + p
            grad = m.sg[c, rp] + m.sg_in[rp]
            v = m.res[rp]
            n, inv = ln_parts(v)
            branch = m.b1[rp]
            up = m.ctd[rp].astype(F32)
            m.acc[1] += grad
            m.acc[2] += grad * n
            back = up + ln_back(grad * scale2, n, inv)
            m.rg[rp] = back
            m.acc[3] += back * branch
            one = (back * gate1).astype(BF16)
            m.og[lax.rem(rp, 4), rp // 4] = one
            m.acc[4] += one.astype(F32)
            branch2 = m.b2[c, rp] + m.b2_in[rp] + m.rb[...]
            m.acc[5] += up * branch2
            interleave(m.rowf, r, p, v + gate2 * branch2)
        m.out[r] = joined(m.rowf, r).astype(BF16)
        return 0

    lax.fori_loop(0, rows, finish, 0)
    out_copy = pltpu.make_async_copy(m.out, m.out_hbm, m.load_sem.at[13])
    out_copy.start()

    to_groups(m.og, m.gg, m.gg_sem, m.gg_sem2)

    pack = []
    for v in (m.acc[3], m.acc[1], m.acc[2], m.acc[5]):
        pair = halves(v)
        for h in range(2):
            pack += [pair[h : h + 1, 0:half], pair[h : h + 1, half:]]
    m.late[b, s] = jnp.concatenate(pack, axis=0).astype(BF16)
    for e in range(1, 4):
        start(send_to(m.late.at[b, s], m.late.at[b, s], m.late_sem, e, lax.rem(b + e, 4), s))
    sums_ob = jnp.sum(m.acc[4], axis=0, keepdims=True)
    sums_rb = jnp.sum(m.acc[0], axis=0, keepdims=True)
    pad_lanes = jnp.zeros((1, half - own), F32)
    pad_rows = jnp.zeros((4, half), F32)
    for t in range(strips):
        piece = jnp.concatenate(
            [
                jnp.where(c == t % 2, m.hkg[t // 2, 0:10], 0.0),
                jnp.concatenate([sums_ob[:, t * own : t * own + own], pad_lanes], axis=1),
                jnp.concatenate([sums_rb[:, t * own : t * own + own], pad_lanes], axis=1),
                pad_rows,
            ],
            axis=0,
        )
        m.piece[t] = piece.astype(BF16)
    for d in range(1, strips):
        t = lax.rem(s + d, strips)
        start(send_to(m.piece.at[t], m.piece_in.at[d], m.piece_sem, d, b, t))

    r_quarter()
    c_half(0)
    c_half(1)

    pass_on(m.gg, m.gg_sem, m.gg_sem2)
    groups_ready(m.gg, m.gg_sem2)
    wo_own = m.wo[pl.ds(pl.multiple_of(c * half, 128), half), :]

    def attended_grad(t, _):
        v = m.gg[pl.ds(2 * t, 2)].reshape(128, width)
        w = dot_nt(v, wo_own).astype(BF16)
        for n in range(3):
            m.da[n, pl.ds(pl.multiple_of(t * 128, 128), 128), :] = w[:, n * 128 : n * 128 + 128]
        return 0

    lax.fori_loop(0, chips, attended_grad, 0)

    for n in range(3):
        other = (1 - c) * 3 + n
        send_to(m.ag.at[other], m.ag.at[other], m.ag_sem, n, b, sibling).wait_recv()
    columns = m.gg[:, :, :, pl.ds(pl.multiple_of(c * half, 128), half)].reshape(total, half)
    full = jnp.concatenate([m.ag[n] for n in range(6)], axis=-1)
    m.jo[3] = dot_tn(full, columns).astype(BF16).reshape(m.jo.shape[1:])
    c_one(7).start()

    lanes_all = lax.broadcasted_iota(jnp.int32, (total, 128), 1) < 64
    for n in range(3):

        def tile(t, _):
            rws = pl.ds(pl.multiple_of(t * 128, 128), 128)
            d2 = m.da[n, rws, :]
            keys = m.qkv[3 + n]
            values = m.qkv[6 + n]
            outs = []
            for h in range(2):
                dp = dot_nt(head(d2, h), values)
                probs = m.probs[n, h, rws, :].astype(F32)
                inner = jnp.sum(probs * dp, axis=-1, keepdims=True)
                grad = (probs * (dp - inner)).astype(BF16)
                m.ds[h, rws, :] = grad
                outs.append(dot(grad, keys))
            m.dqkv[n, rws, :] = (jnp.where(lane, outs[0], outs[1]) * factor).astype(BF16)
            return 0

        lax.fori_loop(0, 4, tile, 0)
        q2 = m.qkv[n]
        d2 = m.da[n]
        dk = [dot_tn(m.ds[h], q2) for h in range(2)]
        m.dqkv[3 + n] = (jnp.where(lanes_all, dk[0], dk[1]) * factor).astype(BF16)
        dv = [dot_tn(m.probs[n, h], d2) for h in range(2)]
        m.dqkv[6 + n] = jnp.where(lanes_all, dv[0], dv[1]).astype(BF16)

    def side(part, rws):
        return jnp.concatenate([m.dqkv[3 * part + n, rws, :] for n in range(3)], axis=-1)

    def partial(core):
        def body(i, _):
            rws = pl.ds(pl.multiple_of((2 * i + core) * 64, 64), 64)
            w = dot_nt(side(0, rws), m.wj[0])
            for part in range(1, 3):
                w = w + dot_nt(side(part, rws), m.wj[part])
            m.mp[core, i] = w
            return 0

        lax.fori_loop(0, chips, body, 0)

    partial(1 - c)
    start(send_to(m.mp.at[1 - c], m.mp_in, m.pair_sem, 4, b, sibling))
    partial(c)
    send_to(m.mp.at[c], m.mp_in, m.pair_sem, 4, b, sibling).wait_recv()
    for d in range(chips):
        i = chip(d)
        low = (m.mp[c, i] + m.mp_in[i]).astype(BF16).reshape(rows // 2, 16, width)
        if d:
            m.mo[i] = low
            start(send_to(m.mo.at[i], m.mr.at[z], m.mr_sem, d, b, 2 * i + c))
        else:
            m.mr[z] = low

    for part in range(3):
        v = m.mg[...].reshape(total, width)
        w = dot_tn(v, side(part, slice(None)))
        m.jo[part] = w.astype(BF16).reshape(m.jo.shape[1:])
        c_one(4 + part).start()

    c_half(2)
    c_half(3)
    r_sum()

    for e in range(1, 4):
        i = lax.rem(b - e + 4, 4)
        send_to(m.late.at[i, s], m.late.at[i, s], m.late_sem, e, i, s).wait_recv()
    for d in range(1, chips):
        start(send_to(m.late.at[:, s], m.late.at[:, s], m.late_sem2, d, b, 2 * chip(d) + c))
    sums = m.piece[s].astype(F32)
    for d in range(1, strips):
        send_to(m.piece.at[0], m.piece_in.at[d], m.piece_sem, d, b, s).wait_recv()
        sums = sums + m.piece_in[d].astype(F32)
    m.small[b] = sums.astype(BF16)
    for e in range(1, 4):
        start(send_to(m.small.at[b], m.small.at[b], m.small_sem, e, lax.rem(b + e, 4), s))

    for d in range(1, chips):
        i = chip(chips - d)
        send_to(m.mo.at[i], m.mr.at[i], m.mr_sem, d, b, 2 * i + c).wait_recv()
    for r in (0, rows - 1):
        for p in range(2):
            m.md[r + 1, p] = m.mr[(r % 2) * 2 + p, r // 2]
    start_edges(m.md, m.md_sem)
    for r in range(1, rows - 1):
        for p in range(2):
            m.md[r + 1, p] = m.mr[(r % 2) * 2 + p, r // 2]

    m.acc1[...] = jnp.zeros_like(m.acc1)

    def mixer_rows(low, high):
        for k in range(width // 128):
            lanes = pl.ds(k * 128, 128)
            weights = [m.mk[t : t + 1, k * 128 : k * 128 + 128] for t in range(9)]

            def line(r, p):
                return m.md[r, p, :, lanes]

            def step(r, carry):
                new = window(line, r + 2)
                three = (carry[0], carry[1], new)
                out = conv(three, weights, True)
                for p in range(2):
                    m.fg[2 * r + p, :, lanes] = out[p]
                centre = [m.fp[r + 1, p, :, lanes].astype(F32) for p in range(2)]
                return carry[1], new, tuple(taps(three, centre, carry[2]))

            begin = tuple(m.acc1[t, :, lanes] for t in range(9))
            _, _, sums = lax.fori_loop(
                low, high, step, (window(line, low), window(line, low + 1), begin)
            )
            for t in range(9):
                m.acc1[t, :, lanes] = sums[t]

    m.acc[1] = jnp.zeros_like(m.acc[1])
    m.acc[2] = jnp.zeros_like(m.acc[2])

    def token_row(r, _):
        for p in range(2):
            rp = 2 * r + p
            grad = m.fg[rp]
            n, inv = ln_parts(m.xd[r, p].astype(F32))
            m.acc[1] += grad
            m.acc[2] += grad * n
            interleave(m.rowf, r, p, m.rg[rp] + ln_back(grad * scale1, n, inv))
        m.tgo[r] = joined(m.rowf, r)
        return 0

    mixer_rows(1, rows - 1)
    lax.fori_loop(1, rows - 1, token_row, 0)
    top_edge(m.md, m.md_sem)
    mixer_rows(0, 1)
    token_row(0, 0)
    bottom_edge(m.md, m.md_sem)
    mixer_rows(rows - 1, rows)
    token_row(rows - 1, 0)
    tg_copy = pltpu.make_async_copy(m.tgo, m.tg_hbm, m.load_sem.at[14])
    tg_copy.start()

    pack = []
    third = width // 3
    for v in (m.acc[1], m.acc[2]):
        pair = halves(v)
        for h in range(2):
            pack += [pair[h : h + 1, k * third : k * third + third] for k in range(3)]
    pack.append(jnp.zeros((4, third), F32))
    m.early[b, s] = jnp.concatenate(pack, axis=0).astype(BF16)
    for e in range(1, 4):
        start(send_to(m.early.at[b, s], m.early.at[b, s], m.early_sem, e, lax.rem(b + e, 4), s))
    mixer_sums = [jnp.sum(m.acc1[t], axis=0, keepdims=True) for t in range(9)]
    mixer_sums = jnp.concatenate(mixer_sums + [jnp.zeros((7, width), F32)], axis=0)
    pad_lanes = jnp.zeros((16, 128 - own), F32)
    for t in range(strips):
        m.mpiece[t] = jnp.concatenate(
            [mixer_sums[:, t * own : t * own + own], pad_lanes], axis=1
        ).astype(BF16)
    for d in range(1, strips):
        t = lax.rem(s + d, strips)
        start(send_to(m.mpiece.at[t], m.mpiece_in.at[d], m.mpiece_sem, d, b, t))

    c_quarter(0)
    for j in range(4, 8):
        c_half(j)
    for d in range(chips):
        i = 2 * chip(chips - d) + c
        if d:
            send_to(m.late.at[:, i], m.late.at[:, i], m.late_sem2, d, b, i).wait_recv()
        start(send_to(m.late.at[:, i], m.late.at[:, i], m.late_sem3, d, b, sibling))
    for e in range(1, 4):
        i = lax.rem(b - e + 4, 4)
        send_to(m.early.at[i, s], m.early.at[i, s], m.early_sem, e, i, s).wait_recv()
    for d in range(1, chips):
        start(send_to(m.early.at[:, s], m.early.at[:, s], m.early_sem2, d, b, 2 * chip(d) + c))
    sums = m.mpiece[s].astype(F32)
    for d in range(1, strips):
        send_to(m.mpiece.at[0], m.mpiece_in.at[d], m.mpiece_sem, d, b, s).wait_recv()
        sums = sums + m.mpiece_in[d].astype(F32)
    m.msmall[b] = sums.astype(BF16)
    for e in range(1, 4):
        start(send_to(m.msmall.at[b], m.msmall.at[b], m.msmall_sem, e, lax.rem(b + e, 4), s))
    c_sum(0)
    c_quarter(1)
    for d in range(chips):
        i = 2 * chip(chips - d) + c
        if d:
            send_to(m.early.at[:, i], m.early.at[:, i], m.early_sem2, d, b, i).wait_recv()
        start(send_to(m.early.at[:, i], m.early.at[:, i], m.early_sem3, d, b, sibling))
    c_sum(1)

    finals = []

    def store(src, dst, index):
        cp = pltpu.make_async_copy(src, dst, m.load_sem.at[index])
        cp.start()
        finals.append(cp)

    for e in range(1, 4):
        i = lax.rem(b - e + 4, 4)
        send_to(m.cond_all.at[i], m.cond_all.at[i], m.cond_sem, e, i, s).wait_recv()
        send_to(m.small.at[i], m.small.at[i], m.small_sem, e, i, s).wait_recv()
        send_to(m.msmall.at[i], m.msmall.at[i], m.msmall_sem, e, i, s).wait_recv()
        send_to(m.r_all.at[i], m.r_all.at[i], m.r4_sem, e, i, s).wait_recv()
    store(m.r_all, m.r_hbm, 15)
    store(m.cond_all, m.cond_hbm, 16)
    store(m.small, m.small_hbm, 17)
    store(m.msmall, m.msmall_hbm, 18)
    for d in range(chips):
        i = 2 * chip(chips - d) + 1 - c
        send_to(m.late.at[:, i], m.late.at[:, i], m.late_sem3, d, b, sibling).wait_recv()
        send_to(m.early.at[:, i], m.early.at[:, i], m.early_sem3, d, b, sibling).wait_recv()
    store(m.late, m.late_hbm, 19)
    store(m.early, m.early_hbm, 20)
    for g in range(2):
        for xs in range(2):
            for cs in range(2):
                source = 2 * c + xs
                e = lax.rem(b - source + 4, 4)
                local = jnp.logical_and(source == b, cs == c)

                @pl.when(jnp.logical_not(local))
                def _():
                    pltpu.make_async_remote_copy(
                        src_ref=m.c_out.at[g],
                        dst_ref=m.c_all.at[g, xs, cs],
                        send_sem=m.c4_sem[0].at[g, e],
                        recv_sem=m.c4_sem[1].at[g, e, cs],
                        device_id=(source, 2 * z + cs),
                        device_id_type=MESH,
                    ).wait_recv()

    store(m.c_all, m.c_hbm, 21)
    for cp in sent:
        cp.wait_send()
    edges_sent(m.fp, m.fp_sem)
    edges_sent(m.md, m.md_sem)

    def drain(n, _):
        halo_sent(m.ex, m.ex_sem, n)
        halo_sent(m.cg, m.cg_sem, n)
        r_one(n).wait_send()
        r_two(n).wait_send()
        return 0

    lax.fori_loop(0, chips, drain, 0)
    for j in range(8):
        c_one(j).wait_send()
        c_two(j).wait_send()
    for d in range(1, chips):
        r_three(d).wait_send()
        r_four(d).wait_send()
        for g in range(2):
            c_three(g, d).wait_send()
            c_four(g, d).wait_send()

    @pl.when(c != y)
    def _():
        for g in range(2):
            c_four(g, 0).wait_send()

    out_copy.wait()
    tg_copy.wait()
    for cp in finals:
        cp.wait()


def block(tokens, mod, mixer, owner, cond, ob, eb, hk, rb, wj, wo, we, wr, cot, strips):
    rows, cols, width = tokens.shape
    chips = strips // 2
    half = width // 2
    total = strips * 64
    blocks = 2 * rows
    chip_rows = 2 * rows
    part = width // chips // 4
    third = width // 3
    shape = jax.ShapeDtypeStruct
    vm = pltpu.VMEM

    def dma(*size):
        return pltpu.SemaphoreType.DMA(size)

    ins = dict(
        tok=tokens, mod=mod, mk=mixer, owner=owner, cond=cond, ob=ob, eb=eb, hk=hk, rb=rb,
        wj_hbm=wj, wo_hbm=wo, we_hbm=we, wr_hbm=wr, cot_hbm=cot,
    )
    outs = dict(
        out_hbm=shape((rows, cols, width), BF16),
        tg_hbm=shape((rows, cols, width), F32),
        r_hbm=shape((4, width // 4, half), BF16),
        c_hbm=shape((2, 2, 2, 4, part, half), BF16),
        cond_hbm=shape((4,) + cond.shape, F32),
        small_hbm=shape((4, 16, half), BF16),
        msmall_hbm=shape((4, 16, 128), BF16),
        late_hbm=shape((4, strips, 16, half), BF16),
        early_hbm=shape((4, strips, 16, third), BF16),
    )
    scratch = dict(
        wj=vm((3, width, half), BF16),
        wo=vm((width, width), BF16),
        we=vm((chips, width, half), BF16),
        wr=vm((chips, half, width), BF16),
        cot=vm((rows, cols, width), BF16),
        cond_all=vm((4,) + cond.shape, F32),
        rowf=vm((rows, width // 128, cols, 128), F32),
        xd=vm((rows, 2, 16, width), BF16),
        fp=vm((rows + 2, 2, 16, width), BF16),
        ms=vm((chips, rows // 2, 16, width), BF16),
        mg=vm((strips, rows // 2, 16, width), BF16),
        qkv=vm((9, total, 128), BF16),
        probs=vm((3, 2, total, total), BF16),
        ag=vm((6, total, 128), BF16),
        ai=vm((6, chips, 64, 128), BF16),
        acc=vm((6, 16, width), F32),
        acc1=vm((9, 8, width), F32),
        ctd=vm((blocks, 16, width), BF16),
        tg=vm((2, blocks, 16, width), BF16),
        tg_t=vm((width, total), BF16),
        sc=vm((2, blocks, 16, width), BF16),
        sc_t=vm((width, total), BF16),
        b1=vm((blocks, 16, width), F32),
        res=vm((blocks, 16, width), F32),
        ex=vm((chips, chip_rows + 2, 2, 16, half), BF16),
        cg=vm((chips, chip_rows + 2, 2, 16, half), BF16),
        agr=vm((2 * blocks, 16, half), F32),
        act=vm((2 * blocks, 16, half), BF16),
        eg=vm((2 * blocks, 16, half), BF16),
        b2=vm((2, blocks, 16, width), F32),
        b2_in=vm((blocks, 16, width), F32),
        sg=vm((2, blocks, 16, width), F32),
        sg_in=vm((blocks, 16, width), F32),
        hkg=vm((chips, 16, half), F32),
        rg=vm((blocks, 16, width), F32),
        og=vm((chips, rows // 2, 16, width), BF16),
        out=vm((rows, cols, width), BF16),
        gg=vm((strips, rows // 2, 16, width), BF16),
        da=vm((3, total, 128), BF16),
        ds=vm((2, total, total), BF16),
        dqkv=vm((9, total, 128), BF16),
        mp=vm((2, chips, 64, width), F32),
        mp_in=vm((chips, 64, width), F32),
        mo=vm((chips, rows // 2, 16, width), BF16),
        mr=vm((chips, rows // 2, 16, width), BF16),
        md=vm((rows + 2, 2, 16, width), BF16),
        fg=vm((blocks, 16, width), F32),
        tgo=vm((rows, cols, width), F32),
        rw=vm((chips, 2, 2, width // 4, half), BF16),
        r1=vm((chips, 2, width // 4, half), BF16),
        r2=vm((chips, width // 4, half), BF16),
        r3=vm((chips, width // 4, half), BF16),
        r_all=vm((4, width // 4, half), BF16),
        ew=vm((4, chips, 2, 2, part, half), BF16),
        jo=vm((4, chips, 2, 2, part, half), BF16),
        c1=vm((8, chips, 2, part, half), BF16),
        c2=vm((8, chips, part, half), BF16),
        c3=vm((2, chips, 4, part, half), BF16),
        c_out=vm((2, 4, part, half), BF16),
        c_all=vm((2, 2, 2, 4, part, half), BF16),
        late=vm((4, strips, 16, half), BF16),
        early=vm((4, strips, 16, third), BF16),
        piece=vm((strips, 16, half), BF16),
        piece_in=vm((strips, 16, half), BF16),
        small=vm((4, 16, half), BF16),
        mpiece=vm((strips, 16, 128), BF16),
        mpiece_in=vm((strips, 16, 128), BF16),
        msmall=vm((4, 16, 128), BF16),
        load_sem=dma(22),
    )
    pairs = dict(
        cond_sem=(4,), fp_sem=(2,), md_sem=(2,), mg_sem=(chips,), mg_sem2=(chips,),
        gg_sem=(chips,), gg_sem2=(chips,), ai_sem=(3, strips), ag_sem=(3,), pair_sem=(5,),
        ex_sem=(2, chips), cg_sem=(2, chips), mr_sem=(chips,),
        r1_sem=(chips,), r2_sem=(chips,), r3_sem=(chips,), r4_sem=(4,),
        c1_sem=(8,), c2_sem=(8,), c3_sem=(2, chips),
        late_sem=(4,), late_sem2=(chips,), late_sem3=(chips,),
        early_sem=(4,), early_sem2=(chips,), early_sem3=(chips,),
        piece_sem=(strips,), small_sem=(4,), mpiece_sem=(strips,), msmall_sem=(4,),
    )
    names = list(ins) + list(outs) + list(scratch)
    shapes = list(scratch.values())
    for size in list(pairs.values()):
        shapes += [dma(*size), dma(*size)]
    shapes += [dma(2, 4), dma(2, 4, 2)]
    plain = len(names)

    def kernel(*refs):
        named = list(refs[:plain])
        sems = refs[plain:]
        both = [(sems[2 * i], sems[2 * i + 1]) for i in range(len(sems) // 2)]
        block_kernel(names + list(pairs) + ["c4_sem"], *named, *both)

    return pl.pallas_call(
        kernel,
        name="block",
        out_shape=tuple(outs.values()),
        in_specs=[WHOLE] * 3 + [SCALARS] + [WHOLE] * 5 + [LEFT] * 5,
        out_specs=(LEFT,) * len(outs),
        scratch_shapes=shapes,
        compiler_params=pltpu.CompilerParams(
            collective_id=0, has_side_effects=True, vmem_limit_bytes=VMEM_BYTES
        ),
    )(*ins.values())


def final_kernel(
    out_in, tg_in, r_ref, c_ref, cond_ref, small_ref, msmall_ref, late_ref, early_ref, aw_hbm,
    out_ref, tg_ref, tab_ref, ad_ref, ab_ref, mix_ref, joint_ref, output_ref, ob_ref,
    expand_ref, eb_ref, hidden_ref, reduce_ref, rb_ref,
    aw, out_v, tg_v, sem,
):
    s = lax.axis_index("strip")
    strips = lax.axis_size("strip")
    width = cond_ref.shape[2] - 256
    own = width // strips
    half = width // 2
    third = width // 3
    copies = [
        pltpu.make_async_copy(out_in, out_v, sem.at[0]),
        pltpu.make_async_copy(tg_in, tg_v, sem.at[1]),
        pltpu.make_async_copy(aw_hbm.at[pl.ds(pl.multiple_of(s * own, 16), own)], aw, sem.at[2]),
    ]
    for cp in copies:
        cp.start()

    stores = [
        pltpu.make_async_copy(out_v, out_ref, sem.at[3]),
        pltpu.make_async_copy(tg_v, tg_ref, sem.at[4]),
    ]

    small = small_ref[0].astype(F32)
    mixer = msmall_ref[0].astype(F32)
    for i in range(1, 4):
        small = small + small_ref[i].astype(F32)
        mixer = mixer + msmall_ref[i].astype(F32)
    hidden_ref[...] = small[0:9]
    eb_ref[...] = small[9:10]
    ob_ref[...] = small[10:11, 0:own]
    rb_ref[...] = small[11:12, 0:own]
    mix_ref[...] = mixer[0:9, 0:own]

    for i in range(2):
        copies[i].wait()
        stores[i].start()

    n = r_ref.shape[1]
    for q in range(4):
        reduce_ref[:, q * n : q * n + n] = r_ref[q].astype(F32).T
    part = c_ref.shape[4]
    for xs in range(2):
        rows = slice(xs * part, xs * part + part)
        for cs in range(2):
            for k in range(4):
                at = (2 * k + cs) * half
                expand_ref[rows, at : at + half] = c_ref[0, xs, cs, k].astype(F32)
                if k < 3:
                    joint_ref[rows, at : at + half] = c_ref[1, xs, cs, k].astype(F32)
            output_ref[rows, cs * half : cs * half + half] = c_ref[1, xs, cs, 3].astype(F32)

    slots = 32
    condition = cond_ref[...].reshape(slots, width + 256)
    labels = condition[:, width : width + 1]
    slot_late = jnp.concatenate([cond_ref[i, 0:1, width + 128 :] for i in range(4)], axis=1)
    slot_early = jnp.concatenate([cond_ref[i, 1:2, width + 128 :] for i in range(4)], axis=1)
    condition = condition[:, 0:width]
    pick = lax.broadcasted_iota(jnp.int32, (width, own), 0) == (
        lax.broadcasted_iota(jnp.int32, (width, own), 1) + s * own
    )
    pick = jnp.where(pick, 1.0, 0.0)
    condition = jnp.dot(
        condition, pick, precision=lax.Precision.HIGHEST, preferred_element_type=F32
    )
    sigmoid = 1.0 / (1.0 + jnp.exp(-condition))
    silu = (condition * sigmoid).astype(BF16)
    slope = sigmoid * (1.0 + condition * (1.0 - sigmoid))

    count = 4 * strips * 16
    row = lax.rem(lax.broadcasted_iota(jnp.int32, (slots, count), 1), 16)
    index = lax.broadcasted_iota(jnp.int32, (slots, count), 0)
    hit_late = index == slot_late.astype(jnp.int32)
    hit_early = index == slot_early.astype(jnp.int32)
    late = late_ref[...].reshape(count, half)
    early = early_ref[...].reshape(count, third)
    copies[2].wait()
    silu_grad = jnp.zeros((slots, own), F32)
    pieces = []
    for i in range(2):
        for k in range(3):
            mine = jnp.logical_or(row == 6 * i + k, row == 6 * i + 3 + k)
            pieces.append((early, jnp.logical_and(hit_early, mine), i * width + k * third, third))
    for i in range(4):
        for k in range(2):
            mine = jnp.logical_or(row == 4 * i + k, row == 4 * i + 2 + k)
            pieces.append((late, jnp.logical_and(hit_late, mine), (2 + i) * width + k * half, half))
    for source, mine, at, size in pieces:
        chosen = jnp.where(mine, 1.0, 0.0).astype(BF16)
        grad = dot(chosen, source)
        ab_ref[:, at : at + size] = jnp.sum(grad, axis=0, keepdims=True)
        low = grad.astype(BF16)
        ad_ref[:, at : at + size] = dot_tn(silu, low)
        silu_grad = silu_grad + dot_nt(low, aw[:, at : at + size])
    classes = tab_ref.shape[1]
    onehot = lax.broadcasted_iota(jnp.int32, (slots, classes), 1) == labels.astype(jnp.int32)
    tab_ref[...] = lax.dot_general(
        silu_grad * slope,
        jnp.where(onehot, 1.0, 0.0),
        TN,
        precision=lax.Precision.HIGHEST,
        preferred_element_type=F32,
    )
    for cp in stores:
        cp.wait()


def final(parts, aw, classes, strips):
    out, tg, r, c, cond, small, msmall, late, early = parts
    width = out.shape[-1]
    own = width // strips
    half = width // 2
    shape = jax.ShapeDtypeStruct
    return pl.pallas_call(
        final_kernel,
        name="final",
        out_shape=(
            shape(out.shape, BF16),
            shape(tg.shape, F32),
            shape((own, classes), F32),
            shape((own, 6 * width), F32),
            shape((1, 6 * width), F32),
            shape((9, own), F32),
            shape((own, 3 * width), F32),
            shape((own, width), F32),
            shape((1, own), F32),
            shape((own, 4 * width), F32),
            shape((1, half), F32),
            shape((9, half), F32),
            shape((half, width), F32),
            shape((1, own), F32),
        ),
        in_specs=[LEFT] * 2 + [WHOLE] * 7 + [LEFT],
        out_specs=(LEFT,) * 2 + (WHOLE,) * 12,
        scratch_shapes=[
            pltpu.VMEM((own, 6 * width), BF16),
            pltpu.VMEM(out.shape, BF16),
            pltpu.VMEM(tg.shape, F32),
            pltpu.SemaphoreType.DMA((5,)),
        ],
        compiler_params=pltpu.CompilerParams(vmem_limit_bytes=VMEM_BYTES),
    )(out, tg, r, c, cond, small, msmall, late, early, aw)


def timestep_features(time_steps, model_width):
    half_width = model_width // 2
    frequencies = jnp.exp(
        -math.log(10000.0) * jnp.arange(half_width, dtype=F32) / half_width
    )
    angles = time_steps.astype(F32)[..., None] * frequencies
    return jnp.concatenate([jnp.cos(angles), jnp.sin(angles)], axis=-1)


def local_grouped(
    tokens, tile_owner, time_steps, class_labels, class_embedding_matrix, adaptive_weight,
    adaptive_bias, mixer_kernel, joint_weight, output_weight, output_bias, expand_weight,
    expand_bias, hidden_kernel, reduce_weight, reduce_bias, output_cotangent,
):
    _, rows, cols, width = tokens.shape
    strips = lax.axis_size("strip")
    s = lax.axis_index("strip")
    b = lax.axis_index("batch")
    classes = class_embedding_matrix.shape[1]
    latents = time_steps.shape[1]
    own = width // strips
    piece = expand_weight.shape[1] // strips
    owner = tile_owner[0].reshape(-1)

    onehot = (class_labels[0][:, None] == jnp.arange(classes, dtype=jnp.int32)).astype(BF16)
    condition = timestep_features(time_steps[0], width) + jnp.einsum(
        "bn,dn->bd", onehot, class_embedding_matrix, preferred_element_type=F32
    )
    silu_cond = jax.nn.silu(condition).astype(BF16)
    modulation = jnp.dot(silu_cond, adaptive_weight, preferred_element_type=F32)
    modulation = modulation + adaptive_bias.astype(F32)
    pair = lax.dynamic_slice_in_dim(owner, 2 * (s * 4 // strips), 2)
    mod = jnp.dot(
        (pair[:, None] == jnp.arange(latents, dtype=jnp.int32)).astype(F32),
        modulation,
        precision=lax.Precision.HIGHEST,
    )
    labels = jnp.broadcast_to(class_labels[0].astype(F32)[:, None], (latents, 128))
    slot_late = jnp.broadcast_to(
        (tile_owner[0] + b * latents).astype(F32)[:, None, None, :, None],
        (4, strips // 4, 4, 2, 2),
    ).reshape(1, -1)
    slot_early = jnp.broadcast_to(
        (tile_owner[0] + b * latents).astype(F32)[:, None, :, None], (4, 2, 2, 3)
    ).reshape(4, 1, 12)
    slot_early = jnp.broadcast_to(
        jnp.pad(slot_early, ((0, 0), (0, 0), (0, 4))), (4, strips // 4, 16)
    ).reshape(1, -1)
    slots = jnp.concatenate([slot_late] + [slot_early] * (latents - 1), axis=0)
    cond = jnp.concatenate([condition, labels, slots], axis=1)
    mixer = mixer_kernel.T.astype(F32)
    hidden = hidden_kernel.T.astype(F32).reshape(9, strips, piece).transpose(1, 0, 2)
    parts = block(
        tokens[0], mod, mixer, owner, cond, output_bias.astype(F32)[None],
        expand_bias.astype(F32).reshape(strips, 1, piece), hidden,
        reduce_bias.astype(F32)[None], joint_weight, output_weight, expand_weight,
        reduce_weight, output_cotangent[0], strips,
    )
    (
        out, tg, table, adaptive, bias, mix, joint, output, ob, expand, eb, hid, reduce, rb,
    ) = final(parts, adaptive_weight, classes, strips)
    bias = lax.dynamic_slice_in_dim(bias.reshape(-1), s * 6 * own, 6 * own)
    return (
        out[None], tg[None], table, adaptive, bias, mix.T, joint, output, ob.reshape(-1),
        expand, eb.reshape(-1), hid.T, reduce, rb.reshape(-1),
    )


EXACT_PRECISION = lax.Precision.HIGHEST


def padded_2(block, sides, width):
    for axis, dim in sides:
        count = lax.axis_size(axis)
        forward = [(i, i + 1) for i in range(count - 1)]
        backward = [(target, source) for source, target in forward]
        low = lax.ppermute(
            lax.slice_in_dim(block, block.shape[dim] - width, None, axis=dim), axis, forward
        )
        high = lax.ppermute(lax.slice_in_dim(block, 0, width, axis=dim), axis, backward)
        block = jnp.concatenate([low, block, high], axis=dim)
    return block


def normalize(values):
    centre = jnp.mean(values, axis=-1, keepdims=True)
    centred = values - centre
    spread = jnp.mean(centred * centred, axis=-1, keepdims=True)
    return centred * lax.rsqrt(spread + EPSILON)


def modulate(values, shifting, scaling):
    return normalize(values) * (1.0 + scaling) + shifting


def depthwise(padded, kernel):
    row_count = padded.shape[-3] - 2
    column_total = padded.shape[-2]
    widened = jnp.pad(padded, [(0, 0)] * (padded.ndim - 2) + [(1, 1), (0, 0)])
    result = jnp.zeros(
        padded.shape[:-3] + (row_count, column_total, padded.shape[-1]), padded.dtype
    )
    for tapping in range(9):
        row_shift = tapping // 3
        col_shift = tapping % 3
        window = lax.slice_in_dim(widened, row_shift, row_shift + row_count, axis=widened.ndim - 3)
        window = lax.slice_in_dim(
            window, col_shift, col_shift + column_total, axis=widened.ndim - 2
        )
        result = result + kernel[:, tapping] * window
    return result


def kernel_grad(padded, gradient):
    row_count = gradient.shape[1]
    column_total = gradient.shape[2]
    widened = jnp.pad(padded, ((0, 0), (0, 0), (1, 1), (0, 0)))
    columns = []
    for tapping in range(9):
        row_shift = tapping // 3
        col_shift = tapping % 3
        window = widened[
            :, row_shift : row_shift + row_count, col_shift : col_shift + column_total, :
        ]
        columns.append(jnp.sum(window * gradient, axis=(0, 1, 2)))
    return jnp.stack(columns, axis=1)


def group_owner(owner):
    canvases, row_count, column_total = owner.shape
    shaped = owner.reshape(canvases, row_count // 2, 2, column_total // 2, 2).transpose(
        0, 2, 4, 1, 3
    )
    return shaped.reshape(canvases, 2, 2, row_count // 2 * (column_total // 2))


def to_groups(tensor, head_count):
    canvases, row_count, column_total, features = tensor.shape
    head_size = features // head_count
    shaped = tensor.reshape(
        canvases, row_count // 2, 2, column_total // 2, 2, head_count, head_size
    )
    shaped = shaped.transpose(0, 2, 4, 5, 1, 3, 6)
    return shaped.reshape(
        canvases, 2, 2, head_count, row_count // 2 * (column_total // 2), head_size
    )


def from_groups(tensor, row_count, column_total):
    canvases, head_count, head_size = (tensor.shape[0], tensor.shape[3], tensor.shape[-1])
    shaped = tensor.reshape(
        canvases, 2, 2, head_count, row_count // 2, column_total // 2, head_size
    )
    shaped = shaped.transpose(0, 4, 1, 5, 2, 3, 6)
    return shaped.reshape(canvases, row_count, column_total, head_count * head_size)


def local(
    tokens,
    tile_owner,
    time_steps,
    class_labels,
    class_embedding_matrix,
    adaptive_weight,
    adaptive_bias,
    mixer_kernel,
    joint_weight,
    output_weight,
    output_bias,
    expand_weight,
    expand_bias,
    hidden_kernel,
    reduce_weight,
    reduce_bias,
    output_cotangent,
):
    canvases, row_count, column_total, model_width = tokens.shape
    head_count = HEADS
    head_size = model_width // head_count
    factor = head_size ** (-0.5)
    half_cols = column_total // 2
    strips = lax.axis_size("strip")
    strip_index = lax.axis_index("strip")
    canvas_rows = row_count * strips
    class_count = class_embedding_matrix.shape[1]
    latent_count = time_steps.shape[1]
    tile_rows = canvas_rows // 4
    full_owner = jnp.broadcast_to(
        tile_owner[:, :, None, :, None], (canvases, 4, tile_rows, 2, half_cols)
    ).reshape(canvases, canvas_rows, column_total)
    local_owner = lax.dynamic_slice_in_dim(full_owner, strip_index * row_count, row_count, 1)
    token_hot = (local_owner[..., None] == jnp.arange(latent_count, dtype=jnp.int32)).astype(
        jnp.float32
    )
    class_onehot = (class_labels[..., None] == jnp.arange(class_count, dtype=jnp.int32)).astype(
        jnp.bfloat16
    )
    class_rows = jnp.einsum(
        "ywj,gj->ywg", class_onehot, class_embedding_matrix, preferred_element_type=jnp.float32
    )
    condition = timestep_features(time_steps, model_width) + class_rows
    silu_value, silu_pull = jax.vjp(jax.nn.silu, condition)
    silu_cond = silu_value.astype(jnp.bfloat16)
    modulation = jnp.einsum(
        "cbd,de->cbe", silu_cond, adaptive_weight, preferred_element_type=jnp.float32
    )
    modulation = modulation + adaptive_bias.astype(jnp.float32)
    token_mod = jnp.einsum("crkb,cbe->crke", token_hot, modulation, precision=EXACT_PRECISION)
    shift_one, scale_one, gate_one, shift_two, scale_two, gate_two = jnp.split(
        token_mod, 6, axis=-1
    )
    inputs = tokens.astype(jnp.float32)
    first_value, first_pull = jax.vjp(modulate, inputs, shift_one, scale_one)
    first = first_value.astype(jnp.bfloat16)
    first_padded = padded_2(first, (("strip", 1),), 1)
    mixer_single_float = mixer_kernel.astype(jnp.float32)
    mixed = depthwise(first_padded.astype(jnp.float32), mixer_single_float).astype(jnp.bfloat16)
    joint = jnp.einsum("crkd,de->crke", mixed, joint_weight, preferred_element_type=jnp.float32)
    query_rows = joint[..., :model_width].astype(jnp.bfloat16)
    keys_local = joint[..., model_width : 2 * model_width].astype(jnp.bfloat16)
    values_local = joint[..., 2 * model_width :].astype(jnp.bfloat16)
    keys_canvas, values_canvas = (
        lax.all_gather(keys_local, "strip", axis=1, tiled=True),
        lax.all_gather(values_local, "strip", axis=1, tiled=True),
    )
    query_groups = to_groups(query_rows, head_count)
    key_groups = to_groups(keys_canvas, head_count)
    value_groups = to_groups(values_canvas, head_count)
    query_owner = group_owner(local_owner)
    key_owner = group_owner(full_owner)
    allowed = (query_owner[..., :, None] == key_owner[..., None, :])[:, :, :, None]

    def attention_scores():
        raw = (
            jnp.einsum(
                "cabhnd,cabhmd->cabhnm",
                query_groups,
                key_groups,
                preferred_element_type=jnp.float32,
            )
            * factor
        )
        return jnp.where(allowed, raw, MASKED)

    scores = attention_scores()
    peak = jnp.max(scores, axis=-1, keepdims=True)
    lifted_float = jnp.exp(scores - peak)
    total = jnp.sum(lifted_float, axis=-1, keepdims=True)
    softened = (lifted_float / total).astype(jnp.bfloat16)
    log_total = peak + jnp.log(total)
    attended_groups = jnp.einsum(
        "cabhnm,cabhmd->cabhnd", softened, value_groups, preferred_element_type=jnp.float32
    )
    attended = from_groups(attended_groups, row_count, column_total).astype(jnp.bfloat16)
    branch_one = jnp.einsum(
        "crkd,de->crke", attended, output_weight, preferred_element_type=jnp.float32
    )
    branch_one = branch_one + output_bias.astype(jnp.float32)
    residual = inputs + gate_one * branch_one
    second_value, second_pull = jax.vjp(modulate, residual, shift_two, scale_two)
    second = second_value.astype(jnp.bfloat16)
    expanded = jnp.einsum(
        "crkd,df->crkf", second, expand_weight, preferred_element_type=jnp.float32
    )
    expanded = (expanded + expand_bias.astype(jnp.float32)).astype(jnp.bfloat16)
    expanded_padded = padded_2(expanded, (("strip", 1),), 1)
    hidden_float = hidden_kernel.astype(jnp.float32)
    conv_out = depthwise(expanded_padded.astype(jnp.float32), hidden_float)
    gelu_value, gelu_pull = jax.vjp(jax.nn.gelu, conv_out)
    activated = gelu_value.astype(jnp.bfloat16)
    branch_two = jnp.einsum(
        "crkf,fd->crkd", activated, reduce_weight, preferred_element_type=jnp.float32
    )
    branch_two = branch_two + reduce_bias.astype(jnp.float32)
    outputs = (residual + gate_two * branch_two).astype(jnp.bfloat16)
    upstream = output_cotangent.astype(jnp.float32)
    two_grad = (upstream * gate_two).astype(jnp.bfloat16)
    gate_two_grad = upstream * branch_two
    reduce_bias_grad = jnp.sum(two_grad.astype(jnp.float32), axis=(0, 1, 2))
    reduce_weight_grad = jnp.einsum(
        "crkf,crkd->fd", activated, two_grad, preferred_element_type=jnp.float32
    )
    activated_grad = jnp.einsum(
        "crkd,fd->crkf", two_grad, reduce_weight, preferred_element_type=jnp.float32
    )
    conv_grad = gelu_pull(activated_grad)[0].astype(jnp.bfloat16)
    conv_padded = padded_2(conv_grad, (("strip", 1),), 1)
    expanded_grad = depthwise(conv_padded.astype(jnp.float32), hidden_float[:, ::-1]).astype(
        jnp.bfloat16
    )
    hidden_kernel_grad = kernel_grad(
        expanded_padded.astype(jnp.float32), conv_grad.astype(jnp.float32)
    )
    expand_bias_grad = jnp.sum(expanded_grad.astype(jnp.float32), axis=(0, 1, 2))
    expand_weight_grad = jnp.einsum(
        "crkd,crkf->df", second, expanded_grad, preferred_element_type=jnp.float32
    )
    second_grad = jnp.einsum(
        "crkf,df->crkd", expanded_grad, expand_weight, preferred_element_type=jnp.float32
    )
    residual_part, shift_two_grad, scale_two_grad = second_pull(second_grad)
    residual_grad = upstream + residual_part
    gate_one_grad = residual_grad * branch_one
    one_grad = (residual_grad * gate_one).astype(jnp.bfloat16)
    output_bias_grad = jnp.sum(one_grad.astype(jnp.float32), axis=(0, 1, 2))
    output_weight_grad = jnp.einsum(
        "crkd,crke->de", attended, one_grad, preferred_element_type=jnp.float32
    )
    attended_grad = jnp.einsum(
        "crke,de->crkd", one_grad, output_weight, preferred_element_type=jnp.float32
    ).astype(jnp.bfloat16)
    attended_grad_groups = to_groups(attended_grad, head_count)
    probs = jnp.exp(attention_scores() - log_total)
    prob_grads = jnp.einsum(
        "cabhnd,cabhmd->cabhnm",
        attended_grad_groups,
        value_groups,
        preferred_element_type=jnp.float32,
    )
    spread_sum = jnp.sum(probs * prob_grads, axis=-1, keepdims=True)
    score_grads = (probs * (prob_grads - spread_sum)).astype(jnp.bfloat16)
    query_grad_groups = (
        jnp.einsum(
            "cabhnm,cabhmd->cabhnd", score_grads, key_groups, preferred_element_type=jnp.float32
        )
        * factor
    )
    query_grad = from_groups(query_grad_groups, row_count, column_total).astype(jnp.bfloat16)
    all_queries, all_attended = (
        lax.all_gather(query_groups, "strip", axis=4, tiled=True),
        lax.all_gather(attended_grad_groups, "strip", axis=4, tiled=True),
    )
    all_logs, all_spreads = (
        lax.all_gather(log_total[..., 0], "strip", axis=4, tiled=True),
        lax.all_gather(spread_sum[..., 0], "strip", axis=4, tiled=True),
    )
    own_keys = to_groups(keys_local, head_count)
    own_values = to_groups(values_local, head_count)
    own_allowed = (key_owner[..., :, None] == query_owner[..., None, :])[:, :, :, None]
    own_scores = (
        jnp.einsum(
            "cabhnd,cabhmd->cabhnm", all_queries, own_keys, preferred_element_type=jnp.float32
        )
        * factor
    )
    own_scores = jnp.where(own_allowed, own_scores, MASKED)
    own_probs = jnp.exp(own_scores - all_logs[..., None])
    own_prob_grads = jnp.einsum(
        "cabhnd,cabhmd->cabhnm", all_attended, own_values, preferred_element_type=jnp.float32
    )
    own_score_grads = (own_probs * (own_prob_grads - all_spreads[..., None])).astype(jnp.bfloat16)
    key_grad_groups = (
        jnp.einsum(
            "cabhnm,cabhnd->cabhmd",
            own_score_grads,
            all_queries,
            preferred_element_type=jnp.float32,
        )
        * factor
    )
    value_grad_groups = jnp.einsum(
        "cabhnm,cabhnd->cabhmd",
        own_probs.astype(jnp.bfloat16),
        all_attended,
        preferred_element_type=jnp.float32,
    )
    key_grad = from_groups(key_grad_groups, row_count, column_total).astype(jnp.bfloat16)
    value_grad = from_groups(value_grad_groups, row_count, column_total).astype(jnp.bfloat16)
    joint_grad = jnp.concatenate([query_grad, key_grad, value_grad], axis=-1)
    joint_weight_grad = jnp.einsum(
        "crkd,crke->de", mixed, joint_grad, preferred_element_type=jnp.float32
    )
    mixed_grad = jnp.einsum(
        "crke,de->crkd", joint_grad, joint_weight, preferred_element_type=jnp.float32
    ).astype(jnp.bfloat16)
    mixed_padded = padded_2(mixed_grad, (("strip", 1),), 1)
    first_grad = depthwise(mixed_padded.astype(jnp.float32), mixer_single_float[:, ::-1])
    mixer_kernel_grad = kernel_grad(
        first_padded.astype(jnp.float32), mixed_grad.astype(jnp.float32)
    )
    input_part, shift_one_grad, scale_one_grad = first_pull(first_grad)
    tokens_grad = residual_grad + input_part
    token_grad = jnp.concatenate(
        [
            shift_one_grad,
            scale_one_grad,
            gate_one_grad,
            shift_two_grad,
            scale_two_grad,
            gate_two_grad,
        ],
        axis=-1,
    )
    modulation_grad = jnp.einsum("crkb,crke->cbe", token_hot, token_grad, precision=EXACT_PRECISION)
    silu_grad = jnp.einsum(
        "cbe,de->cbd",
        modulation_grad,
        adaptive_weight.astype(jnp.float32),
        precision=EXACT_PRECISION,
    )
    conditioning_grad = silu_pull(silu_grad)[0]
    table_grad = jnp.einsum(
        "soy,sok->yk",
        conditioning_grad,
        class_onehot.astype(jnp.float32),
        precision=EXACT_PRECISION,
    )
    adaptive_grad = jnp.einsum(
        "cbd,cbe->de", silu_cond.astype(jnp.float32), modulation_grad, precision=EXACT_PRECISION
    )
    adaptive_bias_grad = jnp.sum(modulation_grad, axis=(0, 1))
    (
        table_shard,
        adaptive_shard,
        adaptive_bias_shard,
        mixer_shard,
        joint_shard,
        output_shard,
        output_bias_shard,
        expand_shard,
        expand_bias_shard,
        hidden_shard,
        reduce_shard,
        reduce_bias_shard,
    ) = (
        lax.psum_scatter(
            table_grad.astype(jnp.bfloat16), "strip", scatter_dimension=0, tiled=True
        ).astype(jnp.float32),
        lax.psum_scatter(
            adaptive_grad.astype(jnp.bfloat16), "strip", scatter_dimension=0, tiled=True
        ).astype(jnp.float32),
        lax.psum_scatter(
            adaptive_bias_grad.astype(jnp.bfloat16), "strip", scatter_dimension=0, tiled=True
        ).astype(jnp.float32),
        lax.psum_scatter(
            mixer_kernel_grad.astype(jnp.bfloat16), "strip", scatter_dimension=0, tiled=True
        ).astype(jnp.float32),
        lax.psum_scatter(
            joint_weight_grad.astype(jnp.bfloat16), "strip", scatter_dimension=0, tiled=True
        ).astype(jnp.float32),
        lax.psum_scatter(
            output_weight_grad.astype(jnp.bfloat16), "strip", scatter_dimension=0, tiled=True
        ).astype(jnp.float32),
        lax.psum_scatter(
            output_bias_grad.astype(jnp.bfloat16), "strip", scatter_dimension=0, tiled=True
        ).astype(jnp.float32),
        lax.psum_scatter(
            expand_weight_grad.astype(jnp.bfloat16), "strip", scatter_dimension=0, tiled=True
        ).astype(jnp.float32),
        lax.psum_scatter(
            expand_bias_grad.astype(jnp.bfloat16), "strip", scatter_dimension=0, tiled=True
        ).astype(jnp.float32),
        lax.psum_scatter(
            hidden_kernel_grad.astype(jnp.bfloat16), "strip", scatter_dimension=0, tiled=True
        ).astype(jnp.float32),
        lax.psum_scatter(
            reduce_weight_grad.astype(jnp.bfloat16), "strip", scatter_dimension=0, tiled=True
        ).astype(jnp.float32),
        lax.psum_scatter(
            reduce_bias_grad.astype(jnp.bfloat16), "strip", scatter_dimension=0, tiled=True
        ).astype(jnp.float32),
    )
    summed = (
        lax.psum(table_shard.astype(jnp.bfloat16), "batch").astype(jnp.float32),
        lax.psum(adaptive_shard.astype(jnp.bfloat16), "batch").astype(jnp.float32),
        lax.psum(adaptive_bias_shard.astype(jnp.bfloat16), "batch").astype(jnp.float32),
        lax.psum(mixer_shard.astype(jnp.bfloat16), "batch").astype(jnp.float32),
        lax.psum(joint_shard.astype(jnp.bfloat16), "batch").astype(jnp.float32),
        lax.psum(output_shard.astype(jnp.bfloat16), "batch").astype(jnp.float32),
        lax.psum(output_bias_shard.astype(jnp.bfloat16), "batch").astype(jnp.float32),
        lax.psum(expand_shard.astype(jnp.bfloat16), "batch").astype(jnp.float32),
        lax.psum(expand_bias_shard.astype(jnp.bfloat16), "batch").astype(jnp.float32),
        lax.psum(hidden_shard.astype(jnp.bfloat16), "batch").astype(jnp.float32),
        lax.psum(reduce_shard.astype(jnp.bfloat16), "batch").astype(jnp.float32),
        lax.psum(reduce_bias_shard.astype(jnp.bfloat16), "batch").astype(jnp.float32),
    )
    return (
        outputs,
        tokens_grad,
        summed[0],
        summed[1],
        summed[2],
        summed[3],
        summed[4],
        summed[5],
        summed[6],
        summed[7],
        summed[8],
        summed[9],
        summed[10],
        summed[11],
    )


def solution(mesh):
    grouped = (mesh.shape["batch"], mesh.shape["strip"]) == (4, 8)
    return jax.shard_map(
        local_grouped if grouped else local,
        mesh=mesh,
        in_specs=(
            P("batch", "strip", None, None),
            P("batch", None, None),
            P("batch", None),
            P("batch", None),
            P(),
            P(),
            P(),
            P(),
            P(),
            P(),
            P(),
            P(),
            P(),
            P(),
            P(),
            P(),
            P("batch", "strip", None, None),
        ),
        out_specs=(
            P("batch", "strip", None, None),
            P("batch", "strip", None, None),
            P("strip", None),
            P("strip", None),
            P("strip"),
            P("strip", None),
            P("strip", None),
            P("strip", None),
            P("strip"),
            P("strip", None),
            P("strip"),
            P("strip", None),
            P("strip", None),
            P("strip"),
        ),
        check_vma=False,
    )
```

```python
import math
from types import SimpleNamespace

import jax
import jax.numpy as jnp
from jax import lax
from jax.experimental import pallas as pl
from jax.experimental.pallas import tpu as pltpu
from jax.sharding import PartitionSpec as P

HEADS = 12
EPSILON = 1e-06
MASKED = -1e30
MESH = pl.DeviceIdType.MESH
F32 = jnp.float32
BF16 = jnp.bfloat16
VMEM_BYTES = 62 * 1024 * 1024
WHOLE = pl.BlockSpec(memory_space=pltpu.VMEM)
LEFT = pl.BlockSpec(memory_space=pl.ANY)
SCALARS = pl.BlockSpec(memory_space=pltpu.SMEM)
NT = (((1,), (1,)), ((), ()))
TN = (((0,), (0,)), ((), ()))


def dot(a, b):
    return jnp.dot(a, b, preferred_element_type=F32)


def dot_nt(a, b):
    return lax.dot_general(a, b, NT, preferred_element_type=F32)


def dot_tn(a, b):
    return lax.dot_general(a, b, TN, preferred_element_type=F32)


def send_to(src, dst, sems, index, batch, strip):
    return pltpu.make_async_remote_copy(
        src_ref=src,
        dst_ref=dst,
        send_sem=sems[0].at[index],
        recv_sem=sems[1].at[index],
        device_id=(batch, strip),
        device_id_type=MESH,
    )


def entry_barrier(strips):
    s = lax.axis_index("strip")
    b = lax.axis_index("batch")
    z = s // 2
    barrier = pltpu.get_barrier_semaphore()
    count = 0
    for d in range(1, strips):
        pl.semaphore_signal(
            barrier, inc=1, device_id=(b, lax.rem(s + d, strips)), device_id_type=MESH
        )
        count += 1
    for e in range(1, 4):
        for core in range(2):
            pl.semaphore_signal(
                barrier, inc=1, device_id=(lax.rem(b + e, 4), 2 * z + core), device_id_type=MESH
            )
            count += 1
    pl.semaphore_wait(barrier, count)


def spread(mod, width):
    return jnp.concatenate(
        [jnp.broadcast_to(mod[0:1], (8, width)), jnp.broadcast_to(mod[1:2], (8, width))], axis=0
    )


def spread_columns(buffer, r, x):
    for k in range(x.shape[-1] // 128):
        buffer[r, k] = x[:, k * 128 : k * 128 + 128]


def every_second(buffer, r, p):
    return jnp.concatenate(
        [buffer[r, k, pl.ds(p, 16, stride=2), :] for k in range(buffer.shape[1])], axis=-1
    )


def interleave(buffer, r, p, x):
    for k in range(x.shape[-1] // 128):
        buffer[r, k, pl.ds(p, 16, stride=2), :] = x[:, k * 128 : k * 128 + 128]


def joined(buffer, r):
    return jnp.concatenate([buffer[r, k] for k in range(buffer.shape[1])], axis=-1)


def ln_parts(x):
    centre = jnp.mean(x, axis=-1, keepdims=True)
    centred = x - centre
    var = jnp.mean(centred * centred, axis=-1, keepdims=True)
    inv = lax.rsqrt(var + EPSILON)
    return centred * inv, inv


def ln_back(grad, n, inv):
    mean0 = jnp.mean(grad, axis=-1, keepdims=True)
    mean1 = jnp.mean(grad * n, axis=-1, keepdims=True)
    return inv * (grad - mean0 - n * mean1)


def window(load, r):
    even = load(r, 0).astype(F32)
    odd = load(r, 1).astype(F32)
    n = even.shape[0]
    j = lax.broadcasted_iota(jnp.int32, even.shape, 0)
    odd_m = jnp.where(j == 0, 0.0, pltpu.roll(odd, 1, 0))
    even_p = jnp.where(j == n - 1, 0.0, pltpu.roll(even, n - 1, 0))
    return odd_m, even, odd, even_p


def conv(rows, weights, flip):
    out = []
    for p in range(2):
        total = None
        for i in range(3):
            for j in range(3):
                t = 3 * i + j
                a = weights[8 - t if flip else t] * rows[i][p + j]
                total = a if total is None else total + a
        out.append(total)
    return out


def taps(rows, centre, sums):
    new = list(sums)
    for i in range(3):
        for j in range(3):
            a = rows[i][j] * centre[0] + rows[i][1 + j] * centre[1]
            t = 8 - (3 * i + j)
            new[t] = sums[t] + (a[0:8] + a[8:16])
    return new


def halves(x):
    return jnp.concatenate(
        [jnp.sum(x[0:8], axis=0, keepdims=True), jnp.sum(x[8:16], axis=0, keepdims=True)], axis=0
    )


def gelu_both(x):
    k0 = math.sqrt(2.0 / math.pi)
    square = x * x
    t = jnp.tanh(k0 * x * (1.0 + 0.044715 * square))
    cdf = 0.5 + 0.5 * t
    slope = cdf + (0.5 * k0) * x * (1.0 - t * t) * (1.0 + (3.0 * 0.044715) * square)
    return x * cdf, slope


def block_kernel(names, *refs):
    m = SimpleNamespace(**dict(zip(names, refs)))
    rows, cols, width = m.tok.shape
    half = width // 2
    strips = lax.axis_size("strip")
    chips = strips // 2
    chip_rows = 2 * rows
    total = strips * 64
    own = width // strips
    s = lax.axis_index("strip")
    b = lax.axis_index("batch")
    z = s // 2
    c = lax.rem(s, 2)
    sibling = 2 * z + 1 - c
    y, x = b // 2, lax.rem(b, 2)
    x_mate = 2 * y + 1 - x
    y_mate = 2 * (1 - y) + x
    sent = []

    def chip(d):
        return lax.rem(z + d, chips)

    def start(copy):
        copy.start()
        sent.append(copy)

    loads = {}

    def load(name, src, dst, index):
        loads[name] = pltpu.make_async_copy(src, dst, m.load_sem.at[index])
        loads[name].start()

    for part in range(3):
        off = pl.multiple_of(part * width + c * half, 128)
        load(f"wj{part}", m.wj_hbm.at[:, pl.ds(off, half)], m.wj.at[part], part)
    load("cot", m.cot_hbm, m.cot, 3)
    load("wo", m.wo_hbm, m.wo, 4)
    for n in range(chips):
        off = pl.multiple_of((2 * n + c) * half, 128)
        spot = pl.ds(n * half, half)
        load(f"we{n}", m.we_hbm.at[:, pl.ds(off, half)], m.we.at[:, spot], 5 + n)
        load(f"wr{n}", m.wr_hbm.at[pl.ds(off, half)], m.wr.at[spot], 5 + chips + n)
    entry_barrier(strips)

    m.cond_all[b] = m.cond[...]
    for e in range(1, 4):
        start(
            send_to(m.cond_all.at[b], m.cond_all.at[b], m.cond_sem, e, lax.rem(b + e, 4), s)
        )

    def block_mod(n):
        return spread(m.mod[:, n * width : (n + 1) * width], width)

    scale1 = 1.0 + block_mod(1)
    shift1 = block_mod(0)

    def first_row(r):
        spread_columns(m.rowf, r, m.tok[r].astype(F32))
        for p in range(2):
            v = every_second(m.rowf, r, p)
            m.xd[r, p] = v.astype(BF16)
            n, _ = ln_parts(v)
            m.fp[r + 1, p] = (n * scale1 + shift1).astype(BF16)

    def edge_sends(buffer, sems):
        up = send_to(buffer.at[1], buffer.at[rows + 1], sems, 0, b, s - 1)
        down = send_to(buffer.at[rows], buffer.at[0], sems, 1, b, s + 1)
        return up, down

    def start_edges(buffer, sems):
        up, down = edge_sends(buffer, sems)

        @pl.when(s > 0)
        def _():
            up.start()

        @pl.when(s < strips - 1)
        def _():
            down.start()

    def edges_sent(buffer, sems):
        up, down = edge_sends(buffer, sems)

        @pl.when(s > 0)
        def _():
            up.wait_send()

        @pl.when(s < strips - 1)
        def _():
            down.wait_send()

    def top_edge(buffer, sems):
        @pl.when(s > 0)
        def _():
            send_to(buffer.at[1], buffer.at[0], sems, 1, b, s - 1).wait_recv()

        @pl.when(s == 0)
        def _():
            buffer[0] = jnp.zeros_like(buffer[0])

    def bottom_edge(buffer, sems):
        @pl.when(s < strips - 1)
        def _():
            send_to(buffer.at[1], buffer.at[rows + 1], sems, 0, b, s + 1).wait_recv()

        @pl.when(s == strips - 1)
        def _():
            buffer[rows + 1] = jnp.zeros_like(buffer[0])

    first_row(0)
    first_row(rows - 1)
    start_edges(m.fp, m.fp_sem)

    def body(r, _):
        first_row(r)
        return 0

    lax.fori_loop(1, rows - 1, body, 0)

    def mixed_rows(low, high):
        for k in range(width // 128):
            lanes = pl.ds(k * 128, 128)
            weights = [m.mk[t : t + 1, k * 128 : k * 128 + 128] for t in range(9)]

            def line(r, p):
                return m.fp[r, p, :, lanes]

            def step(r, carry):
                new = window(line, r + 2)
                out = conv((carry[0], carry[1], new), weights, False)
                for p in range(2):
                    m.ms[lax.rem(r, 2) * 2 + p, r // 2, :, lanes] = out[p].astype(BF16)
                return carry[1], new

            lax.fori_loop(low, high, step, (window(line, low), window(line, low + 1)))

    mixed_rows(1, rows - 1)
    top_edge(m.fp, m.fp_sem)
    mixed_rows(0, 1)
    bottom_edge(m.fp, m.fp_sem)
    mixed_rows(rows - 1, rows)

    def to_groups(source, target, sems, sems2):
        for d in range(1, chips):
            g = chip(d)
            start(send_to(source.at[g], target.at[s], sems, d, b, 2 * g + c))
        target[s] = source[z]

    def pass_on(target, sems, sems2, d):
        i = 2 * chip(chips - d) + c
        if d:
            send_to(target.at[i], target.at[i], sems, d, b, i).wait_recv()
        start(send_to(target.at[i], target.at[i], sems2, d, b, sibling))

    def groups_ready(target, sems2):
        for d in range(chips):
            i = 2 * chip(chips - d) + 1 - c
            send_to(target.at[i], target.at[i], sems2, d, b, sibling).wait_recv()

    to_groups(m.ms, m.mg, m.mg_sem, m.mg_sem2)

    m.acc[...] = jnp.zeros_like(m.acc)
    gate2 = block_mod(5)
    loads["cot"].wait()

    def upstream_row(r, _):
        spread_columns(m.rowf, r, m.cot[r].astype(F32))
        for p in range(2):
            up = every_second(m.rowf, r, p)
            m.ctd[2 * r + p] = up.astype(BF16)
            two = (up * gate2).astype(BF16)
            m.tg[c, 2 * r + p] = two
            m.acc[0] += two.astype(F32)
        return 0

    lax.fori_loop(0, rows, upstream_row, 0)
    start(send_to(m.tg.at[c], m.tg.at[c], m.pair_sem, 0, b, sibling))

    for d in range(chips):
        pass_on(m.mg, m.mg_sem, m.mg_sem2, d)
    groups_ready(m.mg, m.mg_sem2)
    for part in range(3):
        loads[f"wj{part}"].wait()

    v = m.mg[...].reshape(total, width)
    for part in range(3):
        w = dot(v, m.wj[part]).astype(BF16)
        for n in range(3):
            m.qkv[3 * part + n] = w[:, n * 128 : n * 128 + 128]

    where = lax.broadcasted_iota(jnp.int32, (1, total), 1)
    lefts = lax.rem(where, 16) < 8
    key_owner = jnp.zeros((1, total), jnp.int32)
    for t in range(4):
        both = jnp.where(lefts, m.owner[2 * t], m.owner[2 * t + 1])
        key_owner = jnp.where(where // 128 == t, both, key_owner)
    where = lax.broadcasted_iota(jnp.int32, (total, 1), 0)
    lefts = lax.rem(where, 16) < 8
    query_owner = jnp.zeros((total, 1), jnp.int32)
    for t in range(4):
        both = jnp.where(lefts, m.owner[2 * t], m.owner[2 * t + 1])
        query_owner = jnp.where(where // 128 == t, both, query_owner)
    allowed = query_owner == key_owner
    lane = lax.broadcasted_iota(jnp.int32, (total, 128), 1) < 64
    factor = 64 ** -0.5

    def head(v, h):
        return jnp.where(lane if h == 0 else jnp.logical_not(lane), v, jnp.zeros_like(v))

    for n in range(3):
        mine = c * 3 + n
        q2 = (m.qkv[n].astype(F32) * factor).astype(BF16)
        outs = []
        for h in range(2):
            scores = jnp.where(allowed, dot_nt(head(q2, h), m.qkv[3 + n]), MASKED)
            peak = jnp.max(scores, axis=-1, keepdims=True)
            lifted = jnp.exp(scores - peak)
            inv = 1.0 / jnp.sum(lifted, axis=-1, keepdims=True)
            m.probs[n, h] = (lifted * inv).astype(BF16)
            outs.append(dot(lifted.astype(BF16), m.qkv[6 + n]) * inv)
        m.ag[mine] = jnp.where(lane, outs[0], outs[1]).astype(BF16)
        for d in range(1, strips):
            t = lax.rem(s + d, strips)
            start(
                send_to(
                    m.ag.at[mine, pl.ds(pl.multiple_of(t * 64, 64), 64)],
                    m.ai.at[mine, z],
                    m.ai_sem,
                    (n, d),
                    b,
                    t,
                )
            )
        start(send_to(m.ag.at[mine], m.ag.at[mine], m.ag_sem, n, b, sibling))
        m.ai[mine, z] = m.ag[mine, pl.ds(pl.multiple_of(s * 64, 64), 64), :]

    for n in range(3):
        for d in range(1, strips):
            i = lax.rem(s - d + strips, strips)
            spot = lax.rem(i, 2) * 3 + n
            send_to(
                m.ag.at[spot, pl.ds(0, 64)], m.ai.at[spot, i // 2], m.ai_sem, (n, d), b, i
            ).wait_recv()

    gate1 = block_mod(2)
    shift2 = block_mod(3)
    scale2 = 1.0 + block_mod(4)
    loads["wo"].wait()

    v = jnp.concatenate([m.ai[n].reshape(chips * 64, 128) for n in range(6)], axis=-1)
    m.b1[...] = (dot(v, m.wo[...]) + m.ob[...]).reshape(m.b1.shape)

    def residual_row(i, _):
        rp = 4 * lax.rem(i, rows // 2) + i // (rows // 2)
        u = m.xd[rp // 2, lax.rem(rp, 2)].astype(F32) + gate1 * m.b1[i]
        m.res[rp] = u
        n, _ = ln_parts(u)
        m.sc[c, rp] = (n * scale2 + shift2).astype(BF16)
        return 0

    lax.fori_loop(0, 2 * rows, residual_row, 0, unroll=2)
    start(send_to(m.sc.at[c], m.sc.at[c], m.pair_sem, 1, b, sibling))

    def halo_sends(buffer, sems):
        up = send_to(buffer.at[1], buffer.at[chip_rows + 1], sems, 0, b, s - 2)
        down = send_to(buffer.at[chip_rows], buffer.at[0], sems, 1, b, s + 2)
        return up, down

    def start_halo(buffer, sems):
        up, down = halo_sends(buffer, sems)

        @pl.when(z > 0)
        def _():
            up.start()

        @pl.when(z < chips - 1)
        def _():
            down.start()

    def halo_sent(buffer, sems):
        up, down = halo_sends(buffer, sems)

        @pl.when(z > 0)
        def _():
            up.wait_send()

        @pl.when(z < chips - 1)
        def _():
            down.wait_send()

    def take_halo(buffer, sems):
        @pl.when(z > 0)
        def _():
            send_to(buffer.at[1], buffer.at[0], sems, 1, b, s - 2).wait_recv()

        @pl.when(z == 0)
        def _():
            buffer[0] = jnp.zeros_like(buffer[0])

        @pl.when(z < chips - 1)
        def _():
            send_to(buffer.at[1], buffer.at[chip_rows + 1], sems, 0, b, s + 2).wait_recv()

        @pl.when(z == chips - 1)
        def _():
            buffer[chip_rows + 1] = jnp.zeros_like(buffer[0])

    send_to(m.sc.at[c], m.sc.at[1 - c], m.pair_sem, 1, b, sibling).wait_recv()
    for n in range(chips):
        loads[f"we{n}"].wait()
        loads[f"wr{n}"].wait()
    hidden = chips * half
    bias = jnp.concatenate([m.eb[2 * n + c] for n in range(chips)], axis=-1)
    blocks = rows // 2

    def expand(first, second):
        v = jnp.concatenate(
            [m.sc[0, first : first + rows], m.sc[1, second : second + rows]], axis=0
        ).reshape(rows * 32, width)
        w = (dot(v, m.we[...]) + bias).astype(BF16).reshape(rows, 2, 16, hidden)
        m.ex[pl.ds(1 + first // 2, blocks)] = w[0:blocks]
        m.ex[pl.ds(1 + rows + second // 2, blocks)] = w[blocks:]

    expand(0, rows)
    start_halo(m.ex, m.ex_sem)
    expand(rows, 0)
    send_to(m.tg.at[c], m.tg.at[1 - c], m.pair_sem, 0, b, sibling).wait_recv()
    chip_tg = m.tg[...].reshape(total, width)
    for h in range(2):
        m.big[h] = dot_nt(chip_tg, m.wr[h * width : h * width + width, :]).reshape(m.big.shape[1:])

    first_mate, then_mate = (x_mate, y_mate), (y_mate, x_mate)
    part_rows = width // 8

    def r_source(n, h, mine):
        at = pl.ds(h * part_rows, part_rows)
        if h == 0:
            return m.rw.at[n, :, x if mine else 1 - x, at]
        return m.rw.at[n, y if mine else 1 - y, :, at]

    def r_one(n, h):
        return send_to(r_source(n, h, False), m.r1.at[n, h], m.r1_sem, (n, h), first_mate[h], s)

    def r_two(n, h):
        src = m.r1.at[n, h, (1 - y) if h == 0 else (1 - x)]
        return send_to(src, m.r2.at[n, h], m.r2_sem, (n, h), then_mate[h], s)

    def r_three(d):
        n = chip(d)
        return send_to(m.r2.at[n], m.r3.at[d], m.r3_sem, d, b, 2 * n + c)

    def r_four(e):
        return send_to(m.r_all.at[b], m.r_all.at[b], m.r4_sem, e, lax.rem(b + e, 4), s)

    def r_half(n):
        for h in range(2):
            r_one(n, h).wait_recv()
            kept = r_source(n, h, True)[...].astype(F32)
            m.r1[n, h] = (m.r1[n, h].astype(F32) + kept).astype(BF16)
            r_two(n, h).start()

    def r_quarter(d):
        n = chip(d)
        for h in range(2):
            r_two(n, h).wait_recv()
            kept = m.r1[n, h, y if h == 0 else x].astype(F32)
            m.r2[n, h] = (m.r2[n, h].astype(F32) + kept).astype(BF16)
        if d:
            r_three(d).start()

    def r_sum():
        v = m.r2[z].astype(F32)
        for d in range(1, chips):
            r_three(d).wait_recv()
            v = v + m.r3[d].astype(F32)
        m.r_all[b] = v.astype(BF16)
        for e in range(1, 4):
            r_four(e).start()

    def c_source(j, h, mine):
        block = m.ew.at[j] if not isinstance(j, int) or j < 4 else m.jo.at[j - 4]
        at = pl.ds(2 * h, 2)
        if h == 0:
            return block.at[at, :, x if mine else 1 - x]
        return block.at[at, y if mine else 1 - y]

    def c_one(j, h):
        return send_to(c_source(j, h, False), m.c1.at[j, h], m.c1_sem, (j, h), first_mate[h], s)

    def c_two(j, h):
        src = m.c1.at[j, h, :, 1 - y] if h == 0 else m.c1.at[j, h, :, 1 - x]
        return send_to(src, m.c2.at[j, pl.ds(2 * h, 2)], m.c2_sem, (j, h), then_mate[h], s)

    def c_three(j, d):
        t = chip(d)
        return send_to(m.c2.at[j, t], m.c3.at[j, d], m.c3_sem, (j, d), b, 2 * t + c)

    def c_four(g, e):
        return pltpu.make_async_remote_copy(
            src_ref=m.c_out.at[g],
            dst_ref=m.c_all.at[g, x, c],
            send_sem=m.c4_sem[0].at[g, e],
            recv_sem=m.c4_sem[1].at[g, e, c],
            device_id=(lax.rem(b + e, 4), 2 * z + y),
            device_id_type=MESH,
        )

    def c_begin(j):
        for h in range(2):
            c_one(j, h).start()

    def c_half(j):
        for h in range(2):
            c_one(j, h).wait_recv()
            kept = c_source(j, h, True)[...].astype(F32)
            m.c1[j, h] = (m.c1[j, h].astype(F32) + kept).astype(BF16)
            c_two(j, h).start()

    def c_quarter(j):
        for h in range(2):
            c_two(j, h).wait_recv()
            at = pl.ds(2 * h, 2)
            kept = (m.c1[j, h, :, y] if h == 0 else m.c1[j, h, :, x]).astype(F32)
            m.c2[j, at] = (m.c2[j, at].astype(F32) + kept).astype(BF16)

    def c_spread(j):
        for d in range(1, chips):
            c_three(j, d).start()

    def c_sum(g):
        for i in range(4):
            j = 4 * g + i
            v = m.c2[j, z].astype(F32)
            for d in range(1, chips):
                c_three(j, d).wait_recv()
                v = v + m.c3[j, d].astype(F32)
            m.c_out[g, i] = v.astype(BF16)

        @pl.when(c == y)
        def _():
            m.c_all[g, x, c] = m.c_out[g]

        for e in range(1, 4):
            c_four(g, e).start()

        @pl.when(c != y)
        def _():
            c_four(g, 0).start()

    take_halo(m.ex, m.ex_sem)
    for n in range(chips):
        for k in range(3 * n, 3 * n + 3):
            lanes = pl.ds(k * 128, 128)
            inner = pl.ds((k % 3) * 128, 128)
            weights = [m.hk[2 * n + c, t : t + 1, inner] for t in range(9)]
            spot = pl.ds((k % 6) * 128, 128)

            def line(r, p):
                return m.ex[r, p, :, lanes]

            above, here = window(line, 0), window(line, 1)
            for r in range(chip_rows):
                below = window(line, r + 2)
                out = conv((above, here, below), weights, False)
                for p in range(2):
                    value, slope = gelu_both(out[p])
                    rp = 2 * r + p
                    grad = m.big[k // 6, rp // 16, rp % 16, :, spot]
                    m.act[rp, :, lanes] = value.astype(BF16)
                    m.cg[r + 1, p, :, lanes] = (grad * slope).astype(BF16)
                above, here = here, below
        full = m.act[:, :, n * half : n * half + half].reshape(total, half)
        m.rw[n] = dot_tn(chip_tg, full).astype(BF16).reshape(m.rw.shape[1:])
        for h in range(2):
            r_one(n, h).start()
    start_halo(m.cg, m.cg_sem)
    full = m.act[...].reshape(total, hidden)
    m.big[0] = dot(full, m.wr[...]).reshape(m.big.shape[1:])
    b2_copy = send_to(m.big.at[0, 1 - c], m.b2_in, m.pair_sem, 2, b, sibling)
    b2_copy.start()
    m.hkg[...] = jnp.zeros_like(m.hkg)
    take_halo(m.cg, m.cg_sem)
    chip_sc = m.sc[...].reshape(total, width)
    for n in range(chips):
        for k in range(3 * n, 3 * n + 3):
            lanes = pl.ds(k * 128, 128)
            inner = pl.ds((k % 3) * 128, 128)
            weights = [m.hk[2 * n + c, t : t + 1, inner] for t in range(9)]

            def line(r, p):
                return m.cg[r, p, :, lanes]

            above, here = window(line, 0), window(line, 1)
            sums = [jnp.zeros((8, 128), F32) for _ in range(9)]
            total_eg = jnp.zeros((8, 128), F32)
            for r in range(chip_rows):
                below = window(line, r + 2)
                three = (above, here, below)
                low = [v.astype(BF16) for v in conv(three, weights, True)]
                for p in range(2):
                    m.act[2 * r + p, :, lanes] = low[p]
                centre = [m.ex[r + 1, p, :, lanes].astype(F32) for p in range(2)]
                sums = taps(three, centre, sums)
                both = low[0].astype(F32) + low[1].astype(F32)
                total_eg = total_eg + (both[0:8] + both[8:16])
                above, here = here, below
            for t, v in enumerate(sums + [total_eg]):
                m.hkg[n, t : t + 1, inner] = jnp.sum(v, axis=0, keepdims=True)
        full = m.act[:, :, n * half : n * half + half].reshape(total, half)
        m.ew[n] = dot_tn(chip_sc, full).astype(BF16).reshape(m.ew.shape[1:])
        c_begin(n)
        r_half(n)
    full = m.act[...].reshape(total, hidden)
    m.big[1] = dot_nt(full, m.we[...]).reshape(m.big.shape[1:])
    sg_copy = send_to(m.big.at[1, 1 - c], m.sg_in, m.pair_sem, 3, b, sibling)
    sg_copy.start()
    send_to(m.big.at[0, c], m.b2_in, m.pair_sem, 2, b, sibling).wait_recv()
    send_to(m.big.at[1, c], m.sg_in, m.pair_sem, 3, b, sibling).wait_recv()

    def finish(r, _):
        for p in range(2):
            rp = 2 * r + p
            grad = m.big[1, c, rp] + m.sg_in[rp]
            v = m.res[rp]
            n, inv = ln_parts(v)
            branch = m.b1[(rows // 2) * lax.rem(rp, 4) + rp // 4]
            up = m.ctd[rp].astype(F32)
            m.acc[1] += grad
            m.acc[2] += grad * n
            back = up + ln_back(grad * scale2, n, inv)
            m.rg[rp] = back
            m.acc[3] += back * branch
            one = (back * gate1).astype(BF16)
            m.og[lax.rem(rp, 4), rp // 4] = one
            m.acc[4] += one.astype(F32)
            branch2 = m.big[0, c, rp] + m.b2_in[rp] + m.rb[...]
            m.acc[5] += up * branch2
            interleave(m.rowf, r, p, v + gate2 * branch2)
        m.out[r] = joined(m.rowf, r).astype(BF16)
        return 0

    lax.fori_loop(0, rows, finish, 0)
    out_copy = pltpu.make_async_copy(m.out, m.out_hbm, m.load_sem.at[13])
    out_copy.start()

    to_groups(m.og, m.gg, m.gg_sem, m.gg_sem2)

    pack = []
    for v in (m.acc[3], m.acc[1], m.acc[2], m.acc[5]):
        pair = halves(v)
        for h in range(2):
            pack += [pair[h : h + 1, 0:half], pair[h : h + 1, half:]]
    def own_sums(buffer, sems, value):
        buffer[b, c, z] = value.astype(BF16)
        for d in range(1, chips):
            start(send_to(buffer.at[b, c, z], buffer.at[b, c, z], sems, d, b, 2 * chip(d) + c))

    def to_canvases(buffer, sems, sems2):
        for d in range(1, chips):
            i = chip(chips - d)
            send_to(buffer.at[b, c, i], buffer.at[b, c, i], sems, d, b, 2 * i + c).wait_recv()
        for e in range(1, 4):
            start(send_to(buffer.at[b, c], buffer.at[b, c], sems2, e, lax.rem(b + e, 4), s))

    def to_sibling(buffer, sems2, sems3):
        for e in range(1, 4):
            i = lax.rem(b - e + 4, 4)
            send_to(buffer.at[i, c], buffer.at[i, c], sems2, e, i, s).wait_recv()
        start(send_to(buffer.at[:, c], buffer.at[:, c], sems3, 0, b, sibling))

    def from_sibling(buffer, sems3):
        send_to(buffer.at[:, c], buffer.at[:, 1 - c], sems3, 0, b, sibling).wait_recv()

    own_sums(m.late, m.late_sem, jnp.concatenate(pack, axis=0))
    sums_ob = jnp.sum(m.acc[4], axis=0, keepdims=True)
    sums_rb = jnp.sum(m.acc[0], axis=0, keepdims=True)
    pad_lanes = jnp.zeros((1, half - own), F32)
    pad_rows = jnp.zeros((4, half), F32)
    for t in range(strips):
        piece = jnp.concatenate(
            [
                jnp.where(c == t % 2, m.hkg[t // 2, 0:10], 0.0),
                jnp.concatenate([sums_ob[:, t * own : t * own + own], pad_lanes], axis=1),
                jnp.concatenate([sums_rb[:, t * own : t * own + own], pad_lanes], axis=1),
                pad_rows,
            ],
            axis=0,
        )
        m.piece[t] = piece.astype(BF16)
    for d in range(1, strips):
        t = lax.rem(s + d, strips)
        start(send_to(m.piece.at[t], m.piece_in.at[d], m.piece_sem, d, b, t))

    pass_on(m.gg, m.gg_sem, m.gg_sem2, 0)
    c_half(0)
    c_half(1)
    pass_on(m.gg, m.gg_sem, m.gg_sem2, 1)
    c_half(2)
    pass_on(m.gg, m.gg_sem, m.gg_sem2, 2)
    pass_on(m.gg, m.gg_sem, m.gg_sem2, 3)
    c_half(3)
    to_canvases(m.late, m.late_sem, m.late_sem2)
    for d in (1, 2, 3, 0):
        r_quarter(d)
    groups_ready(m.gg, m.gg_sem2)
    wo_own = m.wo[pl.ds(pl.multiple_of(c * half, 128), half), :]
    w = dot_nt(m.gg[...].reshape(total, width), wo_own).astype(BF16)
    for n in range(3):
        m.da[n] = w[:, n * 128 : n * 128 + 128]

    for n in range(3):
        other = (1 - c) * 3 + n
        send_to(m.ag.at[other], m.ag.at[other], m.ag_sem, n, b, sibling).wait_recv()
    columns = m.gg[:, :, :, pl.ds(pl.multiple_of(c * half, 128), half)].reshape(total, half)
    full = jnp.concatenate([m.ag[n] for n in range(6)], axis=-1)
    m.jo[3] = dot_tn(full, columns).astype(BF16).reshape(m.jo.shape[1:])
    c_begin(7)

    tops = lax.broadcasted_iota(jnp.int32, (128, total), 0) < 64
    group = m.mg[...].reshape(total, width)
    for n in range(3):
        d2 = m.da[n]
        outs = []
        for h in range(2):
            dp = dot_nt(head(d2, h), m.qkv[6 + n])
            probs = m.probs[n, h].astype(F32)
            inner = jnp.sum(probs * dp, axis=-1, keepdims=True)
            m.ds[h] = (probs * (dp - inner)).astype(BF16)
            outs.append(dot(m.ds[h], m.qkv[3 + n]))
        dq = (jnp.where(lane, outs[0], outs[1]) * factor).astype(BF16)
        dk = [dot_tn(m.qkv[n], m.ds[h]) for h in range(2)]
        dk = (jnp.where(tops, dk[0], dk[1]) * factor).T.astype(BF16)
        dv = [dot_tn(d2, m.probs[n, h]) for h in range(2)]
        dv = jnp.where(tops, dv[0], dv[1]).T.astype(BF16)
        m.dqkv[n] = dq
        m.dqkv[3 + n] = dk
        m.dqkv[6 + n] = dv
        w = dot_tn(group, jnp.concatenate([dq, dk, dv], axis=-1))
        m.jo[n] = w.astype(BF16).reshape(m.jo.shape[1:])
        c_begin(4 + n)

    b2_copy.wait_send()
    sg_copy.wait_send()

    def partial(core):
        strip_rows = [
            jnp.concatenate(
                [
                    m.dqkv[k, pl.ds(pl.multiple_of((2 * i + core) * 64, 64), 64), :]
                    for i in range(chips)
                ],
                axis=0,
            )
            for k in range(9)
        ]
        w = None
        for part in range(3):
            v = jnp.concatenate(strip_rows[3 * part : 3 * part + 3], axis=-1)
            v = dot_nt(v, m.wj[part])
            w = v if w is None else w + v
        m.big[0, core] = w.reshape(m.big.shape[2:])

    partial(1 - c)
    start(send_to(m.big.at[0, 1 - c], m.mp_in, m.pair_sem, 4, b, sibling))
    partial(c)
    send_to(m.big.at[0, c], m.mp_in, m.pair_sem, 4, b, sibling).wait_recv()
    four = rows // 2
    for d in range(chips):
        i = chip(d)
        at = pl.ds(four * i, four)
        low = (m.big[0, c, at] + m.mp_in[at]).astype(BF16)
        if d:
            m.mo[i] = low
            start(send_to(m.mo.at[i], m.mr.at[z], m.mr_sem, d, b, 2 * i + c))
        else:
            m.mr[z] = low

    for j in range(4):
        c_quarter(j)
    c_spread(0)
    c_spread(1)
    to_sibling(m.late, m.late_sem2, m.late_sem3)
    sums = m.piece[s].astype(F32)
    for d in range(1, strips):
        send_to(m.piece.at[0], m.piece_in.at[d], m.piece_sem, d, b, s).wait_recv()
        sums = sums + m.piece_in[d].astype(F32)
    m.small[b] = sums.astype(BF16)
    for e in range(1, 4):
        start(send_to(m.small.at[b], m.small.at[b], m.small_sem, e, lax.rem(b + e, 4), s))
    c_half(7)
    c_half(4)
    c_half(5)
    r_sum()
    c_half(6)

    for d in range(1, chips):
        i = chip(chips - d)
        send_to(m.mo.at[i], m.mr.at[i], m.mr_sem, d, b, 2 * i + c).wait_recv()
    for r in (0, rows - 1):
        for p in range(2):
            m.md[r + 1, p] = m.mr[(r % 2) * 2 + p, r // 2]
    start_edges(m.md, m.md_sem)
    c_spread(2)
    c_spread(3)
    for r in range(1, rows - 1):
        for p in range(2):
            m.md[r + 1, p] = m.mr[(r % 2) * 2 + p, r // 2]

    m.acc1[...] = jnp.zeros_like(m.acc1)

    def mixer_rows(low, high):
        for k in range(width // 128):
            lanes = pl.ds(k * 128, 128)
            weights = [m.mk[t : t + 1, k * 128 : k * 128 + 128] for t in range(9)]

            def line(r, p):
                return m.md[r, p, :, lanes]

            def step(r, carry):
                new = window(line, r + 2)
                three = (carry[0], carry[1], new)
                out = conv(three, weights, True)
                for p in range(2):
                    m.fg[2 * r + p, :, lanes] = out[p]
                centre = [m.fp[r + 1, p, :, lanes].astype(F32) for p in range(2)]
                return carry[1], new, tuple(taps(three, centre, carry[2]))

            begin = tuple(m.acc1[t, :, lanes] for t in range(9))
            _, _, sums = lax.fori_loop(
                low, high, step, (window(line, low), window(line, low + 1), begin)
            )
            for t in range(9):
                m.acc1[t, :, lanes] = sums[t]

    m.acc[1] = jnp.zeros_like(m.acc[1])
    m.acc[2] = jnp.zeros_like(m.acc[2])

    def token_row(r, _):
        for p in range(2):
            rp = 2 * r + p
            grad = m.fg[rp]
            n, inv = ln_parts(m.xd[r, p].astype(F32))
            m.acc[1] += grad
            m.acc[2] += grad * n
            interleave(m.rowf, r, p, m.rg[rp] + ln_back(grad * scale1, n, inv))
        m.tgo[r] = joined(m.rowf, r)
        return 0

    mixer_rows(1, rows - 1)
    lax.fori_loop(1, rows - 1, token_row, 0)
    top_edge(m.md, m.md_sem)
    mixer_rows(0, 1)
    token_row(0, 0)
    bottom_edge(m.md, m.md_sem)
    mixer_rows(rows - 1, rows)
    token_row(rows - 1, 0)
    tg_copy = pltpu.make_async_copy(m.tgo, m.tg_hbm, m.load_sem.at[14])
    tg_copy.start()

    pack = []
    third = width // 3
    for v in (m.acc[1], m.acc[2]):
        pair = halves(v)
        for h in range(2):
            pack += [pair[h : h + 1, k * third : k * third + third] for k in range(3)]
    pack.append(jnp.zeros((4, third), F32))
    own_sums(m.early, m.early_sem, jnp.concatenate(pack, axis=0))
    mixer_sums = [jnp.sum(m.acc1[t], axis=0, keepdims=True) for t in range(9)]
    mixer_sums = jnp.concatenate(mixer_sums + [jnp.zeros((7, width), F32)], axis=0)
    pad_lanes = jnp.zeros((16, 128 - own), F32)
    for t in range(strips):
        m.mpiece[t] = jnp.concatenate(
            [mixer_sums[:, t * own : t * own + own], pad_lanes], axis=1
        ).astype(BF16)
    for d in range(1, strips):
        t = lax.rem(s + d, strips)
        start(send_to(m.mpiece.at[t], m.mpiece_in.at[d], m.mpiece_sem, d, b, t))

    for j in (7, 4):
        c_quarter(j)
        c_spread(j)
    to_canvases(m.early, m.early_sem, m.early_sem2)
    for j in (5, 6):
        c_quarter(j)
        c_spread(j)
    sums = m.mpiece[s].astype(F32)
    for d in range(1, strips):
        send_to(m.mpiece.at[0], m.mpiece_in.at[d], m.mpiece_sem, d, b, s).wait_recv()
        sums = sums + m.mpiece_in[d].astype(F32)
    m.msmall[b] = sums.astype(BF16)
    for e in range(1, 4):
        start(send_to(m.msmall.at[b], m.msmall.at[b], m.msmall_sem, e, lax.rem(b + e, 4), s))
    c_sum(0)
    to_sibling(m.early, m.early_sem2, m.early_sem3)
    c_sum(1)

    finals = []

    def store(src, dst, index):
        cp = pltpu.make_async_copy(src, dst, m.load_sem.at[index])
        cp.start()
        finals.append(cp)

    for e in range(1, 4):
        i = lax.rem(b - e + 4, 4)
        send_to(m.cond_all.at[i], m.cond_all.at[i], m.cond_sem, e, i, s).wait_recv()
        send_to(m.small.at[i], m.small.at[i], m.small_sem, e, i, s).wait_recv()
        send_to(m.msmall.at[i], m.msmall.at[i], m.msmall_sem, e, i, s).wait_recv()
        send_to(m.r_all.at[i], m.r_all.at[i], m.r4_sem, e, i, s).wait_recv()
    store(m.r_all, m.r_hbm, 15)
    store(m.cond_all, m.cond_hbm, 16)
    store(m.small, m.small_hbm, 17)
    store(m.msmall, m.msmall_hbm, 18)
    from_sibling(m.late, m.late_sem3)
    from_sibling(m.early, m.early_sem3)
    store(m.late, m.late_hbm, 19)
    store(m.early, m.early_hbm, 20)
    for g in range(2):
        for xs in range(2):
            for cs in range(2):
                source = 2 * c + xs
                e = lax.rem(b - source + 4, 4)
                local = jnp.logical_and(source == b, cs == c)

                @pl.when(jnp.logical_not(local))
                def _():
                    pltpu.make_async_remote_copy(
                        src_ref=m.c_out.at[g],
                        dst_ref=m.c_all.at[g, xs, cs],
                        send_sem=m.c4_sem[0].at[g, e],
                        recv_sem=m.c4_sem[1].at[g, e, cs],
                        device_id=(source, 2 * z + cs),
                        device_id_type=MESH,
                    ).wait_recv()

    store(m.c_all, m.c_hbm, 21)
    for cp in sent:
        cp.wait_send()
    edges_sent(m.fp, m.fp_sem)
    edges_sent(m.md, m.md_sem)

    halo_sent(m.ex, m.ex_sem)
    halo_sent(m.cg, m.cg_sem)
    for h in range(2):
        for n in range(chips):
            r_one(n, h).wait_send()
            r_two(n, h).wait_send()
        for j in range(8):
            c_one(j, h).wait_send()
            c_two(j, h).wait_send()
    for d in range(1, chips):
        r_three(d).wait_send()
        r_four(d).wait_send()
        for j in range(8):
            c_three(j, d).wait_send()
        for g in range(2):
            c_four(g, d).wait_send()

    @pl.when(c != y)
    def _():
        for g in range(2):
            c_four(g, 0).wait_send()

    out_copy.wait()
    tg_copy.wait()
    for cp in finals:
        cp.wait()


def block(tokens, mod, mixer, owner, cond, ob, eb, hk, rb, wj, wo, we, wr, cot, strips):
    rows, cols, width = tokens.shape
    chips = strips // 2
    half = width // 2
    total = strips * 64
    blocks = 2 * rows
    chip_rows = 2 * rows
    part = width // chips // 4
    third = width // 3
    shape = jax.ShapeDtypeStruct
    vm = pltpu.VMEM

    def dma(*size):
        return pltpu.SemaphoreType.DMA(size)

    ins = dict(
        tok=tokens, mod=mod, mk=mixer, owner=owner, cond=cond, ob=ob, eb=eb, hk=hk, rb=rb,
        wj_hbm=wj, wo_hbm=wo, we_hbm=we, wr_hbm=wr, cot_hbm=cot,
    )
    outs = dict(
        out_hbm=shape((rows, cols, width), BF16),
        tg_hbm=shape((rows, cols, width), F32),
        r_hbm=shape((4, 2, width // 8, half), BF16),
        c_hbm=shape((2, 2, 2, 4, part, half), BF16),
        cond_hbm=shape((4,) + cond.shape, F32),
        small_hbm=shape((4, 16, half), BF16),
        msmall_hbm=shape((4, 16, 128), BF16),
        late_hbm=shape((4, 2, chips, 16, half), BF16),
        early_hbm=shape((4, 2, chips, 16, third), BF16),
    )
    scratch = dict(
        wj=vm((3, width, half), BF16),
        wo=vm((width, width), BF16),
        we=vm((width, chips * half), BF16),
        wr=vm((chips * half, width), BF16),
        cot=vm((rows, cols, width), BF16),
        cond_all=vm((4,) + cond.shape, F32),
        rowf=vm((rows, width // 128, cols, 128), F32),
        xd=vm((rows, 2, 16, width), BF16),
        fp=vm((rows + 2, 2, 16, width), BF16),
        ms=vm((chips, rows // 2, 16, width), BF16),
        mg=vm((strips, rows // 2, 16, width), BF16),
        qkv=vm((9, total, 128), BF16),
        probs=vm((3, 2, total, total), BF16),
        ag=vm((6, total, 128), BF16),
        ai=vm((6, chips, 64, 128), BF16),
        acc=vm((6, 16, width), F32),
        acc1=vm((9, 8, width), F32),
        ctd=vm((blocks, 16, width), BF16),
        tg=vm((2, blocks, 16, width), BF16),
        sc=vm((2, blocks, 16, width), BF16),
        b1=vm((blocks, 16, width), F32),
        res=vm((blocks, 16, width), F32),
        ex=vm((chip_rows + 2, 2, 16, chips * half), BF16),
        cg=vm((chip_rows + 2, 2, 16, chips * half), BF16),
        act=vm((2 * blocks, 16, chips * half), BF16),
        big=vm((2, 2, blocks, 16, width), F32),
        b2_in=vm((blocks, 16, width), F32),
        sg_in=vm((blocks, 16, width), F32),
        hkg=vm((chips, 16, half), F32),
        rg=vm((blocks, 16, width), F32),
        og=vm((chips, rows // 2, 16, width), BF16),
        out=vm((rows, cols, width), BF16),
        gg=vm((strips, rows // 2, 16, width), BF16),
        da=vm((3, total, 128), BF16),
        ds=vm((2, total, total), BF16),
        dqkv=vm((9, total, 128), BF16),
        mp_in=vm((blocks, 16, width), F32),
        mo=vm((chips, rows // 2, 16, width), BF16),
        mr=vm((chips, rows // 2, 16, width), BF16),
        md=vm((rows + 2, 2, 16, width), BF16),
        fg=vm((blocks, 16, width), F32),
        tgo=vm((rows, cols, width), F32),
        rw=vm((chips, 2, 2, width // 4, half), BF16),
        r1=vm((chips, 2, 2, width // 8, half), BF16),
        r2=vm((chips, 2, width // 8, half), BF16),
        r3=vm((chips, 2, width // 8, half), BF16),
        r_all=vm((4, 2, width // 8, half), BF16),
        ew=vm((4, chips, 2, 2, part, half), BF16),
        jo=vm((4, chips, 2, 2, part, half), BF16),
        c1=vm((8, 2, 2, 2, part, half), BF16),
        c2=vm((8, chips, part, half), BF16),
        c3=vm((8, chips, part, half), BF16),
        c_out=vm((2, 4, part, half), BF16),
        c_all=vm((2, 2, 2, 4, part, half), BF16),
        late=vm((4, 2, chips, 16, half), BF16),
        early=vm((4, 2, chips, 16, third), BF16),
        piece=vm((strips, 16, half), BF16),
        piece_in=vm((strips, 16, half), BF16),
        small=vm((4, 16, half), BF16),
        mpiece=vm((strips, 16, 128), BF16),
        mpiece_in=vm((strips, 16, 128), BF16),
        msmall=vm((4, 16, 128), BF16),
        load_sem=dma(22),
    )
    pairs = dict(
        cond_sem=(4,), fp_sem=(2,), md_sem=(2,), mg_sem=(chips,), mg_sem2=(chips,),
        gg_sem=(chips,), gg_sem2=(chips,), ai_sem=(3, strips), ag_sem=(3,), pair_sem=(5,),
        ex_sem=(2,), cg_sem=(2,), mr_sem=(chips,),
        r1_sem=(chips, 2), r2_sem=(chips, 2), r3_sem=(chips,), r4_sem=(4,),
        c1_sem=(8, 2), c2_sem=(8, 2), c3_sem=(8, chips),
        late_sem=(chips,), late_sem2=(4,), late_sem3=(1,),
        early_sem=(chips,), early_sem2=(4,), early_sem3=(1,),
        piece_sem=(strips,), small_sem=(4,), mpiece_sem=(strips,), msmall_sem=(4,),
    )
    names = list(ins) + list(outs) + list(scratch)
    shapes = list(scratch.values())
    for size in list(pairs.values()):
        shapes += [dma(*size), dma(*size)]
    shapes += [dma(2, 4), dma(2, 4, 2)]
    plain = len(names)

    def kernel(*refs):
        named = list(refs[:plain])
        sems = refs[plain:]
        both = [(sems[2 * i], sems[2 * i + 1]) for i in range(len(sems) // 2)]
        block_kernel(names + list(pairs) + ["c4_sem"], *named, *both)

    return pl.pallas_call(
        kernel,
        name="block",
        out_shape=tuple(outs.values()),
        in_specs=[WHOLE] * 3 + [SCALARS] + [WHOLE] * 5 + [LEFT] * 5,
        out_specs=(LEFT,) * len(outs),
        scratch_shapes=shapes,
        compiler_params=pltpu.CompilerParams(
            collective_id=0, has_side_effects=True, vmem_limit_bytes=VMEM_BYTES
        ),
    )(*ins.values())


def final_kernel(
    out_in, tg_in, r_ref, c_ref, cond_ref, small_ref, msmall_ref, late_ref, early_ref, aw_hbm,
    out_ref, tg_ref, tab_ref, ad_ref, ab_ref, mix_ref, joint_ref, output_ref, ob_ref,
    expand_ref, eb_ref, hidden_ref, reduce_ref, rb_ref,
    aw, out_v, tg_v, sem,
):
    s = lax.axis_index("strip")
    strips = lax.axis_size("strip")
    width = cond_ref.shape[2] - 256
    own = width // strips
    half = width // 2
    third = width // 3
    copies = [
        pltpu.make_async_copy(out_in, out_v, sem.at[0]),
        pltpu.make_async_copy(tg_in, tg_v, sem.at[1]),
        pltpu.make_async_copy(aw_hbm.at[pl.ds(pl.multiple_of(s * own, 16), own)], aw, sem.at[2]),
    ]
    for cp in copies:
        cp.start()

    stores = [
        pltpu.make_async_copy(out_v, out_ref, sem.at[3]),
        pltpu.make_async_copy(tg_v, tg_ref, sem.at[4]),
    ]

    small = small_ref[0].astype(F32)
    mixer = msmall_ref[0].astype(F32)
    for i in range(1, 4):
        small = small + small_ref[i].astype(F32)
        mixer = mixer + msmall_ref[i].astype(F32)
    hidden_ref[...] = small[0:9]
    eb_ref[...] = small[9:10]
    ob_ref[...] = small[10:11, 0:own]
    rb_ref[...] = small[11:12, 0:own]
    mix_ref[...] = mixer[0:9, 0:own]

    for i in range(2):
        copies[i].wait()
        stores[i].start()

    n = width // 4
    for q in range(4):
        reduce_ref[:, q * n : q * n + n] = r_ref[q].reshape(n, half).astype(F32).T
    part = c_ref.shape[4]
    for xs in range(2):
        rows = slice(xs * part, xs * part + part)
        for cs in range(2):
            for k in range(4):
                at = (2 * k + cs) * half
                expand_ref[rows, at : at + half] = c_ref[0, xs, cs, k].astype(F32)
            for k in range(3):
                for p in range(3):
                    at = p * width + cs * half + k * 128
                    joint_ref[rows, at : at + 128] = c_ref[
                        1, xs, cs, k, :, p * 128 : p * 128 + 128
                    ].astype(F32)
            output_ref[rows, cs * half : cs * half + half] = c_ref[1, xs, cs, 3].astype(F32)

    slots = 32
    condition = cond_ref[...].reshape(slots, width + 256)
    labels = condition[:, width : width + 1]
    slot_late = jnp.concatenate([cond_ref[i, 0:1, width + 128 :] for i in range(4)], axis=1)
    slot_early = jnp.concatenate([cond_ref[i, 1:2, width + 128 :] for i in range(4)], axis=1)
    condition = condition[:, 0:width]
    pick = lax.broadcasted_iota(jnp.int32, (width, own), 0) == (
        lax.broadcasted_iota(jnp.int32, (width, own), 1) + s * own
    )
    pick = jnp.where(pick, 1.0, 0.0)
    condition = jnp.dot(
        condition, pick, precision=lax.Precision.HIGHEST, preferred_element_type=F32
    )
    sigmoid = 1.0 / (1.0 + jnp.exp(-condition))
    silu = (condition * sigmoid).astype(BF16)
    slope = sigmoid * (1.0 + condition * (1.0 - sigmoid))

    count = 4 * strips * 16
    row = lax.rem(lax.broadcasted_iota(jnp.int32, (slots, count), 1), 16)
    index = lax.broadcasted_iota(jnp.int32, (slots, count), 0)
    hit_late = index == slot_late.astype(jnp.int32)
    hit_early = index == slot_early.astype(jnp.int32)
    late = late_ref[...].reshape(count, half)
    early = early_ref[...].reshape(count, third)
    copies[2].wait()
    silu_grad = jnp.zeros((slots, own), F32)
    pieces = []
    for i in range(2):
        for k in range(3):
            mine = jnp.logical_or(row == 6 * i + k, row == 6 * i + 3 + k)
            pieces.append((early, jnp.logical_and(hit_early, mine), i * width + k * third, third))
    for i in range(4):
        for k in range(2):
            mine = jnp.logical_or(row == 4 * i + k, row == 4 * i + 2 + k)
            pieces.append((late, jnp.logical_and(hit_late, mine), (2 + i) * width + k * half, half))
    for source, mine, at, size in pieces:
        chosen = jnp.where(mine, 1.0, 0.0).astype(BF16)
        grad = dot(chosen, source)
        ab_ref[:, at : at + size] = jnp.sum(grad, axis=0, keepdims=True)
        low = grad.astype(BF16)
        ad_ref[:, at : at + size] = dot_tn(silu, low)
        silu_grad = silu_grad + dot_nt(low, aw[:, at : at + size])
    classes = tab_ref.shape[1]
    onehot = lax.broadcasted_iota(jnp.int32, (slots, classes), 1) == labels.astype(jnp.int32)
    tab_ref[...] = lax.dot_general(
        silu_grad * slope,
        jnp.where(onehot, 1.0, 0.0),
        TN,
        precision=lax.Precision.HIGHEST,
        preferred_element_type=F32,
    )
    for cp in stores:
        cp.wait()


def final(parts, aw, classes, strips):
    out, tg, r, c, cond, small, msmall, late, early = parts
    width = out.shape[-1]
    own = width // strips
    half = width // 2
    shape = jax.ShapeDtypeStruct
    return pl.pallas_call(
        final_kernel,
        name="final",
        out_shape=(
            shape(out.shape, BF16),
            shape(tg.shape, F32),
            shape((own, classes), F32),
            shape((own, 6 * width), F32),
            shape((1, 6 * width), F32),
            shape((9, own), F32),
            shape((own, 3 * width), F32),
            shape((own, width), F32),
            shape((1, own), F32),
            shape((own, 4 * width), F32),
            shape((1, half), F32),
            shape((9, half), F32),
            shape((half, width), F32),
            shape((1, own), F32),
        ),
        in_specs=[LEFT] * 2 + [WHOLE] * 7 + [LEFT],
        out_specs=(LEFT,) * 2 + (WHOLE,) * 12,
        scratch_shapes=[
            pltpu.VMEM((own, 6 * width), BF16),
            pltpu.VMEM(out.shape, BF16),
            pltpu.VMEM(tg.shape, F32),
            pltpu.SemaphoreType.DMA((5,)),
        ],
        compiler_params=pltpu.CompilerParams(vmem_limit_bytes=VMEM_BYTES),
    )(out, tg, r, c, cond, small, msmall, late, early, aw)


def timestep_features(time_steps, model_width):
    half_width = model_width // 2
    frequencies = jnp.exp(
        -math.log(10000.0) * jnp.arange(half_width, dtype=F32) / half_width
    )
    angles = time_steps.astype(F32)[..., None] * frequencies
    return jnp.concatenate([jnp.cos(angles), jnp.sin(angles)], axis=-1)


def local_grouped(
    tokens, tile_owner, time_steps, class_labels, class_embedding_matrix, adaptive_weight,
    adaptive_bias, mixer_kernel, joint_weight, output_weight, output_bias, expand_weight,
    expand_bias, hidden_kernel, reduce_weight, reduce_bias, output_cotangent,
):
    _, rows, cols, width = tokens.shape
    strips = lax.axis_size("strip")
    s = lax.axis_index("strip")
    b = lax.axis_index("batch")
    classes = class_embedding_matrix.shape[1]
    latents = time_steps.shape[1]
    own = width // strips
    piece = expand_weight.shape[1] // strips
    owner = tile_owner[0].reshape(-1)

    onehot = (class_labels[0][:, None] == jnp.arange(classes, dtype=jnp.int32)).astype(BF16)
    condition = timestep_features(time_steps[0], width) + jnp.einsum(
        "bn,dn->bd", onehot, class_embedding_matrix, preferred_element_type=F32
    )
    silu_cond = jax.nn.silu(condition).astype(BF16)
    modulation = jnp.dot(silu_cond, adaptive_weight, preferred_element_type=F32)
    modulation = modulation + adaptive_bias.astype(F32)
    pair = lax.dynamic_slice_in_dim(owner, 2 * (s * 4 // strips), 2)
    mod = jnp.dot(
        (pair[:, None] == jnp.arange(latents, dtype=jnp.int32)).astype(F32),
        modulation,
        precision=lax.Precision.HIGHEST,
    )
    labels = jnp.broadcast_to(class_labels[0].astype(F32)[:, None], (latents, 128))
    slot = (tile_owner[0] + b * latents).astype(F32)
    slot_late = jnp.broadcast_to(slot[None, :, None, :, None], (2, 4, 4, 2, 2)).reshape(1, -1)
    slot_early = jnp.broadcast_to(slot[:, None, :, None], (4, 2, 2, 3)).reshape(1, 4, 12)
    slot_early = jnp.broadcast_to(
        jnp.pad(slot_early, ((0, 0), (0, 0), (0, 4))), (2, 4, 16)
    ).reshape(1, -1)
    slots = jnp.concatenate([slot_late] + [slot_early] * (latents - 1), axis=0)
    cond = jnp.concatenate([condition, labels, slots], axis=1)
    mixer = mixer_kernel.T.astype(F32)
    hidden = hidden_kernel.T.astype(F32).reshape(9, strips, piece).transpose(1, 0, 2)
    parts = block(
        tokens[0], mod, mixer, owner, cond, output_bias.astype(F32)[None],
        expand_bias.astype(F32).reshape(strips, 1, piece), hidden,
        reduce_bias.astype(F32)[None], joint_weight, output_weight, expand_weight,
        reduce_weight, output_cotangent[0], strips,
    )
    (
        out, tg, table, adaptive, bias, mix, joint, output, ob, expand, eb, hid, reduce, rb,
    ) = final(parts, adaptive_weight, classes, strips)
    bias = lax.dynamic_slice_in_dim(bias.reshape(-1), s * 6 * own, 6 * own)
    return (
        out[None], tg[None], table, adaptive, bias, mix.T, joint, output, ob.reshape(-1),
        expand, eb.reshape(-1), hid.T, reduce, rb.reshape(-1),
    )


EXACT_PRECISION = lax.Precision.HIGHEST


def padded_2(block, sides, width):
    for axis, dim in sides:
        count = lax.axis_size(axis)
        forward = [(i, i + 1) for i in range(count - 1)]
        backward = [(target, source) for source, target in forward]
        low = lax.ppermute(
            lax.slice_in_dim(block, block.shape[dim] - width, None, axis=dim), axis, forward
        )
        high = lax.ppermute(lax.slice_in_dim(block, 0, width, axis=dim), axis, backward)
        block = jnp.concatenate([low, block, high], axis=dim)
    return block


def normalize(values):
    centre = jnp.mean(values, axis=-1, keepdims=True)
    centred = values - centre
    spread = jnp.mean(centred * centred, axis=-1, keepdims=True)
    return centred * lax.rsqrt(spread + EPSILON)


def modulate(values, shifting, scaling):
    return normalize(values) * (1.0 + scaling) + shifting


def depthwise(padded, kernel):
    row_count = padded.shape[-3] - 2
    column_total = padded.shape[-2]
    widened = jnp.pad(padded, [(0, 0)] * (padded.ndim - 2) + [(1, 1), (0, 0)])
    result = jnp.zeros(
        padded.shape[:-3] + (row_count, column_total, padded.shape[-1]), padded.dtype
    )
    for tapping in range(9):
        row_shift = tapping // 3
        col_shift = tapping % 3
        window = lax.slice_in_dim(widened, row_shift, row_shift + row_count, axis=widened.ndim - 3)
        window = lax.slice_in_dim(
            window, col_shift, col_shift + column_total, axis=widened.ndim - 2
        )
        result = result + kernel[:, tapping] * window
    return result


def kernel_grad(padded, gradient):
    row_count = gradient.shape[1]
    column_total = gradient.shape[2]
    widened = jnp.pad(padded, ((0, 0), (0, 0), (1, 1), (0, 0)))
    columns = []
    for tapping in range(9):
        row_shift = tapping // 3
        col_shift = tapping % 3
        window = widened[
            :, row_shift : row_shift + row_count, col_shift : col_shift + column_total, :
        ]
        columns.append(jnp.sum(window * gradient, axis=(0, 1, 2)))
    return jnp.stack(columns, axis=1)


def group_owner(owner):
    canvases, row_count, column_total = owner.shape
    shaped = owner.reshape(canvases, row_count // 2, 2, column_total // 2, 2).transpose(
        0, 2, 4, 1, 3
    )
    return shaped.reshape(canvases, 2, 2, row_count // 2 * (column_total // 2))


def to_groups(tensor, head_count):
    canvases, row_count, column_total, features = tensor.shape
    head_size = features // head_count
    shaped = tensor.reshape(
        canvases, row_count // 2, 2, column_total // 2, 2, head_count, head_size
    )
    shaped = shaped.transpose(0, 2, 4, 5, 1, 3, 6)
    return shaped.reshape(
        canvases, 2, 2, head_count, row_count // 2 * (column_total // 2), head_size
    )


def from_groups(tensor, row_count, column_total):
    canvases, head_count, head_size = (tensor.shape[0], tensor.shape[3], tensor.shape[-1])
    shaped = tensor.reshape(
        canvases, 2, 2, head_count, row_count // 2, column_total // 2, head_size
    )
    shaped = shaped.transpose(0, 4, 1, 5, 2, 3, 6)
    return shaped.reshape(canvases, row_count, column_total, head_count * head_size)


def local(
    tokens,
    tile_owner,
    time_steps,
    class_labels,
    class_embedding_matrix,
    adaptive_weight,
    adaptive_bias,
    mixer_kernel,
    joint_weight,
    output_weight,
    output_bias,
    expand_weight,
    expand_bias,
    hidden_kernel,
    reduce_weight,
    reduce_bias,
    output_cotangent,
):
    canvases, row_count, column_total, model_width = tokens.shape
    head_count = HEADS
    head_size = model_width // head_count
    factor = head_size ** (-0.5)
    half_cols = column_total // 2
    strips = lax.axis_size("strip")
    strip_index = lax.axis_index("strip")
    canvas_rows = row_count * strips
    class_count = class_embedding_matrix.shape[1]
    latent_count = time_steps.shape[1]
    tile_rows = canvas_rows // 4
    full_owner = jnp.broadcast_to(
        tile_owner[:, :, None, :, None], (canvases, 4, tile_rows, 2, half_cols)
    ).reshape(canvases, canvas_rows, column_total)
    local_owner = lax.dynamic_slice_in_dim(full_owner, strip_index * row_count, row_count, 1)
    token_hot = (local_owner[..., None] == jnp.arange(latent_count, dtype=jnp.int32)).astype(
        jnp.float32
    )
    class_onehot = (class_labels[..., None] == jnp.arange(class_count, dtype=jnp.int32)).astype(
        jnp.bfloat16
    )
    class_rows = jnp.einsum(
        "ywj,gj->ywg", class_onehot, class_embedding_matrix, preferred_element_type=jnp.float32
    )
    condition = timestep_features(time_steps, model_width) + class_rows
    silu_value, silu_pull = jax.vjp(jax.nn.silu, condition)
    silu_cond = silu_value.astype(jnp.bfloat16)
    modulation = jnp.einsum(
        "cbd,de->cbe", silu_cond, adaptive_weight, preferred_element_type=jnp.float32
    )
    modulation = modulation + adaptive_bias.astype(jnp.float32)
    token_mod = jnp.einsum("crkb,cbe->crke", token_hot, modulation, precision=EXACT_PRECISION)
    shift_one, scale_one, gate_one, shift_two, scale_two, gate_two = jnp.split(
        token_mod, 6, axis=-1
    )
    inputs = tokens.astype(jnp.float32)
    first_value, first_pull = jax.vjp(modulate, inputs, shift_one, scale_one)
    first = first_value.astype(jnp.bfloat16)
    first_padded = padded_2(first, (("strip", 1),), 1)
    mixer_single_float = mixer_kernel.astype(jnp.float32)
    mixed = depthwise(first_padded.astype(jnp.float32), mixer_single_float).astype(jnp.bfloat16)
    joint = jnp.einsum("crkd,de->crke", mixed, joint_weight, preferred_element_type=jnp.float32)
    query_rows = joint[..., :model_width].astype(jnp.bfloat16)
    keys_local = joint[..., model_width : 2 * model_width].astype(jnp.bfloat16)
    values_local = joint[..., 2 * model_width :].astype(jnp.bfloat16)
    keys_canvas, values_canvas = (
        lax.all_gather(keys_local, "strip", axis=1, tiled=True),
        lax.all_gather(values_local, "strip", axis=1, tiled=True),
    )
    query_groups = to_groups(query_rows, head_count)
    key_groups = to_groups(keys_canvas, head_count)
    value_groups = to_groups(values_canvas, head_count)
    query_owner = group_owner(local_owner)
    key_owner = group_owner(full_owner)
    allowed = (query_owner[..., :, None] == key_owner[..., None, :])[:, :, :, None]

    def attention_scores():
        raw = (
            jnp.einsum(
                "cabhnd,cabhmd->cabhnm",
                query_groups,
                key_groups,
                preferred_element_type=jnp.float32,
            )
            * factor
        )
        return jnp.where(allowed, raw, MASKED)

    scores = attention_scores()
    peak = jnp.max(scores, axis=-1, keepdims=True)
    lifted_float = jnp.exp(scores - peak)
    total = jnp.sum(lifted_float, axis=-1, keepdims=True)
    softened = (lifted_float / total).astype(jnp.bfloat16)
    log_total = peak + jnp.log(total)
    attended_groups = jnp.einsum(
        "cabhnm,cabhmd->cabhnd", softened, value_groups, preferred_element_type=jnp.float32
    )
    attended = from_groups(attended_groups, row_count, column_total).astype(jnp.bfloat16)
    branch_one = jnp.einsum(
        "crkd,de->crke", attended, output_weight, preferred_element_type=jnp.float32
    )
    branch_one = branch_one + output_bias.astype(jnp.float32)
    residual = inputs + gate_one * branch_one
    second_value, second_pull = jax.vjp(modulate, residual, shift_two, scale_two)
    second = second_value.astype(jnp.bfloat16)
    expanded = jnp.einsum(
        "crkd,df->crkf", second, expand_weight, preferred_element_type=jnp.float32
    )
    expanded = (expanded + expand_bias.astype(jnp.float32)).astype(jnp.bfloat16)
    expanded_padded = padded_2(expanded, (("strip", 1),), 1)
    hidden_float = hidden_kernel.astype(jnp.float32)
    conv_out = depthwise(expanded_padded.astype(jnp.float32), hidden_float)
    gelu_value, gelu_pull = jax.vjp(jax.nn.gelu, conv_out)
    activated = gelu_value.astype(jnp.bfloat16)
    branch_two = jnp.einsum(
        "crkf,fd->crkd", activated, reduce_weight, preferred_element_type=jnp.float32
    )
    branch_two = branch_two + reduce_bias.astype(jnp.float32)
    outputs = (residual + gate_two * branch_two).astype(jnp.bfloat16)
    upstream = output_cotangent.astype(jnp.float32)
    two_grad = (upstream * gate_two).astype(jnp.bfloat16)
    gate_two_grad = upstream * branch_two
    reduce_bias_grad = jnp.sum(two_grad.astype(jnp.float32), axis=(0, 1, 2))
    reduce_weight_grad = jnp.einsum(
        "crkf,crkd->fd", activated, two_grad, preferred_element_type=jnp.float32
    )
    activated_grad = jnp.einsum(
        "crkd,fd->crkf", two_grad, reduce_weight, preferred_element_type=jnp.float32
    )
    conv_grad = gelu_pull(activated_grad)[0].astype(jnp.bfloat16)
    conv_padded = padded_2(conv_grad, (("strip", 1),), 1)
    expanded_grad = depthwise(conv_padded.astype(jnp.float32), hidden_float[:, ::-1]).astype(
        jnp.bfloat16
    )
    hidden_kernel_grad = kernel_grad(
        expanded_padded.astype(jnp.float32), conv_grad.astype(jnp.float32)
    )
    expand_bias_grad = jnp.sum(expanded_grad.astype(jnp.float32), axis=(0, 1, 2))
    expand_weight_grad = jnp.einsum(
        "crkd,crkf->df", second, expanded_grad, preferred_element_type=jnp.float32
    )
    second_grad = jnp.einsum(
        "crkf,df->crkd", expanded_grad, expand_weight, preferred_element_type=jnp.float32
    )
    residual_part, shift_two_grad, scale_two_grad = second_pull(second_grad)
    residual_grad = upstream + residual_part
    gate_one_grad = residual_grad * branch_one
    one_grad = (residual_grad * gate_one).astype(jnp.bfloat16)
    output_bias_grad = jnp.sum(one_grad.astype(jnp.float32), axis=(0, 1, 2))
    output_weight_grad = jnp.einsum(
        "crkd,crke->de", attended, one_grad, preferred_element_type=jnp.float32
    )
    attended_grad = jnp.einsum(
        "crke,de->crkd", one_grad, output_weight, preferred_element_type=jnp.float32
    ).astype(jnp.bfloat16)
    attended_grad_groups = to_groups(attended_grad, head_count)
    probs = jnp.exp(attention_scores() - log_total)
    prob_grads = jnp.einsum(
        "cabhnd,cabhmd->cabhnm",
        attended_grad_groups,
        value_groups,
        preferred_element_type=jnp.float32,
    )
    spread_sum = jnp.sum(probs * prob_grads, axis=-1, keepdims=True)
    score_grads = (probs * (prob_grads - spread_sum)).astype(jnp.bfloat16)
    query_grad_groups = (
        jnp.einsum(
            "cabhnm,cabhmd->cabhnd", score_grads, key_groups, preferred_element_type=jnp.float32
        )
        * factor
    )
    query_grad = from_groups(query_grad_groups, row_count, column_total).astype(jnp.bfloat16)
    all_queries, all_attended = (
        lax.all_gather(query_groups, "strip", axis=4, tiled=True),
        lax.all_gather(attended_grad_groups, "strip", axis=4, tiled=True),
    )
    all_logs, all_spreads = (
        lax.all_gather(log_total[..., 0], "strip", axis=4, tiled=True),
        lax.all_gather(spread_sum[..., 0], "strip", axis=4, tiled=True),
    )
    own_keys = to_groups(keys_local, head_count)
    own_values = to_groups(values_local, head_count)
    own_allowed = (key_owner[..., :, None] == query_owner[..., None, :])[:, :, :, None]
    own_scores = (
        jnp.einsum(
            "cabhnd,cabhmd->cabhnm", all_queries, own_keys, preferred_element_type=jnp.float32
        )
        * factor
    )
    own_scores = jnp.where(own_allowed, own_scores, MASKED)
    own_probs = jnp.exp(own_scores - all_logs[..., None])
    own_prob_grads = jnp.einsum(
        "cabhnd,cabhmd->cabhnm", all_attended, own_values, preferred_element_type=jnp.float32
    )
    own_score_grads = (own_probs * (own_prob_grads - all_spreads[..., None])).astype(jnp.bfloat16)
    key_grad_groups = (
        jnp.einsum(
            "cabhnm,cabhnd->cabhmd",
            own_score_grads,
            all_queries,
            preferred_element_type=jnp.float32,
        )
        * factor
    )
    value_grad_groups = jnp.einsum(
        "cabhnm,cabhnd->cabhmd",
        own_probs.astype(jnp.bfloat16),
        all_attended,
        preferred_element_type=jnp.float32,
    )
    key_grad = from_groups(key_grad_groups, row_count, column_total).astype(jnp.bfloat16)
    value_grad = from_groups(value_grad_groups, row_count, column_total).astype(jnp.bfloat16)
    joint_grad = jnp.concatenate([query_grad, key_grad, value_grad], axis=-1)
    joint_weight_grad = jnp.einsum(
        "crkd,crke->de", mixed, joint_grad, preferred_element_type=jnp.float32
    )
    mixed_grad = jnp.einsum(
        "crke,de->crkd", joint_grad, joint_weight, preferred_element_type=jnp.float32
    ).astype(jnp.bfloat16)
    mixed_padded = padded_2(mixed_grad, (("strip", 1),), 1)
    first_grad = depthwise(mixed_padded.astype(jnp.float32), mixer_single_float[:, ::-1])
    mixer_kernel_grad = kernel_grad(
        first_padded.astype(jnp.float32), mixed_grad.astype(jnp.float32)
    )
    input_part, shift_one_grad, scale_one_grad = first_pull(first_grad)
    tokens_grad = residual_grad + input_part
    token_grad = jnp.concatenate(
        [
            shift_one_grad,
            scale_one_grad,
            gate_one_grad,
            shift_two_grad,
            scale_two_grad,
            gate_two_grad,
        ],
        axis=-1,
    )
    modulation_grad = jnp.einsum("crkb,crke->cbe", token_hot, token_grad, precision=EXACT_PRECISION)
    silu_grad = jnp.einsum(
        "cbe,de->cbd",
        modulation_grad,
        adaptive_weight.astype(jnp.float32),
        precision=EXACT_PRECISION,
    )
    conditioning_grad = silu_pull(silu_grad)[0]
    table_grad = jnp.einsum(
        "soy,sok->yk",
        conditioning_grad,
        class_onehot.astype(jnp.float32),
        precision=EXACT_PRECISION,
    )
    adaptive_grad = jnp.einsum(
        "cbd,cbe->de", silu_cond.astype(jnp.float32), modulation_grad, precision=EXACT_PRECISION
    )
    adaptive_bias_grad = jnp.sum(modulation_grad, axis=(0, 1))
    (
        table_shard,
        adaptive_shard,
        adaptive_bias_shard,
        mixer_shard,
        joint_shard,
        output_shard,
        output_bias_shard,
        expand_shard,
        expand_bias_shard,
        hidden_shard,
        reduce_shard,
        reduce_bias_shard,
    ) = (
        lax.psum_scatter(
            table_grad.astype(jnp.bfloat16), "strip", scatter_dimension=0, tiled=True
        ).astype(jnp.float32),
        lax.psum_scatter(
            adaptive_grad.astype(jnp.bfloat16), "strip", scatter_dimension=0, tiled=True
        ).astype(jnp.float32),
        lax.psum_scatter(
            adaptive_bias_grad.astype(jnp.bfloat16), "strip", scatter_dimension=0, tiled=True
        ).astype(jnp.float32),
        lax.psum_scatter(
            mixer_kernel_grad.astype(jnp.bfloat16), "strip", scatter_dimension=0, tiled=True
        ).astype(jnp.float32),
        lax.psum_scatter(
            joint_weight_grad.astype(jnp.bfloat16), "strip", scatter_dimension=0, tiled=True
        ).astype(jnp.float32),
        lax.psum_scatter(
            output_weight_grad.astype(jnp.bfloat16), "strip", scatter_dimension=0, tiled=True
        ).astype(jnp.float32),
        lax.psum_scatter(
            output_bias_grad.astype(jnp.bfloat16), "strip", scatter_dimension=0, tiled=True
        ).astype(jnp.float32),
        lax.psum_scatter(
            expand_weight_grad.astype(jnp.bfloat16), "strip", scatter_dimension=0, tiled=True
        ).astype(jnp.float32),
        lax.psum_scatter(
            expand_bias_grad.astype(jnp.bfloat16), "strip", scatter_dimension=0, tiled=True
        ).astype(jnp.float32),
        lax.psum_scatter(
            hidden_kernel_grad.astype(jnp.bfloat16), "strip", scatter_dimension=0, tiled=True
        ).astype(jnp.float32),
        lax.psum_scatter(
            reduce_weight_grad.astype(jnp.bfloat16), "strip", scatter_dimension=0, tiled=True
        ).astype(jnp.float32),
        lax.psum_scatter(
            reduce_bias_grad.astype(jnp.bfloat16), "strip", scatter_dimension=0, tiled=True
        ).astype(jnp.float32),
    )
    summed = (
        lax.psum(table_shard.astype(jnp.bfloat16), "batch").astype(jnp.float32),
        lax.psum(adaptive_shard.astype(jnp.bfloat16), "batch").astype(jnp.float32),
        lax.psum(adaptive_bias_shard.astype(jnp.bfloat16), "batch").astype(jnp.float32),
        lax.psum(mixer_shard.astype(jnp.bfloat16), "batch").astype(jnp.float32),
        lax.psum(joint_shard.astype(jnp.bfloat16), "batch").astype(jnp.float32),
        lax.psum(output_shard.astype(jnp.bfloat16), "batch").astype(jnp.float32),
        lax.psum(output_bias_shard.astype(jnp.bfloat16), "batch").astype(jnp.float32),
        lax.psum(expand_shard.astype(jnp.bfloat16), "batch").astype(jnp.float32),
        lax.psum(expand_bias_shard.astype(jnp.bfloat16), "batch").astype(jnp.float32),
        lax.psum(hidden_shard.astype(jnp.bfloat16), "batch").astype(jnp.float32),
        lax.psum(reduce_shard.astype(jnp.bfloat16), "batch").astype(jnp.float32),
        lax.psum(reduce_bias_shard.astype(jnp.bfloat16), "batch").astype(jnp.float32),
    )
    return (
        outputs,
        tokens_grad,
        summed[0],
        summed[1],
        summed[2],
        summed[3],
        summed[4],
        summed[5],
        summed[6],
        summed[7],
        summed[8],
        summed[9],
        summed[10],
        summed[11],
    )


def solution(mesh):
    grouped = (mesh.shape["batch"], mesh.shape["strip"]) == (4, 8)
    return jax.shard_map(
        local_grouped if grouped else local,
        mesh=mesh,
        in_specs=(
            P("batch", "strip", None, None),
            P("batch", None, None),
            P("batch", None),
            P("batch", None),
            P(),
            P(),
            P(),
            P(),
            P(),
            P(),
            P(),
            P(),
            P(),
            P(),
            P(),
            P(),
            P("batch", "strip", None, None),
        ),
        out_specs=(
            P("batch", "strip", None, None),
            P("batch", "strip", None, None),
            P("strip", None),
            P("strip", None),
            P("strip"),
            P("strip", None),
            P("strip", None),
            P("strip", None),
            P("strip"),
            P("strip", None),
            P("strip"),
            P("strip", None),
            P("strip", None),
            P("strip"),
        ),
        check_vma=False,
    )
```

```python
import math
from types import SimpleNamespace

import jax
import jax.numpy as jnp
from jax import lax
from jax.experimental import pallas as pl
from jax.experimental.pallas import tpu as pltpu
from jax.sharding import PartitionSpec as P

HEADS = 12
EPSILON = 1e-06
MASKED = -1e30
MESH = pl.DeviceIdType.MESH
F32 = jnp.float32
BF16 = jnp.bfloat16
VMEM_BYTES = 62 * 1024 * 1024
WHOLE = pl.BlockSpec(memory_space=pltpu.VMEM)
LEFT = pl.BlockSpec(memory_space=pl.ANY)
SCALARS = pl.BlockSpec(memory_space=pltpu.SMEM)
NT = (((1,), (1,)), ((), ()))
TN = (((0,), (0,)), ((), ()))


def dot(a, b):
    return jnp.dot(a, b, preferred_element_type=F32)


def dot_nt(a, b):
    return lax.dot_general(a, b, NT, preferred_element_type=F32)


def dot_tn(a, b):
    return lax.dot_general(a, b, TN, preferred_element_type=F32)


def send_to(src, dst, sems, index, batch, strip):
    return pltpu.make_async_remote_copy(
        src_ref=src,
        dst_ref=dst,
        send_sem=sems[0].at[index],
        recv_sem=sems[1].at[index],
        device_id=(batch, strip),
        device_id_type=MESH,
    )


def entry_barrier(strips):
    s = lax.axis_index("strip")
    b = lax.axis_index("batch")
    z = s // 2
    barrier = pltpu.get_barrier_semaphore()
    count = 0
    for d in range(1, strips):
        pl.semaphore_signal(
            barrier, inc=1, device_id=(b, lax.rem(s + d, strips)), device_id_type=MESH
        )
        count += 1
    for e in range(1, 4):
        for core in range(2):
            pl.semaphore_signal(
                barrier, inc=1, device_id=(lax.rem(b + e, 4), 2 * z + core), device_id_type=MESH
            )
            count += 1
    pl.semaphore_wait(barrier, count)


def spread(mod, width):
    return jnp.concatenate(
        [jnp.broadcast_to(mod[0:1], (8, width)), jnp.broadcast_to(mod[1:2], (8, width))], axis=0
    )


def spread_columns(buffer, r, x):
    for k in range(x.shape[-1] // 128):
        buffer[r, k] = x[:, k * 128 : k * 128 + 128]


def every_second(buffer, r, p):
    return jnp.concatenate(
        [buffer[r, k, pl.ds(p, 16, stride=2), :] for k in range(buffer.shape[1])], axis=-1
    )


def interleave(buffer, r, p, x):
    for k in range(x.shape[-1] // 128):
        buffer[r, k, pl.ds(p, 16, stride=2), :] = x[:, k * 128 : k * 128 + 128]


def joined(buffer, r):
    return jnp.concatenate([buffer[r, k] for k in range(buffer.shape[1])], axis=-1)


def ln_parts(x):
    centre = jnp.mean(x, axis=-1, keepdims=True)
    centred = x - centre
    var = jnp.mean(centred * centred, axis=-1, keepdims=True)
    inv = lax.rsqrt(var + EPSILON)
    return centred * inv, inv


def ln_back(grad, n, inv):
    mean0 = jnp.mean(grad, axis=-1, keepdims=True)
    mean1 = jnp.mean(grad * n, axis=-1, keepdims=True)
    return inv * (grad - mean0 - n * mean1)


def window(load, r):
    even = load(r, 0).astype(F32)
    odd = load(r, 1).astype(F32)
    n = even.shape[0]
    j = lax.broadcasted_iota(jnp.int32, even.shape, 0)
    odd_m = jnp.where(j == 0, 0.0, pltpu.roll(odd, 1, 0))
    even_p = jnp.where(j == n - 1, 0.0, pltpu.roll(even, n - 1, 0))
    return odd_m, even, odd, even_p


def conv(rows, weights, flip):
    out = []
    for p in range(2):
        total = None
        for i in range(3):
            for j in range(3):
                t = 3 * i + j
                a = weights[8 - t if flip else t] * rows[i][p + j]
                total = a if total is None else total + a
        out.append(total)
    return out


def taps(rows, centre, sums):
    new = list(sums)
    for i in range(3):
        for j in range(3):
            a = rows[i][j] * centre[0] + rows[i][1 + j] * centre[1]
            t = 8 - (3 * i + j)
            new[t] = sums[t] + (a[0:8] + a[8:16])
    return new


def halves(x):
    return jnp.concatenate(
        [jnp.sum(x[0:8], axis=0, keepdims=True), jnp.sum(x[8:16], axis=0, keepdims=True)], axis=0
    )


def gelu_both(x):
    k0 = math.sqrt(2.0 / math.pi)
    square = x * x
    t = jnp.tanh(k0 * x * (1.0 + 0.044715 * square))
    cdf = 0.5 + 0.5 * t
    slope = cdf + (0.5 * k0) * x * (1.0 - t * t) * (1.0 + (3.0 * 0.044715) * square)
    return x * cdf, slope


def condition_kernel(owner, steps, labels, emb, ab, aw_hbm, mod_ref, cond_ref, aw, sem):
    s = lax.axis_index("strip")
    b = lax.axis_index("batch")
    z = s // 2
    width, classes = emb.shape
    latents = steps.shape[1]
    half = width // 2
    copies = []
    for i in range(6):
        cp = pltpu.make_async_copy(aw_hbm.at[:, pl.ds(i * width, width)], aw.at[i], sem.at[i])
        cp.start()
        copies.append(cp)

    row = lax.broadcasted_iota(jnp.int32, (latents, 1), 0)
    when = jnp.zeros((latents, 1), F32)
    label = jnp.zeros((latents, 1), jnp.int32)
    for i in range(latents):
        when = jnp.where(row == i, steps[0, i].astype(F32), when)
        label = jnp.where(row == i, labels[0, i], label)
    order = lax.broadcasted_iota(jnp.int32, (latents, half), 1).astype(F32)
    angles = when * jnp.exp(-math.log(10000.0) * order / half)
    features = jnp.concatenate([jnp.cos(angles), jnp.sin(angles)], axis=1)
    onehot = lax.broadcasted_iota(jnp.int32, (latents, classes), 1) == label
    condition = features + dot_nt(jnp.where(onehot, 1.0, 0.0).astype(BF16), emb[...])
    silu = (condition / (1.0 + jnp.exp(-condition))).astype(BF16)

    lane = lax.broadcasted_iota(jnp.int32, (latents, 128), 1)
    kind = lax.broadcasted_iota(jnp.int32, (latents, 128), 0)
    line = lax.rem(lane, 16)
    side = jnp.where(kind == 0, lax.rem(line // 2, 2), lax.rem(line // 3, 2))
    tile = lax.rem(lane // 16, 4)
    slots = jnp.zeros((latents, 128), jnp.int32)
    for i in range(4):
        for h in range(2):
            hit = jnp.logical_and(tile == i, side == h)
            slots = jnp.where(hit, owner[0, i, h] + b * latents, slots)
    cond_ref[...] = jnp.concatenate(
        [condition, jnp.broadcast_to(label.astype(F32), (latents, 128)), slots.astype(F32)], axis=1
    )

    bias = ab[...].astype(F32).reshape(1, 6 * width)
    for i in range(6):
        copies[i].wait()
        lanes = slice(i * width, i * width + width)
        table = dot(silu, aw[i]) + bias[:, lanes]
        for h in range(2):
            mine = row == owner[0, z, h]
            mod_ref[h : h + 1, lanes] = jnp.sum(
                jnp.where(mine, table, 0.0), axis=0, keepdims=True
            )


def conditioning(owner, steps, labels, emb, ab, aw):
    width = emb.shape[0]
    latents = steps.shape[1]
    shape = jax.ShapeDtypeStruct
    return pl.pallas_call(
        condition_kernel,
        name="conditioning",
        out_shape=(shape((2, 6 * width), F32), shape((latents, width + 256), F32)),
        in_specs=[SCALARS] * 3 + [WHOLE] * 2 + [LEFT],
        out_specs=(WHOLE, WHOLE),
        scratch_shapes=[pltpu.VMEM((6, width, width), BF16), pltpu.SemaphoreType.DMA((6,))],
        compiler_params=pltpu.CompilerParams(vmem_limit_bytes=VMEM_BYTES),
    )(owner, steps, labels, emb, ab, aw)


def block_kernel(names, *refs):
    m = SimpleNamespace(**dict(zip(names, refs)))
    rows, cols, width = m.tok.shape
    half = width // 2
    strips = lax.axis_size("strip")
    chips = strips // 2
    chip_rows = 2 * rows
    total = strips * 64
    own = width // strips
    s = lax.axis_index("strip")
    b = lax.axis_index("batch")
    z = s // 2
    c = lax.rem(s, 2)
    sibling = 2 * z + 1 - c
    y, x = b // 2, lax.rem(b, 2)
    x_mate = 2 * y + 1 - x
    y_mate = 2 * (1 - y) + x
    sent = []

    def chip(d):
        return lax.rem(z + d, chips)

    def start(copy):
        copy.start()
        sent.append(copy)

    loads = {}

    def load(name, src, dst, index):
        loads[name] = pltpu.make_async_copy(src, dst, m.load_sem.at[index])
        loads[name].start()

    for part in range(3):
        off = pl.multiple_of(part * width + c * half, 128)
        load(f"wj{part}", m.wj_hbm.at[:, pl.ds(off, half)], m.wj.at[part], part)
    load("cot", m.cot_hbm, m.cot, 3)
    load("wo", m.wo_hbm, m.wo, 4)
    for n in range(chips):
        off = pl.multiple_of((2 * n + c) * half, 128)
        spot = pl.ds(n * half, half)
        load(f"we{n}", m.we_hbm.at[:, pl.ds(off, half)], m.we.at[:, spot], 5 + n)
        load(f"wr{n}", m.wr_hbm.at[pl.ds(off, half)], m.wr.at[spot], 5 + chips + n)
    entry_barrier(strips)

    m.mk[...] = m.mixer[...].astype(F32)
    ob = m.ob[...].astype(F32).reshape(1, width)
    rb = m.rb[...].astype(F32).reshape(1, width)
    m.ebf[...] = m.eb[...].astype(F32).reshape(m.ebf.shape)
    for n in range(chips):
        m.hk[n] = m.hidden[:, pl.ds(pl.multiple_of((2 * n + c) * half, 128), half)].astype(F32)

    m.cond_all[b] = m.cond[...]
    for e in range(1, 4):
        start(
            send_to(m.cond_all.at[b], m.cond_all.at[b], m.cond_sem, e, lax.rem(b + e, 4), s)
        )

    def block_mod(n):
        return spread(m.mod[:, n * width : (n + 1) * width], width)

    scale1 = 1.0 + block_mod(1)
    shift1 = block_mod(0)

    def first_row(r):
        spread_columns(m.rowf, r, m.tok[r].astype(F32))
        for p in range(2):
            v = every_second(m.rowf, r, p)
            m.xd[r, p] = v.astype(BF16)
            n, _ = ln_parts(v)
            m.fp[r + 1, p] = (n * scale1 + shift1).astype(BF16)

    def edge_sends(buffer, sems):
        up = send_to(buffer.at[1], buffer.at[rows + 1], sems, 0, b, s - 1)
        down = send_to(buffer.at[rows], buffer.at[0], sems, 1, b, s + 1)
        return up, down

    def start_edges(buffer, sems):
        up, down = edge_sends(buffer, sems)

        @pl.when(s > 0)
        def _():
            up.start()

        @pl.when(s < strips - 1)
        def _():
            down.start()

    def edges_sent(buffer, sems):
        up, down = edge_sends(buffer, sems)

        @pl.when(s > 0)
        def _():
            up.wait_send()

        @pl.when(s < strips - 1)
        def _():
            down.wait_send()

    def top_edge(buffer, sems):
        @pl.when(s > 0)
        def _():
            send_to(buffer.at[1], buffer.at[0], sems, 1, b, s - 1).wait_recv()

        @pl.when(s == 0)
        def _():
            buffer[0] = jnp.zeros_like(buffer[0])

    def bottom_edge(buffer, sems):
        @pl.when(s < strips - 1)
        def _():
            send_to(buffer.at[1], buffer.at[rows + 1], sems, 0, b, s + 1).wait_recv()

        @pl.when(s == strips - 1)
        def _():
            buffer[rows + 1] = jnp.zeros_like(buffer[0])

    first_row(0)
    first_row(rows - 1)
    start_edges(m.fp, m.fp_sem)

    def body(r, _):
        first_row(r)
        return 0

    lax.fori_loop(1, rows - 1, body, 0)

    def mixed_rows(low, high):
        for k in range(width // 128):
            lanes = pl.ds(k * 128, 128)
            weights = [m.mk[t : t + 1, k * 128 : k * 128 + 128] for t in range(9)]

            def line(r, p):
                return m.fp[r, p, :, lanes]

            def step(r, carry):
                new = window(line, r + 2)
                out = conv((carry[0], carry[1], new), weights, False)
                for p in range(2):
                    m.ms[lax.rem(r, 2) * 2 + p, r // 2, :, lanes] = out[p].astype(BF16)
                return carry[1], new

            lax.fori_loop(low, high, step, (window(line, low), window(line, low + 1)))

    mixed_rows(1, rows - 1)
    top_edge(m.fp, m.fp_sem)
    mixed_rows(0, 1)
    bottom_edge(m.fp, m.fp_sem)
    mixed_rows(rows - 1, rows)

    def to_groups(source, target, sems, sems2):
        for d in range(1, chips):
            g = chip(d)
            start(send_to(source.at[g], target.at[s], sems, d, b, 2 * g + c))
        target[s] = source[z]

    def pass_on(target, sems, sems2, d):
        i = 2 * chip(chips - d) + c
        if d:
            send_to(target.at[i], target.at[i], sems, d, b, i).wait_recv()
        start(send_to(target.at[i], target.at[i], sems2, d, b, sibling))

    def groups_ready(target, sems2):
        for d in range(chips):
            i = 2 * chip(chips - d) + 1 - c
            send_to(target.at[i], target.at[i], sems2, d, b, sibling).wait_recv()

    to_groups(m.ms, m.mg, m.mg_sem, m.mg_sem2)

    m.acc[...] = jnp.zeros_like(m.acc)
    gate2 = block_mod(5)
    loads["cot"].wait()

    def upstream_row(r, _):
        spread_columns(m.rowf, r, m.cot[r].astype(F32))
        for p in range(2):
            up = every_second(m.rowf, r, p)
            m.ctd[2 * r + p] = up.astype(BF16)
            two = (up * gate2).astype(BF16)
            m.tg[c, 2 * r + p] = two
            m.acc[0] += two.astype(F32)
        return 0

    lax.fori_loop(0, rows, upstream_row, 0)
    start(send_to(m.tg.at[c], m.tg.at[c], m.pair_sem, 0, b, sibling))

    for d in range(chips):
        pass_on(m.mg, m.mg_sem, m.mg_sem2, d)
    groups_ready(m.mg, m.mg_sem2)
    for part in range(3):
        loads[f"wj{part}"].wait()

    v = m.mg[...].reshape(total, width)
    for part in range(3):
        w = dot(v, m.wj[part]).astype(BF16)
        for n in range(3):
            m.qkv[3 * part + n] = w[:, n * 128 : n * 128 + 128]

    where = lax.broadcasted_iota(jnp.int32, (1, total), 1)
    lefts = lax.rem(where, 16) < 8
    key_owner = jnp.zeros((1, total), jnp.int32)
    for t in range(4):
        both = jnp.where(lefts, m.owner[0, t, 0], m.owner[0, t, 1])
        key_owner = jnp.where(where // 128 == t, both, key_owner)
    where = lax.broadcasted_iota(jnp.int32, (total, 1), 0)
    lefts = lax.rem(where, 16) < 8
    query_owner = jnp.zeros((total, 1), jnp.int32)
    for t in range(4):
        both = jnp.where(lefts, m.owner[0, t, 0], m.owner[0, t, 1])
        query_owner = jnp.where(where // 128 == t, both, query_owner)
    allowed = query_owner == key_owner
    lane = lax.broadcasted_iota(jnp.int32, (total, 128), 1) < 64
    factor = 64 ** -0.5

    def head(v, h):
        return jnp.where(lane if h == 0 else jnp.logical_not(lane), v, jnp.zeros_like(v))

    for n in range(3):
        mine = c * 3 + n
        q2 = (m.qkv[n].astype(F32) * factor).astype(BF16)
        outs = []
        for h in range(2):
            scores = jnp.where(allowed, dot_nt(head(q2, h), m.qkv[3 + n]), MASKED)
            peak = jnp.max(scores, axis=-1, keepdims=True)
            lifted = jnp.exp(scores - peak)
            inv = 1.0 / jnp.sum(lifted, axis=-1, keepdims=True)
            m.probs[n, h] = (lifted * inv).astype(BF16)
            outs.append(dot(lifted.astype(BF16), m.qkv[6 + n]) * inv)
        m.ag[mine] = jnp.where(lane, outs[0], outs[1]).astype(BF16)
        for d in range(1, strips):
            t = lax.rem(s + d, strips)
            start(
                send_to(
                    m.ag.at[mine, pl.ds(pl.multiple_of(t * 64, 64), 64)],
                    m.ai.at[mine, z],
                    m.ai_sem,
                    (n, d),
                    b,
                    t,
                )
            )
        start(send_to(m.ag.at[mine], m.ag.at[mine], m.ag_sem, n, b, sibling))
        m.ai[mine, z] = m.ag[mine, pl.ds(pl.multiple_of(s * 64, 64), 64), :]

    for n in range(3):
        for d in range(1, strips):
            i = lax.rem(s - d + strips, strips)
            spot = lax.rem(i, 2) * 3 + n
            send_to(
                m.ag.at[spot, pl.ds(0, 64)], m.ai.at[spot, i // 2], m.ai_sem, (n, d), b, i
            ).wait_recv()

    gate1 = block_mod(2)
    shift2 = block_mod(3)
    scale2 = 1.0 + block_mod(4)
    loads["wo"].wait()

    v = jnp.concatenate([m.ai[n].reshape(chips * 64, 128) for n in range(6)], axis=-1)
    m.b1[...] = (dot(v, m.wo[...]) + ob).reshape(m.b1.shape)

    def residual_row(i, _):
        rp = 4 * lax.rem(i, rows // 2) + i // (rows // 2)
        u = m.xd[rp // 2, lax.rem(rp, 2)].astype(F32) + gate1 * m.b1[i]
        m.res[rp] = u
        n, _ = ln_parts(u)
        m.sc[c, rp] = (n * scale2 + shift2).astype(BF16)
        return 0

    lax.fori_loop(0, 2 * rows, residual_row, 0, unroll=2)
    start(send_to(m.sc.at[c], m.sc.at[c], m.pair_sem, 1, b, sibling))

    def halo_sends(buffer, sems):
        up = send_to(buffer.at[1], buffer.at[chip_rows + 1], sems, 0, b, s - 2)
        down = send_to(buffer.at[chip_rows], buffer.at[0], sems, 1, b, s + 2)
        return up, down

    def start_halo(buffer, sems):
        up, down = halo_sends(buffer, sems)

        @pl.when(z > 0)
        def _():
            up.start()

        @pl.when(z < chips - 1)
        def _():
            down.start()

    def halo_sent(buffer, sems):
        up, down = halo_sends(buffer, sems)

        @pl.when(z > 0)
        def _():
            up.wait_send()

        @pl.when(z < chips - 1)
        def _():
            down.wait_send()

    def take_halo(buffer, sems):
        @pl.when(z > 0)
        def _():
            send_to(buffer.at[1], buffer.at[0], sems, 1, b, s - 2).wait_recv()

        @pl.when(z == 0)
        def _():
            buffer[0] = jnp.zeros_like(buffer[0])

        @pl.when(z < chips - 1)
        def _():
            send_to(buffer.at[1], buffer.at[chip_rows + 1], sems, 0, b, s + 2).wait_recv()

        @pl.when(z == chips - 1)
        def _():
            buffer[chip_rows + 1] = jnp.zeros_like(buffer[0])

    send_to(m.sc.at[c], m.sc.at[1 - c], m.pair_sem, 1, b, sibling).wait_recv()
    for n in range(chips):
        loads[f"we{n}"].wait()
        loads[f"wr{n}"].wait()
    hidden = chips * half
    bias = jnp.concatenate(
        [m.ebf[:, pl.ds(pl.multiple_of((2 * n + c) * half, 128), half)] for n in range(chips)],
        axis=-1,
    )
    blocks = rows // 2

    def expand(first, second):
        v = jnp.concatenate(
            [m.sc[0, first : first + rows], m.sc[1, second : second + rows]], axis=0
        ).reshape(rows * 32, width)
        w = (dot(v, m.we[...]) + bias).astype(BF16).reshape(rows, 2, 16, hidden)
        m.ex[pl.ds(1 + first // 2, blocks)] = w[0:blocks]
        m.ex[pl.ds(1 + rows + second // 2, blocks)] = w[blocks:]

    expand(0, rows)
    start_halo(m.ex, m.ex_sem)
    expand(rows, 0)
    send_to(m.tg.at[c], m.tg.at[1 - c], m.pair_sem, 0, b, sibling).wait_recv()
    chip_tg = m.tg[...].reshape(total, width)
    for h in range(2):
        m.big[h] = dot_nt(chip_tg, m.wr[h * width : h * width + width, :]).reshape(m.big.shape[1:])

    first_mate, then_mate = (x_mate, y_mate), (y_mate, x_mate)
    part_rows = width // 8

    def r_source(n, h, mine):
        at = pl.ds(h * part_rows, part_rows)
        if h == 0:
            return m.rw.at[n, :, x if mine else 1 - x, at]
        return m.rw.at[n, y if mine else 1 - y, :, at]

    def r_one(n, h):
        return send_to(r_source(n, h, False), m.r1.at[n, h], m.r1_sem, (n, h), first_mate[h], s)

    def r_two(n, h):
        src = m.r1.at[n, h, (1 - y) if h == 0 else (1 - x)]
        return send_to(src, m.r2.at[n, h], m.r2_sem, (n, h), then_mate[h], s)

    def r_three(k):
        z_pair = z + 1 - 2 * lax.rem(z, 2)
        z_far = lax.rem(z + 2, 4)
        dest = z_pair if k < 2 else z_far
        t = (z_pair, 3 - z, z_far)[k]
        return send_to(m.r2.at[t], m.r3.at[k], m.r3_sem, k, b, 2 * dest + c)

    def r_four(e):
        return send_to(m.r_all.at[b], m.r_all.at[b], m.r4_sem, e, lax.rem(b + e, 4), s)

    def r_half(n):
        for h in range(2):
            r_one(n, h).wait_recv()
            kept = r_source(n, h, True)[...].astype(F32)
            m.r1[n, h] = (m.r1[n, h].astype(F32) + kept).astype(BF16)
            r_two(n, h).start()

    def r_quarter(n):
        for h in range(2):
            r_two(n, h).wait_recv()
            kept = m.r1[n, h, y if h == 0 else x].astype(F32)
            m.r2[n, h] = (m.r2[n, h].astype(F32) + kept).astype(BF16)

    def r_spread():
        r_three(1).start()
        r_three(0).start()

    def r_across():
        r_three(1).wait_recv()
        t = lax.rem(z + 2, 4)
        m.r2[t] = (m.r2[t].astype(F32) + m.r3[1].astype(F32)).astype(BF16)
        r_three(2).start()

    def r_sum():
        v = m.r2[z].astype(F32)
        for k in (0, 2):
            r_three(k).wait_recv()
            v = v + m.r3[k].astype(F32)
        m.r_all[b] = v.astype(BF16)
        for e in range(1, 4):
            r_four(e).start()

    def c_source(j, h, mine):
        block = m.ew.at[j] if not isinstance(j, int) or j < 4 else m.jo.at[j - 4]
        at = pl.ds(2 * h, 2)
        if h == 0:
            return block.at[at, :, x if mine else 1 - x]
        return block.at[at, y if mine else 1 - y]

    def c_one(j, h):
        return send_to(c_source(j, h, False), m.c1.at[j, h], m.c1_sem, (j, h), first_mate[h], s)

    def c_two(j, h):
        src = m.c1.at[j, h, :, 1 - y] if h == 0 else m.c1.at[j, h, :, 1 - x]
        return send_to(src, m.c2.at[j, pl.ds(2 * h, 2)], m.c2_sem, (j, h), then_mate[h], s)

    pair_chip = z + 1 - 2 * lax.rem(z, 2)
    far_chip = lax.rem(z + 2, 4)
    last_chip = 3 - z

    def c_three(j, k):
        dest = pair_chip if k < 2 else far_chip
        t = (pair_chip, last_chip, far_chip)[k]
        return send_to(m.c2.at[j, t], m.c3.at[j, k], m.c3_sem, (j, k), b, 2 * dest + c)

    def c_four(j, e):
        return pltpu.make_async_remote_copy(
            src_ref=m.c_out.at[j],
            dst_ref=m.c_all.at[j, x, c],
            send_sem=m.c4_sem[0].at[j, e],
            recv_sem=m.c4_sem[1].at[j, e, c],
            device_id=(lax.rem(b + e, 4), 2 * z + y),
            device_id_type=MESH,
        )

    def c_begin(j):
        for h in range(2):
            c_one(j, h).start()

    def c_half(j):
        for h in range(2):
            c_one(j, h).wait_recv()
            kept = c_source(j, h, True)[...].astype(F32)
            m.c1[j, h] = (m.c1[j, h].astype(F32) + kept).astype(BF16)
            c_two(j, h).start()

    def c_quarter(j):
        for h in range(2):
            c_two(j, h).wait_recv()
            at = pl.ds(2 * h, 2)
            kept = (m.c1[j, h, :, y] if h == 0 else m.c1[j, h, :, x]).astype(F32)
            m.c2[j, at] = (m.c2[j, at].astype(F32) + kept).astype(BF16)

    def c_spread(j):
        c_three(j, 1).start()
        c_three(j, 0).start()

    def c_across(j):
        c_three(j, 1).wait_recv()
        far = m.c2[j, far_chip].astype(F32) + m.c3[j, 1].astype(F32)
        m.c2[j, far_chip] = far.astype(BF16)
        c_three(j, 2).start()

    def c_sum(j):
        v = m.c2[j, z].astype(F32)
        for k in (0, 2):
            c_three(j, k).wait_recv()
            v = v + m.c3[j, k].astype(F32)
        m.c_out[j] = v.astype(BF16)

        @pl.when(c == y)
        def _():
            m.c_all[j, x, c] = m.c_out[j]

        for e in range(1, 4):
            c_four(j, e).start()

        @pl.when(c != y)
        def _():
            c_four(j, 0).start()

    take_halo(m.ex, m.ex_sem)
    for n in range(chips):
        for k in range(3 * n, 3 * n + 3):
            lanes = pl.ds(k * 128, 128)
            inner = pl.ds((k % 3) * 128, 128)
            weights = [m.hk[n, t : t + 1, inner] for t in range(9)]
            spot = pl.ds((k % 6) * 128, 128)

            def line(r, p):
                return m.ex[r, p, :, lanes]

            above, here = window(line, 0), window(line, 1)
            for r in range(chip_rows):
                below = window(line, r + 2)
                out = conv((above, here, below), weights, False)
                for p in range(2):
                    value, slope = gelu_both(out[p])
                    rp = 2 * r + p
                    grad = m.big[k // 6, rp // 16, rp % 16, :, spot]
                    m.act[rp, :, lanes] = value.astype(BF16)
                    m.cg[r + 1, p, :, lanes] = (grad * slope).astype(BF16)
                above, here = here, below
        full = m.act[:, :, n * half : n * half + half].reshape(total, half)
        m.rw[n] = dot_tn(chip_tg, full).astype(BF16).reshape(m.rw.shape[1:])
        for h in range(2):
            r_one(n, h).start()
    start_halo(m.cg, m.cg_sem)
    full = m.act[...].reshape(total, hidden)
    m.big[0] = dot(full, m.wr[...]).reshape(m.big.shape[1:])
    b2_copy = send_to(m.big.at[0, 1 - c], m.b2_in, m.pair_sem, 2, b, sibling)
    b2_copy.start()
    m.hkg[...] = jnp.zeros_like(m.hkg)
    take_halo(m.cg, m.cg_sem)
    chip_sc = m.sc[...].reshape(total, width)
    for n in range(chips):
        for k in range(3 * n, 3 * n + 3):
            lanes = pl.ds(k * 128, 128)
            inner = pl.ds((k % 3) * 128, 128)
            weights = [m.hk[n, t : t + 1, inner] for t in range(9)]

            def line(r, p):
                return m.cg[r, p, :, lanes]

            above, here = window(line, 0), window(line, 1)
            sums = [jnp.zeros((8, 128), F32) for _ in range(9)]
            total_eg = jnp.zeros((8, 128), F32)
            for r in range(chip_rows):
                below = window(line, r + 2)
                three = (above, here, below)
                low = [v.astype(BF16) for v in conv(three, weights, True)]
                for p in range(2):
                    m.act[2 * r + p, :, lanes] = low[p]
                centre = [m.ex[r + 1, p, :, lanes].astype(F32) for p in range(2)]
                sums = taps(three, centre, sums)
                both = low[0].astype(F32) + low[1].astype(F32)
                total_eg = total_eg + (both[0:8] + both[8:16])
                above, here = here, below
            for t, v in enumerate(sums + [total_eg]):
                m.hkg[n, t : t + 1, inner] = jnp.sum(v, axis=0, keepdims=True)
        full = m.act[:, :, n * half : n * half + half].reshape(total, half)
        m.ew[n] = dot_tn(chip_sc, full).astype(BF16).reshape(m.ew.shape[1:])
        c_begin(n)
        r_half(n)
    full = m.act[...].reshape(total, hidden)
    m.big[1] = dot_nt(full, m.we[...]).reshape(m.big.shape[1:])
    sg_copy = send_to(m.big.at[1, 1 - c], m.sg_in, m.pair_sem, 3, b, sibling)
    sg_copy.start()
    send_to(m.big.at[0, c], m.b2_in, m.pair_sem, 2, b, sibling).wait_recv()
    send_to(m.big.at[1, c], m.sg_in, m.pair_sem, 3, b, sibling).wait_recv()

    def finish(r, _):
        for p in range(2):
            rp = 2 * r + p
            grad = m.big[1, c, rp] + m.sg_in[rp]
            v = m.res[rp]
            n, inv = ln_parts(v)
            branch = m.b1[(rows // 2) * lax.rem(rp, 4) + rp // 4]
            up = m.ctd[rp].astype(F32)
            m.acc[1] += grad
            m.acc[2] += grad * n
            back = up + ln_back(grad * scale2, n, inv)
            m.rg[rp] = back
            m.acc[3] += back * branch
            one = (back * gate1).astype(BF16)
            m.og[lax.rem(rp, 4), rp // 4] = one
            m.acc[4] += one.astype(F32)
            branch2 = m.big[0, c, rp] + m.b2_in[rp] + rb
            m.acc[5] += up * branch2
            interleave(m.rowf, r, p, v + gate2 * branch2)
        m.out[r] = joined(m.rowf, r).astype(BF16)
        return 0

    lax.fori_loop(0, rows, finish, 0)
    out_copy = pltpu.make_async_copy(m.out, m.out_hbm, m.load_sem.at[13])
    out_copy.start()

    to_groups(m.og, m.gg, m.gg_sem, m.gg_sem2)

    pack = []
    for v in (m.acc[3], m.acc[1], m.acc[2], m.acc[5]):
        pair = halves(v)
        for h in range(2):
            pack += [pair[h : h + 1, 0:half], pair[h : h + 1, half:]]
    def own_sums(buffer, sems, value):
        buffer[b, c, z] = value.astype(BF16)
        for d in range(1, chips):
            start(send_to(buffer.at[b, c, z], buffer.at[b, c, z], sems, d, b, 2 * chip(d) + c))

    def to_canvases(buffer, sems, sems2):
        for d in range(1, chips):
            i = chip(chips - d)
            send_to(buffer.at[b, c, i], buffer.at[b, c, i], sems, d, b, 2 * i + c).wait_recv()
        for e in range(1, 4):
            start(send_to(buffer.at[b, c], buffer.at[b, c], sems2, e, lax.rem(b + e, 4), s))

    def to_sibling(buffer, sems2, sems3):
        for e in range(1, 4):
            i = lax.rem(b - e + 4, 4)
            send_to(buffer.at[i, c], buffer.at[i, c], sems2, e, i, s).wait_recv()
        start(send_to(buffer.at[:, c], buffer.at[:, c], sems3, 0, b, sibling))

    def from_sibling(buffer, sems3):
        send_to(buffer.at[:, c], buffer.at[:, 1 - c], sems3, 0, b, sibling).wait_recv()

    own_sums(m.late, m.late_sem, jnp.concatenate(pack, axis=0))
    sums_ob = jnp.sum(m.acc[4], axis=0, keepdims=True)
    sums_rb = jnp.sum(m.acc[0], axis=0, keepdims=True)
    pad_lanes = jnp.zeros((1, half - own), F32)
    pad_rows = jnp.zeros((4, half), F32)
    for t in range(strips):
        piece = jnp.concatenate(
            [
                jnp.where(c == t % 2, m.hkg[t // 2, 0:10], 0.0),
                jnp.concatenate([sums_ob[:, t * own : t * own + own], pad_lanes], axis=1),
                jnp.concatenate([sums_rb[:, t * own : t * own + own], pad_lanes], axis=1),
                pad_rows,
            ],
            axis=0,
        )
        m.piece[t] = piece.astype(BF16)
    for d in range(1, strips):
        t = lax.rem(s + d, strips)
        start(send_to(m.piece.at[t], m.piece_in.at[d], m.piece_sem, d, b, t))

    pass_on(m.gg, m.gg_sem, m.gg_sem2, 0)
    c_half(0)
    c_half(1)
    pass_on(m.gg, m.gg_sem, m.gg_sem2, 1)
    c_half(2)
    pass_on(m.gg, m.gg_sem, m.gg_sem2, 2)
    pass_on(m.gg, m.gg_sem, m.gg_sem2, 3)
    c_half(3)
    to_canvases(m.late, m.late_sem, m.late_sem2)
    for n in range(chips):
        r_quarter(n)
    r_spread()
    groups_ready(m.gg, m.gg_sem2)
    wo_own = m.wo[pl.ds(pl.multiple_of(c * half, 128), half), :]
    w = dot_nt(m.gg[...].reshape(total, width), wo_own).astype(BF16)
    for n in range(3):
        m.da[n] = w[:, n * 128 : n * 128 + 128]

    for n in range(3):
        other = (1 - c) * 3 + n
        send_to(m.ag.at[other], m.ag.at[other], m.ag_sem, n, b, sibling).wait_recv()
    columns = m.gg[:, :, :, pl.ds(pl.multiple_of(c * half, 128), half)].reshape(total, half)
    full = jnp.concatenate([m.ag[n] for n in range(6)], axis=-1)
    m.jo[3] = dot_tn(full, columns).astype(BF16).reshape(m.jo.shape[1:])
    c_begin(7)

    tops = lax.broadcasted_iota(jnp.int32, (128, total), 0) < 64
    group = m.mg[...].reshape(total, width)
    for n in range(3):
        d2 = m.da[n]
        outs = []
        for h in range(2):
            dp = dot_nt(head(d2, h), m.qkv[6 + n])
            probs = m.probs[n, h].astype(F32)
            inner = jnp.sum(probs * dp, axis=-1, keepdims=True)
            m.ds[h] = (probs * (dp - inner)).astype(BF16)
            outs.append(dot(m.ds[h], m.qkv[3 + n]))
        dq = (jnp.where(lane, outs[0], outs[1]) * factor).astype(BF16)
        dk = [dot_tn(m.qkv[n], m.ds[h]) for h in range(2)]
        dk = (jnp.where(tops, dk[0], dk[1]) * factor).T.astype(BF16)
        dv = [dot_tn(d2, m.probs[n, h]) for h in range(2)]
        dv = jnp.where(tops, dv[0], dv[1]).T.astype(BF16)
        m.dqkv[n] = dq
        m.dqkv[3 + n] = dk
        m.dqkv[6 + n] = dv
        w = dot_tn(group, jnp.concatenate([dq, dk, dv], axis=-1))
        m.jo[n] = w.astype(BF16).reshape(m.jo.shape[1:])
        c_begin(4 + n)

    r_across()
    for j in range(4):
        c_quarter(j)

    b2_copy.wait_send()
    sg_copy.wait_send()

    def partial(core):
        strip_rows = [
            jnp.concatenate(
                [
                    m.dqkv[k, pl.ds(pl.multiple_of((2 * i + core) * 64, 64), 64), :]
                    for i in range(chips)
                ],
                axis=0,
            )
            for k in range(9)
        ]
        w = None
        for part in range(3):
            v = jnp.concatenate(strip_rows[3 * part : 3 * part + 3], axis=-1)
            v = dot_nt(v, m.wj[part])
            w = v if w is None else w + v
        m.big[0, core] = w.reshape(m.big.shape[2:])

    partial(1 - c)
    start(send_to(m.big.at[0, 1 - c], m.mp_in, m.pair_sem, 4, b, sibling))
    partial(c)
    send_to(m.big.at[0, c], m.mp_in, m.pair_sem, 4, b, sibling).wait_recv()
    four = rows // 2
    for d in range(chips):
        i = chip(d)
        at = pl.ds(four * i, four)
        low = (m.big[0, c, at] + m.mp_in[at]).astype(BF16)
        if d:
            m.mo[i] = low
            start(send_to(m.mo.at[i], m.mr.at[z], m.mr_sem, d, b, 2 * i + c))
        else:
            m.mr[z] = low

    to_sibling(m.late, m.late_sem2, m.late_sem3)
    sums = m.piece[s].astype(F32)
    for d in range(1, strips):
        send_to(m.piece.at[0], m.piece_in.at[d], m.piece_sem, d, b, s).wait_recv()
        sums = sums + m.piece_in[d].astype(F32)
    m.small[b] = sums.astype(BF16)
    for e in range(1, 4):
        start(send_to(m.small.at[b], m.small.at[b], m.small_sem, e, lax.rem(b + e, 4), s))
    c_spread(0)
    c_spread(1)
    c_half(7)
    c_half(4)
    c_half(5)
    c_half(6)

    for d in range(1, chips):
        i = chip(chips - d)
        send_to(m.mo.at[i], m.mr.at[i], m.mr_sem, d, b, 2 * i + c).wait_recv()
    for r in (0, rows - 1):
        for p in range(2):
            m.md[r + 1, p] = m.mr[(r % 2) * 2 + p, r // 2]
    start_edges(m.md, m.md_sem)
    c_spread(2)
    c_spread(3)
    c_across(0)
    c_across(1)
    r_sum()
    for r in range(1, rows - 1):
        for p in range(2):
            m.md[r + 1, p] = m.mr[(r % 2) * 2 + p, r // 2]

    m.acc1[...] = jnp.zeros_like(m.acc1)

    def mixer_rows(low, high):
        for k in range(width // 128):
            lanes = pl.ds(k * 128, 128)
            weights = [m.mk[t : t + 1, k * 128 : k * 128 + 128] for t in range(9)]

            def line(r, p):
                return m.md[r, p, :, lanes]

            def step(r, carry):
                new = window(line, r + 2)
                three = (carry[0], carry[1], new)
                out = conv(three, weights, True)
                for p in range(2):
                    m.fg[2 * r + p, :, lanes] = out[p]
                centre = [m.fp[r + 1, p, :, lanes].astype(F32) for p in range(2)]
                return carry[1], new, tuple(taps(three, centre, carry[2]))

            begin = tuple(m.acc1[t, :, lanes] for t in range(9))
            _, _, sums = lax.fori_loop(
                low, high, step, (window(line, low), window(line, low + 1), begin)
            )
            for t in range(9):
                m.acc1[t, :, lanes] = sums[t]

    m.acc[1] = jnp.zeros_like(m.acc[1])
    m.acc[2] = jnp.zeros_like(m.acc[2])

    def token_row(r, _):
        for p in range(2):
            rp = 2 * r + p
            grad = m.fg[rp]
            n, inv = ln_parts(m.xd[r, p].astype(F32))
            m.acc[1] += grad
            m.acc[2] += grad * n
            interleave(m.rowf, r, p, m.rg[rp] + ln_back(grad * scale1, n, inv))
        m.tgo[r] = joined(m.rowf, r)
        return 0

    mixer_rows(1, rows - 1)
    lax.fori_loop(1, rows - 1, token_row, 0)
    top_edge(m.md, m.md_sem)
    mixer_rows(0, 1)
    token_row(0, 0)
    bottom_edge(m.md, m.md_sem)
    mixer_rows(rows - 1, rows)
    token_row(rows - 1, 0)
    tg_copy = pltpu.make_async_copy(m.tgo, m.tg_hbm, m.load_sem.at[14])
    tg_copy.start()

    pack = []
    third = width // 3
    for v in (m.acc[1], m.acc[2]):
        pair = halves(v)
        for h in range(2):
            pack += [pair[h : h + 1, k * third : k * third + third] for k in range(3)]
    pack.append(jnp.zeros((4, third), F32))
    own_sums(m.early, m.early_sem, jnp.concatenate(pack, axis=0))
    mixer_sums = [jnp.sum(m.acc1[t], axis=0, keepdims=True) for t in range(9)]
    mixer_sums = jnp.concatenate(mixer_sums + [jnp.zeros((7, width), F32)], axis=0)
    pad_lanes = jnp.zeros((16, 128 - own), F32)
    for t in range(strips):
        m.mpiece[t] = jnp.concatenate(
            [mixer_sums[:, t * own : t * own + own], pad_lanes], axis=1
        ).astype(BF16)
    for d in range(1, strips):
        t = lax.rem(s + d, strips)
        start(send_to(m.mpiece.at[t], m.mpiece_in.at[d], m.mpiece_sem, d, b, t))

    for j in (7, 4, 5, 6):
        c_quarter(j)
        c_spread(j)
    c_across(2)
    c_across(3)
    c_sum(0)
    c_sum(1)
    to_canvases(m.early, m.early_sem, m.early_sem2)
    c_across(7)
    c_sum(2)
    c_sum(3)
    c_across(4)
    sums = m.mpiece[s].astype(F32)
    for d in range(1, strips):
        send_to(m.mpiece.at[0], m.mpiece_in.at[d], m.mpiece_sem, d, b, s).wait_recv()
        sums = sums + m.mpiece_in[d].astype(F32)
    m.msmall[b] = sums.astype(BF16)
    for e in range(1, 4):
        start(send_to(m.msmall.at[b], m.msmall.at[b], m.msmall_sem, e, lax.rem(b + e, 4), s))
    c_across(5)
    c_sum(7)
    to_sibling(m.early, m.early_sem2, m.early_sem3)
    c_across(6)
    for j in (4, 5, 6):
        c_sum(j)

    finals = []

    def store(src, dst, index):
        cp = pltpu.make_async_copy(src, dst, m.load_sem.at[index])
        cp.start()
        finals.append(cp)

    for e in range(1, 4):
        i = lax.rem(b - e + 4, 4)
        send_to(m.cond_all.at[i], m.cond_all.at[i], m.cond_sem, e, i, s).wait_recv()
        send_to(m.small.at[i], m.small.at[i], m.small_sem, e, i, s).wait_recv()
        send_to(m.msmall.at[i], m.msmall.at[i], m.msmall_sem, e, i, s).wait_recv()
        send_to(m.r_all.at[i], m.r_all.at[i], m.r4_sem, e, i, s).wait_recv()
    store(m.r_all, m.r_hbm, 15)
    store(m.cond_all, m.cond_hbm, 16)
    store(m.small, m.small_hbm, 17)
    store(m.msmall, m.msmall_hbm, 18)
    from_sibling(m.late, m.late_sem3)
    from_sibling(m.early, m.early_sem3)
    store(m.late, m.late_hbm, 19)
    store(m.early, m.early_hbm, 20)
    for j in range(8):
        for xs in range(2):
            for cs in range(2):
                source = 2 * c + xs
                e = lax.rem(b - source + 4, 4)
                local = jnp.logical_and(source == b, cs == c)

                @pl.when(jnp.logical_not(local))
                def _():
                    pltpu.make_async_remote_copy(
                        src_ref=m.c_out.at[j],
                        dst_ref=m.c_all.at[j, xs, cs],
                        send_sem=m.c4_sem[0].at[j, e],
                        recv_sem=m.c4_sem[1].at[j, e, cs],
                        device_id=(source, 2 * z + cs),
                        device_id_type=MESH,
                    ).wait_recv()

    store(m.c_all, m.c_hbm, 21)
    for cp in sent:
        cp.wait_send()
    edges_sent(m.fp, m.fp_sem)
    edges_sent(m.md, m.md_sem)

    halo_sent(m.ex, m.ex_sem)
    halo_sent(m.cg, m.cg_sem)
    for h in range(2):
        for n in range(chips):
            r_one(n, h).wait_send()
            r_two(n, h).wait_send()
        for j in range(8):
            c_one(j, h).wait_send()
            c_two(j, h).wait_send()
    for k in range(3):
        r_three(k).wait_send()
        r_four(k + 1).wait_send()
        for j in range(8):
            c_three(j, k).wait_send()
            c_four(j, k + 1).wait_send()

    @pl.when(c != y)
    def _():
        for j in range(8):
            c_four(j, 0).wait_send()

    out_copy.wait()
    tg_copy.wait()
    for cp in finals:
        cp.wait()


def block(tokens, mod, mixer, owner, cond, ob, eb, hk, rb, wj, wo, we, wr, cot, strips):
    rows, cols, width = tokens.shape
    chips = strips // 2
    half = width // 2
    total = strips * 64
    blocks = 2 * rows
    chip_rows = 2 * rows
    part = width // chips // 4
    third = width // 3
    shape = jax.ShapeDtypeStruct
    vm = pltpu.VMEM

    def dma(*size):
        return pltpu.SemaphoreType.DMA(size)

    ins = dict(
        tok=tokens, mod=mod, mixer=mixer, owner=owner, cond=cond, ob=ob, eb=eb, hidden=hk, rb=rb,
        wj_hbm=wj, wo_hbm=wo, we_hbm=we, wr_hbm=wr, cot_hbm=cot,
    )
    outs = dict(
        out_hbm=shape((rows, cols, width), BF16),
        tg_hbm=shape((rows, cols, width), F32),
        r_hbm=shape((4, 2, width // 8, half), BF16),
        c_hbm=shape((8, 2, 2, part, half), BF16),
        cond_hbm=shape((4,) + cond.shape, F32),
        small_hbm=shape((4, 16, half), BF16),
        msmall_hbm=shape((4, 16, 128), BF16),
        late_hbm=shape((4, 2, chips, 16, half), BF16),
        early_hbm=shape((4, 2, chips, 16, third), BF16),
    )
    scratch = dict(
        mk=vm((9, width), F32),
        ebf=vm((1, 2 * chips * half), F32),
        hk=vm((chips, 9, half), F32),
        wj=vm((3, width, half), BF16),
        wo=vm((width, width), BF16),
        we=vm((width, chips * half), BF16),
        wr=vm((chips * half, width), BF16),
        cot=vm((rows, cols, width), BF16),
        cond_all=vm((4,) + cond.shape, F32),
        rowf=vm((rows, width // 128, cols, 128), F32),
        xd=vm((rows, 2, 16, width), BF16),
        fp=vm((rows + 2, 2, 16, width), BF16),
        ms=vm((chips, rows // 2, 16, width), BF16),
        mg=vm((strips, rows // 2, 16, width), BF16),
        qkv=vm((9, total, 128), BF16),
        probs=vm((3, 2, total, total), BF16),
        ag=vm((6, total, 128), BF16),
        ai=vm((6, chips, 64, 128), BF16),
        acc=vm((6, 16, width), F32),
        acc1=vm((9, 8, width), F32),
        ctd=vm((blocks, 16, width), BF16),
        tg=vm((2, blocks, 16, width), BF16),
        sc=vm((2, blocks, 16, width), BF16),
        b1=vm((blocks, 16, width), F32),
        res=vm((blocks, 16, width), F32),
        ex=vm((chip_rows + 2, 2, 16, chips * half), BF16),
        cg=vm((chip_rows + 2, 2, 16, chips * half), BF16),
        act=vm((2 * blocks, 16, chips * half), BF16),
        big=vm((2, 2, blocks, 16, width), F32),
        b2_in=vm((blocks, 16, width), F32),
        sg_in=vm((blocks, 16, width), F32),
        hkg=vm((chips, 16, half), F32),
        rg=vm((blocks, 16, width), F32),
        og=vm((chips, rows // 2, 16, width), BF16),
        out=vm((rows, cols, width), BF16),
        gg=vm((strips, rows // 2, 16, width), BF16),
        da=vm((3, total, 128), BF16),
        ds=vm((2, total, total), BF16),
        dqkv=vm((9, total, 128), BF16),
        mp_in=vm((blocks, 16, width), F32),
        mo=vm((chips, rows // 2, 16, width), BF16),
        mr=vm((chips, rows // 2, 16, width), BF16),
        md=vm((rows + 2, 2, 16, width), BF16),
        fg=vm((blocks, 16, width), F32),
        tgo=vm((rows, cols, width), F32),
        rw=vm((chips, 2, 2, width // 4, half), BF16),
        r1=vm((chips, 2, 2, width // 8, half), BF16),
        r2=vm((chips, 2, width // 8, half), BF16),
        r3=vm((3, 2, width // 8, half), BF16),
        r_all=vm((4, 2, width // 8, half), BF16),
        ew=vm((4, chips, 2, 2, part, half), BF16),
        jo=vm((4, chips, 2, 2, part, half), BF16),
        c1=vm((8, 2, 2, 2, part, half), BF16),
        c2=vm((8, chips, part, half), BF16),
        c3=vm((8, 3, part, half), BF16),
        c_out=vm((8, part, half), BF16),
        c_all=vm((8, 2, 2, part, half), BF16),
        late=vm((4, 2, chips, 16, half), BF16),
        early=vm((4, 2, chips, 16, third), BF16),
        piece=vm((strips, 16, half), BF16),
        piece_in=vm((strips, 16, half), BF16),
        small=vm((4, 16, half), BF16),
        mpiece=vm((strips, 16, 128), BF16),
        mpiece_in=vm((strips, 16, 128), BF16),
        msmall=vm((4, 16, 128), BF16),
        load_sem=dma(22),
    )
    pairs = dict(
        cond_sem=(4,), fp_sem=(2,), md_sem=(2,), mg_sem=(chips,), mg_sem2=(chips,),
        gg_sem=(chips,), gg_sem2=(chips,), ai_sem=(3, strips), ag_sem=(3,), pair_sem=(5,),
        ex_sem=(2,), cg_sem=(2,), mr_sem=(chips,),
        r1_sem=(chips, 2), r2_sem=(chips, 2), r3_sem=(3,), r4_sem=(4,),
        c1_sem=(8, 2), c2_sem=(8, 2), c3_sem=(8, 3),
        late_sem=(chips,), late_sem2=(4,), late_sem3=(1,),
        early_sem=(chips,), early_sem2=(4,), early_sem3=(1,),
        piece_sem=(strips,), small_sem=(4,), mpiece_sem=(strips,), msmall_sem=(4,),
    )
    names = list(ins) + list(outs) + list(scratch)
    shapes = list(scratch.values())
    for size in list(pairs.values()):
        shapes += [dma(*size), dma(*size)]
    shapes += [dma(8, 4), dma(8, 4, 2)]
    plain = len(names)

    def kernel(*refs):
        named = list(refs[:plain])
        sems = refs[plain:]
        both = [(sems[2 * i], sems[2 * i + 1]) for i in range(len(sems) // 2)]
        block_kernel(names + list(pairs) + ["c4_sem"], *named, *both)

    return pl.pallas_call(
        kernel,
        name="block",
        out_shape=tuple(outs.values()),
        in_specs=[WHOLE] * 3 + [SCALARS] + [WHOLE] * 5 + [LEFT] * 5,
        out_specs=(LEFT,) * len(outs),
        scratch_shapes=shapes,
        compiler_params=pltpu.CompilerParams(
            collective_id=0, has_side_effects=True, vmem_limit_bytes=VMEM_BYTES
        ),
    )(*ins.values())


def final_kernel(
    out_in, tg_in, r_in, c_in, cond_ref, small_ref, msmall_ref, late_ref, early_ref, aw_hbm,
    out_ref, tg_ref, tab_ref, ad_out, ab_ref, mix_ref, joint_out, output_out, ob_ref,
    expand_out, eb_ref, hidden_ref, reduce_out, rb_ref,
    aw, out_v, tg_v, r_ref, c_ref, ad_ref, joint_ref, output_ref, expand_ref, reduce_ref, sem,
):
    s = lax.axis_index("strip")
    strips = lax.axis_size("strip")
    width = cond_ref.shape[2] - 256
    own = width // strips
    half = width // 2
    third = width // 3
    loads = [
        (r_in, r_ref),
        (c_in, c_ref),
        (aw_hbm.at[pl.ds(pl.multiple_of(s * own, 16), own)], aw),
        (out_in, out_v),
        (tg_in, tg_v),
    ]
    loads = [pltpu.make_async_copy(a, v, sem.at[i]) for i, (a, v) in enumerate(loads)]
    for cp in loads:
        cp.start()
    stores = []

    def store(src, dst):
        cp = pltpu.make_async_copy(src, dst, sem.at[5 + len(stores)])
        cp.start()
        stores.append(cp)

    small = small_ref[0].astype(F32)
    mixer = msmall_ref[0].astype(F32)
    for i in range(1, 4):
        small = small + small_ref[i].astype(F32)
        mixer = mixer + msmall_ref[i].astype(F32)
    hidden_ref[...] = small[0:9]
    eb_ref[...] = small[9]
    ob_ref[...] = small[10, 0:own]
    rb_ref[...] = small[11, 0:own]
    mix_ref[...] = mixer[0:9, 0:own]

    n = width // 4
    loads[0].wait()
    for q in range(4):
        reduce_ref[:, q * n : q * n + n] = r_ref[q].reshape(n, half).astype(F32).T
    store(reduce_ref, reduce_out)
    loads[1].wait()
    part = c_ref.shape[3]
    for xs in range(2):
        rows = slice(xs * part, xs * part + part)
        for cs in range(2):
            for k in range(4):
                at = (2 * k + cs) * half
                expand_ref[rows, at : at + half] = c_ref[k, xs, cs].astype(F32)
            for k in range(3):
                for p in range(3):
                    at = p * width + cs * half + k * 128
                    joint_ref[rows, at : at + 128] = c_ref[
                        4 + k, xs, cs, :, p * 128 : p * 128 + 128
                    ].astype(F32)
            output_ref[rows, cs * half : cs * half + half] = c_ref[7, xs, cs].astype(F32)
    store(expand_ref, expand_out)
    store(joint_ref, joint_out)
    store(output_ref, output_out)
    loads[3].wait()
    store(out_v, out_ref)
    loads[4].wait()
    store(tg_v, tg_ref)

    slots = 32
    condition = cond_ref[...].reshape(slots, width + 256)
    labels = condition[:, width : width + 1]
    slot_late = jnp.concatenate([cond_ref[i, 0:1, width + 128 :] for i in range(4)], axis=1)
    slot_early = jnp.concatenate([cond_ref[i, 1:2, width + 128 :] for i in range(4)], axis=1)
    condition = condition[:, 0:width]
    pick = lax.broadcasted_iota(jnp.int32, (width, own), 0) == (
        lax.broadcasted_iota(jnp.int32, (width, own), 1) + s * own
    )
    pick = jnp.where(pick, 1.0, 0.0)
    condition = jnp.dot(
        condition, pick, precision=lax.Precision.HIGHEST, preferred_element_type=F32
    )
    sigmoid = 1.0 / (1.0 + jnp.exp(-condition))
    silu = (condition * sigmoid).astype(BF16)
    slope = sigmoid * (1.0 + condition * (1.0 - sigmoid))

    count = 4 * strips * 16
    row = lax.rem(lax.broadcasted_iota(jnp.int32, (slots, count), 1), 16)
    index = lax.broadcasted_iota(jnp.int32, (slots, count), 0)
    hit_late = index == slot_late.astype(jnp.int32)
    hit_early = index == slot_early.astype(jnp.int32)
    late = late_ref[...].reshape(count, half)
    early = early_ref[...].reshape(count, third)
    loads[2].wait()
    bias = jnp.zeros((1, 6 * own), F32)
    sums = []
    silu_grad = jnp.zeros((slots, own), F32)
    pieces = []
    for i in range(2):
        for k in range(3):
            mine = jnp.logical_or(row == 6 * i + k, row == 6 * i + 3 + k)
            pieces.append((early, jnp.logical_and(hit_early, mine), i * width + k * third, third))
    for i in range(4):
        for k in range(2):
            mine = jnp.logical_or(row == 4 * i + k, row == 4 * i + 2 + k)
            pieces.append((late, jnp.logical_and(hit_late, mine), (2 + i) * width + k * half, half))
    for source, mine, at, size in pieces:
        chosen = jnp.where(mine, 1.0, 0.0).astype(BF16)
        grad = dot(chosen, source)
        sums.append(jnp.sum(grad, axis=0, keepdims=True))
        low = grad.astype(BF16)
        ad_ref[:, at : at + size] = dot_tn(silu, low)
        silu_grad = silu_grad + dot_nt(low, aw[:, at : at + size])
    store(ad_ref, ad_out)
    sums = jnp.concatenate(sums, axis=1)
    for t in range(strips):
        bias = jnp.where(s == t, sums[:, t * 6 * own : t * 6 * own + 6 * own], bias)
    ab_ref[...] = bias[0]
    classes = tab_ref.shape[1]
    onehot = lax.broadcasted_iota(jnp.int32, (slots, classes), 1) == labels.astype(jnp.int32)
    tab_ref[...] = lax.dot_general(
        silu_grad * slope,
        jnp.where(onehot, 1.0, 0.0),
        TN,
        precision=lax.Precision.HIGHEST,
        preferred_element_type=F32,
    )
    for cp in stores:
        cp.wait()


def final(parts, aw, classes, strips):
    out, tg, r, c = parts[:4]
    width = out.shape[-1]
    own = width // strips
    half = width // 2
    shape = jax.ShapeDtypeStruct
    vm = pltpu.VMEM
    return pl.pallas_call(
        final_kernel,
        name="final",
        out_shape=(
            shape(out.shape, BF16),
            shape(tg.shape, F32),
            shape((own, classes), F32),
            shape((own, 6 * width), F32),
            shape((6 * own,), F32),
            shape((9, own), F32),
            shape((own, 3 * width), F32),
            shape((own, width), F32),
            shape((own,), F32),
            shape((own, 4 * width), F32),
            shape((half,), F32),
            shape((9, half), F32),
            shape((half, width), F32),
            shape((own,), F32),
        ),
        in_specs=[LEFT] * 4 + [WHOLE] * 5 + [LEFT],
        out_specs=(
            LEFT, LEFT, WHOLE, LEFT, WHOLE, WHOLE, LEFT, LEFT, WHOLE, LEFT, WHOLE, WHOLE, LEFT,
            WHOLE,
        ),
        scratch_shapes=[
            vm((own, 6 * width), BF16),
            vm(out.shape, BF16),
            vm(tg.shape, F32),
            vm(r.shape, BF16),
            vm(c.shape, BF16),
            vm((own, 6 * width), F32),
            vm((own, 3 * width), F32),
            vm((own, width), F32),
            vm((own, 4 * width), F32),
            vm((half, width), F32),
            pltpu.SemaphoreType.DMA((12,)),
        ],
        compiler_params=pltpu.CompilerParams(vmem_limit_bytes=VMEM_BYTES),
    )(*parts, aw)


def local_grouped(
    tokens, tile_owner, time_steps, class_labels, class_embedding_matrix, adaptive_weight,
    adaptive_bias, mixer_kernel, joint_weight, output_weight, output_bias, expand_weight,
    expand_bias, hidden_kernel, reduce_weight, reduce_bias, output_cotangent,
):
    strips = lax.axis_size("strip")
    mod, cond = conditioning(
        tile_owner, time_steps, class_labels, class_embedding_matrix, adaptive_bias,
        adaptive_weight,
    )
    parts = block(
        tokens[0], mod, mixer_kernel.T, tile_owner, cond, output_bias, expand_bias,
        hidden_kernel.T, reduce_bias, joint_weight, output_weight, expand_weight, reduce_weight,
        output_cotangent[0], strips,
    )
    classes = class_embedding_matrix.shape[1]
    (
        out, tg, table, adaptive, bias, mixer, joint, output, ob, expand, eb, hidden, reduce, rb,
    ) = final(parts, adaptive_weight, classes, strips)
    return (
        out[None], tg[None], table, adaptive, bias, mixer.T, joint, output, ob, expand, eb,
        hidden.T, reduce, rb,
    )


EXACT_PRECISION = lax.Precision.HIGHEST


def padded_2(block, sides, width):
    for axis, dim in sides:
        count = lax.axis_size(axis)
        forward = [(i, i + 1) for i in range(count - 1)]
        backward = [(target, source) for source, target in forward]
        low = lax.ppermute(
            lax.slice_in_dim(block, block.shape[dim] - width, None, axis=dim), axis, forward
        )
        high = lax.ppermute(lax.slice_in_dim(block, 0, width, axis=dim), axis, backward)
        block = jnp.concatenate([low, block, high], axis=dim)
    return block


def normalize(values):
    centre = jnp.mean(values, axis=-1, keepdims=True)
    centred = values - centre
    spread = jnp.mean(centred * centred, axis=-1, keepdims=True)
    return centred * lax.rsqrt(spread + EPSILON)


def modulate(values, shifting, scaling):
    return normalize(values) * (1.0 + scaling) + shifting


def depthwise(padded, kernel):
    row_count = padded.shape[-3] - 2
    column_total = padded.shape[-2]
    widened = jnp.pad(padded, [(0, 0)] * (padded.ndim - 2) + [(1, 1), (0, 0)])
    result = jnp.zeros(
        padded.shape[:-3] + (row_count, column_total, padded.shape[-1]), padded.dtype
    )
    for tapping in range(9):
        row_shift = tapping // 3
        col_shift = tapping % 3
        window = lax.slice_in_dim(widened, row_shift, row_shift + row_count, axis=widened.ndim - 3)
        window = lax.slice_in_dim(
            window, col_shift, col_shift + column_total, axis=widened.ndim - 2
        )
        result = result + kernel[:, tapping] * window
    return result


def kernel_grad(padded, gradient):
    row_count = gradient.shape[1]
    column_total = gradient.shape[2]
    widened = jnp.pad(padded, ((0, 0), (0, 0), (1, 1), (0, 0)))
    columns = []
    for tapping in range(9):
        row_shift = tapping // 3
        col_shift = tapping % 3
        window = widened[
            :, row_shift : row_shift + row_count, col_shift : col_shift + column_total, :
        ]
        columns.append(jnp.sum(window * gradient, axis=(0, 1, 2)))
    return jnp.stack(columns, axis=1)


def timestep_features(time_steps, model_width):
    half_width = model_width // 2
    frequencies = jnp.exp(
        -math.log(10000.0) * jnp.arange(half_width, dtype=jnp.float32) / half_width
    )
    angles = time_steps.astype(jnp.float32)[..., None] * frequencies
    return jnp.concatenate([jnp.cos(angles), jnp.sin(angles)], axis=-1)


def group_owner(owner):
    canvases, row_count, column_total = owner.shape
    shaped = owner.reshape(canvases, row_count // 2, 2, column_total // 2, 2).transpose(
        0, 2, 4, 1, 3
    )
    return shaped.reshape(canvases, 2, 2, row_count // 2 * (column_total // 2))


def to_groups(tensor, head_count):
    canvases, row_count, column_total, features = tensor.shape
    head_size = features // head_count
    shaped = tensor.reshape(
        canvases, row_count // 2, 2, column_total // 2, 2, head_count, head_size
    )
    shaped = shaped.transpose(0, 2, 4, 5, 1, 3, 6)
    return shaped.reshape(
        canvases, 2, 2, head_count, row_count // 2 * (column_total // 2), head_size
    )


def from_groups(tensor, row_count, column_total):
    canvases, head_count, head_size = (tensor.shape[0], tensor.shape[3], tensor.shape[-1])
    shaped = tensor.reshape(
        canvases, 2, 2, head_count, row_count // 2, column_total // 2, head_size
    )
    shaped = shaped.transpose(0, 4, 1, 5, 2, 3, 6)
    return shaped.reshape(canvases, row_count, column_total, head_count * head_size)


def local(
    tokens,
    tile_owner,
    time_steps,
    class_labels,
    class_embedding_matrix,
    adaptive_weight,
    adaptive_bias,
    mixer_kernel,
    joint_weight,
    output_weight,
    output_bias,
    expand_weight,
    expand_bias,
    hidden_kernel,
    reduce_weight,
    reduce_bias,
    output_cotangent,
):
    canvases, row_count, column_total, model_width = tokens.shape
    head_count = HEADS
    head_size = model_width // head_count
    factor = head_size ** (-0.5)
    half_cols = column_total // 2
    strips = lax.axis_size("strip")
    strip_index = lax.axis_index("strip")
    canvas_rows = row_count * strips
    class_count = class_embedding_matrix.shape[1]
    latent_count = time_steps.shape[1]
    tile_rows = canvas_rows // 4
    full_owner = jnp.broadcast_to(
        tile_owner[:, :, None, :, None], (canvases, 4, tile_rows, 2, half_cols)
    ).reshape(canvases, canvas_rows, column_total)
    local_owner = lax.dynamic_slice_in_dim(full_owner, strip_index * row_count, row_count, 1)
    token_hot = (local_owner[..., None] == jnp.arange(latent_count, dtype=jnp.int32)).astype(
        jnp.float32
    )
    class_onehot = (class_labels[..., None] == jnp.arange(class_count, dtype=jnp.int32)).astype(
        jnp.bfloat16
    )
    class_rows = jnp.einsum(
        "ywj,gj->ywg", class_onehot, class_embedding_matrix, preferred_element_type=jnp.float32
    )
    condition = timestep_features(time_steps, model_width) + class_rows
    silu_value, silu_pull = jax.vjp(jax.nn.silu, condition)
    silu_cond = silu_value.astype(jnp.bfloat16)
    modulation = jnp.einsum(
        "cbd,de->cbe", silu_cond, adaptive_weight, preferred_element_type=jnp.float32
    )
    modulation = modulation + adaptive_bias.astype(jnp.float32)
    token_mod = jnp.einsum("crkb,cbe->crke", token_hot, modulation, precision=EXACT_PRECISION)
    shift_one, scale_one, gate_one, shift_two, scale_two, gate_two = jnp.split(
        token_mod, 6, axis=-1
    )
    inputs = tokens.astype(jnp.float32)
    first_value, first_pull = jax.vjp(modulate, inputs, shift_one, scale_one)
    first = first_value.astype(jnp.bfloat16)
    first_padded = padded_2(first, (("strip", 1),), 1)
    mixer_single_float = mixer_kernel.astype(jnp.float32)
    mixed = depthwise(first_padded.astype(jnp.float32), mixer_single_float).astype(jnp.bfloat16)
    joint = jnp.einsum("crkd,de->crke", mixed, joint_weight, preferred_element_type=jnp.float32)
    query_rows = joint[..., :model_width].astype(jnp.bfloat16)
    keys_local = joint[..., model_width : 2 * model_width].astype(jnp.bfloat16)
    values_local = joint[..., 2 * model_width :].astype(jnp.bfloat16)
    keys_canvas, values_canvas = (
        lax.all_gather(keys_local, "strip", axis=1, tiled=True),
        lax.all_gather(values_local, "strip", axis=1, tiled=True),
    )
    query_groups = to_groups(query_rows, head_count)
    key_groups = to_groups(keys_canvas, head_count)
    value_groups = to_groups(values_canvas, head_count)
    query_owner = group_owner(local_owner)
    key_owner = group_owner(full_owner)
    allowed = (query_owner[..., :, None] == key_owner[..., None, :])[:, :, :, None]

    def attention_scores():
        raw = (
            jnp.einsum(
                "cabhnd,cabhmd->cabhnm",
                query_groups,
                key_groups,
                preferred_element_type=jnp.float32,
            )
            * factor
        )
        return jnp.where(allowed, raw, MASKED)

    scores = attention_scores()
    peak = jnp.max(scores, axis=-1, keepdims=True)
    lifted_float = jnp.exp(scores - peak)
    total = jnp.sum(lifted_float, axis=-1, keepdims=True)
    softened = (lifted_float / total).astype(jnp.bfloat16)
    log_total = peak + jnp.log(total)
    attended_groups = jnp.einsum(
        "cabhnm,cabhmd->cabhnd", softened, value_groups, preferred_element_type=jnp.float32
    )
    attended = from_groups(attended_groups, row_count, column_total).astype(jnp.bfloat16)
    branch_one = jnp.einsum(
        "crkd,de->crke", attended, output_weight, preferred_element_type=jnp.float32
    )
    branch_one = branch_one + output_bias.astype(jnp.float32)
    residual = inputs + gate_one * branch_one
    second_value, second_pull = jax.vjp(modulate, residual, shift_two, scale_two)
    second = second_value.astype(jnp.bfloat16)
    expanded = jnp.einsum(
        "crkd,df->crkf", second, expand_weight, preferred_element_type=jnp.float32
    )
    expanded = (expanded + expand_bias.astype(jnp.float32)).astype(jnp.bfloat16)
    expanded_padded = padded_2(expanded, (("strip", 1),), 1)
    hidden_float = hidden_kernel.astype(jnp.float32)
    conv_out = depthwise(expanded_padded.astype(jnp.float32), hidden_float)
    gelu_value, gelu_pull = jax.vjp(jax.nn.gelu, conv_out)
    activated = gelu_value.astype(jnp.bfloat16)
    branch_two = jnp.einsum(
        "crkf,fd->crkd", activated, reduce_weight, preferred_element_type=jnp.float32
    )
    branch_two = branch_two + reduce_bias.astype(jnp.float32)
    outputs = (residual + gate_two * branch_two).astype(jnp.bfloat16)
    upstream = output_cotangent.astype(jnp.float32)
    two_grad = (upstream * gate_two).astype(jnp.bfloat16)
    gate_two_grad = upstream * branch_two
    reduce_bias_grad = jnp.sum(two_grad.astype(jnp.float32), axis=(0, 1, 2))
    reduce_weight_grad = jnp.einsum(
        "crkf,crkd->fd", activated, two_grad, preferred_element_type=jnp.float32
    )
    activated_grad = jnp.einsum(
        "crkd,fd->crkf", two_grad, reduce_weight, preferred_element_type=jnp.float32
    )
    conv_grad = gelu_pull(activated_grad)[0].astype(jnp.bfloat16)
    conv_padded = padded_2(conv_grad, (("strip", 1),), 1)
    expanded_grad = depthwise(conv_padded.astype(jnp.float32), hidden_float[:, ::-1]).astype(
        jnp.bfloat16
    )
    hidden_kernel_grad = kernel_grad(
        expanded_padded.astype(jnp.float32), conv_grad.astype(jnp.float32)
    )
    expand_bias_grad = jnp.sum(expanded_grad.astype(jnp.float32), axis=(0, 1, 2))
    expand_weight_grad = jnp.einsum(
        "crkd,crkf->df", second, expanded_grad, preferred_element_type=jnp.float32
    )
    second_grad = jnp.einsum(
        "crkf,df->crkd", expanded_grad, expand_weight, preferred_element_type=jnp.float32
    )
    residual_part, shift_two_grad, scale_two_grad = second_pull(second_grad)
    residual_grad = upstream + residual_part
    gate_one_grad = residual_grad * branch_one
    one_grad = (residual_grad * gate_one).astype(jnp.bfloat16)
    output_bias_grad = jnp.sum(one_grad.astype(jnp.float32), axis=(0, 1, 2))
    output_weight_grad = jnp.einsum(
        "crkd,crke->de", attended, one_grad, preferred_element_type=jnp.float32
    )
    attended_grad = jnp.einsum(
        "crke,de->crkd", one_grad, output_weight, preferred_element_type=jnp.float32
    ).astype(jnp.bfloat16)
    attended_grad_groups = to_groups(attended_grad, head_count)
    probs = jnp.exp(attention_scores() - log_total)
    prob_grads = jnp.einsum(
        "cabhnd,cabhmd->cabhnm",
        attended_grad_groups,
        value_groups,
        preferred_element_type=jnp.float32,
    )
    spread_sum = jnp.sum(probs * prob_grads, axis=-1, keepdims=True)
    score_grads = (probs * (prob_grads - spread_sum)).astype(jnp.bfloat16)
    query_grad_groups = (
        jnp.einsum(
            "cabhnm,cabhmd->cabhnd", score_grads, key_groups, preferred_element_type=jnp.float32
        )
        * factor
    )
    query_grad = from_groups(query_grad_groups, row_count, column_total).astype(jnp.bfloat16)
    all_queries, all_attended = (
        lax.all_gather(query_groups, "strip", axis=4, tiled=True),
        lax.all_gather(attended_grad_groups, "strip", axis=4, tiled=True),
    )
    all_logs, all_spreads = (
        lax.all_gather(log_total[..., 0], "strip", axis=4, tiled=True),
        lax.all_gather(spread_sum[..., 0], "strip", axis=4, tiled=True),
    )
    own_keys = to_groups(keys_local, head_count)
    own_values = to_groups(values_local, head_count)
    own_allowed = (key_owner[..., :, None] == query_owner[..., None, :])[:, :, :, None]
    own_scores = (
        jnp.einsum(
            "cabhnd,cabhmd->cabhnm", all_queries, own_keys, preferred_element_type=jnp.float32
        )
        * factor
    )
    own_scores = jnp.where(own_allowed, own_scores, MASKED)
    own_probs = jnp.exp(own_scores - all_logs[..., None])
    own_prob_grads = jnp.einsum(
        "cabhnd,cabhmd->cabhnm", all_attended, own_values, preferred_element_type=jnp.float32
    )
    own_score_grads = (own_probs * (own_prob_grads - all_spreads[..., None])).astype(jnp.bfloat16)
    key_grad_groups = (
        jnp.einsum(
            "cabhnm,cabhnd->cabhmd",
            own_score_grads,
            all_queries,
            preferred_element_type=jnp.float32,
        )
        * factor
    )
    value_grad_groups = jnp.einsum(
        "cabhnm,cabhnd->cabhmd",
        own_probs.astype(jnp.bfloat16),
        all_attended,
        preferred_element_type=jnp.float32,
    )
    key_grad = from_groups(key_grad_groups, row_count, column_total).astype(jnp.bfloat16)
    value_grad = from_groups(value_grad_groups, row_count, column_total).astype(jnp.bfloat16)
    joint_grad = jnp.concatenate([query_grad, key_grad, value_grad], axis=-1)
    joint_weight_grad = jnp.einsum(
        "crkd,crke->de", mixed, joint_grad, preferred_element_type=jnp.float32
    )
    mixed_grad = jnp.einsum(
        "crke,de->crkd", joint_grad, joint_weight, preferred_element_type=jnp.float32
    ).astype(jnp.bfloat16)
    mixed_padded = padded_2(mixed_grad, (("strip", 1),), 1)
    first_grad = depthwise(mixed_padded.astype(jnp.float32), mixer_single_float[:, ::-1])
    mixer_kernel_grad = kernel_grad(
        first_padded.astype(jnp.float32), mixed_grad.astype(jnp.float32)
    )
    input_part, shift_one_grad, scale_one_grad = first_pull(first_grad)
    tokens_grad = residual_grad + input_part
    token_grad = jnp.concatenate(
        [
            shift_one_grad,
            scale_one_grad,
            gate_one_grad,
            shift_two_grad,
            scale_two_grad,
            gate_two_grad,
        ],
        axis=-1,
    )
    modulation_grad = jnp.einsum("crkb,crke->cbe", token_hot, token_grad, precision=EXACT_PRECISION)
    silu_grad = jnp.einsum(
        "cbe,de->cbd",
        modulation_grad,
        adaptive_weight.astype(jnp.float32),
        precision=EXACT_PRECISION,
    )
    conditioning_grad = silu_pull(silu_grad)[0]
    table_grad = jnp.einsum(
        "soy,sok->yk",
        conditioning_grad,
        class_onehot.astype(jnp.float32),
        precision=EXACT_PRECISION,
    )
    adaptive_grad = jnp.einsum(
        "cbd,cbe->de", silu_cond.astype(jnp.float32), modulation_grad, precision=EXACT_PRECISION
    )
    adaptive_bias_grad = jnp.sum(modulation_grad, axis=(0, 1))
    (
        table_shard,
        adaptive_shard,
        adaptive_bias_shard,
        mixer_shard,
        joint_shard,
        output_shard,
        output_bias_shard,
        expand_shard,
        expand_bias_shard,
        hidden_shard,
        reduce_shard,
        reduce_bias_shard,
    ) = (
        lax.psum_scatter(
            table_grad.astype(jnp.bfloat16), "strip", scatter_dimension=0, tiled=True
        ).astype(jnp.float32),
        lax.psum_scatter(
            adaptive_grad.astype(jnp.bfloat16), "strip", scatter_dimension=0, tiled=True
        ).astype(jnp.float32),
        lax.psum_scatter(
            adaptive_bias_grad.astype(jnp.bfloat16), "strip", scatter_dimension=0, tiled=True
        ).astype(jnp.float32),
        lax.psum_scatter(
            mixer_kernel_grad.astype(jnp.bfloat16), "strip", scatter_dimension=0, tiled=True
        ).astype(jnp.float32),
        lax.psum_scatter(
            joint_weight_grad.astype(jnp.bfloat16), "strip", scatter_dimension=0, tiled=True
        ).astype(jnp.float32),
        lax.psum_scatter(
            output_weight_grad.astype(jnp.bfloat16), "strip", scatter_dimension=0, tiled=True
        ).astype(jnp.float32),
        lax.psum_scatter(
            output_bias_grad.astype(jnp.bfloat16), "strip", scatter_dimension=0, tiled=True
        ).astype(jnp.float32),
        lax.psum_scatter(
            expand_weight_grad.astype(jnp.bfloat16), "strip", scatter_dimension=0, tiled=True
        ).astype(jnp.float32),
        lax.psum_scatter(
            expand_bias_grad.astype(jnp.bfloat16), "strip", scatter_dimension=0, tiled=True
        ).astype(jnp.float32),
        lax.psum_scatter(
            hidden_kernel_grad.astype(jnp.bfloat16), "strip", scatter_dimension=0, tiled=True
        ).astype(jnp.float32),
        lax.psum_scatter(
            reduce_weight_grad.astype(jnp.bfloat16), "strip", scatter_dimension=0, tiled=True
        ).astype(jnp.float32),
        lax.psum_scatter(
            reduce_bias_grad.astype(jnp.bfloat16), "strip", scatter_dimension=0, tiled=True
        ).astype(jnp.float32),
    )
    summed = (
        lax.psum(table_shard.astype(jnp.bfloat16), "batch").astype(jnp.float32),
        lax.psum(adaptive_shard.astype(jnp.bfloat16), "batch").astype(jnp.float32),
        lax.psum(adaptive_bias_shard.astype(jnp.bfloat16), "batch").astype(jnp.float32),
        lax.psum(mixer_shard.astype(jnp.bfloat16), "batch").astype(jnp.float32),
        lax.psum(joint_shard.astype(jnp.bfloat16), "batch").astype(jnp.float32),
        lax.psum(output_shard.astype(jnp.bfloat16), "batch").astype(jnp.float32),
        lax.psum(output_bias_shard.astype(jnp.bfloat16), "batch").astype(jnp.float32),
        lax.psum(expand_shard.astype(jnp.bfloat16), "batch").astype(jnp.float32),
        lax.psum(expand_bias_shard.astype(jnp.bfloat16), "batch").astype(jnp.float32),
        lax.psum(hidden_shard.astype(jnp.bfloat16), "batch").astype(jnp.float32),
        lax.psum(reduce_shard.astype(jnp.bfloat16), "batch").astype(jnp.float32),
        lax.psum(reduce_bias_shard.astype(jnp.bfloat16), "batch").astype(jnp.float32),
    )
    return (
        outputs,
        tokens_grad,
        summed[0],
        summed[1],
        summed[2],
        summed[3],
        summed[4],
        summed[5],
        summed[6],
        summed[7],
        summed[8],
        summed[9],
        summed[10],
        summed[11],
    )


def solution(mesh):
    grouped = (mesh.shape["batch"], mesh.shape["strip"]) == (4, 8)
    return jax.shard_map(
        local_grouped if grouped else local,
        mesh=mesh,
        in_specs=(
            P("batch", "strip", None, None),
            P("batch", None, None),
            P("batch", None),
            P("batch", None),
            P(),
            P(),
            P(),
            P(),
            P(),
            P(),
            P(),
            P(),
            P(),
            P(),
            P(),
            P(),
            P("batch", "strip", None, None),
        ),
        out_specs=(
            P("batch", "strip", None, None),
            P("batch", "strip", None, None),
            P("strip", None),
            P("strip", None),
            P("strip"),
            P("strip", None),
            P("strip", None),
            P("strip", None),
            P("strip"),
            P("strip", None),
            P("strip"),
            P("strip", None),
            P("strip", None),
            P("strip"),
        ),
        check_vma=False,
    )
```

```python
import math
from types import SimpleNamespace

import jax
import jax.numpy as jnp
from jax import lax
from jax.experimental import pallas as pl
from jax.experimental.pallas import tpu as pltpu
from jax.sharding import PartitionSpec as P

HEADS = 12
EPSILON = 1e-06
MASKED = -1e30
MESH = pl.DeviceIdType.MESH
F32 = jnp.float32
BF16 = jnp.bfloat16
VMEM_BYTES = 62 * 1024 * 1024
WHOLE = pl.BlockSpec(memory_space=pltpu.VMEM)
LEFT = pl.BlockSpec(memory_space=pl.ANY)
SCALARS = pl.BlockSpec(memory_space=pltpu.SMEM)
NT = (((1,), (1,)), ((), ()))
TN = (((0,), (0,)), ((), ()))


def dot(a, b):
    return jnp.dot(a, b, preferred_element_type=F32)


def dot_nt(a, b):
    return lax.dot_general(a, b, NT, preferred_element_type=F32)


def dot_tn(a, b):
    return lax.dot_general(a, b, TN, preferred_element_type=F32)


def send_to(src, dst, sems, index, batch, strip):
    return pltpu.make_async_remote_copy(
        src_ref=src,
        dst_ref=dst,
        send_sem=sems[0].at[index],
        recv_sem=sems[1].at[index],
        device_id=(batch, strip),
        device_id_type=MESH,
    )


def entry_barrier(strips):
    s = lax.axis_index("strip")
    b = lax.axis_index("batch")
    z = s // 2
    barrier = pltpu.get_barrier_semaphore()
    count = 0
    for d in range(1, strips):
        pl.semaphore_signal(
            barrier, inc=1, device_id=(b, lax.rem(s + d, strips)), device_id_type=MESH
        )
        count += 1
    for e in range(1, 4):
        for core in range(2):
            pl.semaphore_signal(
                barrier, inc=1, device_id=(lax.rem(b + e, 4), 2 * z + core), device_id_type=MESH
            )
            count += 1
    pl.semaphore_wait(barrier, count)


def spread(mod, width):
    return jnp.concatenate(
        [jnp.broadcast_to(mod[0:1], (8, width)), jnp.broadcast_to(mod[1:2], (8, width))], axis=0
    )


def spread_columns(buffer, r, x):
    for k in range(x.shape[-1] // 128):
        buffer[r, k] = x[:, k * 128 : k * 128 + 128]


def every_second(buffer, r, p):
    return jnp.concatenate(
        [buffer[r, k, pl.ds(p, 16, stride=2), :] for k in range(buffer.shape[1])], axis=-1
    )


def interleave(buffer, r, p, x):
    for k in range(x.shape[-1] // 128):
        buffer[r, k, pl.ds(p, 16, stride=2), :] = x[:, k * 128 : k * 128 + 128]


def joined(buffer, r):
    return jnp.concatenate([buffer[r, k] for k in range(buffer.shape[1])], axis=-1)


def ln_parts(x):
    centre = jnp.mean(x, axis=-1, keepdims=True)
    centred = x - centre
    var = jnp.mean(centred * centred, axis=-1, keepdims=True)
    inv = lax.rsqrt(var + EPSILON)
    return centred * inv, inv


def ln_back(grad, n, inv):
    mean0 = jnp.mean(grad, axis=-1, keepdims=True)
    mean1 = jnp.mean(grad * n, axis=-1, keepdims=True)
    return inv * (grad - mean0 - n * mean1)


def window(load, r):
    even = load(r, 0).astype(F32)
    odd = load(r, 1).astype(F32)
    n = even.shape[0]
    j = lax.broadcasted_iota(jnp.int32, even.shape, 0)
    odd_m = jnp.where(j == 0, 0.0, pltpu.roll(odd, 1, 0))
    even_p = jnp.where(j == n - 1, 0.0, pltpu.roll(even, n - 1, 0))
    return odd_m, even, odd, even_p


def conv(rows, weights, flip):
    out = []
    for p in range(2):
        total = None
        for i in range(3):
            for j in range(3):
                t = 3 * i + j
                a = weights[8 - t if flip else t] * rows[i][p + j]
                total = a if total is None else total + a
        out.append(total)
    return out


def taps(rows, centre, sums):
    new = list(sums)
    for i in range(3):
        for j in range(3):
            a = rows[i][j] * centre[0] + rows[i][1 + j] * centre[1]
            t = 8 - (3 * i + j)
            new[t] = sums[t] + (a[0:8] + a[8:16])
    return new


def halves(x):
    return jnp.concatenate(
        [jnp.sum(x[0:8], axis=0, keepdims=True), jnp.sum(x[8:16], axis=0, keepdims=True)], axis=0
    )


def gelu_both(x):
    k0 = math.sqrt(2.0 / math.pi)
    square = x * x
    t = jnp.tanh(k0 * x * (1.0 + 0.044715 * square))
    cdf = 0.5 + 0.5 * t
    slope = cdf + (0.5 * k0) * x * (1.0 - t * t) * (1.0 + (3.0 * 0.044715) * square)
    return x * cdf, slope


def condition_kernel(owner, steps, labels, emb, ab, aw_hbm, mod_ref, cond_ref, aw, sem):
    s = lax.axis_index("strip")
    b = lax.axis_index("batch")
    z = s // 2
    classes, width = emb.shape
    latents = steps.shape[1]
    half = width // 2
    copies = []
    for i in range(6):
        cp = pltpu.make_async_copy(aw_hbm.at[:, pl.ds(i * width, width)], aw.at[i], sem.at[i])
        cp.start()
        copies.append(cp)

    row = lax.broadcasted_iota(jnp.int32, (latents, 1), 0)
    when = jnp.zeros((latents, 1), F32)
    label = jnp.zeros((latents, 1), jnp.int32)
    for i in range(latents):
        when = jnp.where(row == i, steps[0, i].astype(F32), when)
        label = jnp.where(row == i, labels[0, i], label)
    order = lax.broadcasted_iota(jnp.int32, (latents, half), 1).astype(F32)
    angles = when * jnp.exp(-math.log(10000.0) * order / half)
    features = jnp.concatenate([jnp.cos(angles), jnp.sin(angles)], axis=1)
    onehot = lax.broadcasted_iota(jnp.int32, (latents, classes), 1) == label
    condition = features + dot(jnp.where(onehot, 1.0, 0.0).astype(BF16), emb[...])
    silu = (condition / (1.0 + jnp.exp(-condition))).astype(BF16)

    lane = lax.broadcasted_iota(jnp.int32, (latents, 128), 1)
    kind = lax.broadcasted_iota(jnp.int32, (latents, 128), 0)
    line = lax.rem(lane, 16)
    side = jnp.where(kind == 0, lax.rem(line // 2, 2), lax.rem(line // 3, 2))
    tile = lax.rem(lane // 16, 4)
    slots = jnp.zeros((latents, 128), jnp.int32)
    for i in range(4):
        for h in range(2):
            hit = jnp.logical_and(tile == i, side == h)
            slots = jnp.where(hit, owner[0, h, i] + b * latents, slots)
    cond_ref[...] = jnp.concatenate(
        [condition, jnp.broadcast_to(label.astype(F32), (latents, 128)), slots.astype(F32)], axis=1
    )

    bias = ab[...].astype(F32).reshape(1, 6 * width)
    for i in range(6):
        copies[i].wait()
        lanes = slice(i * width, i * width + width)
        table = dot(silu, aw[i]) + bias[:, lanes]
        for h in range(2):
            mine = row == owner[0, h, z]
            mod_ref[h : h + 1, lanes] = jnp.sum(
                jnp.where(mine, table, 0.0), axis=0, keepdims=True
            )


def conditioning(owner, steps, labels, emb, ab, aw):
    width = emb.shape[1]
    latents = steps.shape[1]
    shape = jax.ShapeDtypeStruct
    return pl.pallas_call(
        condition_kernel,
        name="conditioning",
        out_shape=(shape((2, 6 * width), F32), shape((latents, width + 256), F32)),
        in_specs=[SCALARS] * 3 + [WHOLE] * 2 + [LEFT],
        out_specs=(WHOLE, WHOLE),
        scratch_shapes=[pltpu.VMEM((6, width, width), BF16), pltpu.SemaphoreType.DMA((6,))],
        compiler_params=pltpu.CompilerParams(vmem_limit_bytes=VMEM_BYTES),
    )(owner, steps, labels, emb, ab, aw)


def block_kernel(names, *refs):
    m = SimpleNamespace(**dict(zip(names, refs)))
    rows, cols, width = m.tok.shape
    half = width // 2
    strips = lax.axis_size("strip")
    chips = strips // 2
    chip_rows = 2 * rows
    total = strips * 64
    own = width // strips
    s = lax.axis_index("strip")
    b = lax.axis_index("batch")
    z = s // 2
    c = lax.rem(s, 2)
    sibling = 2 * z + 1 - c
    y, x = b // 2, lax.rem(b, 2)
    x_mate = 2 * y + 1 - x
    y_mate = 2 * (1 - y) + x
    sent = []

    def chip(d):
        return lax.rem(z + d, chips)

    def start(copy):
        copy.start()
        sent.append(copy)

    loads = {}

    def load(name, src, dst, index):
        loads[name] = pltpu.make_async_copy(src, dst, m.load_sem.at[index])
        loads[name].start()

    for part in range(3):
        off = pl.multiple_of(part * width + c * half, 128)
        load(f"wj{part}", m.wj_hbm.at[:, pl.ds(off, half)], m.wj.at[part], part)
    load("cot", m.cot_hbm, m.cot, 3)
    load("wo", m.wo_hbm, m.wo, 4)
    for n in range(chips):
        off = pl.multiple_of((2 * n + c) * half, 128)
        spot = pl.ds(n * half, half)
        load(f"we{n}", m.we_hbm.at[:, pl.ds(off, half)], m.we.at[:, spot], 5 + n)
        load(f"wr{n}", m.wr_hbm.at[pl.ds(off, half)], m.wr.at[spot], 5 + chips + n)
    entry_barrier(strips)

    m.mk[...] = m.mixer[...].astype(F32)
    ob = m.ob[...].astype(F32).reshape(1, width)
    rb = m.rb[...].astype(F32).reshape(1, width)
    m.ebf[...] = m.eb[...].astype(F32).reshape(m.ebf.shape)
    for n in range(chips):
        m.hk[n] = m.hidden[:, pl.ds(pl.multiple_of((2 * n + c) * half, 128), half)].astype(F32)

    m.cond_all[b] = m.cond[...]
    for e in range(1, 4):
        start(
            send_to(m.cond_all.at[b], m.cond_all.at[b], m.cond_sem, e, lax.rem(b + e, 4), s)
        )

    def block_mod(n):
        return spread(m.mod[:, n * width : (n + 1) * width], width)

    scale1 = 1.0 + block_mod(1)
    shift1 = block_mod(0)

    def first_row(r):
        spread_columns(m.rowf, r, m.tok[r].astype(F32))
        for p in range(2):
            v = every_second(m.rowf, r, p)
            m.xd[r, p] = v.astype(BF16)
            n, _ = ln_parts(v)
            m.fp[r + 1, p] = (n * scale1 + shift1).astype(BF16)

    def edge_sends(buffer, sems):
        up = send_to(buffer.at[1], buffer.at[rows + 1], sems, 0, b, s - 1)
        down = send_to(buffer.at[rows], buffer.at[0], sems, 1, b, s + 1)
        return up, down

    def start_edges(buffer, sems):
        up, down = edge_sends(buffer, sems)

        @pl.when(s > 0)
        def _():
            up.start()

        @pl.when(s < strips - 1)
        def _():
            down.start()

    def edges_sent(buffer, sems):
        up, down = edge_sends(buffer, sems)

        @pl.when(s > 0)
        def _():
            up.wait_send()

        @pl.when(s < strips - 1)
        def _():
            down.wait_send()

    def top_edge(buffer, sems):
        @pl.when(s > 0)
        def _():
            send_to(buffer.at[1], buffer.at[0], sems, 1, b, s - 1).wait_recv()

        @pl.when(s == 0)
        def _():
            buffer[0] = jnp.zeros_like(buffer[0])

    def bottom_edge(buffer, sems):
        @pl.when(s < strips - 1)
        def _():
            send_to(buffer.at[1], buffer.at[rows + 1], sems, 0, b, s + 1).wait_recv()

        @pl.when(s == strips - 1)
        def _():
            buffer[rows + 1] = jnp.zeros_like(buffer[0])

    first_row(0)
    first_row(rows - 1)
    start_edges(m.fp, m.fp_sem)

    def body(r, _):
        first_row(r)
        return 0

    lax.fori_loop(1, rows - 1, body, 0, unroll=3)

    def mixed_rows(low, high):
        for k in range(width // 128):
            lanes = pl.ds(k * 128, 128)
            weights = [m.mk[t : t + 1, k * 128 : k * 128 + 128] for t in range(9)]

            def line(r, p):
                return m.fp[r, p, :, lanes]

            def step(r, carry):
                new = window(line, r + 2)
                out = conv((carry[0], carry[1], new), weights, False)
                for p in range(2):
                    m.ms[lax.rem(r, 2) * 2 + p, r // 2, :, lanes] = out[p].astype(BF16)
                return carry[1], new

            lax.fori_loop(
                low, high, step, (window(line, low), window(line, low + 1)), unroll=True
            )

    mixed_rows(1, rows - 1)
    top_edge(m.fp, m.fp_sem)
    mixed_rows(0, 1)
    bottom_edge(m.fp, m.fp_sem)
    mixed_rows(rows - 1, rows)

    def to_groups(source, target, sems, sems2):
        for d in range(1, chips):
            g = chip(d)
            start(send_to(source.at[g], target.at[s], sems, d, b, 2 * g + c))
        target[s] = source[z]

    def pass_on(target, sems, sems2, d):
        i = 2 * chip(chips - d) + c
        if d:
            send_to(target.at[i], target.at[i], sems, d, b, i).wait_recv()
        start(send_to(target.at[i], target.at[i], sems2, d, b, sibling))

    def groups_ready(target, sems2):
        for d in range(chips):
            i = 2 * chip(chips - d) + 1 - c
            send_to(target.at[i], target.at[i], sems2, d, b, sibling).wait_recv()

    to_groups(m.ms, m.mg, m.mg_sem, m.mg_sem2)

    m.acc[...] = jnp.zeros_like(m.acc)
    gate2 = block_mod(5)
    loads["cot"].wait()

    def upstream_row(r, _):
        spread_columns(m.rowf, r, m.cot[r].astype(F32))
        for p in range(2):
            up = every_second(m.rowf, r, p)
            m.ctd[2 * r + p] = up.astype(BF16)
            two = (up * gate2).astype(BF16)
            m.tg[c, 2 * r + p] = two
            m.acc[0] += two.astype(F32)
        return 0

    lax.fori_loop(0, rows, upstream_row, 0)
    start(send_to(m.tg.at[c], m.tg.at[c], m.pair_sem, 0, b, sibling))

    for d in range(chips):
        pass_on(m.mg, m.mg_sem, m.mg_sem2, d)
    groups_ready(m.mg, m.mg_sem2)
    for part in range(3):
        loads[f"wj{part}"].wait()

    v = m.mg[...].reshape(total, width)
    for part in range(3):
        w = dot(v, m.wj[part]).astype(BF16)
        for n in range(3):
            m.qkv[3 * part + n] = w[:, n * 128 : n * 128 + 128]

    where = lax.broadcasted_iota(jnp.int32, (1, total), 1)
    lefts = lax.rem(where, 16) < 8
    key_owner = jnp.zeros((1, total), jnp.int32)
    for t in range(4):
        both = jnp.where(lefts, m.owner[0, 0, t], m.owner[0, 1, t])
        key_owner = jnp.where(where // 128 == t, both, key_owner)
    where = lax.broadcasted_iota(jnp.int32, (total, 1), 0)
    lefts = lax.rem(where, 16) < 8
    query_owner = jnp.zeros((total, 1), jnp.int32)
    for t in range(4):
        both = jnp.where(lefts, m.owner[0, 0, t], m.owner[0, 1, t])
        query_owner = jnp.where(where // 128 == t, both, query_owner)
    allowed = query_owner == key_owner
    lane = lax.broadcasted_iota(jnp.int32, (total, 128), 1) < 64
    factor = 64 ** -0.5

    def head(v, h):
        return jnp.where(lane if h == 0 else jnp.logical_not(lane), v, jnp.zeros_like(v))

    for n in range(3):
        mine = c * 3 + n
        q2 = (m.qkv[n].astype(F32) * factor).astype(BF16)
        outs = []
        for h in range(2):
            scores = jnp.where(allowed, dot_nt(head(q2, h), m.qkv[3 + n]), MASKED)
            peak = jnp.max(scores, axis=-1, keepdims=True)
            lifted = jnp.exp(scores - peak)
            inv = 1.0 / jnp.sum(lifted, axis=-1, keepdims=True)
            m.probs[n, h] = (lifted * inv).astype(BF16)
            outs.append(dot(lifted.astype(BF16), m.qkv[6 + n]) * inv)
        m.ag[mine] = jnp.where(lane, outs[0], outs[1]).astype(BF16)
        for d in range(1, strips):
            t = lax.rem(s + d, strips)
            start(
                send_to(
                    m.ag.at[mine, pl.ds(pl.multiple_of(t * 64, 64), 64)],
                    m.ai.at[mine, z],
                    m.ai_sem,
                    (n, d),
                    b,
                    t,
                )
            )
        start(send_to(m.ag.at[mine], m.ag.at[mine], m.ag_sem, n, b, sibling))
        m.ai[mine, z] = m.ag[mine, pl.ds(pl.multiple_of(s * 64, 64), 64), :]

    for n in range(3):
        for d in range(1, strips):
            i = lax.rem(s - d + strips, strips)
            spot = lax.rem(i, 2) * 3 + n
            send_to(
                m.ag.at[spot, pl.ds(0, 64)], m.ai.at[spot, i // 2], m.ai_sem, (n, d), b, i
            ).wait_recv()

    gate1 = block_mod(2)
    shift2 = block_mod(3)
    scale2 = 1.0 + block_mod(4)
    loads["wo"].wait()

    v = jnp.concatenate([m.ai[n].reshape(chips * 64, 128) for n in range(6)], axis=-1)
    m.b1[...] = (dot(v, m.wo[...]) + ob).reshape(m.b1.shape)

    def residual_row(i, _):
        rp = 4 * lax.rem(i, rows // 2) + i // (rows // 2)
        u = m.xd[rp // 2, lax.rem(rp, 2)].astype(F32) + gate1 * m.b1[i]
        m.res[rp] = u
        n, _ = ln_parts(u)
        m.sc[c, rp] = (n * scale2 + shift2).astype(BF16)
        return 0

    lax.fori_loop(0, 2 * rows, residual_row, 0, unroll=4)
    start(send_to(m.sc.at[c], m.sc.at[c], m.pair_sem, 1, b, sibling))

    def halo_sends(buffer, sems):
        up = send_to(buffer.at[1], buffer.at[chip_rows + 1], sems, 0, b, s - 2)
        down = send_to(buffer.at[chip_rows], buffer.at[0], sems, 1, b, s + 2)
        return up, down

    def start_halo(buffer, sems, upward, downward):
        up, down = halo_sends(buffer, sems)

        @pl.when(jnp.logical_and(z > 0, upward))
        def _():
            up.start()

        @pl.when(jnp.logical_and(z < chips - 1, downward))
        def _():
            down.start()

    def halo_sent(buffer, sems):
        up, down = halo_sends(buffer, sems)

        @pl.when(z > 0)
        def _():
            up.wait_send()

        @pl.when(z < chips - 1)
        def _():
            down.wait_send()

    def take_halo(buffer, sems):
        @pl.when(z > 0)
        def _():
            send_to(buffer.at[1], buffer.at[0], sems, 1, b, s - 2).wait_recv()

        @pl.when(z == 0)
        def _():
            buffer[0] = jnp.zeros_like(buffer[0])

        @pl.when(z < chips - 1)
        def _():
            send_to(buffer.at[1], buffer.at[chip_rows + 1], sems, 0, b, s + 2).wait_recv()

        @pl.when(z == chips - 1)
        def _():
            buffer[chip_rows + 1] = jnp.zeros_like(buffer[0])

    for n in range(chips):
        loads[f"we{n}"].wait()
        loads[f"wr{n}"].wait()
    hidden = chips * half
    bias = jnp.concatenate(
        [m.ebf[:, pl.ds(pl.multiple_of((2 * n + c) * half, 128), half)] for n in range(chips)],
        axis=-1,
    )

    def expand(core):
        w = dot(m.sc[core].reshape(rows * 32, width), m.we[...]) + bias
        m.ex[pl.ds(1 + core * rows, rows)] = w.astype(BF16).reshape(rows, 2, 16, hidden)

    expand(c)
    start_halo(m.ex, m.ex_sem, c == 0, c == 1)
    send_to(m.sc.at[c], m.sc.at[1 - c], m.pair_sem, 1, b, sibling).wait_recv()
    expand(1 - c)
    start_halo(m.ex, m.ex_sem, c == 1, c == 0)
    send_to(m.tg.at[c], m.tg.at[1 - c], m.pair_sem, 0, b, sibling).wait_recv()
    chip_tg = m.tg[...].reshape(total, width)
    for h in range(2):
        m.big[h] = dot_nt(chip_tg, m.wr[h * width : h * width + width, :]).reshape(m.big.shape[1:])

    first_mate, then_mate = (x_mate, y_mate), (y_mate, x_mate)
    part_rows = width // 8

    def r_source(n, h, mine):
        at = pl.ds(h * part_rows, part_rows)
        if h == 0:
            return m.rw.at[n, :, x if mine else 1 - x, at]
        return m.rw.at[n, y if mine else 1 - y, :, at]

    def r_one(n, h):
        return send_to(r_source(n, h, False), m.r1.at[n, h], m.r1_sem, (n, h), first_mate[h], s)

    def r_two(n, h):
        src = m.r1.at[n, h, (1 - y) if h == 0 else (1 - x)]
        return send_to(src, m.r2.at[n, h], m.r2_sem, (n, h), then_mate[h], s)

    def r_three(k):
        z_pair = z + 1 - 2 * lax.rem(z, 2)
        z_far = lax.rem(z + 2, 4)
        dest = z_pair if k < 2 else z_far
        t = (z_pair, 3 - z, z_far)[k]
        return send_to(m.r2.at[t], m.r3.at[k], m.r3_sem, k, b, 2 * dest + c)

    def r_four(e):
        return send_to(m.r_all.at[b], m.r_all.at[b], m.r4_sem, e, lax.rem(b + e, 4), s)

    def r_half(n):
        for h in range(2):
            r_one(n, h).wait_recv()
            kept = r_source(n, h, True)[...].astype(F32)
            m.r1[n, h] = (m.r1[n, h].astype(F32) + kept).astype(BF16)
            r_two(n, h).start()

    def r_quarter(n):
        for h in range(2):
            r_two(n, h).wait_recv()
            kept = m.r1[n, h, y if h == 0 else x].astype(F32)
            m.r2[n, h] = (m.r2[n, h].astype(F32) + kept).astype(BF16)

    def r_spread():
        r_three(1).start()
        r_three(0).start()

    def r_across():
        r_three(1).wait_recv()
        t = lax.rem(z + 2, 4)
        m.r2[t] = (m.r2[t].astype(F32) + m.r3[1].astype(F32)).astype(BF16)
        r_three(2).start()

    def r_sum():
        v = m.r2[z].astype(F32)
        for k in (0, 2):
            r_three(k).wait_recv()
            v = v + m.r3[k].astype(F32)
        m.r_all[b] = v.astype(BF16)
        for e in range(1, 4):
            r_four(e).start()

    def c_source(j, h, mine):
        block = m.ew.at[j] if not isinstance(j, int) or j < 4 else m.jo.at[j - 4]
        at = pl.ds(2 * h, 2)
        if h == 0:
            return block.at[at, :, x if mine else 1 - x]
        return block.at[at, y if mine else 1 - y]

    def c_one(j, h):
        return send_to(c_source(j, h, False), m.c1.at[j, h], m.c1_sem, (j, h), first_mate[h], s)

    def c_two(j, h):
        src = m.c1.at[j, h, :, 1 - y] if h == 0 else m.c1.at[j, h, :, 1 - x]
        return send_to(src, m.c2.at[j, pl.ds(2 * h, 2)], m.c2_sem, (j, h), then_mate[h], s)

    pair_chip = z + 1 - 2 * lax.rem(z, 2)
    far_chip = lax.rem(z + 2, 4)
    last_chip = 3 - z

    def c_three(j, k):
        dest = pair_chip if k < 2 else far_chip
        t = (pair_chip, last_chip, far_chip)[k]
        return send_to(m.c2.at[j, t], m.c3.at[j, k], m.c3_sem, (j, k), b, 2 * dest + c)

    def c_four(j, e):
        return pltpu.make_async_remote_copy(
            src_ref=m.c_out.at[j],
            dst_ref=m.c_all.at[j, x, c],
            send_sem=m.c4_sem[0].at[j, e],
            recv_sem=m.c4_sem[1].at[j, e, c],
            device_id=(lax.rem(b + e, 4), 2 * z + y),
            device_id_type=MESH,
        )

    def c_begin(j):
        for h in range(2):
            c_one(j, h).start()

    def c_half(j):
        for h in range(2):
            c_one(j, h).wait_recv()
            kept = c_source(j, h, True)[...].astype(F32)
            m.c1[j, h] = (m.c1[j, h].astype(F32) + kept).astype(BF16)
            c_two(j, h).start()

    def c_quarter(j):
        for h in range(2):
            c_two(j, h).wait_recv()
            at = pl.ds(2 * h, 2)
            kept = (m.c1[j, h, :, y] if h == 0 else m.c1[j, h, :, x]).astype(F32)
            m.c2[j, at] = (m.c2[j, at].astype(F32) + kept).astype(BF16)

    def c_spread(j):
        c_three(j, 1).start()
        c_three(j, 0).start()

    def c_across(j):
        c_three(j, 1).wait_recv()
        far = m.c2[j, far_chip].astype(F32) + m.c3[j, 1].astype(F32)
        m.c2[j, far_chip] = far.astype(BF16)
        c_three(j, 2).start()

    def c_sum(j):
        v = m.c2[j, z].astype(F32)
        for k in (0, 2):
            c_three(j, k).wait_recv()
            v = v + m.c3[j, k].astype(F32)
        m.c_out[j] = v.astype(BF16)

        @pl.when(c == y)
        def _():
            m.c_all[j, x, c] = m.c_out[j]

        for e in range(1, 4):
            c_four(j, e).start()

        @pl.when(c != y)
        def _():
            c_four(j, 0).start()

    take_halo(m.ex, m.ex_sem)

    def activate(n, _):
        for k in range(3):
            lanes = pl.ds(pl.multiple_of(n * half + k * 128, 128), 128)
            inner = pl.ds(k * 128, 128)
            weights = [m.hk[n, t : t + 1, inner] for t in range(9)]
            spot = pl.ds(pl.multiple_of(lax.rem(n, 2) * half + k * 128, 128), 128)

            def line(r, p):
                return m.ex[r, p, :, lanes]

            above, here = window(line, 0), window(line, 1)
            for r in range(chip_rows):
                below = window(line, r + 2)
                out = conv((above, here, below), weights, False)
                for p in range(2):
                    value, slope = gelu_both(out[p])
                    rp = 2 * r + p
                    grad = m.big[n // 2, rp // 16, rp % 16, :, spot]
                    m.act[rp, :, lanes] = value.astype(BF16)
                    m.cg[r + 1, p, :, lanes] = (grad * slope).astype(BF16)
                above, here = here, below
        full = m.act[:, :, pl.ds(pl.multiple_of(n * half, 128), half)].reshape(total, half)
        m.rw[n] = dot_tn(chip_tg, full).astype(BF16).reshape(m.rw.shape[1:])
        for h in range(2):
            r_one(n, h).start()
        return 0

    lax.fori_loop(0, chips, activate, 0)
    start_halo(m.cg, m.cg_sem, True, True)
    full = m.act[...].reshape(total, hidden)
    m.big[0] = dot(full, m.wr[...]).reshape(m.big.shape[1:])
    b2_copy = send_to(m.big.at[0, 1 - c], m.b2_in, m.pair_sem, 2, b, sibling)
    b2_copy.start()
    m.hkg[...] = jnp.zeros_like(m.hkg)
    take_halo(m.cg, m.cg_sem)
    chip_sc = m.sc[...].reshape(total, width)

    def backward(n, _):
        for k in range(3):
            lanes = pl.ds(pl.multiple_of(n * half + k * 128, 128), 128)
            inner = pl.ds(k * 128, 128)
            weights = [m.hk[n, t : t + 1, inner] for t in range(9)]

            def line(r, p):
                return m.cg[r, p, :, lanes]

            above, here = window(line, 0), window(line, 1)
            sums = [jnp.zeros((8, 128), F32) for _ in range(9)]
            total_eg = jnp.zeros((8, 128), F32)
            for r in range(chip_rows):
                below = window(line, r + 2)
                three = (above, here, below)
                low = [v.astype(BF16) for v in conv(three, weights, True)]
                for p in range(2):
                    m.act[2 * r + p, :, lanes] = low[p]
                centre = [m.ex[r + 1, p, :, lanes].astype(F32) for p in range(2)]
                sums = taps(three, centre, sums)
                both = low[0].astype(F32) + low[1].astype(F32)
                total_eg = total_eg + (both[0:8] + both[8:16])
                above, here = here, below
            for t, v in enumerate(sums + [total_eg]):
                m.hkg[n, t : t + 1, inner] = jnp.sum(v, axis=0, keepdims=True)
        full = m.act[:, :, pl.ds(pl.multiple_of(n * half, 128), half)].reshape(total, half)
        m.ew[n] = dot_tn(chip_sc, full).astype(BF16).reshape(m.ew.shape[1:])
        c_begin(n)
        r_half(n)
        return 0

    lax.fori_loop(0, chips, backward, 0)
    for core in (1 - c, c):
        v = m.act[pl.ds(core * 2 * rows, 2 * rows)].reshape(rows * 32, hidden)
        m.big[1, core] = dot_nt(v, m.we[...]).reshape(m.big.shape[2:])
        if core is not c:
            sg_copy = send_to(m.big.at[1, 1 - c], m.sg_in, m.pair_sem, 3, b, sibling)
            sg_copy.start()
    send_to(m.big.at[0, c], m.b2_in, m.pair_sem, 2, b, sibling).wait_recv()
    send_to(m.big.at[1, c], m.sg_in, m.pair_sem, 3, b, sibling).wait_recv()

    def finish(r, _):
        for p in range(2):
            rp = 2 * r + p
            grad = m.big[1, c, rp] + m.sg_in[rp]
            v = m.res[rp]
            n, inv = ln_parts(v)
            branch = m.b1[(rows // 2) * lax.rem(rp, 4) + rp // 4]
            up = m.ctd[rp].astype(F32)
            m.acc[1] += grad
            m.acc[2] += grad * n
            back = up + ln_back(grad * scale2, n, inv)
            m.rg[rp] = back
            m.acc[3] += back * branch
            one = (back * gate1).astype(BF16)
            m.og[lax.rem(rp, 4), rp // 4] = one
            m.acc[4] += one.astype(F32)
            branch2 = m.big[0, c, rp] + m.b2_in[rp] + rb
            m.acc[5] += up * branch2
            interleave(m.rowf, r, p, v + gate2 * branch2)
        m.out[r] = joined(m.rowf, r).astype(BF16)
        return 0

    lax.fori_loop(0, rows, finish, 0, unroll=2)
    out_copy = pltpu.make_async_copy(m.out, m.out_hbm, m.load_sem.at[13])
    out_copy.start()

    to_groups(m.og, m.gg, m.gg_sem, m.gg_sem2)

    pack = []
    for v in (m.acc[3], m.acc[1], m.acc[2], m.acc[5]):
        pair = halves(v)
        for h in range(2):
            pack += [pair[h : h + 1, 0:half], pair[h : h + 1, half:]]
    def own_sums(buffer, sems, value):
        buffer[b, c, z] = value.astype(BF16)
        for d in range(1, chips):
            start(send_to(buffer.at[b, c, z], buffer.at[b, c, z], sems, d, b, 2 * chip(d) + c))

    def to_canvases(buffer, sems, sems2):
        for d in range(1, chips):
            i = chip(chips - d)
            send_to(buffer.at[b, c, i], buffer.at[b, c, i], sems, d, b, 2 * i + c).wait_recv()
        for e in range(1, 4):
            start(send_to(buffer.at[b, c], buffer.at[b, c], sems2, e, lax.rem(b + e, 4), s))

    def to_sibling(buffer, sems2, sems3):
        for e in range(1, 4):
            i = lax.rem(b - e + 4, 4)
            send_to(buffer.at[i, c], buffer.at[i, c], sems2, e, i, s).wait_recv()
        start(send_to(buffer.at[:, c], buffer.at[:, c], sems3, 0, b, sibling))

    def from_sibling(buffer, sems3):
        send_to(buffer.at[:, c], buffer.at[:, 1 - c], sems3, 0, b, sibling).wait_recv()

    own_sums(m.late, m.late_sem, jnp.concatenate(pack, axis=0))
    sums_ob = jnp.sum(m.acc[4], axis=0, keepdims=True)
    sums_rb = jnp.sum(m.acc[0], axis=0, keepdims=True)
    pad_lanes = jnp.zeros((1, half - own), F32)
    pad_rows = jnp.zeros((4, half), F32)
    for t in range(strips):
        piece = jnp.concatenate(
            [
                jnp.where(c == t % 2, m.hkg[t // 2, 0:10], 0.0),
                jnp.concatenate([sums_ob[:, t * own : t * own + own], pad_lanes], axis=1),
                jnp.concatenate([sums_rb[:, t * own : t * own + own], pad_lanes], axis=1),
                pad_rows,
            ],
            axis=0,
        )
        m.piece[t] = piece.astype(BF16)
    for d in range(1, strips):
        t = lax.rem(s + d, strips)
        start(send_to(m.piece.at[t], m.piece_in.at[d], m.piece_sem, d, b, t))

    pass_on(m.gg, m.gg_sem, m.gg_sem2, 0)
    c_half(0)
    c_half(1)
    pass_on(m.gg, m.gg_sem, m.gg_sem2, 1)
    c_half(2)
    pass_on(m.gg, m.gg_sem, m.gg_sem2, 2)
    pass_on(m.gg, m.gg_sem, m.gg_sem2, 3)
    c_half(3)
    to_canvases(m.late, m.late_sem, m.late_sem2)
    for n in range(chips):
        r_quarter(n)
    r_spread()
    groups_ready(m.gg, m.gg_sem2)
    wo_own = m.wo[pl.ds(pl.multiple_of(c * half, 128), half), :]
    w = dot_nt(m.gg[...].reshape(total, width), wo_own).astype(BF16)
    for n in range(3):
        m.da[n] = w[:, n * 128 : n * 128 + 128]

    for n in range(3):
        other = (1 - c) * 3 + n
        send_to(m.ag.at[other], m.ag.at[other], m.ag_sem, n, b, sibling).wait_recv()
    columns = m.gg[:, :, :, pl.ds(pl.multiple_of(c * half, 128), half)].reshape(total, half)
    full = jnp.concatenate([m.ag[n] for n in range(6)], axis=-1)
    m.jo[3] = dot_tn(full, columns).astype(BF16).reshape(m.jo.shape[1:])
    c_begin(7)

    tops = lax.broadcasted_iota(jnp.int32, (128, total), 0) < 64
    group = m.mg[...].reshape(total, width)
    for n in range(3):
        d2 = m.da[n]
        outs = []
        for h in range(2):
            dp = dot_nt(head(d2, h), m.qkv[6 + n])
            probs = m.probs[n, h].astype(F32)
            inner = jnp.sum(probs * dp, axis=-1, keepdims=True)
            m.ds[h] = (probs * (dp - inner)).astype(BF16)
            outs.append(dot(m.ds[h], m.qkv[3 + n]))
        dq = (jnp.where(lane, outs[0], outs[1]) * factor).astype(BF16)
        dk = [dot_tn(m.qkv[n], m.ds[h]) for h in range(2)]
        dk = (jnp.where(tops, dk[0], dk[1]) * factor).T.astype(BF16)
        dv = [dot_tn(d2, m.probs[n, h]) for h in range(2)]
        dv = jnp.where(tops, dv[0], dv[1]).T.astype(BF16)
        m.dqkv[n] = dq
        m.dqkv[3 + n] = dk
        m.dqkv[6 + n] = dv
        w = dot_tn(group, jnp.concatenate([dq, dk, dv], axis=-1))
        m.jo[n] = w.astype(BF16).reshape(m.jo.shape[1:])
        c_begin(4 + n)

    r_across()
    for j in range(4):
        c_quarter(j)

    b2_copy.wait_send()
    sg_copy.wait_send()

    def partial(core):
        strip_rows = [
            jnp.concatenate(
                [
                    m.dqkv[k, pl.ds(pl.multiple_of((2 * i + core) * 64, 64), 64), :]
                    for i in range(chips)
                ],
                axis=0,
            )
            for k in range(9)
        ]
        w = None
        for part in range(3):
            v = jnp.concatenate(strip_rows[3 * part : 3 * part + 3], axis=-1)
            v = dot_nt(v, m.wj[part])
            w = v if w is None else w + v
        m.big[0, core] = w.reshape(m.big.shape[2:])

    partial(1 - c)
    start(send_to(m.big.at[0, 1 - c], m.mp_in, m.pair_sem, 4, b, sibling))
    partial(c)
    send_to(m.big.at[0, c], m.mp_in, m.pair_sem, 4, b, sibling).wait_recv()
    four = rows // 2
    for d in range(chips):
        i = chip(d)
        at = pl.ds(four * i, four)
        low = (m.big[0, c, at] + m.mp_in[at]).astype(BF16)
        if d:
            m.mo[i] = low
            start(send_to(m.mo.at[i], m.mr.at[z], m.mr_sem, d, b, 2 * i + c))
        else:
            m.mr[z] = low

    to_sibling(m.late, m.late_sem2, m.late_sem3)
    sums = m.piece[s].astype(F32)
    for d in range(1, strips):
        send_to(m.piece.at[0], m.piece_in.at[d], m.piece_sem, d, b, s).wait_recv()
        sums = sums + m.piece_in[d].astype(F32)
    m.small[b] = sums.astype(BF16)
    for e in range(1, 4):
        start(send_to(m.small.at[b], m.small.at[b], m.small_sem, e, lax.rem(b + e, 4), s))
    c_spread(0)
    c_spread(1)
    c_half(7)
    c_half(4)
    c_half(5)
    c_half(6)

    for d in range(1, chips):
        i = chip(chips - d)
        send_to(m.mo.at[i], m.mr.at[i], m.mr_sem, d, b, 2 * i + c).wait_recv()
    for r in (0, rows - 1):
        for p in range(2):
            m.md[r + 1, p] = m.mr[(r % 2) * 2 + p, r // 2]
    start_edges(m.md, m.md_sem)
    c_spread(2)
    c_spread(3)
    c_across(0)
    c_across(1)
    r_sum()
    for r in range(1, rows - 1):
        for p in range(2):
            m.md[r + 1, p] = m.mr[(r % 2) * 2 + p, r // 2]

    m.acc1[...] = jnp.zeros_like(m.acc1)

    def mixer_rows(low, high):
        for k in range(width // 128):
            lanes = pl.ds(k * 128, 128)
            weights = [m.mk[t : t + 1, k * 128 : k * 128 + 128] for t in range(9)]

            def line(r, p):
                return m.md[r, p, :, lanes]

            def step(r, carry):
                new = window(line, r + 2)
                three = (carry[0], carry[1], new)
                out = conv(three, weights, True)
                for p in range(2):
                    m.fg[2 * r + p, :, lanes] = out[p]
                centre = [m.fp[r + 1, p, :, lanes].astype(F32) for p in range(2)]
                return carry[1], new, tuple(taps(three, centre, carry[2]))

            begin = tuple(m.acc1[t, :, lanes] for t in range(9))
            _, _, sums = lax.fori_loop(
                low, high, step, (window(line, low), window(line, low + 1), begin), unroll=True
            )
            for t in range(9):
                m.acc1[t, :, lanes] = sums[t]

    m.acc[1] = jnp.zeros_like(m.acc[1])
    m.acc[2] = jnp.zeros_like(m.acc[2])

    def token_row(r, _):
        for p in range(2):
            rp = 2 * r + p
            grad = m.fg[rp]
            n, inv = ln_parts(m.xd[r, p].astype(F32))
            m.acc[1] += grad
            m.acc[2] += grad * n
            interleave(m.rowf, r, p, m.rg[rp] + ln_back(grad * scale1, n, inv))
        m.tgo[r] = joined(m.rowf, r)
        return 0

    mixer_rows(1, rows - 1)
    lax.fori_loop(1, rows - 1, token_row, 0, unroll=3)
    top_edge(m.md, m.md_sem)
    mixer_rows(0, 1)
    token_row(0, 0)
    bottom_edge(m.md, m.md_sem)
    mixer_rows(rows - 1, rows)
    token_row(rows - 1, 0)
    tg_copy = pltpu.make_async_copy(m.tgo, m.tg_hbm, m.load_sem.at[14])
    tg_copy.start()

    pack = []
    third = width // 3
    for v in (m.acc[1], m.acc[2]):
        pair = halves(v)
        for h in range(2):
            pack += [pair[h : h + 1, k * third : k * third + third] for k in range(3)]
    pack.append(jnp.zeros((4, third), F32))
    own_sums(m.early, m.early_sem, jnp.concatenate(pack, axis=0))
    mixer_sums = [jnp.sum(m.acc1[t], axis=0, keepdims=True) for t in range(9)]
    mixer_sums = jnp.concatenate(mixer_sums + [jnp.zeros((7, width), F32)], axis=0)
    pad_lanes = jnp.zeros((16, 128 - own), F32)
    for t in range(strips):
        m.mpiece[t] = jnp.concatenate(
            [mixer_sums[:, t * own : t * own + own], pad_lanes], axis=1
        ).astype(BF16)
    for d in range(1, strips):
        t = lax.rem(s + d, strips)
        start(send_to(m.mpiece.at[t], m.mpiece_in.at[d], m.mpiece_sem, d, b, t))

    for j in (7, 4, 5, 6):
        c_quarter(j)
        c_spread(j)
    c_across(2)
    c_across(3)
    c_sum(0)
    c_sum(1)
    to_canvases(m.early, m.early_sem, m.early_sem2)
    c_across(7)
    c_sum(2)
    c_sum(3)
    c_across(4)
    sums = m.mpiece[s].astype(F32)
    for d in range(1, strips):
        send_to(m.mpiece.at[0], m.mpiece_in.at[d], m.mpiece_sem, d, b, s).wait_recv()
        sums = sums + m.mpiece_in[d].astype(F32)
    m.msmall[b] = sums.astype(BF16)
    for e in range(1, 4):
        start(send_to(m.msmall.at[b], m.msmall.at[b], m.msmall_sem, e, lax.rem(b + e, 4), s))
    c_across(5)
    c_sum(7)
    to_sibling(m.early, m.early_sem2, m.early_sem3)
    c_across(6)
    for j in (4, 5, 6):
        c_sum(j)

    finals = []

    def store(src, dst, index):
        cp = pltpu.make_async_copy(src, dst, m.load_sem.at[index])
        cp.start()
        finals.append(cp)

    for e in range(1, 4):
        i = lax.rem(b - e + 4, 4)
        send_to(m.cond_all.at[i], m.cond_all.at[i], m.cond_sem, e, i, s).wait_recv()
        send_to(m.small.at[i], m.small.at[i], m.small_sem, e, i, s).wait_recv()
        send_to(m.msmall.at[i], m.msmall.at[i], m.msmall_sem, e, i, s).wait_recv()
        send_to(m.r_all.at[i], m.r_all.at[i], m.r4_sem, e, i, s).wait_recv()
    store(m.r_all, m.r_hbm, 15)
    store(m.cond_all, m.cond_hbm, 16)
    store(m.small, m.small_hbm, 17)
    store(m.msmall, m.msmall_hbm, 18)
    from_sibling(m.late, m.late_sem3)
    from_sibling(m.early, m.early_sem3)
    store(m.late, m.late_hbm, 19)
    store(m.early, m.early_hbm, 20)
    for j in range(8):
        for xs in range(2):
            for cs in range(2):
                source = 2 * c + xs
                e = lax.rem(b - source + 4, 4)
                local = jnp.logical_and(source == b, cs == c)

                @pl.when(jnp.logical_not(local))
                def _():
                    pltpu.make_async_remote_copy(
                        src_ref=m.c_out.at[j],
                        dst_ref=m.c_all.at[j, xs, cs],
                        send_sem=m.c4_sem[0].at[j, e],
                        recv_sem=m.c4_sem[1].at[j, e, cs],
                        device_id=(source, 2 * z + cs),
                        device_id_type=MESH,
                    ).wait_recv()

    store(m.c_all, m.c_hbm, 21)
    for cp in sent:
        cp.wait_send()
    edges_sent(m.fp, m.fp_sem)
    edges_sent(m.md, m.md_sem)

    halo_sent(m.ex, m.ex_sem)
    halo_sent(m.cg, m.cg_sem)
    for h in range(2):
        for n in range(chips):
            r_one(n, h).wait_send()
            r_two(n, h).wait_send()
        for j in range(8):
            c_one(j, h).wait_send()
            c_two(j, h).wait_send()
    for k in range(3):
        r_three(k).wait_send()
        r_four(k + 1).wait_send()
        for j in range(8):
            c_three(j, k).wait_send()
            c_four(j, k + 1).wait_send()

    @pl.when(c != y)
    def _():
        for j in range(8):
            c_four(j, 0).wait_send()

    out_copy.wait()
    tg_copy.wait()
    for cp in finals:
        cp.wait()


def block(tokens, mod, mixer, owner, cond, ob, eb, hk, rb, wj, wo, we, wr, cot, strips):
    rows, cols, width = tokens.shape
    chips = strips // 2
    half = width // 2
    total = strips * 64
    blocks = 2 * rows
    chip_rows = 2 * rows
    part = width // chips // 4
    third = width // 3
    shape = jax.ShapeDtypeStruct
    vm = pltpu.VMEM

    def dma(*size):
        return pltpu.SemaphoreType.DMA(size)

    ins = dict(
        tok=tokens, mod=mod, mixer=mixer, owner=owner, cond=cond, ob=ob, eb=eb, hidden=hk, rb=rb,
        wj_hbm=wj, wo_hbm=wo, we_hbm=we, wr_hbm=wr, cot_hbm=cot,
    )
    outs = dict(
        out_hbm=shape((rows, cols, width), BF16),
        tg_hbm=shape((rows, cols, width), F32),
        r_hbm=shape((4, 2, width // 8, half), BF16),
        c_hbm=shape((8, 2, 2, part, half), BF16),
        cond_hbm=shape((4,) + cond.shape, F32),
        small_hbm=shape((4, 16, half), BF16),
        msmall_hbm=shape((4, 16, 128), BF16),
        late_hbm=shape((4, 2, chips, 16, half), BF16),
        early_hbm=shape((4, 2, chips, 16, third), BF16),
    )
    scratch = dict(
        mk=vm((9, width), F32),
        ebf=vm((1, 2 * chips * half), F32),
        hk=vm((chips, 9, half), F32),
        wj=vm((3, width, half), BF16),
        wo=vm((width, width), BF16),
        we=vm((width, chips * half), BF16),
        wr=vm((chips * half, width), BF16),
        cot=vm((rows, cols, width), BF16),
        cond_all=vm((4,) + cond.shape, F32),
        rowf=vm((rows, width // 128, cols, 128), F32),
        xd=vm((rows, 2, 16, width), BF16),
        fp=vm((rows + 2, 2, 16, width), BF16),
        ms=vm((chips, rows // 2, 16, width), BF16),
        mg=vm((strips, rows // 2, 16, width), BF16),
        qkv=vm((9, total, 128), BF16),
        probs=vm((3, 2, total, total), BF16),
        ag=vm((6, total, 128), BF16),
        ai=vm((6, chips, 64, 128), BF16),
        acc=vm((6, 16, width), F32),
        acc1=vm((9, 8, width), F32),
        ctd=vm((blocks, 16, width), BF16),
        tg=vm((2, blocks, 16, width), BF16),
        sc=vm((2, blocks, 16, width), BF16),
        b1=vm((blocks, 16, width), F32),
        res=vm((blocks, 16, width), F32),
        ex=vm((chip_rows + 2, 2, 16, chips * half), BF16),
        cg=vm((chip_rows + 2, 2, 16, chips * half), BF16),
        act=vm((2 * blocks, 16, chips * half), BF16),
        big=vm((2, 2, blocks, 16, width), F32),
        b2_in=vm((blocks, 16, width), F32),
        sg_in=vm((blocks, 16, width), F32),
        hkg=vm((chips, 16, half), F32),
        rg=vm((blocks, 16, width), F32),
        og=vm((chips, rows // 2, 16, width), BF16),
        out=vm((rows, cols, width), BF16),
        gg=vm((strips, rows // 2, 16, width), BF16),
        da=vm((3, total, 128), BF16),
        ds=vm((2, total, total), BF16),
        dqkv=vm((9, total, 128), BF16),
        mp_in=vm((blocks, 16, width), F32),
        mo=vm((chips, rows // 2, 16, width), BF16),
        mr=vm((chips, rows // 2, 16, width), BF16),
        md=vm((rows + 2, 2, 16, width), BF16),
        fg=vm((blocks, 16, width), F32),
        tgo=vm((rows, cols, width), F32),
        rw=vm((chips, 2, 2, width // 4, half), BF16),
        r1=vm((chips, 2, 2, width // 8, half), BF16),
        r2=vm((chips, 2, width // 8, half), BF16),
        r3=vm((3, 2, width // 8, half), BF16),
        r_all=vm((4, 2, width // 8, half), BF16),
        ew=vm((4, chips, 2, 2, part, half), BF16),
        jo=vm((4, chips, 2, 2, part, half), BF16),
        c1=vm((8, 2, 2, 2, part, half), BF16),
        c2=vm((8, chips, part, half), BF16),
        c3=vm((8, 3, part, half), BF16),
        c_out=vm((8, part, half), BF16),
        c_all=vm((8, 2, 2, part, half), BF16),
        late=vm((4, 2, chips, 16, half), BF16),
        early=vm((4, 2, chips, 16, third), BF16),
        piece=vm((strips, 16, half), BF16),
        piece_in=vm((strips, 16, half), BF16),
        small=vm((4, 16, half), BF16),
        mpiece=vm((strips, 16, 128), BF16),
        mpiece_in=vm((strips, 16, 128), BF16),
        msmall=vm((4, 16, 128), BF16),
        load_sem=dma(22),
    )
    pairs = dict(
        cond_sem=(4,), fp_sem=(2,), md_sem=(2,), mg_sem=(chips,), mg_sem2=(chips,),
        gg_sem=(chips,), gg_sem2=(chips,), ai_sem=(3, strips), ag_sem=(3,), pair_sem=(5,),
        ex_sem=(2,), cg_sem=(2,), mr_sem=(chips,),
        r1_sem=(chips, 2), r2_sem=(chips, 2), r3_sem=(3,), r4_sem=(4,),
        c1_sem=(8, 2), c2_sem=(8, 2), c3_sem=(8, 3),
        late_sem=(chips,), late_sem2=(4,), late_sem3=(1,),
        early_sem=(chips,), early_sem2=(4,), early_sem3=(1,),
        piece_sem=(strips,), small_sem=(4,), mpiece_sem=(strips,), msmall_sem=(4,),
    )
    names = list(ins) + list(outs) + list(scratch)
    shapes = list(scratch.values())
    for size in list(pairs.values()):
        shapes += [dma(*size), dma(*size)]
    shapes += [dma(8, 4), dma(8, 4, 2)]
    plain = len(names)

    def kernel(*refs):
        named = list(refs[:plain])
        sems = refs[plain:]
        both = [(sems[2 * i], sems[2 * i + 1]) for i in range(len(sems) // 2)]
        block_kernel(names + list(pairs) + ["c4_sem"], *named, *both)

    return pl.pallas_call(
        kernel,
        name="block",
        out_shape=tuple(outs.values()),
        in_specs=[WHOLE] * 3 + [SCALARS] + [WHOLE] * 5 + [LEFT] * 5,
        out_specs=(LEFT,) * len(outs),
        scratch_shapes=shapes,
        compiler_params=pltpu.CompilerParams(
            collective_id=0, has_side_effects=True, vmem_limit_bytes=VMEM_BYTES
        ),
    )(*ins.values())


def final_kernel(
    out_in, tg_in, r_in, c_in, cond_ref, small_ref, msmall_ref, late_ref, early_ref, aw_hbm,
    out_ref, tg_ref, tab_ref, ad_out, ab_ref, mix_ref, joint_out, output_out, ob_ref,
    expand_out, eb_ref, hidden_ref, reduce_out, rb_ref,
    aw, out_v, tg_v, r_ref, c_ref, ad_ref, joint_ref, output_ref, expand_ref, reduce_ref, sem,
):
    s = lax.axis_index("strip")
    strips = lax.axis_size("strip")
    width = cond_ref.shape[2] - 256
    own = width // strips
    half = width // 2
    third = width // 3
    loads = [
        (r_in, r_ref),
        (c_in, c_ref),
        (aw_hbm.at[pl.ds(pl.multiple_of(s * own, 16), own)], aw),
        (out_in, out_v),
        (tg_in, tg_v),
    ]
    loads = [pltpu.make_async_copy(a, v, sem.at[i]) for i, (a, v) in enumerate(loads)]
    for cp in loads:
        cp.start()
    stores = []

    def store(src, dst):
        cp = pltpu.make_async_copy(src, dst, sem.at[5 + len(stores)])
        cp.start()
        stores.append(cp)

    small = small_ref[0].astype(F32)
    mixer = msmall_ref[0].astype(F32)
    for i in range(1, 4):
        small = small + small_ref[i].astype(F32)
        mixer = mixer + msmall_ref[i].astype(F32)
    hidden_ref[...] = small[0:9]
    eb_ref[...] = small[9]
    ob_ref[...] = small[10, 0:own]
    rb_ref[...] = small[11, 0:own]
    mix_ref[...] = mixer[0:9, 0:own]

    n = width // 4
    loads[0].wait()
    for q in range(4):
        reduce_ref[:, q * n : q * n + n] = r_ref[q].reshape(n, half).astype(F32).T
    store(reduce_ref, reduce_out)
    loads[1].wait()
    part = c_ref.shape[3]
    for xs in range(2):
        rows = slice(xs * part, xs * part + part)
        for cs in range(2):
            for k in range(4):
                at = (2 * k + cs) * half
                expand_ref[rows, at : at + half] = c_ref[k, xs, cs].astype(F32)
            for k in range(3):
                for p in range(3):
                    at = p * width + cs * half + k * 128
                    joint_ref[rows, at : at + 128] = c_ref[
                        4 + k, xs, cs, :, p * 128 : p * 128 + 128
                    ].astype(F32)
            output_ref[rows, cs * half : cs * half + half] = c_ref[7, xs, cs].astype(F32)
    store(expand_ref, expand_out)
    store(joint_ref, joint_out)
    store(output_ref, output_out)
    loads[3].wait()
    store(out_v, out_ref)
    loads[4].wait()
    store(tg_v, tg_ref)

    slots = 32
    condition = cond_ref[...].reshape(slots, width + 256)
    labels = condition[:, width : width + 1]
    slot_late = jnp.concatenate([cond_ref[i, 0:1, width + 128 :] for i in range(4)], axis=1)
    slot_early = jnp.concatenate([cond_ref[i, 1:2, width + 128 :] for i in range(4)], axis=1)
    condition = condition[:, 0:width]
    pick = lax.broadcasted_iota(jnp.int32, (width, own), 0) == (
        lax.broadcasted_iota(jnp.int32, (width, own), 1) + s * own
    )
    pick = jnp.where(pick, 1.0, 0.0)
    condition = jnp.dot(
        condition, pick, precision=lax.Precision.HIGHEST, preferred_element_type=F32
    )
    sigmoid = 1.0 / (1.0 + jnp.exp(-condition))
    silu = (condition * sigmoid).astype(BF16)
    slope = sigmoid * (1.0 + condition * (1.0 - sigmoid))

    count = 4 * strips * 16
    row = lax.rem(lax.broadcasted_iota(jnp.int32, (slots, count), 1), 16)
    index = lax.broadcasted_iota(jnp.int32, (slots, count), 0)
    hit_late = index == slot_late.astype(jnp.int32)
    hit_early = index == slot_early.astype(jnp.int32)
    late = late_ref[...].reshape(count, half)
    early = early_ref[...].reshape(count, third)
    loads[2].wait()
    bias = jnp.zeros((1, 6 * own), F32)
    sums = []
    silu_grad = jnp.zeros((slots, own), F32)
    pieces = []
    for i in range(2):
        for k in range(3):
            mine = jnp.logical_or(row == 6 * i + k, row == 6 * i + 3 + k)
            pieces.append((early, jnp.logical_and(hit_early, mine), i * width + k * third, third))
    for i in range(4):
        for k in range(2):
            mine = jnp.logical_or(row == 4 * i + k, row == 4 * i + 2 + k)
            pieces.append((late, jnp.logical_and(hit_late, mine), (2 + i) * width + k * half, half))
    for source, mine, at, size in pieces:
        chosen = jnp.where(mine, 1.0, 0.0).astype(BF16)
        grad = dot(chosen, source)
        sums.append(jnp.sum(grad, axis=0, keepdims=True))
        low = grad.astype(BF16)
        ad_ref[:, at : at + size] = dot_tn(silu, low)
        silu_grad = silu_grad + dot_nt(low, aw[:, at : at + size])
    store(ad_ref, ad_out)
    sums = jnp.concatenate(sums, axis=1)
    for t in range(strips):
        bias = jnp.where(s == t, sums[:, t * 6 * own : t * 6 * own + 6 * own], bias)
    ab_ref[...] = bias[0]
    classes = tab_ref.shape[1]
    onehot = lax.broadcasted_iota(jnp.int32, (slots, classes), 1) == labels.astype(jnp.int32)
    tab_ref[...] = lax.dot_general(
        silu_grad * slope,
        jnp.where(onehot, 1.0, 0.0),
        TN,
        precision=lax.Precision.HIGHEST,
        preferred_element_type=F32,
    )
    for cp in stores:
        cp.wait()


def final(parts, aw, classes, strips):
    out, tg, r, c = parts[:4]
    width = out.shape[-1]
    own = width // strips
    half = width // 2
    shape = jax.ShapeDtypeStruct
    vm = pltpu.VMEM
    return pl.pallas_call(
        final_kernel,
        name="final",
        out_shape=(
            shape(out.shape, BF16),
            shape(tg.shape, F32),
            shape((own, classes), F32),
            shape((own, 6 * width), F32),
            shape((6 * own,), F32),
            shape((9, own), F32),
            shape((own, 3 * width), F32),
            shape((own, width), F32),
            shape((own,), F32),
            shape((own, 4 * width), F32),
            shape((half,), F32),
            shape((9, half), F32),
            shape((half, width), F32),
            shape((own,), F32),
        ),
        in_specs=[LEFT] * 4 + [WHOLE] * 5 + [LEFT],
        out_specs=(
            LEFT, LEFT, WHOLE, LEFT, WHOLE, WHOLE, LEFT, LEFT, WHOLE, LEFT, WHOLE, WHOLE, LEFT,
            WHOLE,
        ),
        scratch_shapes=[
            vm((own, 6 * width), BF16),
            vm(out.shape, BF16),
            vm(tg.shape, F32),
            vm(r.shape, BF16),
            vm(c.shape, BF16),
            vm((own, 6 * width), F32),
            vm((own, 3 * width), F32),
            vm((own, width), F32),
            vm((own, 4 * width), F32),
            vm((half, width), F32),
            pltpu.SemaphoreType.DMA((12,)),
        ],
        compiler_params=pltpu.CompilerParams(vmem_limit_bytes=VMEM_BYTES),
    )(*parts, aw)


def local_grouped(
    tokens, tile_owner, time_steps, class_labels, class_embedding_matrix, adaptive_weight,
    adaptive_bias, mixer_kernel, joint_weight, output_weight, output_bias, expand_weight,
    expand_bias, hidden_kernel, reduce_weight, reduce_bias, output_cotangent,
):
    strips = lax.axis_size("strip")
    owner = tile_owner.transpose(0, 2, 1)
    mod, cond = conditioning(
        owner, time_steps, class_labels, class_embedding_matrix.T, adaptive_bias,
        adaptive_weight,
    )
    parts = block(
        tokens[0], mod, mixer_kernel.T, owner, cond, output_bias, expand_bias,
        hidden_kernel.T, reduce_bias, joint_weight, output_weight, expand_weight, reduce_weight,
        output_cotangent[0], strips,
    )
    classes = class_embedding_matrix.shape[1]
    (
        out, tg, table, adaptive, bias, mixer, joint, output, ob, expand, eb, hidden, reduce, rb,
    ) = final(parts, adaptive_weight, classes, strips)
    return (
        out[None], tg[None], table, adaptive, bias, mixer.T, joint, output, ob, expand, eb,
        hidden.T, reduce, rb,
    )


EXACT_PRECISION = lax.Precision.HIGHEST


def padded_2(block, sides, width):
    for axis, dim in sides:
        count = lax.axis_size(axis)
        forward = [(i, i + 1) for i in range(count - 1)]
        backward = [(target, source) for source, target in forward]
        low = lax.ppermute(
            lax.slice_in_dim(block, block.shape[dim] - width, None, axis=dim), axis, forward
        )
        high = lax.ppermute(lax.slice_in_dim(block, 0, width, axis=dim), axis, backward)
        block = jnp.concatenate([low, block, high], axis=dim)
    return block


def normalize(values):
    centre = jnp.mean(values, axis=-1, keepdims=True)
    centred = values - centre
    spread = jnp.mean(centred * centred, axis=-1, keepdims=True)
    return centred * lax.rsqrt(spread + EPSILON)


def modulate(values, shifting, scaling):
    return normalize(values) * (1.0 + scaling) + shifting


def depthwise(padded, kernel):
    row_count = padded.shape[-3] - 2
    column_total = padded.shape[-2]
    widened = jnp.pad(padded, [(0, 0)] * (padded.ndim - 2) + [(1, 1), (0, 0)])
    result = jnp.zeros(
        padded.shape[:-3] + (row_count, column_total, padded.shape[-1]), padded.dtype
    )
    for tapping in range(9):
        row_shift = tapping // 3
        col_shift = tapping % 3
        window = lax.slice_in_dim(widened, row_shift, row_shift + row_count, axis=widened.ndim - 3)
        window = lax.slice_in_dim(
            window, col_shift, col_shift + column_total, axis=widened.ndim - 2
        )
        result = result + kernel[:, tapping] * window
    return result


def kernel_grad(padded, gradient):
    row_count = gradient.shape[1]
    column_total = gradient.shape[2]
    widened = jnp.pad(padded, ((0, 0), (0, 0), (1, 1), (0, 0)))
    columns = []
    for tapping in range(9):
        row_shift = tapping // 3
        col_shift = tapping % 3
        window = widened[
            :, row_shift : row_shift + row_count, col_shift : col_shift + column_total, :
        ]
        columns.append(jnp.sum(window * gradient, axis=(0, 1, 2)))
    return jnp.stack(columns, axis=1)


def timestep_features(time_steps, model_width):
    half_width = model_width // 2
    frequencies = jnp.exp(
        -math.log(10000.0) * jnp.arange(half_width, dtype=jnp.float32) / half_width
    )
    angles = time_steps.astype(jnp.float32)[..., None] * frequencies
    return jnp.concatenate([jnp.cos(angles), jnp.sin(angles)], axis=-1)


def group_owner(owner):
    canvases, row_count, column_total = owner.shape
    shaped = owner.reshape(canvases, row_count // 2, 2, column_total // 2, 2).transpose(
        0, 2, 4, 1, 3
    )
    return shaped.reshape(canvases, 2, 2, row_count // 2 * (column_total // 2))


def to_groups(tensor, head_count):
    canvases, row_count, column_total, features = tensor.shape
    head_size = features // head_count
    shaped = tensor.reshape(
        canvases, row_count // 2, 2, column_total // 2, 2, head_count, head_size
    )
    shaped = shaped.transpose(0, 2, 4, 5, 1, 3, 6)
    return shaped.reshape(
        canvases, 2, 2, head_count, row_count // 2 * (column_total // 2), head_size
    )


def from_groups(tensor, row_count, column_total):
    canvases, head_count, head_size = (tensor.shape[0], tensor.shape[3], tensor.shape[-1])
    shaped = tensor.reshape(
        canvases, 2, 2, head_count, row_count // 2, column_total // 2, head_size
    )
    shaped = shaped.transpose(0, 4, 1, 5, 2, 3, 6)
    return shaped.reshape(canvases, row_count, column_total, head_count * head_size)


def local(
    tokens,
    tile_owner,
    time_steps,
    class_labels,
    class_embedding_matrix,
    adaptive_weight,
    adaptive_bias,
    mixer_kernel,
    joint_weight,
    output_weight,
    output_bias,
    expand_weight,
    expand_bias,
    hidden_kernel,
    reduce_weight,
    reduce_bias,
    output_cotangent,
):
    canvases, row_count, column_total, model_width = tokens.shape
    head_count = HEADS
    head_size = model_width // head_count
    factor = head_size ** (-0.5)
    half_cols = column_total // 2
    strips = lax.axis_size("strip")
    strip_index = lax.axis_index("strip")
    canvas_rows = row_count * strips
    class_count = class_embedding_matrix.shape[1]
    latent_count = time_steps.shape[1]
    tile_rows = canvas_rows // 4
    full_owner = jnp.broadcast_to(
        tile_owner[:, :, None, :, None], (canvases, 4, tile_rows, 2, half_cols)
    ).reshape(canvases, canvas_rows, column_total)
    local_owner = lax.dynamic_slice_in_dim(full_owner, strip_index * row_count, row_count, 1)
    token_hot = (local_owner[..., None] == jnp.arange(latent_count, dtype=jnp.int32)).astype(
        jnp.float32
    )
    class_onehot = (class_labels[..., None] == jnp.arange(class_count, dtype=jnp.int32)).astype(
        jnp.bfloat16
    )
    class_rows = jnp.einsum(
        "ywj,gj->ywg", class_onehot, class_embedding_matrix, preferred_element_type=jnp.float32
    )
    condition = timestep_features(time_steps, model_width) + class_rows
    silu_value, silu_pull = jax.vjp(jax.nn.silu, condition)
    silu_cond = silu_value.astype(jnp.bfloat16)
    modulation = jnp.einsum(
        "cbd,de->cbe", silu_cond, adaptive_weight, preferred_element_type=jnp.float32
    )
    modulation = modulation + adaptive_bias.astype(jnp.float32)
    token_mod = jnp.einsum("crkb,cbe->crke", token_hot, modulation, precision=EXACT_PRECISION)
    shift_one, scale_one, gate_one, shift_two, scale_two, gate_two = jnp.split(
        token_mod, 6, axis=-1
    )
    inputs = tokens.astype(jnp.float32)
    first_value, first_pull = jax.vjp(modulate, inputs, shift_one, scale_one)
    first = first_value.astype(jnp.bfloat16)
    first_padded = padded_2(first, (("strip", 1),), 1)
    mixer_single_float = mixer_kernel.astype(jnp.float32)
    mixed = depthwise(first_padded.astype(jnp.float32), mixer_single_float).astype(jnp.bfloat16)
    joint = jnp.einsum("crkd,de->crke", mixed, joint_weight, preferred_element_type=jnp.float32)
    query_rows = joint[..., :model_width].astype(jnp.bfloat16)
    keys_local = joint[..., model_width : 2 * model_width].astype(jnp.bfloat16)
    values_local = joint[..., 2 * model_width :].astype(jnp.bfloat16)
    keys_canvas, values_canvas = (
        lax.all_gather(keys_local, "strip", axis=1, tiled=True),
        lax.all_gather(values_local, "strip", axis=1, tiled=True),
    )
    query_groups = to_groups(query_rows, head_count)
    key_groups = to_groups(keys_canvas, head_count)
    value_groups = to_groups(values_canvas, head_count)
    query_owner = group_owner(local_owner)
    key_owner = group_owner(full_owner)
    allowed = (query_owner[..., :, None] == key_owner[..., None, :])[:, :, :, None]

    def attention_scores():
        raw = (
            jnp.einsum(
                "cabhnd,cabhmd->cabhnm",
                query_groups,
                key_groups,
                preferred_element_type=jnp.float32,
            )
            * factor
        )
        return jnp.where(allowed, raw, MASKED)

    scores = attention_scores()
    peak = jnp.max(scores, axis=-1, keepdims=True)
    lifted_float = jnp.exp(scores - peak)
    total = jnp.sum(lifted_float, axis=-1, keepdims=True)
    softened = (lifted_float / total).astype(jnp.bfloat16)
    log_total = peak + jnp.log(total)
    attended_groups = jnp.einsum(
        "cabhnm,cabhmd->cabhnd", softened, value_groups, preferred_element_type=jnp.float32
    )
    attended = from_groups(attended_groups, row_count, column_total).astype(jnp.bfloat16)
    branch_one = jnp.einsum(
        "crkd,de->crke", attended, output_weight, preferred_element_type=jnp.float32
    )
    branch_one = branch_one + output_bias.astype(jnp.float32)
    residual = inputs + gate_one * branch_one
    second_value, second_pull = jax.vjp(modulate, residual, shift_two, scale_two)
    second = second_value.astype(jnp.bfloat16)
    expanded = jnp.einsum(
        "crkd,df->crkf", second, expand_weight, preferred_element_type=jnp.float32
    )
    expanded = (expanded + expand_bias.astype(jnp.float32)).astype(jnp.bfloat16)
    expanded_padded = padded_2(expanded, (("strip", 1),), 1)
    hidden_float = hidden_kernel.astype(jnp.float32)
    conv_out = depthwise(expanded_padded.astype(jnp.float32), hidden_float)
    gelu_value, gelu_pull = jax.vjp(jax.nn.gelu, conv_out)
    activated = gelu_value.astype(jnp.bfloat16)
    branch_two = jnp.einsum(
        "crkf,fd->crkd", activated, reduce_weight, preferred_element_type=jnp.float32
    )
    branch_two = branch_two + reduce_bias.astype(jnp.float32)
    outputs = (residual + gate_two * branch_two).astype(jnp.bfloat16)
    upstream = output_cotangent.astype(jnp.float32)
    two_grad = (upstream * gate_two).astype(jnp.bfloat16)
    gate_two_grad = upstream * branch_two
    reduce_bias_grad = jnp.sum(two_grad.astype(jnp.float32), axis=(0, 1, 2))
    reduce_weight_grad = jnp.einsum(
        "crkf,crkd->fd", activated, two_grad, preferred_element_type=jnp.float32
    )
    activated_grad = jnp.einsum(
        "crkd,fd->crkf", two_grad, reduce_weight, preferred_element_type=jnp.float32
    )
    conv_grad = gelu_pull(activated_grad)[0].astype(jnp.bfloat16)
    conv_padded = padded_2(conv_grad, (("strip", 1),), 1)
    expanded_grad = depthwise(conv_padded.astype(jnp.float32), hidden_float[:, ::-1]).astype(
        jnp.bfloat16
    )
    hidden_kernel_grad = kernel_grad(
        expanded_padded.astype(jnp.float32), conv_grad.astype(jnp.float32)
    )
    expand_bias_grad = jnp.sum(expanded_grad.astype(jnp.float32), axis=(0, 1, 2))
    expand_weight_grad = jnp.einsum(
        "crkd,crkf->df", second, expanded_grad, preferred_element_type=jnp.float32
    )
    second_grad = jnp.einsum(
        "crkf,df->crkd", expanded_grad, expand_weight, preferred_element_type=jnp.float32
    )
    residual_part, shift_two_grad, scale_two_grad = second_pull(second_grad)
    residual_grad = upstream + residual_part
    gate_one_grad = residual_grad * branch_one
    one_grad = (residual_grad * gate_one).astype(jnp.bfloat16)
    output_bias_grad = jnp.sum(one_grad.astype(jnp.float32), axis=(0, 1, 2))
    output_weight_grad = jnp.einsum(
        "crkd,crke->de", attended, one_grad, preferred_element_type=jnp.float32
    )
    attended_grad = jnp.einsum(
        "crke,de->crkd", one_grad, output_weight, preferred_element_type=jnp.float32
    ).astype(jnp.bfloat16)
    attended_grad_groups = to_groups(attended_grad, head_count)
    probs = jnp.exp(attention_scores() - log_total)
    prob_grads = jnp.einsum(
        "cabhnd,cabhmd->cabhnm",
        attended_grad_groups,
        value_groups,
        preferred_element_type=jnp.float32,
    )
    spread_sum = jnp.sum(probs * prob_grads, axis=-1, keepdims=True)
    score_grads = (probs * (prob_grads - spread_sum)).astype(jnp.bfloat16)
    query_grad_groups = (
        jnp.einsum(
            "cabhnm,cabhmd->cabhnd", score_grads, key_groups, preferred_element_type=jnp.float32
        )
        * factor
    )
    query_grad = from_groups(query_grad_groups, row_count, column_total).astype(jnp.bfloat16)
    all_queries, all_attended = (
        lax.all_gather(query_groups, "strip", axis=4, tiled=True),
        lax.all_gather(attended_grad_groups, "strip", axis=4, tiled=True),
    )
    all_logs, all_spreads = (
        lax.all_gather(log_total[..., 0], "strip", axis=4, tiled=True),
        lax.all_gather(spread_sum[..., 0], "strip", axis=4, tiled=True),
    )
    own_keys = to_groups(keys_local, head_count)
    own_values = to_groups(values_local, head_count)
    own_allowed = (key_owner[..., :, None] == query_owner[..., None, :])[:, :, :, None]
    own_scores = (
        jnp.einsum(
            "cabhnd,cabhmd->cabhnm", all_queries, own_keys, preferred_element_type=jnp.float32
        )
        * factor
    )
    own_scores = jnp.where(own_allowed, own_scores, MASKED)
    own_probs = jnp.exp(own_scores - all_logs[..., None])
    own_prob_grads = jnp.einsum(
        "cabhnd,cabhmd->cabhnm", all_attended, own_values, preferred_element_type=jnp.float32
    )
    own_score_grads = (own_probs * (own_prob_grads - all_spreads[..., None])).astype(jnp.bfloat16)
    key_grad_groups = (
        jnp.einsum(
            "cabhnm,cabhnd->cabhmd",
            own_score_grads,
            all_queries,
            preferred_element_type=jnp.float32,
        )
        * factor
    )
    value_grad_groups = jnp.einsum(
        "cabhnm,cabhnd->cabhmd",
        own_probs.astype(jnp.bfloat16),
        all_attended,
        preferred_element_type=jnp.float32,
    )
    key_grad = from_groups(key_grad_groups, row_count, column_total).astype(jnp.bfloat16)
    value_grad = from_groups(value_grad_groups, row_count, column_total).astype(jnp.bfloat16)
    joint_grad = jnp.concatenate([query_grad, key_grad, value_grad], axis=-1)
    joint_weight_grad = jnp.einsum(
        "crkd,crke->de", mixed, joint_grad, preferred_element_type=jnp.float32
    )
    mixed_grad = jnp.einsum(
        "crke,de->crkd", joint_grad, joint_weight, preferred_element_type=jnp.float32
    ).astype(jnp.bfloat16)
    mixed_padded = padded_2(mixed_grad, (("strip", 1),), 1)
    first_grad = depthwise(mixed_padded.astype(jnp.float32), mixer_single_float[:, ::-1])
    mixer_kernel_grad = kernel_grad(
        first_padded.astype(jnp.float32), mixed_grad.astype(jnp.float32)
    )
    input_part, shift_one_grad, scale_one_grad = first_pull(first_grad)
    tokens_grad = residual_grad + input_part
    token_grad = jnp.concatenate(
        [
            shift_one_grad,
            scale_one_grad,
            gate_one_grad,
            shift_two_grad,
            scale_two_grad,
            gate_two_grad,
        ],
        axis=-1,
    )
    modulation_grad = jnp.einsum("crkb,crke->cbe", token_hot, token_grad, precision=EXACT_PRECISION)
    silu_grad = jnp.einsum(
        "cbe,de->cbd",
        modulation_grad,
        adaptive_weight.astype(jnp.float32),
        precision=EXACT_PRECISION,
    )
    conditioning_grad = silu_pull(silu_grad)[0]
    table_grad = jnp.einsum(
        "soy,sok->yk",
        conditioning_grad,
        class_onehot.astype(jnp.float32),
        precision=EXACT_PRECISION,
    )
    adaptive_grad = jnp.einsum(
        "cbd,cbe->de", silu_cond.astype(jnp.float32), modulation_grad, precision=EXACT_PRECISION
    )
    adaptive_bias_grad = jnp.sum(modulation_grad, axis=(0, 1))
    (
        table_shard,
        adaptive_shard,
        adaptive_bias_shard,
        mixer_shard,
        joint_shard,
        output_shard,
        output_bias_shard,
        expand_shard,
        expand_bias_shard,
        hidden_shard,
        reduce_shard,
        reduce_bias_shard,
    ) = (
        lax.psum_scatter(
            table_grad.astype(jnp.bfloat16), "strip", scatter_dimension=0, tiled=True
        ).astype(jnp.float32),
        lax.psum_scatter(
            adaptive_grad.astype(jnp.bfloat16), "strip", scatter_dimension=0, tiled=True
        ).astype(jnp.float32),
        lax.psum_scatter(
            adaptive_bias_grad.astype(jnp.bfloat16), "strip", scatter_dimension=0, tiled=True
        ).astype(jnp.float32),
        lax.psum_scatter(
            mixer_kernel_grad.astype(jnp.bfloat16), "strip", scatter_dimension=0, tiled=True
        ).astype(jnp.float32),
        lax.psum_scatter(
            joint_weight_grad.astype(jnp.bfloat16), "strip", scatter_dimension=0, tiled=True
        ).astype(jnp.float32),
        lax.psum_scatter(
            output_weight_grad.astype(jnp.bfloat16), "strip", scatter_dimension=0, tiled=True
        ).astype(jnp.float32),
        lax.psum_scatter(
            output_bias_grad.astype(jnp.bfloat16), "strip", scatter_dimension=0, tiled=True
        ).astype(jnp.float32),
        lax.psum_scatter(
            expand_weight_grad.astype(jnp.bfloat16), "strip", scatter_dimension=0, tiled=True
        ).astype(jnp.float32),
        lax.psum_scatter(
            expand_bias_grad.astype(jnp.bfloat16), "strip", scatter_dimension=0, tiled=True
        ).astype(jnp.float32),
        lax.psum_scatter(
            hidden_kernel_grad.astype(jnp.bfloat16), "strip", scatter_dimension=0, tiled=True
        ).astype(jnp.float32),
        lax.psum_scatter(
            reduce_weight_grad.astype(jnp.bfloat16), "strip", scatter_dimension=0, tiled=True
        ).astype(jnp.float32),
        lax.psum_scatter(
            reduce_bias_grad.astype(jnp.bfloat16), "strip", scatter_dimension=0, tiled=True
        ).astype(jnp.float32),
    )
    summed = (
        lax.psum(table_shard.astype(jnp.bfloat16), "batch").astype(jnp.float32),
        lax.psum(adaptive_shard.astype(jnp.bfloat16), "batch").astype(jnp.float32),
        lax.psum(adaptive_bias_shard.astype(jnp.bfloat16), "batch").astype(jnp.float32),
        lax.psum(mixer_shard.astype(jnp.bfloat16), "batch").astype(jnp.float32),
        lax.psum(joint_shard.astype(jnp.bfloat16), "batch").astype(jnp.float32),
        lax.psum(output_shard.astype(jnp.bfloat16), "batch").astype(jnp.float32),
        lax.psum(output_bias_shard.astype(jnp.bfloat16), "batch").astype(jnp.float32),
        lax.psum(expand_shard.astype(jnp.bfloat16), "batch").astype(jnp.float32),
        lax.psum(expand_bias_shard.astype(jnp.bfloat16), "batch").astype(jnp.float32),
        lax.psum(hidden_shard.astype(jnp.bfloat16), "batch").astype(jnp.float32),
        lax.psum(reduce_shard.astype(jnp.bfloat16), "batch").astype(jnp.float32),
        lax.psum(reduce_bias_shard.astype(jnp.bfloat16), "batch").astype(jnp.float32),
    )
    return (
        outputs,
        tokens_grad,
        summed[0],
        summed[1],
        summed[2],
        summed[3],
        summed[4],
        summed[5],
        summed[6],
        summed[7],
        summed[8],
        summed[9],
        summed[10],
        summed[11],
    )


def solution(mesh):
    grouped = (mesh.shape["batch"], mesh.shape["strip"]) == (4, 8)
    return jax.shard_map(
        local_grouped if grouped else local,
        mesh=mesh,
        in_specs=(
            P("batch", "strip", None, None),
            P("batch", None, None),
            P("batch", None),
            P("batch", None),
            P(),
            P(),
            P(),
            P(),
            P(),
            P(),
            P(),
            P(),
            P(),
            P(),
            P(),
            P(),
            P("batch", "strip", None, None),
        ),
        out_specs=(
            P("batch", "strip", None, None),
            P("batch", "strip", None, None),
            P("strip", None),
            P("strip", None),
            P("strip"),
            P("strip", None),
            P("strip", None),
            P("strip", None),
            P("strip"),
            P("strip", None),
            P("strip"),
            P("strip", None),
            P("strip", None),
            P("strip"),
        ),
        check_vma=False,
    )
```

```python
import math
from types import SimpleNamespace

import jax
import jax.numpy as jnp
from jax import lax
from jax.experimental import pallas as pl
from jax.experimental.pallas import tpu as pltpu
from jax.sharding import PartitionSpec as P

HEADS = 12
EPSILON = 1e-06
MASKED = -1e30
MESH = pl.DeviceIdType.MESH
F32 = jnp.float32
BF16 = jnp.bfloat16
VMEM_BYTES = 62 * 1024 * 1024
WHOLE = pl.BlockSpec(memory_space=pltpu.VMEM)
LEFT = pl.BlockSpec(memory_space=pl.ANY)
SCALARS = pl.BlockSpec(memory_space=pltpu.SMEM)
NT = (((1,), (1,)), ((), ()))
TN = (((0,), (0,)), ((), ()))


def dot(a, b):
    return jnp.dot(a, b, preferred_element_type=F32)


def dot_nt(a, b):
    return lax.dot_general(a, b, NT, preferred_element_type=F32)


def dot_tn(a, b):
    return lax.dot_general(a, b, TN, preferred_element_type=F32)


def send_to(src, dst, sems, index, batch, strip):
    return pltpu.make_async_remote_copy(
        src_ref=src,
        dst_ref=dst,
        send_sem=sems[0].at[index],
        recv_sem=sems[1].at[index],
        device_id=(batch, strip),
        device_id_type=MESH,
    )


def entry_signals(strips):
    s = lax.axis_index("strip")
    b = lax.axis_index("batch")
    z = s // 2
    barrier = pltpu.get_barrier_semaphore()
    count = 0
    for d in range(1, strips):
        pl.semaphore_signal(
            barrier, inc=1, device_id=(b, lax.rem(s + d, strips)), device_id_type=MESH
        )
        count += 1
    for e in range(1, 4):
        for core in range(2):
            pl.semaphore_signal(
                barrier, inc=1, device_id=(lax.rem(b + e, 4), 2 * z + core), device_id_type=MESH
            )
            count += 1
    return count


def entry_wait(count):
    pl.semaphore_wait(pltpu.get_barrier_semaphore(), count)


def spread(mod, width):
    return jnp.concatenate(
        [jnp.broadcast_to(mod[0:1], (8, width)), jnp.broadcast_to(mod[1:2], (8, width))], axis=0
    )


def spread_columns(buffer, r, x):
    for k in range(x.shape[-1] // 128):
        buffer[r, k] = x[:, k * 128 : k * 128 + 128]


def every_second(buffer, r, p):
    return jnp.concatenate(
        [buffer[r, k, pl.ds(p, 16, stride=2), :] for k in range(buffer.shape[1])], axis=-1
    )


def interleave(buffer, r, p, x):
    for k in range(x.shape[-1] // 128):
        buffer[r, k, pl.ds(p, 16, stride=2), :] = x[:, k * 128 : k * 128 + 128]


def joined(buffer, r):
    return jnp.concatenate([buffer[r, k] for k in range(buffer.shape[1])], axis=-1)


def ln_parts(x):
    centre = jnp.mean(x, axis=-1, keepdims=True)
    centred = x - centre
    var = jnp.mean(centred * centred, axis=-1, keepdims=True)
    inv = lax.rsqrt(var + EPSILON)
    return centred * inv, inv


def ln_back(grad, n, inv):
    mean0 = jnp.mean(grad, axis=-1, keepdims=True)
    mean1 = jnp.mean(grad * n, axis=-1, keepdims=True)
    return inv * (grad - mean0 - n * mean1)


def window(load, r):
    even = load(r, 0).astype(F32)
    odd = load(r, 1).astype(F32)
    n = even.shape[0]
    j = lax.broadcasted_iota(jnp.int32, even.shape, 0)
    odd_m = jnp.where(j == 0, 0.0, pltpu.roll(odd, 1, 0))
    even_p = jnp.where(j == n - 1, 0.0, pltpu.roll(even, n - 1, 0))
    return odd_m, even, odd, even_p


def conv(rows, weights, flip):
    out = []
    for p in range(2):
        total = None
        for i in range(3):
            for j in range(3):
                t = 3 * i + j
                a = weights[8 - t if flip else t] * rows[i][p + j]
                total = a if total is None else total + a
        out.append(total)
    return out


def taps(rows, centre, sums):
    new = list(sums)
    for i in range(3):
        for j in range(3):
            a = rows[i][j] * centre[0] + rows[i][1 + j] * centre[1]
            t = 8 - (3 * i + j)
            new[t] = sums[t] + (a[0:8] + a[8:16])
    return new


def halves(x):
    return jnp.concatenate(
        [jnp.sum(x[0:8], axis=0, keepdims=True), jnp.sum(x[8:16], axis=0, keepdims=True)], axis=0
    )


def gelu_both(x):
    k0 = math.sqrt(2.0 / math.pi)
    square = x * x
    t = jnp.tanh(k0 * x * (1.0 + 0.044715 * square))
    cdf = 0.5 + 0.5 * t
    slope = cdf + (0.5 * k0) * x * (1.0 - t * t) * (1.0 + (3.0 * 0.044715) * square)
    return x * cdf, slope


def block_kernel(names, *refs):
    m = SimpleNamespace(**dict(zip(names, refs)))
    rows, cols, width = m.tok.shape
    half = width // 2
    strips = lax.axis_size("strip")
    chips = strips // 2
    chip_rows = 2 * rows
    total = strips * 64
    own = width // strips
    s = lax.axis_index("strip")
    b = lax.axis_index("batch")
    z = s // 2
    c = lax.rem(s, 2)
    sibling = 2 * z + 1 - c
    y, x = b // 2, lax.rem(b, 2)
    x_mate = 2 * y + 1 - x
    y_mate = 2 * (1 - y) + x
    sent = []

    def chip(d):
        return lax.rem(z + d, chips)

    def start(copy):
        copy.start()
        sent.append(copy)

    loads = {}

    def load(name, src, dst, index):
        loads[name] = pltpu.make_async_copy(src, dst, m.load_sem.at[index])
        loads[name].start()

    load("emb", m.emb_hbm, m.emb, 22)
    for i in range(12):
        lanes = pl.ds(i * half, half)
        src = m.aw4_hbm.at[:, :, :, lanes] if i < 4 else m.aw5_hbm.at[:, :, :, :, lanes]
        load(f"aw{i}", src, (m.rw, m.ew, m.jo)[i // 4].at[i % 4], 23 + i)
    greet = entry_signals(strips)
    for part in range(3):
        off = pl.multiple_of(part * width + c * half, 128)
        load(f"wj{part}", m.wj_hbm.at[:, pl.ds(off, half)], m.wj.at[part], part)
    load("cot", m.cot_hbm, m.cot, 3)
    load("wo", m.wo_hbm, m.wo, 4)
    for n in range(chips):
        off = pl.multiple_of((2 * n + c) * half, 128)
        spot = pl.ds(n * half, half)
        load(f"we{n}", m.we_hbm.at[:, pl.ds(off, half)], m.we.at[:, spot], 5 + n)
        load(f"wr{n}", m.wr_hbm.at[pl.ds(off, half)], m.wr.at[spot], 5 + chips + n)

    latents = m.steps.shape[1]
    classes = m.emb.shape[0]
    row = lax.broadcasted_iota(jnp.int32, (latents, 1), 0)
    when = jnp.zeros((latents, 1), F32)
    label = jnp.zeros((latents, 1), jnp.int32)
    for i in range(latents):
        when = jnp.where(row == i, m.steps[0, i].astype(F32), when)
        label = jnp.where(row == i, m.labels[0, i], label)
    order = lax.broadcasted_iota(jnp.int32, (latents, half), 1).astype(F32)
    angles = when * jnp.exp(-math.log(10000.0) * order / half)
    features = jnp.concatenate([jnp.cos(angles), jnp.sin(angles)], axis=1)
    onehot = lax.broadcasted_iota(jnp.int32, (latents, classes), 1) == label
    onehot = jnp.where(onehot, 1.0, 0.0).astype(BF16)

    lane = lax.broadcasted_iota(jnp.int32, (latents, 128), 1)
    kind = lax.broadcasted_iota(jnp.int32, (latents, 128), 0)
    line = lax.rem(lane, 16)
    side = jnp.where(kind == 0, lax.rem(line // 2, 2), lax.rem(line // 3, 2))
    tile = lax.rem(lane // 16, 4)
    slots = jnp.zeros((latents, 128), jnp.int32)
    for i in range(4):
        for h in range(2):
            hit = jnp.logical_and(tile == i, side == h)
            slots = jnp.where(hit, m.owner[0, h, i] + b * latents, slots)
    loads["emb"].wait()
    condition = features + dot(onehot, m.emb[...])
    silu = (condition / (1.0 + jnp.exp(-condition))).astype(BF16)
    m.cond_all[b] = jnp.concatenate(
        [condition, jnp.broadcast_to(label.astype(F32), (latents, 128)), slots.astype(F32)], axis=1
    )
    bias = m.ab[...].astype(F32).reshape(1, 6 * width)
    for g, held in enumerate((m.rw, m.ew, m.jo)):
        for i in range(4):
            loads[f"aw{4 * g + i}"].wait()
        weights = jnp.concatenate([held[i].reshape(width, half) for i in range(4)], axis=1)
        lanes = slice(g * 2 * width, (g + 1) * 2 * width)
        table = dot(silu, weights) + bias[:, lanes]
        for h in range(2):
            mine = row == m.owner[0, h, z]
            m.mod[h : h + 1, lanes] = jnp.sum(jnp.where(mine, table, 0.0), axis=0, keepdims=True)
    entry_wait(greet)

    m.mk[...] = m.mixer[...].astype(F32)
    ob = m.ob[...].astype(F32).reshape(1, width)
    rb = m.rb[...].astype(F32).reshape(1, width)
    m.ebf[...] = m.eb[...].astype(F32).reshape(m.ebf.shape)
    for n in range(chips):
        m.hk[n] = m.hidden[:, pl.ds(pl.multiple_of((2 * n + c) * half, 128), half)].astype(F32)

    for e in range(1, 4):
        start(
            send_to(m.cond_all.at[b], m.cond_all.at[b], m.cond_sem, e, lax.rem(b + e, 4), s)
        )

    def block_mod(n):
        return spread(m.mod[:, n * width : (n + 1) * width], width)

    scale1 = 1.0 + block_mod(1)
    shift1 = block_mod(0)

    def first_row(r):
        spread_columns(m.rowf, r, m.tok[r].astype(F32))
        for p in range(2):
            v = every_second(m.rowf, r, p)
            m.xd[r, p] = v.astype(BF16)
            n, _ = ln_parts(v)
            m.fp[r + 1, p] = (n * scale1 + shift1).astype(BF16)

    def edge_sends(buffer, sems):
        up = send_to(buffer.at[1], buffer.at[rows + 1], sems, 0, b, s - 1)
        down = send_to(buffer.at[rows], buffer.at[0], sems, 1, b, s + 1)
        return up, down

    def start_edges(buffer, sems):
        up, down = edge_sends(buffer, sems)

        @pl.when(s > 0)
        def _():
            up.start()

        @pl.when(s < strips - 1)
        def _():
            down.start()

    def edges_sent(buffer, sems):
        up, down = edge_sends(buffer, sems)

        @pl.when(s > 0)
        def _():
            up.wait_send()

        @pl.when(s < strips - 1)
        def _():
            down.wait_send()

    def top_edge(buffer, sems):
        @pl.when(s > 0)
        def _():
            send_to(buffer.at[1], buffer.at[0], sems, 1, b, s - 1).wait_recv()

        @pl.when(s == 0)
        def _():
            buffer[0] = jnp.zeros_like(buffer[0])

    def bottom_edge(buffer, sems):
        @pl.when(s < strips - 1)
        def _():
            send_to(buffer.at[1], buffer.at[rows + 1], sems, 0, b, s + 1).wait_recv()

        @pl.when(s == strips - 1)
        def _():
            buffer[rows + 1] = jnp.zeros_like(buffer[0])

    first_row(0)
    first_row(rows - 1)
    start_edges(m.fp, m.fp_sem)

    def body(r, _):
        first_row(r)
        return 0

    lax.fori_loop(1, rows - 1, body, 0, unroll=3)

    def mixed_rows(low, high):
        for k in range(width // 128):
            lanes = pl.ds(k * 128, 128)
            weights = [m.mk[t : t + 1, k * 128 : k * 128 + 128] for t in range(9)]

            def line(r, p):
                return m.fp[r, p, :, lanes]

            def step(r, carry):
                new = window(line, r + 2)
                out = conv((carry[0], carry[1], new), weights, False)
                for p in range(2):
                    m.ms[lax.rem(r, 2) * 2 + p, r // 2, :, lanes] = out[p].astype(BF16)
                return carry[1], new

            lax.fori_loop(
                low, high, step, (window(line, low), window(line, low + 1)), unroll=True
            )

    mixed_rows(1, rows - 1)
    top_edge(m.fp, m.fp_sem)
    mixed_rows(0, 1)
    bottom_edge(m.fp, m.fp_sem)
    mixed_rows(rows - 1, rows)

    def to_groups(source, target, sems, sems2):
        for d in range(1, chips):
            g = chip(d)
            start(send_to(source.at[g], target.at[s], sems, d, b, 2 * g + c))
        target[s] = source[z]

    def pass_on(target, sems, sems2, d):
        i = 2 * chip(chips - d) + c
        if d:
            send_to(target.at[i], target.at[i], sems, d, b, i).wait_recv()
        start(send_to(target.at[i], target.at[i], sems2, d, b, sibling))

    def groups_ready(target, sems2):
        for d in range(chips):
            i = 2 * chip(chips - d) + 1 - c
            send_to(target.at[i], target.at[i], sems2, d, b, sibling).wait_recv()

    to_groups(m.ms, m.mg, m.mg_sem, m.mg_sem2)

    m.acc[...] = jnp.zeros_like(m.acc)
    gate2 = block_mod(5)
    loads["cot"].wait()

    def upstream_row(r, _):
        spread_columns(m.rowf, r, m.cot[r].astype(F32))
        for p in range(2):
            up = every_second(m.rowf, r, p)
            m.ctd[2 * r + p] = up.astype(BF16)
            two = (up * gate2).astype(BF16)
            m.tg[c, 2 * r + p] = two
            m.acc[0] += two.astype(F32)
        return 0

    lax.fori_loop(0, rows, upstream_row, 0)
    start(send_to(m.tg.at[c], m.tg.at[c], m.pair_sem, 0, b, sibling))

    for d in range(chips):
        pass_on(m.mg, m.mg_sem, m.mg_sem2, d)
    groups_ready(m.mg, m.mg_sem2)
    for part in range(3):
        loads[f"wj{part}"].wait()

    v = m.mg[...].reshape(total, width)
    for part in range(3):
        w = dot(v, m.wj[part]).astype(BF16)
        for n in range(3):
            m.qkv[3 * part + n] = w[:, n * 128 : n * 128 + 128]

    where = lax.broadcasted_iota(jnp.int32, (1, total), 1)
    lefts = lax.rem(where, 16) < 8
    key_owner = jnp.zeros((1, total), jnp.int32)
    for t in range(4):
        both = jnp.where(lefts, m.owner[0, 0, t], m.owner[0, 1, t])
        key_owner = jnp.where(where // 128 == t, both, key_owner)
    where = lax.broadcasted_iota(jnp.int32, (total, 1), 0)
    lefts = lax.rem(where, 16) < 8
    query_owner = jnp.zeros((total, 1), jnp.int32)
    for t in range(4):
        both = jnp.where(lefts, m.owner[0, 0, t], m.owner[0, 1, t])
        query_owner = jnp.where(where // 128 == t, both, query_owner)
    allowed = query_owner == key_owner
    lane = lax.broadcasted_iota(jnp.int32, (total, 128), 1) < 64
    factor = 64 ** -0.5

    def head(v, h):
        return jnp.where(lane if h == 0 else jnp.logical_not(lane), v, jnp.zeros_like(v))

    for n in range(3):
        mine = c * 3 + n
        q2 = (m.qkv[n].astype(F32) * factor).astype(BF16)
        outs = []
        for h in range(2):
            scores = jnp.where(allowed, dot_nt(head(q2, h), m.qkv[3 + n]), MASKED)
            peak = jnp.max(scores, axis=-1, keepdims=True)
            lifted = jnp.exp(scores - peak)
            inv = 1.0 / jnp.sum(lifted, axis=-1, keepdims=True)
            m.probs[n, h] = (lifted * inv).astype(BF16)
            outs.append(dot(lifted.astype(BF16), m.qkv[6 + n]) * inv)
        m.ag[mine] = jnp.where(lane, outs[0], outs[1]).astype(BF16)
        for d in range(1, strips):
            t = lax.rem(s + d, strips)
            start(
                send_to(
                    m.ag.at[mine, pl.ds(pl.multiple_of(t * 64, 64), 64)],
                    m.ai.at[mine, z],
                    m.ai_sem,
                    (n, d),
                    b,
                    t,
                )
            )
        start(send_to(m.ag.at[mine], m.ag.at[mine], m.ag_sem, n, b, sibling))
        m.ai[mine, z] = m.ag[mine, pl.ds(pl.multiple_of(s * 64, 64), 64), :]

    for n in range(chips):
        loads[f"wr{n}"].wait()
    send_to(m.tg.at[c], m.tg.at[1 - c], m.pair_sem, 0, b, sibling).wait_recv()
    chip_tg = m.tg[...].reshape(total, width)
    for h in range(2):
        m.big[h] = dot_nt(chip_tg, m.wr[h * width : h * width + width, :]).reshape(m.big.shape[1:])

    for n in range(3):
        for d in range(1, strips):
            i = lax.rem(s - d + strips, strips)
            spot = lax.rem(i, 2) * 3 + n
            send_to(
                m.ag.at[spot, pl.ds(0, 64)], m.ai.at[spot, i // 2], m.ai_sem, (n, d), b, i
            ).wait_recv()

    gate1 = block_mod(2)
    shift2 = block_mod(3)
    scale2 = 1.0 + block_mod(4)
    loads["wo"].wait()

    v = jnp.concatenate([m.ai[n].reshape(chips * 64, 128) for n in range(6)], axis=-1)
    m.b1[...] = (dot(v, m.wo[...]) + ob).reshape(m.b1.shape)

    def residual_row(i, _):
        rp = 4 * lax.rem(i, rows // 2) + i // (rows // 2)
        u = m.xd[rp // 2, lax.rem(rp, 2)].astype(F32) + gate1 * m.b1[i]
        m.res[rp] = u
        n, _ = ln_parts(u)
        m.sc[c, rp] = (n * scale2 + shift2).astype(BF16)
        return 0

    lax.fori_loop(0, 2 * rows, residual_row, 0, unroll=4)
    start(send_to(m.sc.at[c], m.sc.at[c], m.pair_sem, 1, b, sibling))

    def halo_sends(buffer, sems, n):
        at = slice(None) if n is None else pl.ds(pl.multiple_of(n * half, 128), half)
        k = 0 if n is None else n
        first, last = buffer.at[1, :, :, at], buffer.at[chip_rows, :, :, at]
        up = send_to(first, buffer.at[chip_rows + 1, :, :, at], sems, (0, k), b, s - 2)
        down = send_to(last, buffer.at[0, :, :, at], sems, (1, k), b, s + 2)
        return up, down

    def start_halo(buffer, sems, upward, downward, n=None):
        up, down = halo_sends(buffer, sems, n)

        @pl.when(jnp.logical_and(z > 0, upward))
        def _():
            up.start()

        @pl.when(jnp.logical_and(z < chips - 1, downward))
        def _():
            down.start()

    def halo_sent(buffer, sems, n=None):
        up, down = halo_sends(buffer, sems, n)

        @pl.when(z > 0)
        def _():
            up.wait_send()

        @pl.when(z < chips - 1)
        def _():
            down.wait_send()

    def take_halo(buffer, sems, n=None):
        at = slice(None) if n is None else pl.ds(n * half, half)
        k = 0 if n is None else n
        above, below = buffer.at[0, :, :, at], buffer.at[chip_rows + 1, :, :, at]

        @pl.when(z > 0)
        def _():
            send_to(above, above, sems, (1, k), b, s - 2).wait_recv()

        @pl.when(z == 0)
        def _():
            above[...] = jnp.zeros(above.shape, BF16)

        @pl.when(z < chips - 1)
        def _():
            send_to(below, below, sems, (0, k), b, s + 2).wait_recv()

        @pl.when(z == chips - 1)
        def _():
            below[...] = jnp.zeros(below.shape, BF16)

    for n in range(chips):
        loads[f"we{n}"].wait()
    hidden = chips * half
    bias = jnp.concatenate(
        [m.ebf[:, pl.ds(pl.multiple_of((2 * n + c) * half, 128), half)] for n in range(chips)],
        axis=-1,
    )

    def expand(core):
        w = dot(m.sc[core].reshape(rows * 32, width), m.we[...]) + bias
        m.ex[pl.ds(1 + core * rows, rows)] = w.astype(BF16).reshape(rows, 2, 16, hidden)

    expand(c)
    start_halo(m.ex, m.ex_sem, c == 0, c == 1)
    send_to(m.sc.at[c], m.sc.at[1 - c], m.pair_sem, 1, b, sibling).wait_recv()
    expand(1 - c)
    start_halo(m.ex, m.ex_sem, c == 1, c == 0)
    first_mate, then_mate = (x_mate, y_mate), (y_mate, x_mate)
    pair_chip = z + 1 - 2 * lax.rem(z, 2)
    far_chip = lax.rem(z + 2, 4)
    last_chip = 3 - z

    def block_order(i):
        high, low = z // 2, lax.rem(z, 2)
        flip_high, flip_low = 1 - lax.rem(i, 2), 1 - i // 2
        high = high + flip_high - 2 * high * flip_high
        low = low + flip_low - 2 * low * flip_low
        return 2 * high + low

    sub = width // 12
    upper = pl.ds(0, sub)

    def u_three(k):
        dest = pair_chip if k < 2 else far_chip
        src = m.u3.at[1] if k == 2 else m.rw.at[pair_chip if k == 0 else last_chip, :, :, upper]
        return send_to(src, m.u3.at[k], m.u3_sem, k, b, 2 * dest + c)

    def u_across():
        u_three(1).wait_recv()
        for i in range(2):
            v = m.u3[1, i].astype(F32) + m.rw[far_chip, i, :, upper].astype(F32)
            m.u3[1, i] = v.astype(BF16)
        u_three(2).start()

    def u_one(h):
        at = pl.ds(h * sub // 2, sub // 2)
        src = m.u0.at[:, 1 - x, at] if h == 0 else m.u0.at[1 - y, :, at]
        return send_to(src, m.u1.at[h], m.u1_sem, h, first_mate[h], s)

    def u_two(h):
        src = m.u1.at[h, (1 - y) if h == 0 else (1 - x)]
        return send_to(src, m.u2.at[h], m.u2_sem, h, then_mate[h], s)

    def u_begin():
        for k in (0, 2):
            u_three(k).wait_recv()
        for i in range(2):
            v = m.rw[z, i, :, upper].astype(F32) + m.u3[0, i].astype(F32)
            m.u0[i] = (v + m.u3[2, i].astype(F32)).astype(BF16)
        for h in range(2):
            u_one(h).start()

    def u_half():
        for h in range(2):
            u_one(h).wait_recv()
            at = pl.ds(h * sub // 2, sub // 2)
            kept = m.u0[:, x, at] if h == 0 else m.u0[y, :, at]
            m.u1[h] = (m.u1[h].astype(F32) + kept.astype(F32)).astype(BF16)
            u_two(h).start()

    def u_sum():
        for h in range(2):
            u_two(h).wait_recv()
            kept = m.u1[h, y if h == 0 else x].astype(F32)
            at = pl.ds(h * sub // 2, sub // 2)
            m.r_all[b, 0, at] = (m.u2[h].astype(F32) + kept).astype(BF16)
        r_four(0, 0).start()
        r_four(0, 1).start()

    def r_source(n, h, mine):
        at = pl.ds(sub + h * sub, sub)
        if h == 0:
            return m.rw.at[n, :, x if mine else 1 - x, at]
        return m.rw.at[n, y if mine else 1 - y, :, at]

    def r_one(n, h):
        return send_to(r_source(n, h, False), m.r1.at[n, h], m.r1_sem, (n, h), first_mate[h], s)

    def r_two(n, h):
        src = m.r1.at[n, h, (1 - y) if h == 0 else (1 - x)]
        return send_to(src, m.r2.at[n, h], m.r2_sem, (n, h), then_mate[h], s)

    def r_three(k):
        dest = pair_chip if k < 2 else far_chip
        t = (pair_chip, last_chip, far_chip)[k]
        return send_to(m.r2.at[t], m.r3.at[k], m.r3_sem, k, b, 2 * dest + c)

    def r_four(g, e):
        spot = m.r_all.at[b, g]
        return send_to(spot, spot, m.r4_sem, (g, e), (x_mate, y_mate)[e], s)

    def r_relay(g, wait):
        source, dest = (x_mate, y_mate) if g < 2 else (y_mate, x_mate)
        spot = m.r_all.at[source, g]
        copy = send_to(spot, spot, m.r4_sem, (g, 2), dest, s)
        if wait:
            copy.wait_send()
            return
        send_to(spot, spot, m.r4_sem, (g, 0 if g < 2 else 1), source, s).wait_recv()
        copy.start()

    def r_arrive(g):
        source, e = (y_mate, 1) if g < 2 else (x_mate, 0)
        spot = m.r_all.at[source, g]
        send_to(spot, spot, m.r4_sem, (g, e), source, s).wait_recv()
        spot = m.r_all.at[3 - b, g]
        send_to(spot, spot, m.r4_sem, (g, 2), source, s).wait_recv()

    def r_half(n):
        for h in range(2):
            r_one(n, h).wait_recv()
            kept = r_source(n, h, True)[...].astype(F32)
            m.r1[n, h] = (m.r1[n, h].astype(F32) + kept).astype(BF16)
            r_two(n, h).start()

    def r_quarter(n):
        for h in range(2):
            r_two(n, h).wait_recv()
            kept = m.r1[n, h, y if h == 0 else x].astype(F32)
            m.r2[n, h] = (m.r2[n, h].astype(F32) + kept).astype(BF16)

    def r_spread():
        r_three(1).start()
        r_three(0).start()

    def r_across():
        r_three(1).wait_recv()
        m.r2[far_chip] = (m.r2[far_chip].astype(F32) + m.r3[1].astype(F32)).astype(BF16)
        r_three(2).start()

    def r_sum():
        v = m.r2[z].astype(F32)
        for k in (0, 2):
            r_three(k).wait_recv()
            v = v + m.r3[k].astype(F32)
        m.r_all[b, pl.ds(1, 2)] = v.astype(BF16)
        for g in (1, 2):
            r_four(g, 0).start()
            r_four(g, 1).start()

    def c_source(j, h, mine):
        block = m.ew.at[j] if not isinstance(j, int) or j < 4 else m.jo.at[j - 4]
        at = pl.ds(2 * h, 2)
        if h == 0:
            return block.at[at, :, x if mine else 1 - x]
        return block.at[at, y if mine else 1 - y]

    def c_one(j, h):
        return send_to(c_source(j, h, False), m.c1.at[j, h], m.c1_sem, (j, h), first_mate[h], s)

    def c_two(j, h):
        src = m.c1.at[j, h, :, 1 - y] if h == 0 else m.c1.at[j, h, :, 1 - x]
        return send_to(src, m.c2.at[j, pl.ds(2 * h, 2)], m.c2_sem, (j, h), then_mate[h], s)

    def c_three(j, k):
        dest = pair_chip if k < 2 else far_chip
        t = (pair_chip, last_chip, far_chip)[k]
        return send_to(m.c2.at[j, t], m.c3.at[j, k], m.c3_sem, (j, k), b, 2 * dest + c)

    def c_copy(j, src, xs, cs, kind, batch, strip):
        return pltpu.make_async_remote_copy(
            src_ref=src,
            dst_ref=m.c_all.at[j, xs, cs],
            send_sem=m.c4_sem[0].at[j, kind],
            recv_sem=m.c4_sem[1].at[j, kind, cs],
            device_id=(batch, strip),
            device_id_type=MESH,
        )

    def c_four(j, kind):
        return c_copy(j, m.c_out.at[j], x, c, kind, (b, x_mate, y_mate)[kind], 2 * z + y)

    def c_got(j, kind, cs):
        xs = 1 - x if kind == 1 else x
        c_copy(j, m.c_out.at[j], xs, cs, kind, b, s).wait_recv()

    def c_passing(j, along_y):
        xs, dest = (1 - x, y_mate) if along_y else (x, x_mate)
        return pltpu.make_async_remote_copy(
            src_ref=m.c_all.at[j, xs],
            dst_ref=m.c_all.at[j, xs],
            send_sem=m.c4_sem[0].at[j, 3],
            recv_sem=m.c4_sem[1].at[j, 3, 0],
            device_id=(dest, s),
            device_id_type=MESH,
        )

    def c_relay(j, along_y):
        @pl.when((c == y) if along_y else (c != y))
        def _():
            for cs in range(2):
                c_got(j, 1 if along_y else 2, cs)
            c_passing(j, along_y).start()

    def c_arrive(j, along_y):
        @pl.when(c == y)
        def _():
            c_copy(j, m.c_out.at[j], x, 1 - c, 0, b, sibling).wait_recv()
            if not along_y:
                for cs in range(2):
                    c_got(j, 1, cs)

        @pl.when(c != y)
        def _():
            if along_y:
                for cs in range(2):
                    c_got(j, 2, cs)
            spot = m.c_all.at[j, 1 - x]
            pltpu.make_async_remote_copy(
                src_ref=spot,
                dst_ref=spot,
                send_sem=m.c4_sem[0].at[j, 3],
                recv_sem=m.c4_sem[1].at[j, 3, 0],
                device_id=(b, s),
                device_id_type=MESH,
            ).wait_recv()

    def c_gone(j, along_y):
        c_four(j, 1).wait_send()
        c_four(j, 2).wait_send()

        @pl.when(c != y)
        def _():
            c_four(j, 0).wait_send()

        @pl.when((c == y) if along_y else (c != y))
        def _():
            c_passing(j, along_y).wait_send()

    def c_begin(j):
        for h in range(2):
            c_one(j, h).start()

    def c_half(j):
        for h in range(2):
            c_one(j, h).wait_recv()
            kept = c_source(j, h, True)[...].astype(F32)
            m.c1[j, h] = (m.c1[j, h].astype(F32) + kept).astype(BF16)
            c_two(j, h).start()

    def c_quarter(j):
        for h in range(2):
            c_two(j, h).wait_recv()
            at = pl.ds(2 * h, 2)
            kept = (m.c1[j, h, :, y] if h == 0 else m.c1[j, h, :, x]).astype(F32)
            m.c2[j, at] = (m.c2[j, at].astype(F32) + kept).astype(BF16)

    def c_spread(j):
        c_three(j, 1).start()
        c_three(j, 0).start()

    def c_across(j):
        c_three(j, 1).wait_recv()
        far = m.c2[j, far_chip].astype(F32) + m.c3[j, 1].astype(F32)
        m.c2[j, far_chip] = far.astype(BF16)
        c_three(j, 2).start()

    def c_sum(j):
        v = m.c2[j, z].astype(F32)
        for k in (0, 2):
            c_three(j, k).wait_recv()
            v = v + m.c3[j, k].astype(F32)
        m.c_out[j] = v.astype(BF16)

        @pl.when(c == y)
        def _():
            m.c_all[j, x, c] = m.c_out[j]

        c_four(j, 1).start()
        c_four(j, 2).start()

        @pl.when(c != y)
        def _():
            c_four(j, 0).start()

    def activate(i, early):
        n = block_order(i)
        for k in range(3):
            lanes = pl.ds(pl.multiple_of(n * half + k * 128, 128), 128)
            inner = pl.ds(k * 128, 128)
            weights = [m.hk[n, t : t + 1, inner] for t in range(9)]
            spot = pl.ds(pl.multiple_of(lax.rem(n, 2) * half + k * 128, 128), 128)

            def line(r, p):
                return m.ex[r, p, :, lanes]

            def rows_of(low, high):
                above, here = window(line, low), window(line, low + 1)
                for r in range(low, high):
                    below = window(line, r + 2)
                    out = conv((above, here, below), weights, False)
                    for p in range(2):
                        value, slope = gelu_both(out[p])
                        rp = 2 * r + p
                        grad = m.big[n // 2, rp // 16, rp % 16, :, spot]
                        m.act[rp, :, lanes] = value.astype(BF16)
                        m.cg[r + 1, p, :, lanes] = (grad * slope).astype(BF16)
                    above, here = here, below

            if early is None:
                rows_of(0, chip_rows)
            elif early:
                rows_of(1, chip_rows - 1)
            else:
                rows_of(0, 1)
                rows_of(chip_rows - 1, chip_rows)

    def activated(i):
        n = block_order(i)
        at = pl.ds(pl.multiple_of(n * half, 128), half)
        start_halo(m.cg, m.cg_sem, True, True, n)
        full = m.act[:, :, at].reshape(total, half)
        m.rw[n] = dot_tn(chip_tg, full).astype(BF16).reshape(m.rw.shape[1:])
        for h in range(2):
            r_one(n, h).start()

    activate(0, True)
    take_halo(m.ex, m.ex_sem)
    activate(0, False)
    activated(0)
    u_three(1).start()

    def next_block(i, _):
        activate(i, None)
        activated(i)
        return 0

    lax.fori_loop(1, chips, next_block, 0)
    u_three(0).start()
    full = m.act[...].reshape(total, hidden)
    m.big[0] = dot(full, m.wr[...]).reshape(m.big.shape[1:])
    b2_copy = send_to(m.big.at[0, 1 - c], m.b2_in, m.pair_sem, 2, b, sibling)
    b2_copy.start()
    m.hkg[...] = jnp.zeros_like(m.hkg)
    for n in range(chips):
        take_halo(m.cg, m.cg_sem, n)
    u_across()
    chip_sc = m.sc[...].reshape(total, width)

    def backward(n, _):
        for k in range(3):
            lanes = pl.ds(pl.multiple_of(n * half + k * 128, 128), 128)
            inner = pl.ds(k * 128, 128)
            weights = [m.hk[n, t : t + 1, inner] for t in range(9)]

            def line(r, p):
                return m.cg[r, p, :, lanes]

            above, here = window(line, 0), window(line, 1)
            sums = [jnp.zeros((8, 128), F32) for _ in range(9)]
            total_eg = jnp.zeros((8, 128), F32)
            for r in range(chip_rows):
                below = window(line, r + 2)
                three = (above, here, below)
                low = [v.astype(BF16) for v in conv(three, weights, True)]
                for p in range(2):
                    m.act[2 * r + p, :, lanes] = low[p]
                centre = [m.ex[r + 1, p, :, lanes].astype(F32) for p in range(2)]
                sums = taps(three, centre, sums)
                both = low[0].astype(F32) + low[1].astype(F32)
                total_eg = total_eg + (both[0:8] + both[8:16])
                above, here = here, below
            for t, v in enumerate(sums + [total_eg]):
                m.hkg[n, t : t + 1, inner] = jnp.sum(v, axis=0, keepdims=True)
        full = m.act[:, :, pl.ds(pl.multiple_of(n * half, 128), half)].reshape(total, half)
        m.ew[n] = dot_tn(chip_sc, full).astype(BF16).reshape(m.ew.shape[1:])
        c_begin(n)
        r_half(block_order(n))
        return 0

    lax.fori_loop(0, chips, backward, 0)
    for core in (1 - c, c):
        v = m.act[pl.ds(core * 2 * rows, 2 * rows)].reshape(rows * 32, hidden)
        m.big[1, core] = dot_nt(v, m.we[...]).reshape(m.big.shape[2:])
        if core is not c:
            sg_copy = send_to(m.big.at[1, 1 - c], m.sg_in, m.pair_sem, 3, b, sibling)
            sg_copy.start()
    send_to(m.big.at[0, c], m.b2_in, m.pair_sem, 2, b, sibling).wait_recv()
    send_to(m.big.at[1, c], m.sg_in, m.pair_sem, 3, b, sibling).wait_recv()

    def finish(r, _):
        for p in range(2):
            rp = 2 * r + p
            grad = m.big[1, c, rp] + m.sg_in[rp]
            v = m.res[rp]
            n, inv = ln_parts(v)
            branch = m.b1[(rows // 2) * lax.rem(rp, 4) + rp // 4]
            up = m.ctd[rp].astype(F32)
            m.acc[1] += grad
            m.acc[2] += grad * n
            back = up + ln_back(grad * scale2, n, inv)
            m.rg[rp] = back
            m.acc[3] += back * branch
            one = (back * gate1).astype(BF16)
            m.og[lax.rem(rp, 4), rp // 4] = one
            m.acc[4] += one.astype(F32)
            branch2 = m.big[0, c, rp] + m.b2_in[rp] + rb
            m.acc[5] += up * branch2
            interleave(m.rowf, r, p, v + gate2 * branch2)
        m.out[r] = joined(m.rowf, r).astype(BF16)
        return 0

    lax.fori_loop(0, rows, finish, 0, unroll=2)
    out_copy = pltpu.make_async_copy(m.out, m.out_hbm, m.load_sem.at[13])
    out_copy.start()

    to_groups(m.og, m.gg, m.gg_sem, m.gg_sem2)

    pack = []
    for v in (m.acc[3], m.acc[1], m.acc[2], m.acc[5]):
        pair = halves(v)
        for h in range(2):
            pack += [pair[h : h + 1, 0:half], pair[h : h + 1, half:]]
    def own_sums(buffer, sems, value):
        buffer[b, c, z] = value.astype(BF16)
        for d in range(1, chips):
            start(send_to(buffer.at[b, c, z], buffer.at[b, c, z], sems, d, b, 2 * chip(d) + c))

    def to_canvases(buffer, sems, sems2):
        for d in range(1, chips):
            i = chip(chips - d)
            send_to(buffer.at[b, c, i], buffer.at[b, c, i], sems, d, b, 2 * i + c).wait_recv()
        for e in range(1, 4):
            start(send_to(buffer.at[b, c], buffer.at[b, c], sems2, e, lax.rem(b + e, 4), s))

    def to_sibling(buffer, sems2, sems3):
        for e in range(1, 4):
            i = lax.rem(b - e + 4, 4)
            send_to(buffer.at[i, c], buffer.at[i, c], sems2, e, i, s).wait_recv()
        start(send_to(buffer.at[:, c], buffer.at[:, c], sems3, 0, b, sibling))

    def from_sibling(buffer, sems3):
        send_to(buffer.at[:, c], buffer.at[:, 1 - c], sems3, 0, b, sibling).wait_recv()

    own_sums(m.late, m.late_sem, jnp.concatenate(pack, axis=0))
    sums_ob = jnp.sum(m.acc[4], axis=0, keepdims=True)
    sums_rb = jnp.sum(m.acc[0], axis=0, keepdims=True)
    pad_lanes = jnp.zeros((1, half - own), F32)
    pad_rows = jnp.zeros((4, half), F32)
    for t in range(strips):
        piece = jnp.concatenate(
            [
                jnp.where(c == t % 2, m.hkg[t // 2, 0:10], 0.0),
                jnp.concatenate([sums_ob[:, t * own : t * own + own], pad_lanes], axis=1),
                jnp.concatenate([sums_rb[:, t * own : t * own + own], pad_lanes], axis=1),
                pad_rows,
            ],
            axis=0,
        )
        m.piece[t] = piece.astype(BF16)
    for d in range(1, strips):
        t = lax.rem(s + d, strips)
        start(send_to(m.piece.at[t], m.piece_in.at[d], m.piece_sem, d, b, t))

    pass_on(m.gg, m.gg_sem, m.gg_sem2, 0)
    c_half(0)
    u_begin()
    c_half(1)
    pass_on(m.gg, m.gg_sem, m.gg_sem2, 1)
    c_half(2)
    pass_on(m.gg, m.gg_sem, m.gg_sem2, 2)
    pass_on(m.gg, m.gg_sem, m.gg_sem2, 3)
    u_half()
    c_half(3)
    for n in range(chips):
        r_quarter(n)
    r_spread()
    groups_ready(m.gg, m.gg_sem2)
    wo_own = m.wo[pl.ds(pl.multiple_of(c * half, 128), half), :]
    w = dot_nt(m.gg[...].reshape(total, width), wo_own).astype(BF16)
    for n in range(3):
        m.da[n] = w[:, n * 128 : n * 128 + 128]

    for n in range(3):
        other = (1 - c) * 3 + n
        send_to(m.ag.at[other], m.ag.at[other], m.ag_sem, n, b, sibling).wait_recv()
    columns = m.gg[:, :, :, pl.ds(pl.multiple_of(c * half, 128), half)].reshape(total, half)
    full = jnp.concatenate([m.ag[n] for n in range(6)], axis=-1)
    m.jo[3] = dot_tn(full, columns).astype(BF16).reshape(m.jo.shape[1:])
    c_begin(7)
    for j in range(3):
        c_quarter(j)
        c_spread(j)

    tops = lax.broadcasted_iota(jnp.int32, (128, total), 0) < 64
    group = m.mg[...].reshape(total, width)
    for n in range(3):
        d2 = m.da[n]
        outs = []
        for h in range(2):
            dp = dot_nt(head(d2, h), m.qkv[6 + n])
            probs = m.probs[n, h].astype(F32)
            inner = jnp.sum(probs * dp, axis=-1, keepdims=True)
            m.ds[h] = (probs * (dp - inner)).astype(BF16)
            outs.append(dot(m.ds[h], m.qkv[3 + n]))
        dq = (jnp.where(lane, outs[0], outs[1]) * factor).astype(BF16)
        dk = [dot_tn(m.qkv[n], m.ds[h]) for h in range(2)]
        dk = (jnp.where(tops, dk[0], dk[1]) * factor).T.astype(BF16)
        dv = [dot_tn(d2, m.probs[n, h]) for h in range(2)]
        dv = jnp.where(tops, dv[0], dv[1]).T.astype(BF16)
        m.dqkv[n] = dq
        m.dqkv[3 + n] = dk
        m.dqkv[6 + n] = dv
        w = dot_tn(group, jnp.concatenate([dq, dk, dv], axis=-1))
        m.jo[n] = w.astype(BF16).reshape(m.jo.shape[1:])
        c_begin(4 + n)

    r_across()
    c_quarter(3)
    c_spread(3)

    b2_copy.wait_send()
    sg_copy.wait_send()

    def partial(core):
        strip_rows = [
            jnp.concatenate(
                [
                    m.dqkv[k, pl.ds(pl.multiple_of((2 * i + core) * 64, 64), 64), :]
                    for i in range(chips)
                ],
                axis=0,
            )
            for k in range(9)
        ]
        w = None
        for part in range(3):
            v = jnp.concatenate(strip_rows[3 * part : 3 * part + 3], axis=-1)
            v = dot_nt(v, m.wj[part])
            w = v if w is None else w + v
        m.big[0, core] = w.reshape(m.big.shape[2:])

    partial(1 - c)
    start(send_to(m.big.at[0, 1 - c], m.mp_in, m.pair_sem, 4, b, sibling))
    partial(c)
    send_to(m.big.at[0, c], m.mp_in, m.pair_sem, 4, b, sibling).wait_recv()
    four = rows // 2
    for d in range(chips):
        i = chip(d)
        at = pl.ds(four * i, four)
        low = (m.big[0, c, at] + m.mp_in[at]).astype(BF16)
        if d:
            m.mo[i] = low
            start(send_to(m.mo.at[i], m.mr.at[z], m.mr_sem, d, b, 2 * i + c))
        else:
            m.mr[z] = low

    for j in range(4):
        c_across(j)
    sums = m.piece[s].astype(F32)
    for d in range(1, strips):
        send_to(m.piece.at[0], m.piece_in.at[d], m.piece_sem, d, b, s).wait_recv()
        sums = sums + m.piece_in[d].astype(F32)
    m.small[b] = sums.astype(BF16)
    for e in range(1, 4):
        start(send_to(m.small.at[b], m.small.at[b], m.small_sem, e, lax.rem(b + e, 4), s))
    c_half(7)
    c_half(4)
    c_half(5)
    c_half(6)
    to_canvases(m.late, m.late_sem, m.late_sem2)
    u_sum()
    r_sum()
    for j in (7, 4):
        c_quarter(j)
        c_spread(j)

    for d in range(1, chips):
        i = chip(chips - d)
        send_to(m.mo.at[i], m.mr.at[i], m.mr_sem, d, b, 2 * i + c).wait_recv()
    for r in (0, rows - 1):
        for p in range(2):
            m.md[r + 1, p] = m.mr[(r % 2) * 2 + p, r // 2]
    start_edges(m.md, m.md_sem)
    c_quarter(5)
    c_spread(5)
    c_across(7)
    c_sum(0)
    c_sum(1)
    for r in range(1, rows - 1):
        for p in range(2):
            m.md[r + 1, p] = m.mr[(r % 2) * 2 + p, r // 2]

    m.acc1[...] = jnp.zeros_like(m.acc1)

    def mixer_rows(low, high):
        for k in range(width // 128):
            lanes = pl.ds(k * 128, 128)
            weights = [m.mk[t : t + 1, k * 128 : k * 128 + 128] for t in range(9)]

            def line(r, p):
                return m.md[r, p, :, lanes]

            def step(r, carry):
                new = window(line, r + 2)
                three = (carry[0], carry[1], new)
                out = conv(three, weights, True)
                for p in range(2):
                    m.fg[2 * r + p, :, lanes] = out[p]
                centre = [m.fp[r + 1, p, :, lanes].astype(F32) for p in range(2)]
                return carry[1], new, tuple(taps(three, centre, carry[2]))

            begin = tuple(m.acc1[t, :, lanes] for t in range(9))
            _, _, sums = lax.fori_loop(
                low, high, step, (window(line, low), window(line, low + 1), begin), unroll=True
            )
            for t in range(9):
                m.acc1[t, :, lanes] = sums[t]

    m.acc[1] = jnp.zeros_like(m.acc[1])
    m.acc[2] = jnp.zeros_like(m.acc[2])

    def token_row(r, _):
        for p in range(2):
            rp = 2 * r + p
            grad = m.fg[rp]
            n, inv = ln_parts(m.xd[r, p].astype(F32))
            m.acc[1] += grad
            m.acc[2] += grad * n
            interleave(m.rowf, r, p, m.rg[rp] + ln_back(grad * scale1, n, inv))
        m.tgo[r] = joined(m.rowf, r)
        return 0

    mixer_rows(1, rows - 1)
    lax.fori_loop(1, rows - 1, token_row, 0, unroll=3)
    c_quarter(6)
    c_spread(6)
    c_across(4)
    c_sum(2)
    c_sum(3)
    top_edge(m.md, m.md_sem)
    mixer_rows(0, 1)
    token_row(0, 0)
    bottom_edge(m.md, m.md_sem)
    mixer_rows(rows - 1, rows)
    token_row(rows - 1, 0)
    tg_copy = pltpu.make_async_copy(m.tgo, m.tg_hbm, m.load_sem.at[14])
    tg_copy.start()

    pack = []
    third = width // 3
    for v in (m.acc[1], m.acc[2]):
        pair = halves(v)
        for h in range(2):
            pack += [pair[h : h + 1, k * third : k * third + third] for k in range(3)]
    pack.append(jnp.zeros((4, third), F32))
    own_sums(m.early, m.early_sem, jnp.concatenate(pack, axis=0))
    mixer_sums = [jnp.sum(m.acc1[t], axis=0, keepdims=True) for t in range(9)]
    mixer_sums = jnp.concatenate(mixer_sums + [jnp.zeros((7, width), F32)], axis=0)
    pad_lanes = jnp.zeros((16, 128 - own), F32)
    for t in range(strips):
        m.mpiece[t] = jnp.concatenate(
            [mixer_sums[:, t * own : t * own + own], pad_lanes], axis=1
        ).astype(BF16)
    for d in range(1, strips):
        t = lax.rem(s + d, strips)
        start(send_to(m.mpiece.at[t], m.mpiece_in.at[d], m.mpiece_sem, d, b, t))

    c_across(5)
    for g in range(3):
        r_relay(g, False)
    for i in range(2):
        c_relay(i, i % 2 == 0)
    c_across(6)
    c_sum(7)
    to_canvases(m.early, m.early_sem, m.early_sem2)
    c_sum(4)
    sums = m.mpiece[s].astype(F32)
    for d in range(1, strips):
        send_to(m.mpiece.at[0], m.mpiece_in.at[d], m.mpiece_sem, d, b, s).wait_recv()
        sums = sums + m.mpiece_in[d].astype(F32)
    m.msmall[b] = sums.astype(BF16)
    for e in range(1, 4):
        start(send_to(m.msmall.at[b], m.msmall.at[b], m.msmall_sem, e, lax.rem(b + e, 4), s))
    c_sum(5)
    c_sum(6)
    for i in range(2, 4):
        c_relay(i, i % 2 == 0)
    to_sibling(m.late, m.late_sem2, m.late_sem3)
    to_sibling(m.early, m.early_sem2, m.early_sem3)
    j_order = (7, 4, 5, 6)
    for i in range(4):
        c_relay(j_order[i], i % 2 == 0)

    finals = []

    def store(src, dst, index):
        cp = pltpu.make_async_copy(src, dst, m.load_sem.at[index])
        cp.start()
        finals.append(cp)

    for e in range(1, 4):
        i = lax.rem(b - e + 4, 4)
        send_to(m.cond_all.at[i], m.cond_all.at[i], m.cond_sem, e, i, s).wait_recv()
        send_to(m.small.at[i], m.small.at[i], m.small_sem, e, i, s).wait_recv()
        send_to(m.msmall.at[i], m.msmall.at[i], m.msmall_sem, e, i, s).wait_recv()
    for g in range(3):
        r_arrive(g)
    store(m.r_all, m.r_hbm, 15)
    store(m.cond_all, m.cond_hbm, 16)
    store(m.small, m.small_hbm, 17)
    store(m.msmall, m.msmall_hbm, 18)
    from_sibling(m.late, m.late_sem3)
    from_sibling(m.early, m.early_sem3)
    store(m.late, m.late_hbm, 19)
    store(m.early, m.early_hbm, 20)
    for i in range(4):
        c_arrive(i, i % 2 == 0)
    for i in range(4):
        c_arrive(j_order[i], i % 2 == 0)
    store(m.c_all, m.c_hbm, 21)
    for cp in sent:
        cp.wait_send()
    edges_sent(m.fp, m.fp_sem)
    edges_sent(m.md, m.md_sem)

    halo_sent(m.ex, m.ex_sem)
    for n in range(chips):
        halo_sent(m.cg, m.cg_sem, n)
    for h in range(2):
        u_one(h).wait_send()
        u_two(h).wait_send()
        for n in range(chips):
            r_one(n, h).wait_send()
            r_two(n, h).wait_send()
        for j in range(8):
            c_one(j, h).wait_send()
            c_two(j, h).wait_send()
    for k in range(3):
        r_three(k).wait_send()
        u_three(k).wait_send()
        r_four(k, 0).wait_send()
        r_four(k, 1).wait_send()
        r_relay(k, True)
        for j in range(8):
            c_three(j, k).wait_send()

    for i in range(4):
        c_gone(i, i % 2 == 0)
        c_gone(j_order[i], i % 2 == 0)
    out_copy.wait()
    tg_copy.wait()
    for cp in finals:
        cp.wait()


def block(
    tokens, mixer, owner, steps, labels, emb, aw, ab, ob, eb, hk, rb, wj, wo, we, wr, cot, strips
):
    rows, cols, width = tokens.shape
    chips = strips // 2
    half = width // 2
    total = strips * 64
    blocks = 2 * rows
    chip_rows = 2 * rows
    part = width // chips // 4
    third = width // 3
    cond = (steps.shape[1], width + 256)
    shape = jax.ShapeDtypeStruct
    vm = pltpu.VMEM

    def dma(*size):
        return pltpu.SemaphoreType.DMA(size)

    ins = dict(
        tok=tokens, mixer=mixer, owner=owner, steps=steps, labels=labels, ab=ab, ob=ob, eb=eb,
        hidden=hk, rb=rb, emb_hbm=emb, aw4_hbm=aw.reshape(2, 2, width // 4, 6 * width),
        aw5_hbm=aw.reshape(chips, 2, 2, part, 6 * width), wj_hbm=wj, wo_hbm=wo, we_hbm=we, wr_hbm=wr, cot_hbm=cot,
    )
    outs = dict(
        out_hbm=shape((rows, cols, width), BF16),
        tg_hbm=shape((rows, cols, width), F32),
        r_hbm=shape((4, 3, width // 12, half), BF16),
        c_hbm=shape((8, 2, 2, part, half), BF16),
        cond_hbm=shape((4,) + cond, F32),
        small_hbm=shape((4, 16, half), BF16),
        msmall_hbm=shape((4, 16, 128), BF16),
        late_hbm=shape((4, 2, chips, 16, half), BF16),
        early_hbm=shape((4, 2, chips, 16, third), BF16),
    )
    scratch = dict(
        emb=vm(emb.shape, BF16),
        mod=vm((2, 6 * width), F32),
        mk=vm((9, width), F32),
        ebf=vm((1, 2 * chips * half), F32),
        hk=vm((chips, 9, half), F32),
        wj=vm((3, width, half), BF16),
        wo=vm((width, width), BF16),
        we=vm((width, chips * half), BF16),
        wr=vm((chips * half, width), BF16),
        cot=vm((rows, cols, width), BF16),
        cond_all=vm((4,) + cond, F32),
        rowf=vm((rows, width // 128, cols, 128), F32),
        xd=vm((rows, 2, 16, width), BF16),
        fp=vm((rows + 2, 2, 16, width), BF16),
        ms=vm((chips, rows // 2, 16, width), BF16),
        mg=vm((strips, rows // 2, 16, width), BF16),
        qkv=vm((9, total, 128), BF16),
        probs=vm((3, 2, total, total), BF16),
        ag=vm((6, total, 128), BF16),
        ai=vm((6, chips, 64, 128), BF16),
        acc=vm((6, 16, width), F32),
        acc1=vm((9, 8, width), F32),
        ctd=vm((blocks, 16, width), BF16),
        tg=vm((2, blocks, 16, width), BF16),
        sc=vm((2, blocks, 16, width), BF16),
        b1=vm((blocks, 16, width), F32),
        res=vm((blocks, 16, width), F32),
        ex=vm((chip_rows + 2, 2, 16, chips * half), BF16),
        cg=vm((chip_rows + 2, 2, 16, chips * half), BF16),
        act=vm((2 * blocks, 16, chips * half), BF16),
        big=vm((2, 2, blocks, 16, width), F32),
        b2_in=vm((blocks, 16, width), F32),
        sg_in=vm((blocks, 16, width), F32),
        hkg=vm((chips, 16, half), F32),
        rg=vm((blocks, 16, width), F32),
        og=vm((chips, rows // 2, 16, width), BF16),
        out=vm((rows, cols, width), BF16),
        gg=vm((strips, rows // 2, 16, width), BF16),
        da=vm((3, total, 128), BF16),
        ds=vm((2, total, total), BF16),
        dqkv=vm((9, total, 128), BF16),
        mp_in=vm((blocks, 16, width), F32),
        mo=vm((chips, rows // 2, 16, width), BF16),
        mr=vm((chips, rows // 2, 16, width), BF16),
        md=vm((rows + 2, 2, 16, width), BF16),
        fg=vm((blocks, 16, width), F32),
        tgo=vm((rows, cols, width), F32),
        rw=vm((chips, 2, 2, width // 4, half), BF16),
        r1=vm((chips, 2, 2, width // 12, half), BF16),
        r2=vm((chips, 2, width // 12, half), BF16),
        r3=vm((3, 2, width // 12, half), BF16),
        u3=vm((3, 2, 2, width // 12, half), BF16),
        u0=vm((2, 2, width // 12, half), BF16),
        u1=vm((2, 2, width // 24, half), BF16),
        u2=vm((2, width // 24, half), BF16),
        r_all=vm((4, 3, width // 12, half), BF16),
        ew=vm((4, chips, 2, 2, part, half), BF16),
        jo=vm((4, chips, 2, 2, part, half), BF16),
        c1=vm((8, 2, 2, 2, part, half), BF16),
        c2=vm((8, chips, part, half), BF16),
        c3=vm((8, 3, part, half), BF16),
        c_out=vm((8, part, half), BF16),
        c_all=vm((8, 2, 2, part, half), BF16),
        late=vm((4, 2, chips, 16, half), BF16),
        early=vm((4, 2, chips, 16, third), BF16),
        piece=vm((strips, 16, half), BF16),
        piece_in=vm((strips, 16, half), BF16),
        small=vm((4, 16, half), BF16),
        mpiece=vm((strips, 16, 128), BF16),
        mpiece_in=vm((strips, 16, 128), BF16),
        msmall=vm((4, 16, 128), BF16),
        load_sem=dma(35),
    )
    pairs = dict(
        cond_sem=(4,), fp_sem=(2,), md_sem=(2,), mg_sem=(chips,), mg_sem2=(chips,),
        gg_sem=(chips,), gg_sem2=(chips,), ai_sem=(3, strips), ag_sem=(3,), pair_sem=(5,),
        ex_sem=(2, 1), cg_sem=(2, chips), mr_sem=(chips,),
        r1_sem=(chips, 2), r2_sem=(chips, 2), r3_sem=(3,), r4_sem=(3, 3), u3_sem=(3,), u1_sem=(2,), u2_sem=(2,),
        c1_sem=(8, 2), c2_sem=(8, 2), c3_sem=(8, 3),
        late_sem=(chips,), late_sem2=(4,), late_sem3=(1,),
        early_sem=(chips,), early_sem2=(4,), early_sem3=(1,),
        piece_sem=(strips,), small_sem=(4,), mpiece_sem=(strips,), msmall_sem=(4,),
    )
    names = list(ins) + list(outs) + list(scratch)
    shapes = list(scratch.values())
    for size in list(pairs.values()):
        shapes += [dma(*size), dma(*size)]
    shapes += [dma(8, 4), dma(8, 4, 2)]
    plain = len(names)

    def kernel(*refs):
        named = list(refs[:plain])
        sems = refs[plain:]
        both = [(sems[2 * i], sems[2 * i + 1]) for i in range(len(sems) // 2)]
        block_kernel(names + list(pairs) + ["c4_sem"], *named, *both)

    return pl.pallas_call(
        kernel,
        name="block",
        out_shape=tuple(outs.values()),
        in_specs=[WHOLE] * 2 + [SCALARS] * 3 + [WHOLE] * 5 + [LEFT] * 8,
        out_specs=(LEFT,) * len(outs),
        scratch_shapes=shapes,
        compiler_params=pltpu.CompilerParams(
            collective_id=0, has_side_effects=True, vmem_limit_bytes=VMEM_BYTES
        ),
    )(*ins.values())


def final_kernel(
    out_in, tg_in, r_in, c_in, cond_ref, small_ref, msmall_ref, late_ref, early_ref, aw_hbm,
    out_ref, tg_ref, tab_ref, ad_out, ab_ref, mix_ref, joint_out, output_out, ob_ref,
    expand_out, eb_ref, hidden_ref, reduce_out, rb_ref,
    aw, out_v, tg_v, r_ref, c_ref, ad_ref, joint_ref, output_ref, expand_ref, reduce_ref, sem,
):
    s = lax.axis_index("strip")
    strips = lax.axis_size("strip")
    width = cond_ref.shape[2] - 256
    own = width // strips
    half = width // 2
    loads = [
        (r_in, r_ref),
        (c_in, c_ref),
        (aw_hbm.at[pl.ds(pl.multiple_of(s * own, 16), own)], aw),
        (out_in, out_v),
        (tg_in, tg_v),
    ]
    loads = [pltpu.make_async_copy(a, v, sem.at[i]) for i, (a, v) in enumerate(loads)]
    for cp in loads:
        cp.start()
    stores = []

    def store(src, dst):
        cp = pltpu.make_async_copy(src, dst, sem.at[5 + len(stores)])
        cp.start()
        stores.append(cp)

    small = small_ref[0].astype(F32)
    mixer = msmall_ref[0].astype(F32)
    for i in range(1, 4):
        small = small + small_ref[i].astype(F32)
        mixer = mixer + msmall_ref[i].astype(F32)
    hidden_ref[...] = small[0:9]
    eb_ref[...] = small[9]
    ob_ref[...] = small[10, 0:own]
    rb_ref[...] = small[11, 0:own]
    mix_ref[...] = mixer[0:9, 0:own]

    n = width // 4
    loads[0].wait()
    for q in range(4):
        reduce_ref[:, q * n : q * n + n] = r_ref[q].reshape(n, half).astype(F32).T
    store(reduce_ref, reduce_out)
    loads[1].wait()
    part = c_ref.shape[3]
    for xs in range(2):
        rows = slice(xs * part, xs * part + part)
        for cs in range(2):
            for k in range(4):
                at = (2 * k + cs) * half
                expand_ref[rows, at : at + half] = c_ref[k, xs, cs].astype(F32)
            for k in range(3):
                for p in range(3):
                    at = p * width + cs * half + k * 128
                    joint_ref[rows, at : at + 128] = c_ref[
                        4 + k, xs, cs, :, p * 128 : p * 128 + 128
                    ].astype(F32)
            output_ref[rows, cs * half : cs * half + half] = c_ref[7, xs, cs].astype(F32)
    store(expand_ref, expand_out)
    store(joint_ref, joint_out)
    store(output_ref, output_out)
    loads[3].wait()
    store(out_v, out_ref)
    loads[4].wait()
    store(tg_v, tg_ref)

    slots = 32
    condition = cond_ref[...].reshape(slots, width + 256)
    labels = condition[:, width : width + 1]
    slot_late = jnp.concatenate([cond_ref[i, 0:1, width + 128 :] for i in range(4)], axis=1)
    slot_early = jnp.concatenate([cond_ref[i, 1:2, width + 128 :] for i in range(4)], axis=1)
    condition = condition[:, 0:width]
    pick = lax.broadcasted_iota(jnp.int32, (width, own), 0) == (
        lax.broadcasted_iota(jnp.int32, (width, own), 1) + s * own
    )
    pick = jnp.where(pick, 1.0, 0.0)
    condition = jnp.dot(
        condition, pick, precision=lax.Precision.HIGHEST, preferred_element_type=F32
    )
    sigmoid = 1.0 / (1.0 + jnp.exp(-condition))
    silu = (condition * sigmoid).astype(BF16)
    slope = sigmoid * (1.0 + condition * (1.0 - sigmoid))

    count = 4 * strips * 16

    def by_slot(source, slot, parts, period):
        groups = parts * (16 // period)
        index = lax.broadcasted_iota(jnp.int32, (groups * slots, count), 0)
        row = lax.rem(lax.broadcasted_iota(jnp.int32, (groups * slots, count), 1), 16)
        group = index // slots
        mine = jnp.logical_and(
            row // period == group // parts, lax.rem(row, parts) == lax.rem(group, parts)
        )
        mine = jnp.logical_and(mine, lax.rem(index, slots) == slot.astype(jnp.int32))
        grad = dot(jnp.where(mine, 1.0, 0.0).astype(BF16), source[...].reshape(count, source.shape[-1]))
        return [grad[k * slots : k * slots + slots] for k in range(groups)]

    pieces = by_slot(early_ref, slot_early, 3, 6) + by_slot(late_ref, slot_late, 2, 4)
    grad = jnp.concatenate(pieces, axis=1)
    sums = jnp.sum(grad, axis=0, keepdims=True)
    low = grad.astype(BF16)
    ad_ref[...] = dot_tn(silu, low)
    loads[2].wait()
    silu_grad = dot_nt(low, aw[...])
    store(ad_ref, ad_out)
    bias = jnp.zeros((1, 6 * own), F32)
    for t in range(strips):
        bias = jnp.where(s == t, sums[:, t * 6 * own : t * 6 * own + 6 * own], bias)
    ab_ref[...] = bias[0]
    classes = tab_ref.shape[1]
    onehot = lax.broadcasted_iota(jnp.int32, (slots, classes), 1) == labels.astype(jnp.int32)
    tab_ref[...] = lax.dot_general(
        silu_grad * slope,
        jnp.where(onehot, 1.0, 0.0),
        TN,
        precision=lax.Precision.HIGHEST,
        preferred_element_type=F32,
    )
    for cp in stores:
        cp.wait()


def final(parts, aw, classes, strips):
    out, tg, r, c = parts[:4]
    width = out.shape[-1]
    own = width // strips
    half = width // 2
    shape = jax.ShapeDtypeStruct
    vm = pltpu.VMEM
    return pl.pallas_call(
        final_kernel,
        name="final",
        out_shape=(
            shape(out.shape, BF16),
            shape(tg.shape, F32),
            shape((own, classes), F32),
            shape((own, 6 * width), F32),
            shape((6 * own,), F32),
            shape((9, own), F32),
            shape((own, 3 * width), F32),
            shape((own, width), F32),
            shape((own,), F32),
            shape((own, 4 * width), F32),
            shape((half,), F32),
            shape((9, half), F32),
            shape((half, width), F32),
            shape((own,), F32),
        ),
        in_specs=[LEFT] * 4 + [WHOLE] * 5 + [LEFT],
        out_specs=(
            LEFT, LEFT, WHOLE, LEFT, WHOLE, WHOLE, LEFT, LEFT, WHOLE, LEFT, WHOLE, WHOLE, LEFT,
            WHOLE,
        ),
        scratch_shapes=[
            vm((own, 6 * width), BF16),
            vm(out.shape, BF16),
            vm(tg.shape, F32),
            vm(r.shape, BF16),
            vm(c.shape, BF16),
            vm((own, 6 * width), F32),
            vm((own, 3 * width), F32),
            vm((own, width), F32),
            vm((own, 4 * width), F32),
            vm((half, width), F32),
            pltpu.SemaphoreType.DMA((12,)),
        ],
        compiler_params=pltpu.CompilerParams(vmem_limit_bytes=VMEM_BYTES),
    )(*parts, aw)


def local_grouped(
    tokens, tile_owner, time_steps, class_labels, class_embedding_matrix, adaptive_weight,
    adaptive_bias, mixer_kernel, joint_weight, output_weight, output_bias, expand_weight,
    expand_bias, hidden_kernel, reduce_weight, reduce_bias, output_cotangent,
):
    strips = lax.axis_size("strip")
    owner = tile_owner.transpose(0, 2, 1)
    parts = block(
        tokens[0], mixer_kernel.T, owner, time_steps, class_labels, class_embedding_matrix.T,
        adaptive_weight, adaptive_bias, output_bias, expand_bias, hidden_kernel.T, reduce_bias,
        joint_weight, output_weight, expand_weight, reduce_weight, output_cotangent[0], strips,
    )
    classes = class_embedding_matrix.shape[1]
    (
        out, tg, table, adaptive, bias, mixer, joint, output, ob, expand, eb, hidden, reduce, rb,
    ) = final(parts, adaptive_weight, classes, strips)
    return (
        out[None], tg[None], table, adaptive, bias, mixer.T, joint, output, ob, expand, eb,
        hidden.T, reduce, rb,
    )


EXACT_PRECISION = lax.Precision.HIGHEST


def padded_2(block, sides, width):
    for axis, dim in sides:
        count = lax.axis_size(axis)
        forward = [(i, i + 1) for i in range(count - 1)]
        backward = [(target, source) for source, target in forward]
        low = lax.ppermute(
            lax.slice_in_dim(block, block.shape[dim] - width, None, axis=dim), axis, forward
        )
        high = lax.ppermute(lax.slice_in_dim(block, 0, width, axis=dim), axis, backward)
        block = jnp.concatenate([low, block, high], axis=dim)
    return block


def normalize(values):
    centre = jnp.mean(values, axis=-1, keepdims=True)
    centred = values - centre
    spread = jnp.mean(centred * centred, axis=-1, keepdims=True)
    return centred * lax.rsqrt(spread + EPSILON)


def modulate(values, shifting, scaling):
    return normalize(values) * (1.0 + scaling) + shifting


def depthwise(padded, kernel):
    row_count = padded.shape[-3] - 2
    column_total = padded.shape[-2]
    widened = jnp.pad(padded, [(0, 0)] * (padded.ndim - 2) + [(1, 1), (0, 0)])
    result = jnp.zeros(
        padded.shape[:-3] + (row_count, column_total, padded.shape[-1]), padded.dtype
    )
    for tapping in range(9):
        row_shift = tapping // 3
        col_shift = tapping % 3
        window = lax.slice_in_dim(widened, row_shift, row_shift + row_count, axis=widened.ndim - 3)
        window = lax.slice_in_dim(
            window, col_shift, col_shift + column_total, axis=widened.ndim - 2
        )
        result = result + kernel[:, tapping] * window
    return result


def kernel_grad(padded, gradient):
    row_count = gradient.shape[1]
    column_total = gradient.shape[2]
    widened = jnp.pad(padded, ((0, 0), (0, 0), (1, 1), (0, 0)))
    columns = []
    for tapping in range(9):
        row_shift = tapping // 3
        col_shift = tapping % 3
        window = widened[
            :, row_shift : row_shift + row_count, col_shift : col_shift + column_total, :
        ]
        columns.append(jnp.sum(window * gradient, axis=(0, 1, 2)))
    return jnp.stack(columns, axis=1)


def timestep_features(time_steps, model_width):
    half_width = model_width // 2
    frequencies = jnp.exp(
        -math.log(10000.0) * jnp.arange(half_width, dtype=jnp.float32) / half_width
    )
    angles = time_steps.astype(jnp.float32)[..., None] * frequencies
    return jnp.concatenate([jnp.cos(angles), jnp.sin(angles)], axis=-1)


def group_owner(owner):
    canvases, row_count, column_total = owner.shape
    shaped = owner.reshape(canvases, row_count // 2, 2, column_total // 2, 2).transpose(
        0, 2, 4, 1, 3
    )
    return shaped.reshape(canvases, 2, 2, row_count // 2 * (column_total // 2))


def to_groups(tensor, head_count):
    canvases, row_count, column_total, features = tensor.shape
    head_size = features // head_count
    shaped = tensor.reshape(
        canvases, row_count // 2, 2, column_total // 2, 2, head_count, head_size
    )
    shaped = shaped.transpose(0, 2, 4, 5, 1, 3, 6)
    return shaped.reshape(
        canvases, 2, 2, head_count, row_count // 2 * (column_total // 2), head_size
    )


def from_groups(tensor, row_count, column_total):
    canvases, head_count, head_size = (tensor.shape[0], tensor.shape[3], tensor.shape[-1])
    shaped = tensor.reshape(
        canvases, 2, 2, head_count, row_count // 2, column_total // 2, head_size
    )
    shaped = shaped.transpose(0, 4, 1, 5, 2, 3, 6)
    return shaped.reshape(canvases, row_count, column_total, head_count * head_size)


def local(
    tokens,
    tile_owner,
    time_steps,
    class_labels,
    class_embedding_matrix,
    adaptive_weight,
    adaptive_bias,
    mixer_kernel,
    joint_weight,
    output_weight,
    output_bias,
    expand_weight,
    expand_bias,
    hidden_kernel,
    reduce_weight,
    reduce_bias,
    output_cotangent,
):
    canvases, row_count, column_total, model_width = tokens.shape
    head_count = HEADS
    head_size = model_width // head_count
    factor = head_size ** (-0.5)
    half_cols = column_total // 2
    strips = lax.axis_size("strip")
    strip_index = lax.axis_index("strip")
    canvas_rows = row_count * strips
    class_count = class_embedding_matrix.shape[1]
    latent_count = time_steps.shape[1]
    tile_rows = canvas_rows // 4
    full_owner = jnp.broadcast_to(
        tile_owner[:, :, None, :, None], (canvases, 4, tile_rows, 2, half_cols)
    ).reshape(canvases, canvas_rows, column_total)
    local_owner = lax.dynamic_slice_in_dim(full_owner, strip_index * row_count, row_count, 1)
    token_hot = (local_owner[..., None] == jnp.arange(latent_count, dtype=jnp.int32)).astype(
        jnp.float32
    )
    class_onehot = (class_labels[..., None] == jnp.arange(class_count, dtype=jnp.int32)).astype(
        jnp.bfloat16
    )
    class_rows = jnp.einsum(
        "ywj,gj->ywg", class_onehot, class_embedding_matrix, preferred_element_type=jnp.float32
    )
    condition = timestep_features(time_steps, model_width) + class_rows
    silu_value, silu_pull = jax.vjp(jax.nn.silu, condition)
    silu_cond = silu_value.astype(jnp.bfloat16)
    modulation = jnp.einsum(
        "cbd,de->cbe", silu_cond, adaptive_weight, preferred_element_type=jnp.float32
    )
    modulation = modulation + adaptive_bias.astype(jnp.float32)
    token_mod = jnp.einsum("crkb,cbe->crke", token_hot, modulation, precision=EXACT_PRECISION)
    shift_one, scale_one, gate_one, shift_two, scale_two, gate_two = jnp.split(
        token_mod, 6, axis=-1
    )
    inputs = tokens.astype(jnp.float32)
    first_value, first_pull = jax.vjp(modulate, inputs, shift_one, scale_one)
    first = first_value.astype(jnp.bfloat16)
    first_padded = padded_2(first, (("strip", 1),), 1)
    mixer_single_float = mixer_kernel.astype(jnp.float32)
    mixed = depthwise(first_padded.astype(jnp.float32), mixer_single_float).astype(jnp.bfloat16)
    joint = jnp.einsum("crkd,de->crke", mixed, joint_weight, preferred_element_type=jnp.float32)
    query_rows = joint[..., :model_width].astype(jnp.bfloat16)
    keys_local = joint[..., model_width : 2 * model_width].astype(jnp.bfloat16)
    values_local = joint[..., 2 * model_width :].astype(jnp.bfloat16)
    keys_canvas, values_canvas = (
        lax.all_gather(keys_local, "strip", axis=1, tiled=True),
        lax.all_gather(values_local, "strip", axis=1, tiled=True),
    )
    query_groups = to_groups(query_rows, head_count)
    key_groups = to_groups(keys_canvas, head_count)
    value_groups = to_groups(values_canvas, head_count)
    query_owner = group_owner(local_owner)
    key_owner = group_owner(full_owner)
    allowed = (query_owner[..., :, None] == key_owner[..., None, :])[:, :, :, None]

    def attention_scores():
        raw = (
            jnp.einsum(
                "cabhnd,cabhmd->cabhnm",
                query_groups,
                key_groups,
                preferred_element_type=jnp.float32,
            )
            * factor
        )
        return jnp.where(allowed, raw, MASKED)

    scores = attention_scores()
    peak = jnp.max(scores, axis=-1, keepdims=True)
    lifted_float = jnp.exp(scores - peak)
    total = jnp.sum(lifted_float, axis=-1, keepdims=True)
    softened = (lifted_float / total).astype(jnp.bfloat16)
    log_total = peak + jnp.log(total)
    attended_groups = jnp.einsum(
        "cabhnm,cabhmd->cabhnd", softened, value_groups, preferred_element_type=jnp.float32
    )
    attended = from_groups(attended_groups, row_count, column_total).astype(jnp.bfloat16)
    branch_one = jnp.einsum(
        "crkd,de->crke", attended, output_weight, preferred_element_type=jnp.float32
    )
    branch_one = branch_one + output_bias.astype(jnp.float32)
    residual = inputs + gate_one * branch_one
    second_value, second_pull = jax.vjp(modulate, residual, shift_two, scale_two)
    second = second_value.astype(jnp.bfloat16)
    expanded = jnp.einsum(
        "crkd,df->crkf", second, expand_weight, preferred_element_type=jnp.float32
    )
    expanded = (expanded + expand_bias.astype(jnp.float32)).astype(jnp.bfloat16)
    expanded_padded = padded_2(expanded, (("strip", 1),), 1)
    hidden_float = hidden_kernel.astype(jnp.float32)
    conv_out = depthwise(expanded_padded.astype(jnp.float32), hidden_float)
    gelu_value, gelu_pull = jax.vjp(jax.nn.gelu, conv_out)
    activated = gelu_value.astype(jnp.bfloat16)
    branch_two = jnp.einsum(
        "crkf,fd->crkd", activated, reduce_weight, preferred_element_type=jnp.float32
    )
    branch_two = branch_two + reduce_bias.astype(jnp.float32)
    outputs = (residual + gate_two * branch_two).astype(jnp.bfloat16)
    upstream = output_cotangent.astype(jnp.float32)
    two_grad = (upstream * gate_two).astype(jnp.bfloat16)
    gate_two_grad = upstream * branch_two
    reduce_bias_grad = jnp.sum(two_grad.astype(jnp.float32), axis=(0, 1, 2))
    reduce_weight_grad = jnp.einsum(
        "crkf,crkd->fd", activated, two_grad, preferred_element_type=jnp.float32
    )
    activated_grad = jnp.einsum(
        "crkd,fd->crkf", two_grad, reduce_weight, preferred_element_type=jnp.float32
    )
    conv_grad = gelu_pull(activated_grad)[0].astype(jnp.bfloat16)
    conv_padded = padded_2(conv_grad, (("strip", 1),), 1)
    expanded_grad = depthwise(conv_padded.astype(jnp.float32), hidden_float[:, ::-1]).astype(
        jnp.bfloat16
    )
    hidden_kernel_grad = kernel_grad(
        expanded_padded.astype(jnp.float32), conv_grad.astype(jnp.float32)
    )
    expand_bias_grad = jnp.sum(expanded_grad.astype(jnp.float32), axis=(0, 1, 2))
    expand_weight_grad = jnp.einsum(
        "crkd,crkf->df", second, expanded_grad, preferred_element_type=jnp.float32
    )
    second_grad = jnp.einsum(
        "crkf,df->crkd", expanded_grad, expand_weight, preferred_element_type=jnp.float32
    )
    residual_part, shift_two_grad, scale_two_grad = second_pull(second_grad)
    residual_grad = upstream + residual_part
    gate_one_grad = residual_grad * branch_one
    one_grad = (residual_grad * gate_one).astype(jnp.bfloat16)
    output_bias_grad = jnp.sum(one_grad.astype(jnp.float32), axis=(0, 1, 2))
    output_weight_grad = jnp.einsum(
        "crkd,crke->de", attended, one_grad, preferred_element_type=jnp.float32
    )
    attended_grad = jnp.einsum(
        "crke,de->crkd", one_grad, output_weight, preferred_element_type=jnp.float32
    ).astype(jnp.bfloat16)
    attended_grad_groups = to_groups(attended_grad, head_count)
    probs = jnp.exp(attention_scores() - log_total)
    prob_grads = jnp.einsum(
        "cabhnd,cabhmd->cabhnm",
        attended_grad_groups,
        value_groups,
        preferred_element_type=jnp.float32,
    )
    spread_sum = jnp.sum(probs * prob_grads, axis=-1, keepdims=True)
    score_grads = (probs * (prob_grads - spread_sum)).astype(jnp.bfloat16)
    query_grad_groups = (
        jnp.einsum(
            "cabhnm,cabhmd->cabhnd", score_grads, key_groups, preferred_element_type=jnp.float32
        )
        * factor
    )
    query_grad = from_groups(query_grad_groups, row_count, column_total).astype(jnp.bfloat16)
    all_queries, all_attended = (
        lax.all_gather(query_groups, "strip", axis=4, tiled=True),
        lax.all_gather(attended_grad_groups, "strip", axis=4, tiled=True),
    )
    all_logs, all_spreads = (
        lax.all_gather(log_total[..., 0], "strip", axis=4, tiled=True),
        lax.all_gather(spread_sum[..., 0], "strip", axis=4, tiled=True),
    )
    own_keys = to_groups(keys_local, head_count)
    own_values = to_groups(values_local, head_count)
    own_allowed = (key_owner[..., :, None] == query_owner[..., None, :])[:, :, :, None]
    own_scores = (
        jnp.einsum(
            "cabhnd,cabhmd->cabhnm", all_queries, own_keys, preferred_element_type=jnp.float32
        )
        * factor
    )
    own_scores = jnp.where(own_allowed, own_scores, MASKED)
    own_probs = jnp.exp(own_scores - all_logs[..., None])
    own_prob_grads = jnp.einsum(
        "cabhnd,cabhmd->cabhnm", all_attended, own_values, preferred_element_type=jnp.float32
    )
    own_score_grads = (own_probs * (own_prob_grads - all_spreads[..., None])).astype(jnp.bfloat16)
    key_grad_groups = (
        jnp.einsum(
            "cabhnm,cabhnd->cabhmd",
            own_score_grads,
            all_queries,
            preferred_element_type=jnp.float32,
        )
        * factor
    )
    value_grad_groups = jnp.einsum(
        "cabhnm,cabhnd->cabhmd",
        own_probs.astype(jnp.bfloat16),
        all_attended,
        preferred_element_type=jnp.float32,
    )
    key_grad = from_groups(key_grad_groups, row_count, column_total).astype(jnp.bfloat16)
    value_grad = from_groups(value_grad_groups, row_count, column_total).astype(jnp.bfloat16)
    joint_grad = jnp.concatenate([query_grad, key_grad, value_grad], axis=-1)
    joint_weight_grad = jnp.einsum(
        "crkd,crke->de", mixed, joint_grad, preferred_element_type=jnp.float32
    )
    mixed_grad = jnp.einsum(
        "crke,de->crkd", joint_grad, joint_weight, preferred_element_type=jnp.float32
    ).astype(jnp.bfloat16)
    mixed_padded = padded_2(mixed_grad, (("strip", 1),), 1)
    first_grad = depthwise(mixed_padded.astype(jnp.float32), mixer_single_float[:, ::-1])
    mixer_kernel_grad = kernel_grad(
        first_padded.astype(jnp.float32), mixed_grad.astype(jnp.float32)
    )
    input_part, shift_one_grad, scale_one_grad = first_pull(first_grad)
    tokens_grad = residual_grad + input_part
    token_grad = jnp.concatenate(
        [
            shift_one_grad,
            scale_one_grad,
            gate_one_grad,
            shift_two_grad,
            scale_two_grad,
            gate_two_grad,
        ],
        axis=-1,
    )
    modulation_grad = jnp.einsum("crkb,crke->cbe", token_hot, token_grad, precision=EXACT_PRECISION)
    silu_grad = jnp.einsum(
        "cbe,de->cbd",
        modulation_grad,
        adaptive_weight.astype(jnp.float32),
        precision=EXACT_PRECISION,
    )
    conditioning_grad = silu_pull(silu_grad)[0]
    table_grad = jnp.einsum(
        "soy,sok->yk",
        conditioning_grad,
        class_onehot.astype(jnp.float32),
        precision=EXACT_PRECISION,
    )
    adaptive_grad = jnp.einsum(
        "cbd,cbe->de", silu_cond.astype(jnp.float32), modulation_grad, precision=EXACT_PRECISION
    )
    adaptive_bias_grad = jnp.sum(modulation_grad, axis=(0, 1))
    (
        table_shard,
        adaptive_shard,
        adaptive_bias_shard,
        mixer_shard,
        joint_shard,
        output_shard,
        output_bias_shard,
        expand_shard,
        expand_bias_shard,
        hidden_shard,
        reduce_shard,
        reduce_bias_shard,
    ) = (
        lax.psum_scatter(
            table_grad.astype(jnp.bfloat16), "strip", scatter_dimension=0, tiled=True
        ).astype(jnp.float32),
        lax.psum_scatter(
            adaptive_grad.astype(jnp.bfloat16), "strip", scatter_dimension=0, tiled=True
        ).astype(jnp.float32),
        lax.psum_scatter(
            adaptive_bias_grad.astype(jnp.bfloat16), "strip", scatter_dimension=0, tiled=True
        ).astype(jnp.float32),
        lax.psum_scatter(
            mixer_kernel_grad.astype(jnp.bfloat16), "strip", scatter_dimension=0, tiled=True
        ).astype(jnp.float32),
        lax.psum_scatter(
            joint_weight_grad.astype(jnp.bfloat16), "strip", scatter_dimension=0, tiled=True
        ).astype(jnp.float32),
        lax.psum_scatter(
            output_weight_grad.astype(jnp.bfloat16), "strip", scatter_dimension=0, tiled=True
        ).astype(jnp.float32),
        lax.psum_scatter(
            output_bias_grad.astype(jnp.bfloat16), "strip", scatter_dimension=0, tiled=True
        ).astype(jnp.float32),
        lax.psum_scatter(
            expand_weight_grad.astype(jnp.bfloat16), "strip", scatter_dimension=0, tiled=True
        ).astype(jnp.float32),
        lax.psum_scatter(
            expand_bias_grad.astype(jnp.bfloat16), "strip", scatter_dimension=0, tiled=True
        ).astype(jnp.float32),
        lax.psum_scatter(
            hidden_kernel_grad.astype(jnp.bfloat16), "strip", scatter_dimension=0, tiled=True
        ).astype(jnp.float32),
        lax.psum_scatter(
            reduce_weight_grad.astype(jnp.bfloat16), "strip", scatter_dimension=0, tiled=True
        ).astype(jnp.float32),
        lax.psum_scatter(
            reduce_bias_grad.astype(jnp.bfloat16), "strip", scatter_dimension=0, tiled=True
        ).astype(jnp.float32),
    )
    summed = (
        lax.psum(table_shard.astype(jnp.bfloat16), "batch").astype(jnp.float32),
        lax.psum(adaptive_shard.astype(jnp.bfloat16), "batch").astype(jnp.float32),
        lax.psum(adaptive_bias_shard.astype(jnp.bfloat16), "batch").astype(jnp.float32),
        lax.psum(mixer_shard.astype(jnp.bfloat16), "batch").astype(jnp.float32),
        lax.psum(joint_shard.astype(jnp.bfloat16), "batch").astype(jnp.float32),
        lax.psum(output_shard.astype(jnp.bfloat16), "batch").astype(jnp.float32),
        lax.psum(output_bias_shard.astype(jnp.bfloat16), "batch").astype(jnp.float32),
        lax.psum(expand_shard.astype(jnp.bfloat16), "batch").astype(jnp.float32),
        lax.psum(expand_bias_shard.astype(jnp.bfloat16), "batch").astype(jnp.float32),
        lax.psum(hidden_shard.astype(jnp.bfloat16), "batch").astype(jnp.float32),
        lax.psum(reduce_shard.astype(jnp.bfloat16), "batch").astype(jnp.float32),
        lax.psum(reduce_bias_shard.astype(jnp.bfloat16), "batch").astype(jnp.float32),
    )
    return (
        outputs,
        tokens_grad,
        summed[0],
        summed[1],
        summed[2],
        summed[3],
        summed[4],
        summed[5],
        summed[6],
        summed[7],
        summed[8],
        summed[9],
        summed[10],
        summed[11],
    )


def solution(mesh):
    grouped = (mesh.shape["batch"], mesh.shape["strip"]) == (4, 8)
    return jax.shard_map(
        local_grouped if grouped else local,
        mesh=mesh,
        in_specs=(
            P("batch", "strip", None, None),
            P("batch", None, None),
            P("batch", None),
            P("batch", None),
            P(),
            P(),
            P(),
            P(),
            P(),
            P(),
            P(),
            P(),
            P(),
            P(),
            P(),
            P(),
            P("batch", "strip", None, None),
        ),
        out_specs=(
            P("batch", "strip", None, None),
            P("batch", "strip", None, None),
            P("strip", None),
            P("strip", None),
            P("strip"),
            P("strip", None),
            P("strip", None),
            P("strip", None),
            P("strip"),
            P("strip", None),
            P("strip"),
            P("strip", None),
            P("strip", None),
            P("strip"),
        ),
        check_vma=False,
    )
```

```python
import math
from types import SimpleNamespace

import jax
import jax.numpy as jnp
from jax import lax
from jax.experimental import pallas as pl
from jax.experimental.pallas import tpu as pltpu
from jax.sharding import PartitionSpec as P

HEADS = 12
EPSILON = 1e-06
MASKED = -1e30
MESH = pl.DeviceIdType.MESH
F32 = jnp.float32
BF16 = jnp.bfloat16
VMEM_BYTES = 62 * 1024 * 1024
WHOLE = pl.BlockSpec(memory_space=pltpu.VMEM)
LEFT = pl.BlockSpec(memory_space=pl.ANY)
SCALARS = pl.BlockSpec(memory_space=pltpu.SMEM)
NT = (((1,), (1,)), ((), ()))
TN = (((0,), (0,)), ((), ()))


def dot(a, b):
    return jnp.dot(a, b, preferred_element_type=F32)


def dot_nt(a, b):
    return lax.dot_general(a, b, NT, preferred_element_type=F32)


def dot_tn(a, b):
    return lax.dot_general(a, b, TN, preferred_element_type=F32)


def send_to(src, dst, sems, index, batch, strip):
    return pltpu.make_async_remote_copy(
        src_ref=src,
        dst_ref=dst,
        send_sem=sems[0].at[index],
        recv_sem=sems[1].at[index],
        device_id=(batch, strip),
        device_id_type=MESH,
    )


def entry_signals(strips):
    s = lax.axis_index("strip")
    b = lax.axis_index("batch")
    z = s // 2
    barrier = pltpu.get_barrier_semaphore()
    count = 0
    for d in range(1, strips):
        pl.semaphore_signal(
            barrier, inc=1, device_id=(b, lax.rem(s + d, strips)), device_id_type=MESH
        )
        count += 1
    for e in range(1, 4):
        for core in range(2):
            pl.semaphore_signal(
                barrier, inc=1, device_id=(lax.rem(b + e, 4), 2 * z + core), device_id_type=MESH
            )
            count += 1
    return count


def entry_wait(count):
    pl.semaphore_wait(pltpu.get_barrier_semaphore(), count)


def spread(mod, width):
    return jnp.concatenate(
        [jnp.broadcast_to(mod[0:1], (8, width)), jnp.broadcast_to(mod[1:2], (8, width))], axis=0
    )


def spread_columns(buffer, r, x):
    for k in range(x.shape[-1] // 128):
        buffer[r, k] = x[:, k * 128 : k * 128 + 128]


def every_second(buffer, r, p):
    return jnp.concatenate(
        [buffer[r, k, pl.ds(p, 16, stride=2), :] for k in range(buffer.shape[1])], axis=-1
    )


def interleave(buffer, r, p, x):
    for k in range(x.shape[-1] // 128):
        buffer[r, k, pl.ds(p, 16, stride=2), :] = x[:, k * 128 : k * 128 + 128]


def joined(buffer, r):
    return jnp.concatenate([buffer[r, k] for k in range(buffer.shape[1])], axis=-1)


def ln_parts(x):
    centre = jnp.mean(x, axis=-1, keepdims=True)
    centred = x - centre
    var = jnp.mean(centred * centred, axis=-1, keepdims=True)
    inv = lax.rsqrt(var + EPSILON)
    return centred * inv, inv


def ln_back(grad, n, inv):
    mean0 = jnp.mean(grad, axis=-1, keepdims=True)
    mean1 = jnp.mean(grad * n, axis=-1, keepdims=True)
    return inv * (grad - mean0 - n * mean1)


def window(load, r):
    even = load(r, 0).astype(F32)
    odd = load(r, 1).astype(F32)
    n = even.shape[0]
    j = lax.broadcasted_iota(jnp.int32, even.shape, 0)
    odd_m = jnp.where(j == 0, 0.0, pltpu.roll(odd, 1, 0))
    even_p = jnp.where(j == n - 1, 0.0, pltpu.roll(even, n - 1, 0))
    return odd_m, even, odd, even_p


def conv(rows, weights, flip):
    out = []
    for p in range(2):
        total = None
        for i in range(3):
            for j in range(3):
                t = 3 * i + j
                a = weights[8 - t if flip else t] * rows[i][p + j]
                total = a if total is None else total + a
        out.append(total)
    return out


def taps(rows, centre, sums):
    new = list(sums)
    for i in range(3):
        for j in range(3):
            a = rows[i][j] * centre[0] + rows[i][1 + j] * centre[1]
            t = 8 - (3 * i + j)
            new[t] = sums[t] + (a[0:8] + a[8:16])
    return new


def halves(x):
    return jnp.concatenate(
        [jnp.sum(x[0:8], axis=0, keepdims=True), jnp.sum(x[8:16], axis=0, keepdims=True)], axis=0
    )


def gelu_both(x):
    k0 = math.sqrt(2.0 / math.pi)
    square = x * x
    t = jnp.tanh(k0 * x * (1.0 + 0.044715 * square))
    cdf = 0.5 + 0.5 * t
    slope = cdf + (0.5 * k0) * x * (1.0 - t * t) * (1.0 + (3.0 * 0.044715) * square)
    return x * cdf, slope


def block_kernel(names, *refs):
    m = SimpleNamespace(**dict(zip(names, refs)))
    rows, cols, width = m.tok.shape
    half = width // 2
    strips = lax.axis_size("strip")
    chips = strips // 2
    chip_rows = 2 * rows
    total = strips * 64
    own = width // strips
    part = width // chips // 4
    s = lax.axis_index("strip")
    b = lax.axis_index("batch")
    z = s // 2
    c = lax.rem(s, 2)
    sibling = 2 * z + 1 - c
    y, x = b // 2, lax.rem(b, 2)
    x_mate = 2 * y + 1 - x
    y_mate = 2 * (1 - y) + x
    sent = []

    def chip(d):
        return lax.rem(z + d, chips)

    def start(copy):
        copy.start()
        sent.append(copy)

    loads = {}

    def load(name, src, dst, index):
        loads[name] = pltpu.make_async_copy(src, dst, m.load_sem.at[index])
        loads[name].start()

    load("emb", m.emb_hbm, m.emb, 22)
    for i in range(12):
        lanes = pl.ds(i * half, half)
        src = m.aw4_hbm.at[:, :, :, lanes] if i < 4 else m.aw5_hbm.at[:, :, :, :, lanes]
        load(f"aw{i}", src, (m.rw, m.ew, m.jo)[i // 4].at[i % 4], 23 + i)
    greet = entry_signals(strips)
    for k in range(3):
        off = pl.multiple_of(k * width + c * half, 128)
        load(f"wj{k}", m.wj_hbm.at[:, pl.ds(off, half)], m.wj.at[k], k)
    load("cot", m.cot_hbm, m.cot, 3)
    load("wo", m.wo_hbm, m.wo, 4)
    for n in range(chips):
        off = pl.multiple_of((2 * n + c) * half, 128)
        spot = pl.ds(n * half, half)
        load(f"we{n}", m.we_hbm.at[:, pl.ds(off, half)], m.we.at[:, spot], 5 + n)
        load(f"wr{n}", m.wr_hbm.at[pl.ds(off, half)], m.wr.at[spot], 5 + chips + n)

    latents = m.steps.shape[1]
    classes = m.emb.shape[0]
    row = lax.broadcasted_iota(jnp.int32, (latents, 1), 0)
    when = jnp.zeros((latents, 1), F32)
    label = jnp.zeros((latents, 1), jnp.int32)
    for i in range(latents):
        when = jnp.where(row == i, m.steps[0, i].astype(F32), when)
        label = jnp.where(row == i, m.labels[0, i], label)
    order = lax.broadcasted_iota(jnp.int32, (latents, half), 1).astype(F32)
    angles = when * jnp.exp(-math.log(10000.0) * order / half)
    features = jnp.concatenate([jnp.cos(angles), jnp.sin(angles)], axis=1)
    onehot = lax.broadcasted_iota(jnp.int32, (latents, classes), 1) == label
    onehot = jnp.where(onehot, 1.0, 0.0).astype(BF16)

    lane = lax.broadcasted_iota(jnp.int32, (latents, 128), 1)
    kind = lax.broadcasted_iota(jnp.int32, (latents, 128), 0)
    line = lax.rem(lane, 16)
    side = jnp.where(kind == 0, lax.rem(line // 2, 2), lax.rem(line // 3, 2))
    tile = lax.rem(lane // 16, 4)
    slots = jnp.zeros((latents, 128), jnp.int32)
    for i in range(4):
        for h in range(2):
            hit = jnp.logical_and(tile == i, side == h)
            slots = jnp.where(hit, m.owner[0, h, i] + b * latents, slots)
    loads["emb"].wait()
    condition = features + dot(onehot, m.emb[...])
    silu = (condition / (1.0 + jnp.exp(-condition))).astype(BF16)
    m.cond_all[b] = jnp.concatenate(
        [condition, jnp.broadcast_to(label.astype(F32), (latents, 128)), slots.astype(F32)], axis=1
    )
    bias = m.ab[...].astype(F32).reshape(1, 6 * width)
    for g, held in enumerate((m.rw, m.ew, m.jo)):
        for i in range(4):
            loads[f"aw{4 * g + i}"].wait()
        weights = jnp.concatenate([held[i].reshape(width, half) for i in range(4)], axis=1)
        lanes = slice(g * 2 * width, (g + 1) * 2 * width)
        table = dot(silu, weights) + bias[:, lanes]
        for h in range(2):
            mine = row == m.owner[0, h, z]
            m.mod[h : h + 1, lanes] = jnp.sum(jnp.where(mine, table, 0.0), axis=0, keepdims=True)
    entry_wait(greet)

    m.mk[...] = m.mixer[...].astype(F32)
    ob = m.ob[...].astype(F32).reshape(1, width)
    rb = m.rb[...].astype(F32).reshape(1, width)
    m.ebf[...] = m.eb[...].astype(F32).reshape(m.ebf.shape)
    for n in range(chips):
        m.hk[n] = m.hidden[:, pl.ds(pl.multiple_of((2 * n + c) * half, 128), half)].astype(F32)

    for e in range(1, 4):
        start(
            send_to(m.cond_all.at[b], m.cond_all.at[b], m.cond_sem, e, lax.rem(b + e, 4), s)
        )

    def block_mod(n):
        return spread(m.mod[:, n * width : (n + 1) * width], width)

    scale1 = 1.0 + block_mod(1)
    shift1 = block_mod(0)

    def first_row(r):
        spread_columns(m.rowf, r, m.tok[r].astype(F32))
        for p in range(2):
            v = every_second(m.rowf, r, p)
            m.xd[r, p] = v.astype(BF16)
            n, _ = ln_parts(v)
            m.fp[r + 1, p] = (n * scale1 + shift1).astype(BF16)

    def edge_sends(buffer, sems):
        up = send_to(buffer.at[1], buffer.at[rows + 1], sems, 0, b, s - 1)
        down = send_to(buffer.at[rows], buffer.at[0], sems, 1, b, s + 1)
        return up, down

    def start_edges(buffer, sems):
        up, down = edge_sends(buffer, sems)

        @pl.when(s > 0)
        def _():
            up.start()

        @pl.when(s < strips - 1)
        def _():
            down.start()

    def edges_sent(buffer, sems):
        up, down = edge_sends(buffer, sems)

        @pl.when(s > 0)
        def _():
            up.wait_send()

        @pl.when(s < strips - 1)
        def _():
            down.wait_send()

    def top_edge(buffer, sems):
        @pl.when(s > 0)
        def _():
            send_to(buffer.at[1], buffer.at[0], sems, 1, b, s - 1).wait_recv()

        @pl.when(s == 0)
        def _():
            buffer[0] = jnp.zeros_like(buffer[0])

    def bottom_edge(buffer, sems):
        @pl.when(s < strips - 1)
        def _():
            send_to(buffer.at[1], buffer.at[rows + 1], sems, 0, b, s + 1).wait_recv()

        @pl.when(s == strips - 1)
        def _():
            buffer[rows + 1] = jnp.zeros_like(buffer[0])

    first_row(0)
    first_row(rows - 1)
    start_edges(m.fp, m.fp_sem)

    def body(r, _):
        first_row(r)
        return 0

    lax.fori_loop(1, rows - 1, body, 0, unroll=3)

    four = rows // 2

    def inner_rows(g):
        return pl.ds(1 - g // 2, four - 1)

    def edge_row(g):
        return pl.ds((g // 2) * (four - 1), 1)

    inner_edge = (inner_rows, edge_row)

    def to_groups(source, target, sems, piece, at):
        for d in range(1, chips):
            g = chip(d)
            rws = at(g)
            start(
                send_to(source.at[g, rws], target.at[s, rws], sems, (piece, d), b, 2 * g + c)
            )

    def pass_on(target, sems, sems2, d, pieces):
        i = 2 * chip(chips - d) + c
        if d:
            for k, at in enumerate(pieces):
                spot = target.at[i, at(z)]
                send_to(spot, spot, sems, (k, d), b, i).wait_recv()
        start(send_to(target.at[i], target.at[i], sems2, d, b, sibling))

    def groups_ready(target, sems2):
        for d in range(chips):
            i = 2 * chip(chips - d) + 1 - c
            send_to(target.at[i], target.at[i], sems2, d, b, sibling).wait_recv()

    def mixed_rows(low, high):
        for k in range(width // 128):
            lanes = pl.ds(k * 128, 128)
            weights = [m.mk[t : t + 1, k * 128 : k * 128 + 128] for t in range(9)]

            def line(r, p):
                return m.fp[r, p, :, lanes]

            def step(r, carry):
                new = window(line, r + 2)
                out = conv((carry[0], carry[1], new), weights, False)
                for p in range(2):
                    m.ms[lax.rem(r, 2) * 2 + p, r // 2, :, lanes] = out[p].astype(BF16)
                return carry[1], new

            lax.fori_loop(
                low, high, step, (window(line, low), window(line, low + 1)), unroll=True
            )

    mixed_rows(1, rows - 1)
    to_groups(m.ms, m.mg, m.mg_sem, 0, inner_rows)
    top_edge(m.fp, m.fp_sem)
    mixed_rows(0, 1)
    bottom_edge(m.fp, m.fp_sem)
    mixed_rows(rows - 1, rows)

    to_groups(m.ms, m.mg, m.mg_sem, 1, edge_row)
    m.mg[s] = m.ms[z]

    m.acc[...] = jnp.zeros_like(m.acc)
    gate2 = block_mod(5)
    loads["cot"].wait()

    def upstream_row(r, _):
        spread_columns(m.rowf, r, m.cot[r].astype(F32))
        for p in range(2):
            up = every_second(m.rowf, r, p)
            m.ctd[2 * r + p] = up.astype(BF16)
            two = (up * gate2).astype(BF16)
            m.tg[c, 2 * r + p] = two
            m.acc[0] += two.astype(F32)
        return 0

    lax.fori_loop(0, rows, upstream_row, 0)
    start(send_to(m.tg.at[c], m.tg.at[c], m.pair_sem, 0, b, sibling))

    for d in range(chips):
        pass_on(m.mg, m.mg_sem, m.mg_sem2, d, inner_edge)
    groups_ready(m.mg, m.mg_sem2)
    for k in range(3):
        loads[f"wj{k}"].wait()

    v = m.mg[...].reshape(total, width)
    for k in range(3):
        w = dot(v, m.wj[k]).astype(BF16)
        for n in range(3):
            m.qkv[3 * k + n] = w[:, n * 128 : n * 128 + 128]

    where = lax.broadcasted_iota(jnp.int32, (1, total), 1)
    lefts = lax.rem(where, 16) < 8
    key_owner = jnp.zeros((1, total), jnp.int32)
    for t in range(4):
        both = jnp.where(lefts, m.owner[0, 0, t], m.owner[0, 1, t])
        key_owner = jnp.where(where // 128 == t, both, key_owner)
    where = lax.broadcasted_iota(jnp.int32, (total, 1), 0)
    lefts = lax.rem(where, 16) < 8
    query_owner = jnp.zeros((total, 1), jnp.int32)
    for t in range(4):
        both = jnp.where(lefts, m.owner[0, 0, t], m.owner[0, 1, t])
        query_owner = jnp.where(where // 128 == t, both, query_owner)
    allowed = query_owner == key_owner
    lane = lax.broadcasted_iota(jnp.int32, (total, 128), 1) < 64
    factor = 64 ** -0.5

    def head(v, h):
        return jnp.where(lane if h == 0 else jnp.logical_not(lane), v, jnp.zeros_like(v))

    for n in range(3):
        mine = c * 3 + n
        q2 = (m.qkv[n].astype(F32) * factor).astype(BF16)
        outs = []
        for h in range(2):
            scores = jnp.where(allowed, dot_nt(head(q2, h), m.qkv[3 + n]), MASKED)
            peak = jnp.max(scores, axis=-1, keepdims=True)
            lifted = jnp.exp(scores - peak)
            inv = 1.0 / jnp.sum(lifted, axis=-1, keepdims=True)
            m.probs[n, h] = (lifted * inv).astype(BF16)
            outs.append(dot(lifted.astype(BF16), m.qkv[6 + n]) * inv)
        m.ag[mine] = jnp.where(lane, outs[0], outs[1]).astype(BF16)
        for d in range(1, strips):
            t = lax.rem(s + d, strips)
            start(
                send_to(
                    m.ag.at[mine, pl.ds(pl.multiple_of(t * 64, 64), 64)],
                    m.ai.at[mine, z],
                    m.ai_sem,
                    (n, d),
                    b,
                    t,
                )
            )
        start(send_to(m.ag.at[mine], m.ag.at[mine], m.ag_sem, n, b, sibling))
        m.ai[mine, z] = m.ag[mine, pl.ds(pl.multiple_of(s * 64, 64), 64), :]

    for n in range(chips):
        loads[f"wr{n}"].wait()
    send_to(m.tg.at[c], m.tg.at[1 - c], m.pair_sem, 0, b, sibling).wait_recv()
    chip_tg = m.tg[...].reshape(total, width)
    for h in range(2):
        m.big[h] = dot_nt(chip_tg, m.wr[h * width : h * width + width, :]).reshape(m.big.shape[1:])

    for n in range(3):
        for d in range(1, strips):
            i = lax.rem(s - d + strips, strips)
            spot = lax.rem(i, 2) * 3 + n
            send_to(
                m.ag.at[spot, pl.ds(0, 64)], m.ai.at[spot, i // 2], m.ai_sem, (n, d), b, i
            ).wait_recv()

    gate1 = block_mod(2)
    shift2 = block_mod(3)
    scale2 = 1.0 + block_mod(4)
    loads["wo"].wait()

    v = jnp.concatenate([m.ai[n].reshape(chips * 64, 128) for n in range(6)], axis=-1)
    m.b1[...] = (dot(v, m.wo[...]) + ob).reshape(m.b1.shape)

    def residual_row(i, _):
        rp = 4 * lax.rem(i, rows // 2) + i // (rows // 2)
        u = m.xd[rp // 2, lax.rem(rp, 2)].astype(F32) + gate1 * m.b1[i]
        m.res[rp] = u
        n, _ = ln_parts(u)
        m.sc[c, rp] = (n * scale2 + shift2).astype(BF16)
        return 0

    lax.fori_loop(0, 2 * rows, residual_row, 0, unroll=4)
    start(send_to(m.sc.at[c], m.sc.at[c], m.pair_sem, 1, b, sibling))

    def block_order(i, at_chip=None):
        at_chip = z if at_chip is None else at_chip
        high, low = at_chip // 2, lax.rem(at_chip, 2)
        flip_high, flip_low = 1 - lax.rem(i, 2), 1 - i // 2
        high = high + flip_high - 2 * high * flip_high
        low = low + flip_low - 2 * low * flip_low
        return 2 * high + low

    def halo_sends(buffer, sems, up_block, down_block):
        up_at = pl.ds(pl.multiple_of(up_block * half, 128), half)
        down_at = pl.ds(pl.multiple_of(down_block * half, 128), half)
        first, last = buffer.at[1, :, :, up_at], buffer.at[chip_rows, :, :, down_at]
        above = buffer.at[0, :, :, down_at]
        below = buffer.at[chip_rows + 1, :, :, up_at]
        up = send_to(first, below, sems, (0, up_block), b, s - 2)
        down = send_to(last, above, sems, (1, down_block), b, s + 2)
        return up, down

    def start_halo(buffer, sems, upward, downward, up_block, down_block):
        up, down = halo_sends(buffer, sems, up_block, down_block)

        @pl.when(jnp.logical_and(z > 0, upward))
        def _():
            up.start()

        @pl.when(jnp.logical_and(z < chips - 1, downward))
        def _():
            down.start()

    def halo_sent(buffer, sems, n):
        up, down = halo_sends(buffer, sems, n, n)

        @pl.when(z > 0)
        def _():
            up.wait_send()

        @pl.when(z < chips - 1)
        def _():
            down.wait_send()

    def take_halo(buffer, sems, n):
        at = pl.ds(pl.multiple_of(n * half, 128), half)
        k = n
        above, below = buffer.at[0, :, :, at], buffer.at[chip_rows + 1, :, :, at]

        @pl.when(z > 0)
        def _():
            send_to(above, above, sems, (1, k), b, s - 2).wait_recv()

        @pl.when(z == 0)
        def _():
            above[...] = jnp.zeros(above.shape, BF16)

        @pl.when(z < chips - 1)
        def _():
            send_to(below, below, sems, (0, k), b, s + 2).wait_recv()

        @pl.when(z == chips - 1)
        def _():
            below[...] = jnp.zeros(below.shape, BF16)

    for n in range(chips):
        loads[f"we{n}"].wait()
    hidden = chips * half
    bias = jnp.concatenate(
        [m.ebf[:, pl.ds(pl.multiple_of((2 * n + c) * half, 128), half)] for n in range(chips)],
        axis=-1,
    )

    def expand(core):
        w = dot(m.sc[core].reshape(rows * 32, width), m.we[...]) + bias
        m.ex[pl.ds(1 + core * rows, rows)] = w.astype(BF16).reshape(rows, 2, 16, hidden)

    expand(c)
    def edges_leave(upward, downward):
        for i in range(chips):
            start_halo(
                m.ex, m.ex_sem, upward, downward, block_order(i, z - 1), block_order(i, z + 1)
            )

    edges_leave(c == 0, c == 1)
    send_to(m.sc.at[c], m.sc.at[1 - c], m.pair_sem, 1, b, sibling).wait_recv()
    expand(1 - c)
    edges_leave(c == 1, c == 0)
    first_mate, then_mate = (x_mate, y_mate), (y_mate, x_mate)
    pair_chip = z + 1 - 2 * lax.rem(z, 2)
    far_chip = lax.rem(z + 2, 4)
    last_chip = 3 - z

    sub = width // 12
    upper = pl.ds(0, sub)

    def u_three(k):
        dest = pair_chip if k < 2 else far_chip
        src = m.u3.at[1] if k == 2 else m.rw.at[pair_chip if k == 0 else last_chip, :, :, upper]
        return send_to(src, m.u3.at[k], m.u3_sem, k, b, 2 * dest + c)

    def u_across():
        u_three(1).wait_recv()
        for i in range(2):
            v = m.u3[1, i].astype(F32) + m.rw[far_chip, i, :, upper].astype(F32)
            m.u3[1, i] = v.astype(BF16)
        u_three(2).start()

    def u_one(h):
        at = pl.ds(h * sub // 2, sub // 2)
        src = m.u0.at[:, 1 - x, at] if h == 0 else m.u0.at[1 - y, :, at]
        return send_to(src, m.u1.at[h], m.u1_sem, h, first_mate[h], s)

    def u_two(h):
        src = m.u1.at[h, (1 - y) if h == 0 else (1 - x)]
        return send_to(src, m.u2.at[h], m.u2_sem, h, then_mate[h], s)

    def u_begin():
        for k in (0, 2):
            u_three(k).wait_recv()
        for i in range(2):
            v = m.rw[z, i, :, upper].astype(F32) + m.u3[0, i].astype(F32)
            m.u0[i] = (v + m.u3[2, i].astype(F32)).astype(BF16)
        for h in range(2):
            u_one(h).start()

    def u_half():
        for h in range(2):
            u_one(h).wait_recv()
            at = pl.ds(h * sub // 2, sub // 2)
            kept = m.u0[:, x, at] if h == 0 else m.u0[y, :, at]
            m.u1[h] = (m.u1[h].astype(F32) + kept.astype(F32)).astype(BF16)
            u_two(h).start()

    def u_sum():
        for h in range(2):
            u_two(h).wait_recv()
            kept = m.u1[h, y if h == 0 else x].astype(F32)
            at = pl.ds(h * sub // 2, sub // 2)
            m.r_all[b, 0, at] = (m.u2[h].astype(F32) + kept).astype(BF16)
        r_four(0, 0).start()
        r_four(0, 1).start()

    def r_source(n, h, mine):
        at = pl.ds(sub + h * sub, sub)
        if h == 0:
            return m.rw.at[n, :, x if mine else 1 - x, at]
        return m.rw.at[n, y if mine else 1 - y, :, at]

    def r_one(n, h):
        return send_to(r_source(n, h, False), m.r1.at[n, h], m.r1_sem, (n, h), first_mate[h], s)

    def r_two(n, h):
        src = m.r1.at[n, h, (1 - y) if h == 0 else (1 - x)]
        return send_to(src, m.r2.at[n, h], m.r2_sem, (n, h), then_mate[h], s)

    def r_three(k):
        dest = pair_chip if k < 2 else far_chip
        t = (pair_chip, last_chip, far_chip)[k]
        return send_to(m.r2.at[t], m.r3.at[k], m.r3_sem, k, b, 2 * dest + c)

    def r_four(g, e):
        spot = m.r_all.at[b, g]
        return send_to(spot, spot, m.r4_sem, (g, e), (x_mate, y_mate)[e], s)

    def r_relay(g, wait):
        source, dest = (x_mate, y_mate) if g < 2 else (y_mate, x_mate)
        spot = m.r_all.at[source, g]
        copy = send_to(spot, spot, m.r4_sem, (g, 2), dest, s)
        if wait:
            copy.wait_send()
            return
        send_to(spot, spot, m.r4_sem, (g, 0 if g < 2 else 1), source, s).wait_recv()
        copy.start()

    def r_arrive(g):
        source, e = (y_mate, 1) if g < 2 else (x_mate, 0)
        spot = m.r_all.at[source, g]
        send_to(spot, spot, m.r4_sem, (g, e), source, s).wait_recv()
        spot = m.r_all.at[3 - b, g]
        send_to(spot, spot, m.r4_sem, (g, 2), source, s).wait_recv()

    def r_half(n):
        for h in range(2):
            r_one(n, h).wait_recv()
            kept = r_source(n, h, True)[...].astype(F32)
            m.r1[n, h] = (m.r1[n, h].astype(F32) + kept).astype(BF16)
            r_two(n, h).start()

    def r_quarter(n):
        for h in range(2):
            r_two(n, h).wait_recv()
            kept = m.r1[n, h, y if h == 0 else x].astype(F32)
            m.r2[n, h] = (m.r2[n, h].astype(F32) + kept).astype(BF16)

    def r_spread():
        r_three(1).start()
        r_three(0).start()

    def r_across():
        r_three(1).wait_recv()
        m.r2[far_chip] = (m.r2[far_chip].astype(F32) + m.r3[1].astype(F32)).astype(BF16)
        r_three(2).start()

    def r_sum():
        v = m.r2[z].astype(F32)
        for k in (0, 2):
            r_three(k).wait_recv()
            v = v + m.r3[k].astype(F32)
        m.r_all[b, pl.ds(1, 2)] = v.astype(BF16)
        for g in (1, 2):
            r_four(g, 0).start()
            r_four(g, 1).start()

    def c_source(j, h, mine):
        block = m.ew.at[j] if not isinstance(j, int) or j < 4 else m.jo.at[j - 4]
        at = pl.ds(2 * h, 2)
        if h == 0:
            return block.at[at, :, x if mine else 1 - x]
        return block.at[at, y if mine else 1 - y]

    def c_one(j, h):
        return send_to(c_source(j, h, False), m.c1.at[j, h], m.c1_sem, (j, h), first_mate[h], s)

    def c_two(j, h):
        src = m.c1.at[j, h, :, 1 - y] if h == 0 else m.c1.at[j, h, :, 1 - x]
        return send_to(src, m.c2.at[j, pl.ds(2 * h, 2)], m.c2_sem, (j, h), then_mate[h], s)

    def c_three(j, k):
        dest = pair_chip if k < 2 else far_chip
        t = (pair_chip, last_chip, far_chip)[k]
        return send_to(m.c2.at[j, t], m.c3.at[j, k], m.c3_sem, (j, k), b, 2 * dest + c)

    def c_copy(j, src, xs, cs, kind, batch, strip):
        return pltpu.make_async_remote_copy(
            src_ref=src,
            dst_ref=m.c_all.at[j, xs, cs],
            send_sem=m.c4_sem[0].at[j, kind],
            recv_sem=m.c4_sem[1].at[j, kind, cs],
            device_id=(batch, strip),
            device_id_type=MESH,
        )

    def c_four(j, kind):
        return c_copy(j, m.c_out.at[j], x, c, kind, (b, x_mate, y_mate)[kind], 2 * z + y)

    def c_got(j, kind, cs):
        xs = 1 - x if kind == 1 else x
        c_copy(j, m.c_out.at[j], xs, cs, kind, b, s).wait_recv()

    def c_passing(j, along_y):
        xs, dest = (1 - x, y_mate) if along_y else (x, x_mate)
        return pltpu.make_async_remote_copy(
            src_ref=m.c_all.at[j, xs],
            dst_ref=m.c_all.at[j, xs],
            send_sem=m.c4_sem[0].at[j, 3],
            recv_sem=m.c4_sem[1].at[j, 3, 0],
            device_id=(dest, s),
            device_id_type=MESH,
        )

    def c_relay(j, along_y):
        @pl.when((c == y) if along_y else (c != y))
        def _():
            for cs in range(2):
                c_got(j, 1 if along_y else 2, cs)
            c_passing(j, along_y).start()

    def c_arrive(j, along_y):
        @pl.when(c == y)
        def _():
            c_copy(j, m.c_out.at[j], x, 1 - c, 0, b, sibling).wait_recv()
            if not along_y:
                for cs in range(2):
                    c_got(j, 1, cs)

        @pl.when(c != y)
        def _():
            if along_y:
                for cs in range(2):
                    c_got(j, 2, cs)
            spot = m.c_all.at[j, 1 - x]
            pltpu.make_async_remote_copy(
                src_ref=spot,
                dst_ref=spot,
                send_sem=m.c4_sem[0].at[j, 3],
                recv_sem=m.c4_sem[1].at[j, 3, 0],
                device_id=(b, s),
                device_id_type=MESH,
            ).wait_recv()

    def c_gone(j, along_y):
        c_four(j, 1).wait_send()
        c_four(j, 2).wait_send()

        @pl.when(c != y)
        def _():
            c_four(j, 0).wait_send()

        @pl.when((c == y) if along_y else (c != y))
        def _():
            c_passing(j, along_y).wait_send()

    def c_begin(j):
        for h in range(2):
            c_one(j, h).start()

    def c_half(j):
        for h in range(2):
            c_one(j, h).wait_recv()
            kept = c_source(j, h, True)[...].astype(F32)
            m.c1[j, h] = (m.c1[j, h].astype(F32) + kept).astype(BF16)
            c_two(j, h).start()

    def c_quarter(j):
        for h in range(2):
            c_two(j, h).wait_recv()
            at = pl.ds(2 * h, 2)
            kept = (m.c1[j, h, :, y] if h == 0 else m.c1[j, h, :, x]).astype(F32)
            m.c2[j, at] = (m.c2[j, at].astype(F32) + kept).astype(BF16)

    def c_spread(j):
        c_three(j, 1).start()
        c_three(j, 0).start()

    def c_across(j):
        c_three(j, 1).wait_recv()
        far = m.c2[j, far_chip].astype(F32) + m.c3[j, 1].astype(F32)
        m.c2[j, far_chip] = far.astype(BF16)
        c_three(j, 2).start()

    def c_sum(j):
        v = m.c2[j, z].astype(F32)
        for k in (0, 2):
            c_three(j, k).wait_recv()
            v = v + m.c3[j, k].astype(F32)
        m.c_out[j] = v.astype(BF16)
        c_finished(j)

    def c_finished(j):
        @pl.when(c == y)
        def _():
            m.c_all[j, x, c] = m.c_out[j]

        c_four(j, 1).start()
        c_four(j, 2).start()

        @pl.when(c != y)
        def _():
            c_four(j, 0).start()

    def v_three(k):
        dest = pair_chip if k < 2 else far_chip
        src = m.v3.at[1] if k == 2 else m.ew.at[3, pair_chip if k == 0 else last_chip]
        return send_to(src, m.v3.at[k], m.v3_sem, k, b, 2 * dest + c)

    def v_across():
        v_three(1).wait_recv()
        m.v3[1] = (m.v3[1].astype(F32) + m.ew[3, far_chip].astype(F32)).astype(BF16)
        v_three(2).start()

    v_rows = (pl.ds(0, 32), pl.ds(32, part - 32))

    def v_one(h):
        src = m.v0.at[:, 1 - x, v_rows[0]] if h == 0 else m.v0.at[1 - y, :, v_rows[1]]
        return send_to(src, (m.v1a, m.v1b)[h], m.v1_sem, h, first_mate[h], s)

    def v_two(h):
        src = m.v1a.at[1 - y] if h == 0 else m.v1b.at[1 - x]
        return send_to(src, (m.v2a, m.v2b)[h], m.v2_sem, h, then_mate[h], s)

    def v_begin():
        for k in (0, 2):
            v_three(k).wait_recv()
        v = m.ew[3, z].astype(F32) + m.v3[0].astype(F32) + m.v3[2].astype(F32)
        m.v0[...] = v.astype(BF16)
        for h in range(2):
            v_one(h).start()

    def v_half():
        for h in range(2):
            v_one(h).wait_recv()
            held = (m.v1a, m.v1b)[h]
            kept = m.v0[:, x, v_rows[0]] if h == 0 else m.v0[y, :, v_rows[1]]
            held[...] = (held[...].astype(F32) + kept.astype(F32)).astype(BF16)
            v_two(h).start()

    def v_sum():
        for h in range(2):
            v_two(h).wait_recv()
            kept = m.v1a[y] if h == 0 else m.v1b[x]
            v = (m.v2a, m.v2b)[h][...].astype(F32) + kept.astype(F32)
            m.c_out[3, v_rows[h]] = v.astype(BF16)
        c_finished(3)

    def activate(i, early):
        n = block_order(i)
        for k in range(3):
            lanes = pl.ds(pl.multiple_of(n * half + k * 128, 128), 128)
            inner = pl.ds(k * 128, 128)
            weights = [m.hk[n, t : t + 1, inner] for t in range(9)]
            spot = pl.ds(pl.multiple_of(lax.rem(n, 2) * half + k * 128, 128), 128)

            def line(r, p):
                return m.ex[r, p, :, lanes]

            def rows_of(low, high):
                above, here = window(line, low), window(line, low + 1)
                for r in range(low, high):
                    below = window(line, r + 2)
                    out = conv((above, here, below), weights, False)
                    for p in range(2):
                        value, slope = gelu_both(out[p])
                        rp = 2 * r + p
                        grad = m.big[n // 2, rp // 16, rp % 16, :, spot]
                        m.act[rp, :, lanes] = value.astype(BF16)
                        m.cg[r + 1, p, :, lanes] = (grad * slope).astype(BF16)
                    above, here = here, below

            if early is None:
                rows_of(0, chip_rows)
            elif early:
                rows_of(1, chip_rows - 1)
            else:
                rows_of(0, 1)
                rows_of(chip_rows - 1, chip_rows)

    def activated(i):
        n = block_order(i)
        at = pl.ds(pl.multiple_of(n * half, 128), half)
        start_halo(m.cg, m.cg_sem, True, True, n, n)
        full = m.act[:, :, at].reshape(total, half)
        m.rw[n] = dot_tn(chip_tg, full).astype(BF16).reshape(m.rw.shape[1:])
        for h in range(2):
            r_one(n, h).start()

    activate(0, True)
    take_halo(m.ex, m.ex_sem, block_order(0))
    activate(0, False)
    activated(0)
    u_three(1).start()
    for i in range(1, chips):
        take_halo(m.ex, m.ex_sem, block_order(i))

    def next_block(i, _):
        activate(i, None)
        activated(i)
        return 0

    lax.fori_loop(1, chips, next_block, 0)
    u_three(0).start()
    full = m.act[...].reshape(total, hidden)
    m.big[0] = dot(full, m.wr[...]).reshape(m.big.shape[1:])
    b2_copy = send_to(m.big.at[0, 1 - c], m.b2_in, m.pair_sem, 2, b, sibling)
    b2_copy.start()
    m.hkg[...] = jnp.zeros_like(m.hkg)
    for n in range(chips):
        take_halo(m.cg, m.cg_sem, n)
    u_across()
    chip_sc = m.sc[...].reshape(total, width)

    def backward(n, _):
        for k in range(3):
            lanes = pl.ds(pl.multiple_of(n * half + k * 128, 128), 128)
            inner = pl.ds(k * 128, 128)
            weights = [m.hk[n, t : t + 1, inner] for t in range(9)]

            def line(r, p):
                return m.cg[r, p, :, lanes]

            above, here = window(line, 0), window(line, 1)
            sums = [jnp.zeros((8, 128), F32) for _ in range(9)]
            total_eg = jnp.zeros((8, 128), F32)
            for r in range(chip_rows):
                below = window(line, r + 2)
                three = (above, here, below)
                low = [v.astype(BF16) for v in conv(three, weights, True)]
                for p in range(2):
                    m.act[2 * r + p, :, lanes] = low[p]
                centre = [m.ex[r + 1, p, :, lanes].astype(F32) for p in range(2)]
                sums = taps(three, centre, sums)
                both = low[0].astype(F32) + low[1].astype(F32)
                total_eg = total_eg + (both[0:8] + both[8:16])
                above, here = here, below
            for t, v in enumerate(sums + [total_eg]):
                m.hkg[n, t : t + 1, inner] = jnp.sum(v, axis=0, keepdims=True)
        full = m.act[:, :, pl.ds(pl.multiple_of(n * half, 128), half)].reshape(total, half)
        m.ew[n] = dot_tn(chip_sc, full).astype(BF16).reshape(m.ew.shape[1:])
        @pl.when(n < 3)
        def _():
            c_begin(n)

        r_half(block_order(n))
        return 0

    lax.fori_loop(0, chips, backward, 0)
    v_three(1).start()
    v_three(0).start()
    for core in (1 - c, c):
        v = m.act[pl.ds(core * 2 * rows, 2 * rows)].reshape(rows * 32, hidden)
        m.big[1, core] = dot_nt(v, m.we[...]).reshape(m.big.shape[2:])
        if core is not c:
            sg_copy = send_to(m.big.at[1, 1 - c], m.sg_in, m.pair_sem, 3, b, sibling)
            sg_copy.start()
    send_to(m.big.at[0, c], m.b2_in, m.pair_sem, 2, b, sibling).wait_recv()
    send_to(m.big.at[1, c], m.sg_in, m.pair_sem, 3, b, sibling).wait_recv()

    def finish(r, _):
        for p in range(2):
            rp = 2 * r + p
            grad = m.big[1, c, rp] + m.sg_in[rp]
            v = m.res[rp]
            n, inv = ln_parts(v)
            branch = m.b1[(rows // 2) * lax.rem(rp, 4) + rp // 4]
            up = m.ctd[rp].astype(F32)
            m.acc[1] += grad
            m.acc[2] += grad * n
            back = up + ln_back(grad * scale2, n, inv)
            m.rg[rp] = back
            m.acc[3] += back * branch
            one = (back * gate1).astype(BF16)
            m.og[lax.rem(rp, 4), rp // 4] = one
            m.acc[4] += one.astype(F32)
            branch2 = m.big[0, c, rp] + m.b2_in[rp] + rb
            m.acc[5] += up * branch2
            interleave(m.rowf, r, p, v + gate2 * branch2)
        m.out[r] = joined(m.rowf, r).astype(BF16)
        return 0

    def first_half(g):
        return pl.ds(0, four // 2)

    def second_half(g):
        return pl.ds(four // 2, four // 2)

    both_halves = (first_half, second_half)
    for k, at in enumerate(both_halves):
        lax.fori_loop(k * four, (k + 1) * four, finish, 0, unroll=2)
        to_groups(m.og, m.gg, m.gg_sem, k, at)
    out_copy = pltpu.make_async_copy(m.out, m.out_hbm, m.load_sem.at[13])
    out_copy.start()

    m.gg[s] = m.og[z]

    pack = []
    for v in (m.acc[3], m.acc[1], m.acc[2], m.acc[5]):
        pair = halves(v)
        for h in range(2):
            pack += [pair[h : h + 1, 0:half], pair[h : h + 1, half:]]
    def own_sums(buffer, sems, value):
        buffer[b, c, z] = value.astype(BF16)
        for d in range(1, chips):
            start(send_to(buffer.at[b, c, z], buffer.at[b, c, z], sems, d, b, 2 * chip(d) + c))

    def to_canvases(buffer, sems, sems2):
        for d in range(1, chips):
            i = chip(chips - d)
            send_to(buffer.at[b, c, i], buffer.at[b, c, i], sems, d, b, 2 * i + c).wait_recv()
        for e in range(1, 4):
            start(send_to(buffer.at[b, c], buffer.at[b, c], sems2, e, lax.rem(b + e, 4), s))

    def to_sibling(buffer, sems2, sems3):
        for e in range(1, 4):
            i = lax.rem(b - e + 4, 4)
            send_to(buffer.at[i, c], buffer.at[i, c], sems2, e, i, s).wait_recv()
        start(send_to(buffer.at[:, c], buffer.at[:, c], sems3, 0, b, sibling))

    def from_sibling(buffer, sems3):
        send_to(buffer.at[:, c], buffer.at[:, 1 - c], sems3, 0, b, sibling).wait_recv()

    own_sums(m.late, m.late_sem, jnp.concatenate(pack, axis=0))
    for t in range(chips):
        m.piece[t] = m.hkg[t].astype(BF16)
    for d in range(1, chips):
        t = chip(d)
        start(send_to(m.piece.at[t], m.piece_in.at[d], m.piece_sem, d, b, 2 * t + c))

    pass_on(m.gg, m.gg_sem, m.gg_sem2, 0, both_halves)
    c_half(0)
    u_begin()
    c_half(1)
    pass_on(m.gg, m.gg_sem, m.gg_sem2, 1, both_halves)
    v_across()
    c_half(2)
    pass_on(m.gg, m.gg_sem, m.gg_sem2, 2, both_halves)
    pass_on(m.gg, m.gg_sem, m.gg_sem2, 3, both_halves)
    u_half()
    for n in range(chips):
        r_quarter(n)
    r_spread()
    groups_ready(m.gg, m.gg_sem2)
    wo_own = m.wo[pl.ds(pl.multiple_of(c * half, 128), half), :]
    w = dot_nt(m.gg[...].reshape(total, width), wo_own).astype(BF16)
    for n in range(3):
        m.da[n] = w[:, n * 128 : n * 128 + 128]

    for n in range(3):
        other = (1 - c) * 3 + n
        send_to(m.ag.at[other], m.ag.at[other], m.ag_sem, n, b, sibling).wait_recv()
    columns = m.gg[:, :, :, pl.ds(pl.multiple_of(c * half, 128), half)].reshape(total, half)
    full = jnp.concatenate([m.ag[n] for n in range(6)], axis=-1)
    m.jo[3] = dot_tn(full, columns).astype(BF16).reshape(m.jo.shape[1:])
    c_begin(7)
    for j in range(3):
        c_quarter(j)
        c_spread(j)

    tops = lax.broadcasted_iota(jnp.int32, (128, total), 0) < 64
    group = m.mg[...].reshape(total, width)
    for n in range(3):
        d2 = m.da[n]
        outs = []
        for h in range(2):
            dp = dot_nt(head(d2, h), m.qkv[6 + n])
            probs = m.probs[n, h].astype(F32)
            inner = jnp.sum(probs * dp, axis=-1, keepdims=True)
            m.ds[h] = (probs * (dp - inner)).astype(BF16)
            outs.append(dot(m.ds[h], m.qkv[3 + n]))
        dq = (jnp.where(lane, outs[0], outs[1]) * factor).astype(BF16)
        dk = [dot_tn(m.qkv[n], m.ds[h]) for h in range(2)]
        dk = (jnp.where(tops, dk[0], dk[1]) * factor).T.astype(BF16)
        dv = [dot_tn(d2, m.probs[n, h]) for h in range(2)]
        dv = jnp.where(tops, dv[0], dv[1]).T.astype(BF16)
        m.dqkv[n] = dq
        m.dqkv[3 + n] = dk
        m.dqkv[6 + n] = dv
        w = dot_tn(group, jnp.concatenate([dq, dk, dv], axis=-1))
        m.jo[n] = w.astype(BF16).reshape(m.jo.shape[1:])
        c_begin(4 + n)

    v_begin()
    r_across()

    b2_copy.wait_send()
    sg_copy.wait_send()

    def partial(core):
        strip_rows = [
            jnp.concatenate(
                [
                    m.dqkv[k, pl.ds(pl.multiple_of((2 * i + core) * 64, 64), 64), :]
                    for i in range(chips)
                ],
                axis=0,
            )
            for k in range(9)
        ]
        weights = jnp.concatenate([m.wj[k] for k in range(3)], axis=-1)
        w = dot_nt(jnp.concatenate(strip_rows, axis=-1), weights)
        m.big[0, core] = w.reshape(m.big.shape[2:])

    partial(1 - c)
    start(send_to(m.big.at[0, 1 - c], m.mp_in, m.pair_sem, 4, b, sibling))
    partial(c)
    c_half(7)
    for j in range(3):
        c_across(j)
    send_to(m.big.at[0, c], m.mp_in, m.pair_sem, 4, b, sibling).wait_recv()
    for d in range(chips):
        i = chip(d)
        at = pl.ds(four * i, four)
        low = (m.big[0, c, at] + m.mp_in[at]).astype(BF16)
        if d:
            m.mo[i] = low
            start(send_to(m.mo.at[i], m.mr.at[z], m.mr_sem, d, b, 2 * i + c))
        else:
            m.mr[z] = low

    c_half(4)
    sums = m.piece[z].astype(F32)
    for d in range(1, chips):
        send_to(m.piece.at[0], m.piece_in.at[d], m.piece_sem, d, b, s).wait_recv()
        sums = sums + m.piece_in[d].astype(F32)
    m.small[b] = sums.astype(BF16)
    for e in range(1, 4):
        start(send_to(m.small.at[b], m.small.at[b], m.small_sem, e, lax.rem(b + e, 4), s))
    c_half(5)
    c_half(6)
    v_half()
    u_sum()
    to_canvases(m.late, m.late_sem, m.late_sem2)
    r_sum()
    for j in (7, 4):
        c_quarter(j)
        c_spread(j)
    for j in range(3):
        c_sum(j)
    for j in (5, 6):
        c_quarter(j)
        c_spread(j)

    for d in range(1, chips):
        i = chip(chips - d)
        send_to(m.mo.at[i], m.mr.at[i], m.mr_sem, d, b, 2 * i + c).wait_recv()
    for r in (0, rows - 1):
        for p in range(2):
            m.md[r + 1, p] = m.mr[(r % 2) * 2 + p, r // 2]
    start_edges(m.md, m.md_sem)
    c_across(7)
    for r in range(1, rows - 1):
        for p in range(2):
            m.md[r + 1, p] = m.mr[(r % 2) * 2 + p, r // 2]

    m.acc1[...] = jnp.zeros_like(m.acc1)

    def mixer_rows(low, high):
        for k in range(width // 128):
            lanes = pl.ds(k * 128, 128)
            weights = [m.mk[t : t + 1, k * 128 : k * 128 + 128] for t in range(9)]

            def line(r, p):
                return m.md[r, p, :, lanes]

            def step(r, carry):
                new = window(line, r + 2)
                three = (carry[0], carry[1], new)
                out = conv(three, weights, True)
                for p in range(2):
                    m.fg[2 * r + p, :, lanes] = out[p]
                centre = [m.fp[r + 1, p, :, lanes].astype(F32) for p in range(2)]
                return carry[1], new, tuple(taps(three, centre, carry[2]))

            begin = tuple(m.acc1[t, :, lanes] for t in range(9))
            _, _, sums = lax.fori_loop(
                low, high, step, (window(line, low), window(line, low + 1), begin), unroll=True
            )
            for t in range(9):
                m.acc1[t, :, lanes] = sums[t]

    m.acc[1] = jnp.zeros_like(m.acc[1])
    m.acc[2] = jnp.zeros_like(m.acc[2])

    def token_row(r, _):
        for p in range(2):
            rp = 2 * r + p
            grad = m.fg[rp]
            n, inv = ln_parts(m.xd[r, p].astype(F32))
            m.acc[1] += grad
            m.acc[2] += grad * n
            interleave(m.rowf, r, p, m.rg[rp] + ln_back(grad * scale1, n, inv))
        m.tgo[r] = joined(m.rowf, r)
        return 0

    mixer_rows(1, rows - 1)
    lax.fori_loop(1, rows - 1, token_row, 0, unroll=3)
    c_across(4)
    v_sum()
    c_across(5)
    top_edge(m.md, m.md_sem)
    mixer_rows(0, 1)
    token_row(0, 0)
    bottom_edge(m.md, m.md_sem)
    mixer_rows(rows - 1, rows)
    token_row(rows - 1, 0)
    tg_copy = pltpu.make_async_copy(m.tgo, m.tg_hbm, m.load_sem.at[14])
    tg_copy.start()

    pack = []
    third = width // 3
    for v in (m.acc[1], m.acc[2]):
        pair = halves(v)
        for h in range(2):
            pack += [pair[h : h + 1, k * third : k * third + third] for k in range(3)]
    pack.append(jnp.zeros((4, third), F32))
    own_sums(m.early, m.early_sem, jnp.concatenate(pack, axis=0))
    mixer_sums = [jnp.sum(m.acc1[t], axis=0, keepdims=True) for t in range(9)]
    mixer_sums += [jnp.sum(m.acc[k], axis=0, keepdims=True) for k in (4, 0)]
    mixer_sums = jnp.concatenate(mixer_sums + [jnp.zeros((5, width), F32)], axis=0)
    pad_lanes = jnp.zeros((16, 128 - own), F32)
    for t in range(strips):
        m.mpiece[t] = jnp.concatenate(
            [mixer_sums[:, t * own : t * own + own], pad_lanes], axis=1
        ).astype(BF16)
    for d in range(1, strips):
        t = lax.rem(s + d, strips)
        start(send_to(m.mpiece.at[t], m.mpiece_in.at[d], m.mpiece_sem, d, b, t))

    c_across(6)
    c_sum(7)
    c_sum(4)
    for g in range(3):
        r_relay(g, False)
    for i in range(2):
        c_relay(i, i % 2 == 0)
    c_sum(5)
    to_canvases(m.early, m.early_sem, m.early_sem2)
    c_sum(6)
    sums = m.mpiece[s].astype(F32)
    for d in range(1, strips):
        send_to(m.mpiece.at[0], m.mpiece_in.at[d], m.mpiece_sem, d, b, s).wait_recv()
        sums = sums + m.mpiece_in[d].astype(F32)
    m.msmall[b] = sums.astype(BF16)
    for e in range(1, 4):
        start(send_to(m.msmall.at[b], m.msmall.at[b], m.msmall_sem, e, lax.rem(b + e, 4), s))
    for i in range(2, 4):
        c_relay(i, i % 2 == 0)
    j_order = (7, 4, 5, 6)
    for i in range(4):
        c_relay(j_order[i], i % 2 == 0)
    to_sibling(m.late, m.late_sem2, m.late_sem3)
    to_sibling(m.early, m.early_sem2, m.early_sem3)

    finals = []

    def store(src, dst, index):
        cp = pltpu.make_async_copy(src, dst, m.load_sem.at[index])
        cp.start()
        finals.append(cp)

    for e in range(1, 4):
        i = lax.rem(b - e + 4, 4)
        send_to(m.cond_all.at[i], m.cond_all.at[i], m.cond_sem, e, i, s).wait_recv()
        send_to(m.small.at[i], m.small.at[i], m.small_sem, e, i, s).wait_recv()
        send_to(m.msmall.at[i], m.msmall.at[i], m.msmall_sem, e, i, s).wait_recv()
    for g in range(3):
        r_arrive(g)
    store(m.r_all, m.r_hbm, 15)
    store(m.cond_all, m.cond_hbm, 16)
    store(m.small, m.small_hbm, 17)
    store(m.msmall, m.msmall_hbm, 18)
    from_sibling(m.late, m.late_sem3)
    from_sibling(m.early, m.early_sem3)
    store(m.late, m.late_hbm, 19)
    store(m.early, m.early_hbm, 20)
    for i in range(4):
        c_arrive(i, i % 2 == 0)
    store(m.c_all.at[pl.ds(0, 4)], m.c_hbm.at[pl.ds(0, 4)], 35)
    for i in range(4):
        c_arrive(j_order[i], i % 2 == 0)
    store(m.c_all.at[pl.ds(4, 4)], m.c_hbm.at[pl.ds(4, 4)], 21)
    for cp in sent:
        cp.wait_send()
    edges_sent(m.fp, m.fp_sem)
    edges_sent(m.md, m.md_sem)

    for n in range(chips):
        halo_sent(m.ex, m.ex_sem, n)
        halo_sent(m.cg, m.cg_sem, n)
    for h in range(2):
        u_one(h).wait_send()
        u_two(h).wait_send()
        for n in range(chips):
            r_one(n, h).wait_send()
            r_two(n, h).wait_send()
        v_one(h).wait_send()
        v_two(h).wait_send()
        for j in (0, 1, 2, 4, 5, 6, 7):
            c_one(j, h).wait_send()
            c_two(j, h).wait_send()
    for k in range(3):
        r_three(k).wait_send()
        u_three(k).wait_send()
        r_four(k, 0).wait_send()
        r_four(k, 1).wait_send()
        r_relay(k, True)
        v_three(k).wait_send()
        for j in (0, 1, 2, 4, 5, 6, 7):
            c_three(j, k).wait_send()

    for i in range(4):
        c_gone(i, i % 2 == 0)
        c_gone(j_order[i], i % 2 == 0)
    out_copy.wait()
    tg_copy.wait()
    for cp in finals:
        cp.wait()


def block(
    tokens, mixer, owner, steps, labels, emb, aw, ab, ob, eb, hk, rb, wj, wo, we, wr, cot, strips
):
    rows, cols, width = tokens.shape
    chips = strips // 2
    half = width // 2
    total = strips * 64
    blocks = 2 * rows
    chip_rows = 2 * rows
    part = width // chips // 4
    third = width // 3
    cond = (steps.shape[1], width + 256)
    shape = jax.ShapeDtypeStruct
    vm = pltpu.VMEM

    def dma(*size):
        return pltpu.SemaphoreType.DMA(size)

    ins = dict(
        tok=tokens, mixer=mixer, owner=owner, steps=steps, labels=labels, ab=ab, ob=ob, eb=eb,
        hidden=hk, rb=rb, emb_hbm=emb, aw4_hbm=aw.reshape(2, 2, width // 4, 6 * width),
        aw5_hbm=aw.reshape(chips, 2, 2, part, 6 * width), wj_hbm=wj, wo_hbm=wo, we_hbm=we, wr_hbm=wr, cot_hbm=cot,
    )
    outs = dict(
        out_hbm=shape((rows, cols, width), BF16),
        tg_hbm=shape((rows, cols, width), F32),
        r_hbm=shape((4, 3, width // 12, half), BF16),
        c_hbm=shape((8, 2, 2, part, half), BF16),
        cond_hbm=shape((4,) + cond, F32),
        small_hbm=shape((4, 16, half), BF16),
        msmall_hbm=shape((4, 16, 128), BF16),
        late_hbm=shape((4, 2, chips, 16, half), BF16),
        early_hbm=shape((4, 2, chips, 16, third), BF16),
    )
    scratch = dict(
        emb=vm(emb.shape, BF16),
        mod=vm((2, 6 * width), F32),
        mk=vm((9, width), F32),
        ebf=vm((1, 2 * chips * half), F32),
        hk=vm((chips, 9, half), F32),
        wj=vm((3, width, half), BF16),
        wo=vm((width, width), BF16),
        we=vm((width, chips * half), BF16),
        wr=vm((chips * half, width), BF16),
        cot=vm((rows, cols, width), BF16),
        cond_all=vm((4,) + cond, F32),
        rowf=vm((rows, width // 128, cols, 128), F32),
        xd=vm((rows, 2, 16, width), BF16),
        fp=vm((rows + 2, 2, 16, width), BF16),
        ms=vm((chips, rows // 2, 16, width), BF16),
        mg=vm((strips, rows // 2, 16, width), BF16),
        qkv=vm((9, total, 128), BF16),
        probs=vm((3, 2, total, total), BF16),
        ag=vm((6, total, 128), BF16),
        ai=vm((6, chips, 64, 128), BF16),
        acc=vm((6, 16, width), F32),
        acc1=vm((9, 8, width), F32),
        ctd=vm((blocks, 16, width), BF16),
        tg=vm((2, blocks, 16, width), BF16),
        sc=vm((2, blocks, 16, width), BF16),
        b1=vm((blocks, 16, width), F32),
        res=vm((blocks, 16, width), F32),
        ex=vm((chip_rows + 2, 2, 16, chips * half), BF16),
        cg=vm((chip_rows + 2, 2, 16, chips * half), BF16),
        act=vm((2 * blocks, 16, chips * half), BF16),
        big=vm((2, 2, blocks, 16, width), F32),
        b2_in=vm((blocks, 16, width), F32),
        sg_in=vm((blocks, 16, width), F32),
        hkg=vm((chips, 16, half), F32),
        rg=vm((blocks, 16, width), F32),
        og=vm((chips, rows // 2, 16, width), BF16),
        out=vm((rows, cols, width), BF16),
        gg=vm((strips, rows // 2, 16, width), BF16),
        da=vm((3, total, 128), BF16),
        ds=vm((2, total, total), BF16),
        dqkv=vm((9, total, 128), BF16),
        mp_in=vm((blocks, 16, width), F32),
        mo=vm((chips, rows // 2, 16, width), BF16),
        mr=vm((chips, rows // 2, 16, width), BF16),
        md=vm((rows + 2, 2, 16, width), BF16),
        fg=vm((blocks, 16, width), F32),
        tgo=vm((rows, cols, width), F32),
        rw=vm((chips, 2, 2, width // 4, half), BF16),
        r1=vm((chips, 2, 2, width // 12, half), BF16),
        r2=vm((chips, 2, width // 12, half), BF16),
        r3=vm((3, 2, width // 12, half), BF16),
        u3=vm((3, 2, 2, width // 12, half), BF16),
        u0=vm((2, 2, width // 12, half), BF16),
        u1=vm((2, 2, width // 24, half), BF16),
        u2=vm((2, width // 24, half), BF16),
        r_all=vm((4, 3, width // 12, half), BF16),
        ew=vm((4, chips, 2, 2, part, half), BF16),
        jo=vm((4, chips, 2, 2, part, half), BF16),
        c1=vm((8, 2, 2, 2, part, half), BF16),
        c2=vm((8, chips, part, half), BF16),
        c3=vm((8, 3, part, half), BF16),
        c_out=vm((8, part, half), BF16),
        c_all=vm((8, 2, 2, part, half), BF16),
        v3=vm((3, 2, 2, part, half), BF16),
        v0=vm((2, 2, part, half), BF16),
        v1a=vm((2, 32, half), BF16),
        v1b=vm((2, part - 32, half), BF16),
        v2a=vm((32, half), BF16),
        v2b=vm((part - 32, half), BF16),
        late=vm((4, 2, chips, 16, half), BF16),
        early=vm((4, 2, chips, 16, third), BF16),
        piece=vm((chips, 16, half), BF16),
        piece_in=vm((chips, 16, half), BF16),
        small=vm((4, 16, half), BF16),
        mpiece=vm((strips, 16, 128), BF16),
        mpiece_in=vm((strips, 16, 128), BF16),
        msmall=vm((4, 16, 128), BF16),
        load_sem=dma(36),
    )
    pairs = dict(
        cond_sem=(4,), fp_sem=(2,), md_sem=(2,), mg_sem=(2, chips), mg_sem2=(chips,),
        gg_sem=(2, chips), gg_sem2=(chips,), ai_sem=(3, strips), ag_sem=(3,), pair_sem=(5,),
        ex_sem=(2, chips), cg_sem=(2, chips), mr_sem=(chips,),
        r1_sem=(chips, 2), r2_sem=(chips, 2), r3_sem=(3,), r4_sem=(3, 3), u3_sem=(3,), u1_sem=(2,), u2_sem=(2,),
        v3_sem=(3,), v1_sem=(2,), v2_sem=(2,),
        c1_sem=(8, 2), c2_sem=(8, 2), c3_sem=(8, 3),
        late_sem=(chips,), late_sem2=(4,), late_sem3=(1,),
        early_sem=(chips,), early_sem2=(4,), early_sem3=(1,),
        piece_sem=(chips,), small_sem=(4,), mpiece_sem=(strips,), msmall_sem=(4,),
    )
    names = list(ins) + list(outs) + list(scratch)
    shapes = list(scratch.values())
    for size in list(pairs.values()):
        shapes += [dma(*size), dma(*size)]
    shapes += [dma(8, 4), dma(8, 4, 2)]
    plain = len(names)

    def kernel(*refs):
        named = list(refs[:plain])
        sems = refs[plain:]
        both = [(sems[2 * i], sems[2 * i + 1]) for i in range(len(sems) // 2)]
        block_kernel(names + list(pairs) + ["c4_sem"], *named, *both)

    return pl.pallas_call(
        kernel,
        name="block",
        out_shape=tuple(outs.values()),
        in_specs=[WHOLE] * 2 + [SCALARS] * 3 + [WHOLE] * 5 + [LEFT] * 8,
        out_specs=(LEFT,) * len(outs),
        scratch_shapes=shapes,
        compiler_params=pltpu.CompilerParams(
            collective_id=0, has_side_effects=True, vmem_limit_bytes=VMEM_BYTES
        ),
    )(*ins.values())


def final_kernel(
    out_in, tg_in, r_in, c_in, cond_ref, small_ref, msmall_ref, late_ref, early_ref, aw_hbm,
    out_ref, tg_ref, tab_ref, ad_out, ab_ref, mix_ref, joint_out, output_out, ob_ref,
    expand_out, eb_ref, hidden_ref, reduce_out, rb_ref,
    aw, out_v, tg_v, r_ref, c_ref, ad_ref, joint_ref, output_ref, expand_ref, reduce_ref, sem,
):
    s = lax.axis_index("strip")
    strips = lax.axis_size("strip")
    width = cond_ref.shape[2] - 256
    own = width // strips
    half = width // 2
    loads = [
        (r_in, r_ref),
        (c_in, c_ref),
        (aw_hbm.at[pl.ds(pl.multiple_of(s * own, 16), own)], aw),
        (out_in, out_v),
        (tg_in, tg_v),
    ]
    loads = [pltpu.make_async_copy(a, v, sem.at[i]) for i, (a, v) in enumerate(loads)]
    for cp in loads:
        cp.start()
    stores = []

    def store(src, dst):
        cp = pltpu.make_async_copy(src, dst, sem.at[5 + len(stores)])
        cp.start()
        stores.append(cp)

    small = small_ref[0].astype(F32)
    mixer = msmall_ref[0].astype(F32)
    for i in range(1, 4):
        small = small + small_ref[i].astype(F32)
        mixer = mixer + msmall_ref[i].astype(F32)
    hidden_ref[...] = small[0:9]
    eb_ref[...] = small[9]
    ob_ref[...] = mixer[9, 0:own]
    rb_ref[...] = mixer[10, 0:own]
    mix_ref[...] = mixer[0:9, 0:own]

    n = width // 4
    loads[0].wait()
    for q in range(4):
        reduce_ref[:, q * n : q * n + n] = r_ref[q].reshape(n, half).astype(F32).T
    store(reduce_ref, reduce_out)
    loads[1].wait()
    part = c_ref.shape[3]
    for xs in range(2):
        rows = slice(xs * part, xs * part + part)
        for cs in range(2):
            for k in range(4):
                at = (2 * k + cs) * half
                expand_ref[rows, at : at + half] = c_ref[k, xs, cs].astype(F32)
            for k in range(3):
                for p in range(3):
                    at = p * width + cs * half + k * 128
                    joint_ref[rows, at : at + 128] = c_ref[
                        4 + k, xs, cs, :, p * 128 : p * 128 + 128
                    ].astype(F32)
            output_ref[rows, cs * half : cs * half + half] = c_ref[7, xs, cs].astype(F32)
    store(expand_ref, expand_out)
    store(joint_ref, joint_out)
    store(output_ref, output_out)
    loads[3].wait()
    store(out_v, out_ref)
    loads[4].wait()
    store(tg_v, tg_ref)

    slots = 32
    condition = cond_ref[...].reshape(slots, width + 256)
    labels = condition[:, width : width + 1]
    slot_late = jnp.concatenate([cond_ref[i, 0:1, width + 128 :] for i in range(4)], axis=1)
    slot_early = jnp.concatenate([cond_ref[i, 1:2, width + 128 :] for i in range(4)], axis=1)
    condition = condition[:, 0:width]
    pick = lax.broadcasted_iota(jnp.int32, (width, own), 0) == (
        lax.broadcasted_iota(jnp.int32, (width, own), 1) + s * own
    )
    pick = jnp.where(pick, 1.0, 0.0)
    condition = jnp.dot(
        condition, pick, precision=lax.Precision.HIGHEST, preferred_element_type=F32
    )
    sigmoid = 1.0 / (1.0 + jnp.exp(-condition))
    silu = (condition * sigmoid).astype(BF16)
    slope = sigmoid * (1.0 + condition * (1.0 - sigmoid))

    count = 4 * strips * 16

    def by_slot(source, slot, parts, period):
        groups = parts * (16 // period)
        index = lax.broadcasted_iota(jnp.int32, (groups * slots, count), 0)
        row = lax.rem(lax.broadcasted_iota(jnp.int32, (groups * slots, count), 1), 16)
        group = index // slots
        mine = jnp.logical_and(
            row // period == group // parts, lax.rem(row, parts) == lax.rem(group, parts)
        )
        mine = jnp.logical_and(mine, lax.rem(index, slots) == slot.astype(jnp.int32))
        grad = dot(jnp.where(mine, 1.0, 0.0).astype(BF16), source[...].reshape(count, source.shape[-1]))
        return [grad[k * slots : k * slots + slots] for k in range(groups)]

    pieces = by_slot(early_ref, slot_early, 3, 6) + by_slot(late_ref, slot_late, 2, 4)
    grad = jnp.concatenate(pieces, axis=1)
    sums = jnp.sum(grad, axis=0, keepdims=True)
    low = grad.astype(BF16)
    ad_ref[...] = dot_tn(silu, low)
    loads[2].wait()
    silu_grad = dot_nt(low, aw[...])
    store(ad_ref, ad_out)
    bias = jnp.zeros((1, 6 * own), F32)
    for t in range(strips):
        bias = jnp.where(s == t, sums[:, t * 6 * own : t * 6 * own + 6 * own], bias)
    ab_ref[...] = bias[0]
    classes = tab_ref.shape[1]
    onehot = lax.broadcasted_iota(jnp.int32, (slots, classes), 1) == labels.astype(jnp.int32)
    tab_ref[...] = lax.dot_general(
        silu_grad * slope,
        jnp.where(onehot, 1.0, 0.0),
        TN,
        precision=lax.Precision.HIGHEST,
        preferred_element_type=F32,
    )
    for cp in stores:
        cp.wait()


def final(parts, aw, classes, strips):
    out, tg, r, c = parts[:4]
    width = out.shape[-1]
    own = width // strips
    half = width // 2
    shape = jax.ShapeDtypeStruct
    vm = pltpu.VMEM
    return pl.pallas_call(
        final_kernel,
        name="final",
        out_shape=(
            shape(out.shape, BF16),
            shape(tg.shape, F32),
            shape((own, classes), F32),
            shape((own, 6 * width), F32),
            shape((6 * own,), F32),
            shape((9, own), F32),
            shape((own, 3 * width), F32),
            shape((own, width), F32),
            shape((own,), F32),
            shape((own, 4 * width), F32),
            shape((half,), F32),
            shape((9, half), F32),
            shape((half, width), F32),
            shape((own,), F32),
        ),
        in_specs=[LEFT] * 4 + [WHOLE] * 5 + [LEFT],
        out_specs=(
            LEFT, LEFT, WHOLE, LEFT, WHOLE, WHOLE, LEFT, LEFT, WHOLE, LEFT, WHOLE, WHOLE, LEFT,
            WHOLE,
        ),
        scratch_shapes=[
            vm((own, 6 * width), BF16),
            vm(out.shape, BF16),
            vm(tg.shape, F32),
            vm(r.shape, BF16),
            vm(c.shape, BF16),
            vm((own, 6 * width), F32),
            vm((own, 3 * width), F32),
            vm((own, width), F32),
            vm((own, 4 * width), F32),
            vm((half, width), F32),
            pltpu.SemaphoreType.DMA((12,)),
        ],
        compiler_params=pltpu.CompilerParams(vmem_limit_bytes=VMEM_BYTES),
    )(*parts, aw)


def local_grouped(
    tokens, tile_owner, time_steps, class_labels, class_embedding_matrix, adaptive_weight,
    adaptive_bias, mixer_kernel, joint_weight, output_weight, output_bias, expand_weight,
    expand_bias, hidden_kernel, reduce_weight, reduce_bias, output_cotangent,
):
    strips = lax.axis_size("strip")
    owner = tile_owner.transpose(0, 2, 1)
    parts = block(
        tokens[0], mixer_kernel.T, owner, time_steps, class_labels, class_embedding_matrix.T,
        adaptive_weight, adaptive_bias, output_bias, expand_bias, hidden_kernel.T, reduce_bias,
        joint_weight, output_weight, expand_weight, reduce_weight, output_cotangent[0], strips,
    )
    classes = class_embedding_matrix.shape[1]
    (
        out, tg, table, adaptive, bias, mixer, joint, output, ob, expand, eb, hidden, reduce, rb,
    ) = final(parts, adaptive_weight, classes, strips)
    return (
        out[None], tg[None], table, adaptive, bias, mixer.T, joint, output, ob, expand, eb,
        hidden.T, reduce, rb,
    )


EXACT_PRECISION = lax.Precision.HIGHEST


def padded_2(block, sides, width):
    for axis, dim in sides:
        count = lax.axis_size(axis)
        forward = [(i, i + 1) for i in range(count - 1)]
        backward = [(target, source) for source, target in forward]
        low = lax.ppermute(
            lax.slice_in_dim(block, block.shape[dim] - width, None, axis=dim), axis, forward
        )
        high = lax.ppermute(lax.slice_in_dim(block, 0, width, axis=dim), axis, backward)
        block = jnp.concatenate([low, block, high], axis=dim)
    return block


def normalize(values):
    centre = jnp.mean(values, axis=-1, keepdims=True)
    centred = values - centre
    spread = jnp.mean(centred * centred, axis=-1, keepdims=True)
    return centred * lax.rsqrt(spread + EPSILON)


def modulate(values, shifting, scaling):
    return normalize(values) * (1.0 + scaling) + shifting


def depthwise(padded, kernel):
    row_count = padded.shape[-3] - 2
    column_total = padded.shape[-2]
    widened = jnp.pad(padded, [(0, 0)] * (padded.ndim - 2) + [(1, 1), (0, 0)])
    result = jnp.zeros(
        padded.shape[:-3] + (row_count, column_total, padded.shape[-1]), padded.dtype
    )
    for tapping in range(9):
        row_shift = tapping // 3
        col_shift = tapping % 3
        window = lax.slice_in_dim(widened, row_shift, row_shift + row_count, axis=widened.ndim - 3)
        window = lax.slice_in_dim(
            window, col_shift, col_shift + column_total, axis=widened.ndim - 2
        )
        result = result + kernel[:, tapping] * window
    return result


def kernel_grad(padded, gradient):
    row_count = gradient.shape[1]
    column_total = gradient.shape[2]
    widened = jnp.pad(padded, ((0, 0), (0, 0), (1, 1), (0, 0)))
    columns = []
    for tapping in range(9):
        row_shift = tapping // 3
        col_shift = tapping % 3
        window = widened[
            :, row_shift : row_shift + row_count, col_shift : col_shift + column_total, :
        ]
        columns.append(jnp.sum(window * gradient, axis=(0, 1, 2)))
    return jnp.stack(columns, axis=1)


def timestep_features(time_steps, model_width):
    half_width = model_width // 2
    frequencies = jnp.exp(
        -math.log(10000.0) * jnp.arange(half_width, dtype=jnp.float32) / half_width
    )
    angles = time_steps.astype(jnp.float32)[..., None] * frequencies
    return jnp.concatenate([jnp.cos(angles), jnp.sin(angles)], axis=-1)


def group_owner(owner):
    canvases, row_count, column_total = owner.shape
    shaped = owner.reshape(canvases, row_count // 2, 2, column_total // 2, 2).transpose(
        0, 2, 4, 1, 3
    )
    return shaped.reshape(canvases, 2, 2, row_count // 2 * (column_total // 2))


def to_groups(tensor, head_count):
    canvases, row_count, column_total, features = tensor.shape
    head_size = features // head_count
    shaped = tensor.reshape(
        canvases, row_count // 2, 2, column_total // 2, 2, head_count, head_size
    )
    shaped = shaped.transpose(0, 2, 4, 5, 1, 3, 6)
    return shaped.reshape(
        canvases, 2, 2, head_count, row_count // 2 * (column_total // 2), head_size
    )


def from_groups(tensor, row_count, column_total):
    canvases, head_count, head_size = (tensor.shape[0], tensor.shape[3], tensor.shape[-1])
    shaped = tensor.reshape(
        canvases, 2, 2, head_count, row_count // 2, column_total // 2, head_size
    )
    shaped = shaped.transpose(0, 4, 1, 5, 2, 3, 6)
    return shaped.reshape(canvases, row_count, column_total, head_count * head_size)


def local(
    tokens,
    tile_owner,
    time_steps,
    class_labels,
    class_embedding_matrix,
    adaptive_weight,
    adaptive_bias,
    mixer_kernel,
    joint_weight,
    output_weight,
    output_bias,
    expand_weight,
    expand_bias,
    hidden_kernel,
    reduce_weight,
    reduce_bias,
    output_cotangent,
):
    canvases, row_count, column_total, model_width = tokens.shape
    head_count = HEADS
    head_size = model_width // head_count
    factor = head_size ** (-0.5)
    half_cols = column_total // 2
    strips = lax.axis_size("strip")
    strip_index = lax.axis_index("strip")
    canvas_rows = row_count * strips
    class_count = class_embedding_matrix.shape[1]
    latent_count = time_steps.shape[1]
    tile_rows = canvas_rows // 4
    full_owner = jnp.broadcast_to(
        tile_owner[:, :, None, :, None], (canvases, 4, tile_rows, 2, half_cols)
    ).reshape(canvases, canvas_rows, column_total)
    local_owner = lax.dynamic_slice_in_dim(full_owner, strip_index * row_count, row_count, 1)
    token_hot = (local_owner[..., None] == jnp.arange(latent_count, dtype=jnp.int32)).astype(
        jnp.float32
    )
    class_onehot = (class_labels[..., None] == jnp.arange(class_count, dtype=jnp.int32)).astype(
        jnp.bfloat16
    )
    class_rows = jnp.einsum(
        "ywj,gj->ywg", class_onehot, class_embedding_matrix, preferred_element_type=jnp.float32
    )
    condition = timestep_features(time_steps, model_width) + class_rows
    silu_value, silu_pull = jax.vjp(jax.nn.silu, condition)
    silu_cond = silu_value.astype(jnp.bfloat16)
    modulation = jnp.einsum(
        "cbd,de->cbe", silu_cond, adaptive_weight, preferred_element_type=jnp.float32
    )
    modulation = modulation + adaptive_bias.astype(jnp.float32)
    token_mod = jnp.einsum("crkb,cbe->crke", token_hot, modulation, precision=EXACT_PRECISION)
    shift_one, scale_one, gate_one, shift_two, scale_two, gate_two = jnp.split(
        token_mod, 6, axis=-1
    )
    inputs = tokens.astype(jnp.float32)
    first_value, first_pull = jax.vjp(modulate, inputs, shift_one, scale_one)
    first = first_value.astype(jnp.bfloat16)
    first_padded = padded_2(first, (("strip", 1),), 1)
    mixer_single_float = mixer_kernel.astype(jnp.float32)
    mixed = depthwise(first_padded.astype(jnp.float32), mixer_single_float).astype(jnp.bfloat16)
    joint = jnp.einsum("crkd,de->crke", mixed, joint_weight, preferred_element_type=jnp.float32)
    query_rows = joint[..., :model_width].astype(jnp.bfloat16)
    keys_local = joint[..., model_width : 2 * model_width].astype(jnp.bfloat16)
    values_local = joint[..., 2 * model_width :].astype(jnp.bfloat16)
    keys_canvas, values_canvas = (
        lax.all_gather(keys_local, "strip", axis=1, tiled=True),
        lax.all_gather(values_local, "strip", axis=1, tiled=True),
    )
    query_groups = to_groups(query_rows, head_count)
    key_groups = to_groups(keys_canvas, head_count)
    value_groups = to_groups(values_canvas, head_count)
    query_owner = group_owner(local_owner)
    key_owner = group_owner(full_owner)
    allowed = (query_owner[..., :, None] == key_owner[..., None, :])[:, :, :, None]

    def attention_scores():
        raw = (
            jnp.einsum(
                "cabhnd,cabhmd->cabhnm",
                query_groups,
                key_groups,
                preferred_element_type=jnp.float32,
            )
            * factor
        )
        return jnp.where(allowed, raw, MASKED)

    scores = attention_scores()
    peak = jnp.max(scores, axis=-1, keepdims=True)
    lifted_float = jnp.exp(scores - peak)
    total = jnp.sum(lifted_float, axis=-1, keepdims=True)
    softened = (lifted_float / total).astype(jnp.bfloat16)
    log_total = peak + jnp.log(total)
    attended_groups = jnp.einsum(
        "cabhnm,cabhmd->cabhnd", softened, value_groups, preferred_element_type=jnp.float32
    )
    attended = from_groups(attended_groups, row_count, column_total).astype(jnp.bfloat16)
    branch_one = jnp.einsum(
        "crkd,de->crke", attended, output_weight, preferred_element_type=jnp.float32
    )
    branch_one = branch_one + output_bias.astype(jnp.float32)
    residual = inputs + gate_one * branch_one
    second_value, second_pull = jax.vjp(modulate, residual, shift_two, scale_two)
    second = second_value.astype(jnp.bfloat16)
    expanded = jnp.einsum(
        "crkd,df->crkf", second, expand_weight, preferred_element_type=jnp.float32
    )
    expanded = (expanded + expand_bias.astype(jnp.float32)).astype(jnp.bfloat16)
    expanded_padded = padded_2(expanded, (("strip", 1),), 1)
    hidden_float = hidden_kernel.astype(jnp.float32)
    conv_out = depthwise(expanded_padded.astype(jnp.float32), hidden_float)
    gelu_value, gelu_pull = jax.vjp(jax.nn.gelu, conv_out)
    activated = gelu_value.astype(jnp.bfloat16)
    branch_two = jnp.einsum(
        "crkf,fd->crkd", activated, reduce_weight, preferred_element_type=jnp.float32
    )
    branch_two = branch_two + reduce_bias.astype(jnp.float32)
    outputs = (residual + gate_two * branch_two).astype(jnp.bfloat16)
    upstream = output_cotangent.astype(jnp.float32)
    two_grad = (upstream * gate_two).astype(jnp.bfloat16)
    gate_two_grad = upstream * branch_two
    reduce_bias_grad = jnp.sum(two_grad.astype(jnp.float32), axis=(0, 1, 2))
    reduce_weight_grad = jnp.einsum(
        "crkf,crkd->fd", activated, two_grad, preferred_element_type=jnp.float32
    )
    activated_grad = jnp.einsum(
        "crkd,fd->crkf", two_grad, reduce_weight, preferred_element_type=jnp.float32
    )
    conv_grad = gelu_pull(activated_grad)[0].astype(jnp.bfloat16)
    conv_padded = padded_2(conv_grad, (("strip", 1),), 1)
    expanded_grad = depthwise(conv_padded.astype(jnp.float32), hidden_float[:, ::-1]).astype(
        jnp.bfloat16
    )
    hidden_kernel_grad = kernel_grad(
        expanded_padded.astype(jnp.float32), conv_grad.astype(jnp.float32)
    )
    expand_bias_grad = jnp.sum(expanded_grad.astype(jnp.float32), axis=(0, 1, 2))
    expand_weight_grad = jnp.einsum(
        "crkd,crkf->df", second, expanded_grad, preferred_element_type=jnp.float32
    )
    second_grad = jnp.einsum(
        "crkf,df->crkd", expanded_grad, expand_weight, preferred_element_type=jnp.float32
    )
    residual_part, shift_two_grad, scale_two_grad = second_pull(second_grad)
    residual_grad = upstream + residual_part
    gate_one_grad = residual_grad * branch_one
    one_grad = (residual_grad * gate_one).astype(jnp.bfloat16)
    output_bias_grad = jnp.sum(one_grad.astype(jnp.float32), axis=(0, 1, 2))
    output_weight_grad = jnp.einsum(
        "crkd,crke->de", attended, one_grad, preferred_element_type=jnp.float32
    )
    attended_grad = jnp.einsum(
        "crke,de->crkd", one_grad, output_weight, preferred_element_type=jnp.float32
    ).astype(jnp.bfloat16)
    attended_grad_groups = to_groups(attended_grad, head_count)
    probs = jnp.exp(attention_scores() - log_total)
    prob_grads = jnp.einsum(
        "cabhnd,cabhmd->cabhnm",
        attended_grad_groups,
        value_groups,
        preferred_element_type=jnp.float32,
    )
    spread_sum = jnp.sum(probs * prob_grads, axis=-1, keepdims=True)
    score_grads = (probs * (prob_grads - spread_sum)).astype(jnp.bfloat16)
    query_grad_groups = (
        jnp.einsum(
            "cabhnm,cabhmd->cabhnd", score_grads, key_groups, preferred_element_type=jnp.float32
        )
        * factor
    )
    query_grad = from_groups(query_grad_groups, row_count, column_total).astype(jnp.bfloat16)
    all_queries, all_attended = (
        lax.all_gather(query_groups, "strip", axis=4, tiled=True),
        lax.all_gather(attended_grad_groups, "strip", axis=4, tiled=True),
    )
    all_logs, all_spreads = (
        lax.all_gather(log_total[..., 0], "strip", axis=4, tiled=True),
        lax.all_gather(spread_sum[..., 0], "strip", axis=4, tiled=True),
    )
    own_keys = to_groups(keys_local, head_count)
    own_values = to_groups(values_local, head_count)
    own_allowed = (key_owner[..., :, None] == query_owner[..., None, :])[:, :, :, None]
    own_scores = (
        jnp.einsum(
            "cabhnd,cabhmd->cabhnm", all_queries, own_keys, preferred_element_type=jnp.float32
        )
        * factor
    )
    own_scores = jnp.where(own_allowed, own_scores, MASKED)
    own_probs = jnp.exp(own_scores - all_logs[..., None])
    own_prob_grads = jnp.einsum(
        "cabhnd,cabhmd->cabhnm", all_attended, own_values, preferred_element_type=jnp.float32
    )
    own_score_grads = (own_probs * (own_prob_grads - all_spreads[..., None])).astype(jnp.bfloat16)
    key_grad_groups = (
        jnp.einsum(
            "cabhnm,cabhnd->cabhmd",
            own_score_grads,
            all_queries,
            preferred_element_type=jnp.float32,
        )
        * factor
    )
    value_grad_groups = jnp.einsum(
        "cabhnm,cabhnd->cabhmd",
        own_probs.astype(jnp.bfloat16),
        all_attended,
        preferred_element_type=jnp.float32,
    )
    key_grad = from_groups(key_grad_groups, row_count, column_total).astype(jnp.bfloat16)
    value_grad = from_groups(value_grad_groups, row_count, column_total).astype(jnp.bfloat16)
    joint_grad = jnp.concatenate([query_grad, key_grad, value_grad], axis=-1)
    joint_weight_grad = jnp.einsum(
        "crkd,crke->de", mixed, joint_grad, preferred_element_type=jnp.float32
    )
    mixed_grad = jnp.einsum(
        "crke,de->crkd", joint_grad, joint_weight, preferred_element_type=jnp.float32
    ).astype(jnp.bfloat16)
    mixed_padded = padded_2(mixed_grad, (("strip", 1),), 1)
    first_grad = depthwise(mixed_padded.astype(jnp.float32), mixer_single_float[:, ::-1])
    mixer_kernel_grad = kernel_grad(
        first_padded.astype(jnp.float32), mixed_grad.astype(jnp.float32)
    )
    input_part, shift_one_grad, scale_one_grad = first_pull(first_grad)
    tokens_grad = residual_grad + input_part
    token_grad = jnp.concatenate(
        [
            shift_one_grad,
            scale_one_grad,
            gate_one_grad,
            shift_two_grad,
            scale_two_grad,
            gate_two_grad,
        ],
        axis=-1,
    )
    modulation_grad = jnp.einsum("crkb,crke->cbe", token_hot, token_grad, precision=EXACT_PRECISION)
    silu_grad = jnp.einsum(
        "cbe,de->cbd",
        modulation_grad,
        adaptive_weight.astype(jnp.float32),
        precision=EXACT_PRECISION,
    )
    conditioning_grad = silu_pull(silu_grad)[0]
    table_grad = jnp.einsum(
        "soy,sok->yk",
        conditioning_grad,
        class_onehot.astype(jnp.float32),
        precision=EXACT_PRECISION,
    )
    adaptive_grad = jnp.einsum(
        "cbd,cbe->de", silu_cond.astype(jnp.float32), modulation_grad, precision=EXACT_PRECISION
    )
    adaptive_bias_grad = jnp.sum(modulation_grad, axis=(0, 1))
    (
        table_shard,
        adaptive_shard,
        adaptive_bias_shard,
        mixer_shard,
        joint_shard,
        output_shard,
        output_bias_shard,
        expand_shard,
        expand_bias_shard,
        hidden_shard,
        reduce_shard,
        reduce_bias_shard,
    ) = (
        lax.psum_scatter(
            table_grad.astype(jnp.bfloat16), "strip", scatter_dimension=0, tiled=True
        ).astype(jnp.float32),
        lax.psum_scatter(
            adaptive_grad.astype(jnp.bfloat16), "strip", scatter_dimension=0, tiled=True
        ).astype(jnp.float32),
        lax.psum_scatter(
            adaptive_bias_grad.astype(jnp.bfloat16), "strip", scatter_dimension=0, tiled=True
        ).astype(jnp.float32),
        lax.psum_scatter(
            mixer_kernel_grad.astype(jnp.bfloat16), "strip", scatter_dimension=0, tiled=True
        ).astype(jnp.float32),
        lax.psum_scatter(
            joint_weight_grad.astype(jnp.bfloat16), "strip", scatter_dimension=0, tiled=True
        ).astype(jnp.float32),
        lax.psum_scatter(
            output_weight_grad.astype(jnp.bfloat16), "strip", scatter_dimension=0, tiled=True
        ).astype(jnp.float32),
        lax.psum_scatter(
            output_bias_grad.astype(jnp.bfloat16), "strip", scatter_dimension=0, tiled=True
        ).astype(jnp.float32),
        lax.psum_scatter(
            expand_weight_grad.astype(jnp.bfloat16), "strip", scatter_dimension=0, tiled=True
        ).astype(jnp.float32),
        lax.psum_scatter(
            expand_bias_grad.astype(jnp.bfloat16), "strip", scatter_dimension=0, tiled=True
        ).astype(jnp.float32),
        lax.psum_scatter(
            hidden_kernel_grad.astype(jnp.bfloat16), "strip", scatter_dimension=0, tiled=True
        ).astype(jnp.float32),
        lax.psum_scatter(
            reduce_weight_grad.astype(jnp.bfloat16), "strip", scatter_dimension=0, tiled=True
        ).astype(jnp.float32),
        lax.psum_scatter(
            reduce_bias_grad.astype(jnp.bfloat16), "strip", scatter_dimension=0, tiled=True
        ).astype(jnp.float32),
    )
    summed = (
        lax.psum(table_shard.astype(jnp.bfloat16), "batch").astype(jnp.float32),
        lax.psum(adaptive_shard.astype(jnp.bfloat16), "batch").astype(jnp.float32),
        lax.psum(adaptive_bias_shard.astype(jnp.bfloat16), "batch").astype(jnp.float32),
        lax.psum(mixer_shard.astype(jnp.bfloat16), "batch").astype(jnp.float32),
        lax.psum(joint_shard.astype(jnp.bfloat16), "batch").astype(jnp.float32),
        lax.psum(output_shard.astype(jnp.bfloat16), "batch").astype(jnp.float32),
        lax.psum(output_bias_shard.astype(jnp.bfloat16), "batch").astype(jnp.float32),
        lax.psum(expand_shard.astype(jnp.bfloat16), "batch").astype(jnp.float32),
        lax.psum(expand_bias_shard.astype(jnp.bfloat16), "batch").astype(jnp.float32),
        lax.psum(hidden_shard.astype(jnp.bfloat16), "batch").astype(jnp.float32),
        lax.psum(reduce_shard.astype(jnp.bfloat16), "batch").astype(jnp.float32),
        lax.psum(reduce_bias_shard.astype(jnp.bfloat16), "batch").astype(jnp.float32),
    )
    return (
        outputs,
        tokens_grad,
        summed[0],
        summed[1],
        summed[2],
        summed[3],
        summed[4],
        summed[5],
        summed[6],
        summed[7],
        summed[8],
        summed[9],
        summed[10],
        summed[11],
    )


def solution(mesh):
    grouped = (mesh.shape["batch"], mesh.shape["strip"]) == (4, 8)
    return jax.shard_map(
        local_grouped if grouped else local,
        mesh=mesh,
        in_specs=(
            P("batch", "strip", None, None),
            P("batch", None, None),
            P("batch", None),
            P("batch", None),
            P(),
            P(),
            P(),
            P(),
            P(),
            P(),
            P(),
            P(),
            P(),
            P(),
            P(),
            P(),
            P("batch", "strip", None, None),
        ),
        out_specs=(
            P("batch", "strip", None, None),
            P("batch", "strip", None, None),
            P("strip", None),
            P("strip", None),
            P("strip"),
            P("strip", None),
            P("strip", None),
            P("strip", None),
            P("strip"),
            P("strip", None),
            P("strip"),
            P("strip", None),
            P("strip", None),
            P("strip"),
        ),
        check_vma=False,
    )
```

```python
import math
from types import SimpleNamespace

import jax
import jax.numpy as jnp
from jax import lax
from jax.experimental import pallas as pl
from jax.experimental.pallas import tpu as pltpu
from jax.sharding import PartitionSpec as P

HEADS = 12
EPSILON = 1e-06
MASKED = -1e30
MESH = pl.DeviceIdType.MESH
F32 = jnp.float32
BF16 = jnp.bfloat16
VMEM_BYTES = 62 * 1024 * 1024
WHOLE = pl.BlockSpec(memory_space=pltpu.VMEM)
LEFT = pl.BlockSpec(memory_space=pl.ANY)
SCALARS = pl.BlockSpec(memory_space=pltpu.SMEM)
NT = (((1,), (1,)), ((), ()))
TN = (((0,), (0,)), ((), ()))


def dot(a, b):
    return jnp.dot(a, b, preferred_element_type=F32)


def dot_nt(a, b):
    return lax.dot_general(a, b, NT, preferred_element_type=F32)


def dot_tn(a, b):
    return lax.dot_general(a, b, TN, preferred_element_type=F32)


def send_to(src, dst, sems, index, batch, strip):
    return pltpu.make_async_remote_copy(
        src_ref=src,
        dst_ref=dst,
        send_sem=sems[0].at[index],
        recv_sem=sems[1].at[index],
        device_id=(batch, strip),
        device_id_type=MESH,
    )


def entry_signals(strips):
    s = lax.axis_index("strip")
    b = lax.axis_index("batch")
    z = s // 2
    barrier = pltpu.get_barrier_semaphore()
    count = 0
    for d in range(1, strips):
        pl.semaphore_signal(
            barrier, inc=1, device_id=(b, lax.rem(s + d, strips)), device_id_type=MESH
        )
        count += 1
    for e in range(1, 4):
        for core in range(2):
            pl.semaphore_signal(
                barrier, inc=1, device_id=(lax.rem(b + e, 4), 2 * z + core), device_id_type=MESH
            )
            count += 1
    return count


def entry_wait(count):
    pl.semaphore_wait(pltpu.get_barrier_semaphore(), count)


def spread(mod, width):
    return jnp.concatenate(
        [jnp.broadcast_to(mod[0:1], (8, width)), jnp.broadcast_to(mod[1:2], (8, width))], axis=0
    )


def spread_columns(buffer, r, x):
    for k in range(x.shape[-1] // 128):
        buffer[r, k] = x[:, k * 128 : k * 128 + 128]


def every_second(buffer, r, p):
    return jnp.concatenate(
        [buffer[r, k, pl.ds(p, 16, stride=2), :] for k in range(buffer.shape[1])], axis=-1
    )


def interleave(buffer, r, p, x):
    for k in range(x.shape[-1] // 128):
        buffer[r, k, pl.ds(p, 16, stride=2), :] = x[:, k * 128 : k * 128 + 128]


def joined(buffer, r):
    return jnp.concatenate([buffer[r, k] for k in range(buffer.shape[1])], axis=-1)


def ln_parts(x):
    centre = jnp.mean(x, axis=-1, keepdims=True)
    centred = x - centre
    var = jnp.mean(centred * centred, axis=-1, keepdims=True)
    inv = lax.rsqrt(var + EPSILON)
    return centred * inv, inv


def ln_back(grad, n, inv):
    mean0 = jnp.mean(grad, axis=-1, keepdims=True)
    mean1 = jnp.mean(grad * n, axis=-1, keepdims=True)
    return inv * (grad - mean0 - n * mean1)


def window(load, r):
    even = load(r, 0).astype(F32)
    odd = load(r, 1).astype(F32)
    n = even.shape[0]
    j = lax.broadcasted_iota(jnp.int32, even.shape, 0)
    odd_m = jnp.where(j == 0, 0.0, pltpu.roll(odd, 1, 0))
    even_p = jnp.where(j == n - 1, 0.0, pltpu.roll(even, n - 1, 0))
    return odd_m, even, odd, even_p


def conv(rows, weights, flip):
    out = []
    for p in range(2):
        total = None
        for i in range(3):
            for j in range(3):
                t = 3 * i + j
                a = weights[8 - t if flip else t] * rows[i][p + j]
                total = a if total is None else total + a
        out.append(total)
    return out


def taps(rows, centre, sums):
    new = list(sums)
    for i in range(3):
        for j in range(3):
            a = rows[i][j] * centre[0] + rows[i][1 + j] * centre[1]
            t = 8 - (3 * i + j)
            new[t] = sums[t] + (a[0:8] + a[8:16])
    return new


def halves(x):
    return jnp.concatenate(
        [jnp.sum(x[0:8], axis=0, keepdims=True), jnp.sum(x[8:16], axis=0, keepdims=True)], axis=0
    )


def gelu_both(x):
    k0 = math.sqrt(2.0 / math.pi)
    square = x * x
    t = jnp.tanh(k0 * x * (1.0 + 0.044715 * square))
    cdf = 0.5 + 0.5 * t
    slope = cdf + (0.5 * k0) * x * (1.0 - t * t) * (1.0 + (3.0 * 0.044715) * square)
    return x * cdf, slope


def block_kernel(names, *refs):
    m = SimpleNamespace(**dict(zip(names, refs)))
    rows, cols, width = m.tok.shape
    half = width // 2
    strips = lax.axis_size("strip")
    chips = strips // 2
    chip_rows = 2 * rows
    total = strips * 64
    own = width // strips
    part = width // chips // 4
    s = lax.axis_index("strip")
    b = lax.axis_index("batch")
    z = s // 2
    c = lax.rem(s, 2)
    sibling = 2 * z + 1 - c
    y, x = b // 2, lax.rem(b, 2)
    x_mate = 2 * y + 1 - x
    y_mate = 2 * (1 - y) + x
    sent = []

    def chip(d):
        return lax.rem(z + d, chips)

    def start(copy):
        copy.start()
        sent.append(copy)

    loads = {}

    def load(name, src, dst, index):
        loads[name] = pltpu.make_async_copy(src, dst, m.load_sem.at[index])
        loads[name].start()

    load("emb", m.emb_hbm, m.emb, 22)
    for i in range(12):
        lanes = pl.ds(i * half, half)
        src = m.aw4_hbm.at[:, :, :, lanes] if i < 4 else m.aw5_hbm.at[:, :, :, :, lanes]
        load(f"aw{i}", src, (m.rw, m.ew, m.jo)[i // 4].at[i % 4], 23 + i)
    greet = entry_signals(strips)
    for k in range(3):
        off = pl.multiple_of(k * width + c * half, 128)
        load(f"wj{k}", m.wj_hbm.at[:, pl.ds(off, half)], m.wj.at[k], k)
    load("cot", m.cot_hbm, m.cot, 3)
    load("wo", m.wo_hbm, m.wo, 4)
    for n in range(chips):
        off = pl.multiple_of((2 * n + c) * half, 128)
        spot = pl.ds(n * half, half)
        load(f"we{n}", m.we_hbm.at[:, pl.ds(off, half)], m.we.at[:, spot], 5 + n)
        load(f"wr{n}", m.wr_hbm.at[pl.ds(off, half)], m.wr.at[spot], 5 + chips + n)

    latents = m.steps.shape[1]
    classes = m.emb.shape[0]
    row = lax.broadcasted_iota(jnp.int32, (latents, 1), 0)
    when = jnp.zeros((latents, 1), F32)
    label = jnp.zeros((latents, 1), jnp.int32)
    for i in range(latents):
        when = jnp.where(row == i, m.steps[0, i].astype(F32), when)
        label = jnp.where(row == i, m.labels[0, i], label)
    order = lax.broadcasted_iota(jnp.int32, (latents, half), 1).astype(F32)
    angles = when * jnp.exp(-math.log(10000.0) * order / half)
    features = jnp.concatenate([jnp.cos(angles), jnp.sin(angles)], axis=1)
    onehot = lax.broadcasted_iota(jnp.int32, (latents, classes), 1) == label
    onehot = jnp.where(onehot, 1.0, 0.0).astype(BF16)

    lane = lax.broadcasted_iota(jnp.int32, (latents, 128), 1)
    kind = lax.broadcasted_iota(jnp.int32, (latents, 128), 0)
    line = lax.rem(lane, 16)
    side = jnp.where(kind == 0, lax.rem(line // 2, 2), lax.rem(line // 3, 2))
    tile = lax.rem(lane // 16, 4)
    slots = jnp.zeros((latents, 128), jnp.int32)
    for i in range(4):
        for h in range(2):
            hit = jnp.logical_and(tile == i, side == h)
            slots = jnp.where(hit, m.owner[0, h, i] + b * latents, slots)
    m.mk[...] = m.mixer[...].astype(F32)
    ob = m.ob[...].astype(F32).reshape(1, width)
    rb = m.rb[...].astype(F32).reshape(1, width)
    m.ebf[...] = m.eb[...].astype(F32).reshape(m.ebf.shape)
    for n in range(chips):
        m.hk[n] = m.hidden[:, pl.ds(pl.multiple_of((2 * n + c) * half, 128), half)].astype(F32)

    def normal_row(r, _):
        spread_columns(m.rowf, r, m.tok[r].astype(F32))
        for p in range(2):
            v = every_second(m.rowf, r, p)
            m.xd[r, p] = v.astype(BF16)
            m.fg[2 * r + p] = ln_parts(v)[0]
        return 0

    lax.fori_loop(0, rows, normal_row, 0, unroll=4)
    loads["emb"].wait()
    condition = features + dot(onehot, m.emb[...])
    silu = (condition / (1.0 + jnp.exp(-condition))).astype(BF16)
    m.cond_all[b] = jnp.concatenate(
        [condition, jnp.broadcast_to(label.astype(F32), (latents, 128)), slots.astype(F32)], axis=1
    )
    bias = m.ab[...].astype(F32).reshape(1, 6 * width)
    for g, held in enumerate((m.rw, m.ew, m.jo)):
        for i in range(4):
            loads[f"aw{4 * g + i}"].wait()
        weights = jnp.concatenate([held[i].reshape(width, half) for i in range(4)], axis=1)
        lanes = slice(g * 2 * width, (g + 1) * 2 * width)
        table = dot(silu, weights) + bias[:, lanes]
        for h in range(2):
            mine = row == m.owner[0, h, z]
            m.mod[h : h + 1, lanes] = jnp.sum(jnp.where(mine, table, 0.0), axis=0, keepdims=True)
    entry_wait(greet)

    for e in range(1, 4):
        start(
            send_to(m.cond_all.at[b], m.cond_all.at[b], m.cond_sem, e, lax.rem(b + e, 4), s)
        )

    def block_mod(n):
        return spread(m.mod[:, n * width : (n + 1) * width], width)

    scale1 = 1.0 + block_mod(1)
    shift1 = block_mod(0)

    def first_row(r):
        for p in range(2):
            m.fp[r + 1, p] = (m.fg[2 * r + p] * scale1 + shift1).astype(BF16)

    def edge_sends(buffer, sems):
        up = send_to(buffer.at[1], buffer.at[rows + 1], sems, 0, b, s - 1)
        down = send_to(buffer.at[rows], buffer.at[0], sems, 1, b, s + 1)
        return up, down

    def start_edges(buffer, sems):
        up, down = edge_sends(buffer, sems)

        @pl.when(s > 0)
        def _():
            up.start()

        @pl.when(s < strips - 1)
        def _():
            down.start()

    def edges_sent(buffer, sems):
        up, down = edge_sends(buffer, sems)

        @pl.when(s > 0)
        def _():
            up.wait_send()

        @pl.when(s < strips - 1)
        def _():
            down.wait_send()

    def top_edge(buffer, sems):
        @pl.when(s > 0)
        def _():
            send_to(buffer.at[1], buffer.at[0], sems, 1, b, s - 1).wait_recv()

        @pl.when(s == 0)
        def _():
            buffer[0] = jnp.zeros_like(buffer[0])

    def bottom_edge(buffer, sems):
        @pl.when(s < strips - 1)
        def _():
            send_to(buffer.at[1], buffer.at[rows + 1], sems, 0, b, s + 1).wait_recv()

        @pl.when(s == strips - 1)
        def _():
            buffer[rows + 1] = jnp.zeros_like(buffer[0])

    first_row(0)
    first_row(rows - 1)
    start_edges(m.fp, m.fp_sem)

    def body(r, _):
        first_row(r)
        return 0

    lax.fori_loop(1, rows - 1, body, 0, unroll=3)

    four = rows // 2

    def inner_rows(g):
        return pl.ds(1 - g // 2, four - 1)

    def edge_row(g):
        return pl.ds((g // 2) * (four - 1), 1)

    inner_edge = (inner_rows, edge_row)

    def to_groups(source, target, sems, piece, at):
        for d in range(1, chips):
            g = chip(d)
            rws = at(g)
            start(
                send_to(source.at[g, rws], target.at[s, rws], sems, (piece, d), b, 2 * g + c)
            )

    def pass_on(target, sems, sems2, d, pieces):
        i = 2 * chip(chips - d) + c
        if d:
            for k, at in enumerate(pieces):
                spot = target.at[i, at(z)]
                send_to(spot, spot, sems, (k, d), b, i).wait_recv()
        start(send_to(target.at[i], target.at[i], sems2, d, b, sibling))

    def groups_ready(target, sems2):
        for d in range(chips):
            i = 2 * chip(chips - d) + 1 - c
            send_to(target.at[i], target.at[i], sems2, d, b, sibling).wait_recv()

    def mixed_rows(low, high):
        for k in range(width // 128):
            lanes = pl.ds(k * 128, 128)
            weights = [m.mk[t : t + 1, k * 128 : k * 128 + 128] for t in range(9)]

            def line(r, p):
                return m.fp[r, p, :, lanes]

            def step(r, carry):
                new = window(line, r + 2)
                out = conv((carry[0], carry[1], new), weights, False)
                for p in range(2):
                    m.ms[lax.rem(r, 2) * 2 + p, r // 2, :, lanes] = out[p].astype(BF16)
                return carry[1], new

            lax.fori_loop(
                low, high, step, (window(line, low), window(line, low + 1)), unroll=True
            )

    mixed_rows(1, rows - 1)
    to_groups(m.ms, m.mg, m.mg_sem, 0, inner_rows)
    top_edge(m.fp, m.fp_sem)
    mixed_rows(0, 1)
    bottom_edge(m.fp, m.fp_sem)
    mixed_rows(rows - 1, rows)

    to_groups(m.ms, m.mg, m.mg_sem, 1, edge_row)
    m.mg[s] = m.ms[z]

    m.acc[...] = jnp.zeros_like(m.acc)
    gate2 = block_mod(5)
    loads["cot"].wait()

    def upstream_row(r, _):
        spread_columns(m.rowf, r, m.cot[r].astype(F32))
        for p in range(2):
            up = every_second(m.rowf, r, p)
            m.ctd[2 * r + p] = up.astype(BF16)
            two = (up * gate2).astype(BF16)
            m.tg[c, 2 * r + p] = two
            m.acc[0] += two.astype(F32)
        return 0

    lax.fori_loop(0, rows, upstream_row, 0)
    start(send_to(m.tg.at[c], m.tg.at[c], m.pair_sem, 0, b, sibling))

    for d in range(chips):
        pass_on(m.mg, m.mg_sem, m.mg_sem2, d, inner_edge)
    groups_ready(m.mg, m.mg_sem2)
    for k in range(3):
        loads[f"wj{k}"].wait()

    v = m.mg[...].reshape(total, width)
    for k in range(3):
        w = dot(v, m.wj[k]).astype(BF16)
        for n in range(3):
            m.qkv[3 * k + n] = w[:, n * 128 : n * 128 + 128]

    where = lax.broadcasted_iota(jnp.int32, (1, total), 1)
    lefts = lax.rem(where, 16) < 8
    key_owner = jnp.zeros((1, total), jnp.int32)
    for t in range(4):
        both = jnp.where(lefts, m.owner[0, 0, t], m.owner[0, 1, t])
        key_owner = jnp.where(where // 128 == t, both, key_owner)
    where = lax.broadcasted_iota(jnp.int32, (total, 1), 0)
    lefts = lax.rem(where, 16) < 8
    query_owner = jnp.zeros((total, 1), jnp.int32)
    for t in range(4):
        both = jnp.where(lefts, m.owner[0, 0, t], m.owner[0, 1, t])
        query_owner = jnp.where(where // 128 == t, both, query_owner)
    allowed = query_owner == key_owner
    lane = lax.broadcasted_iota(jnp.int32, (total, 128), 1) < 64
    factor = 64 ** -0.5

    def head(v, h):
        return jnp.where(lane if h == 0 else jnp.logical_not(lane), v, jnp.zeros_like(v))

    for n in range(3):
        mine = c * 3 + n
        q2 = (m.qkv[n].astype(F32) * factor).astype(BF16)
        outs = []
        for h in range(2):
            scores = jnp.where(allowed, dot_nt(head(q2, h), m.qkv[3 + n]), MASKED)
            peak = jnp.max(scores, axis=-1, keepdims=True)
            lifted = jnp.exp(scores - peak)
            inv = 1.0 / jnp.sum(lifted, axis=-1, keepdims=True)
            m.probs[n, h] = (lifted * inv).astype(BF16)
            outs.append(dot(lifted.astype(BF16), m.qkv[6 + n]) * inv)
        m.ag[mine] = jnp.where(lane, outs[0], outs[1]).astype(BF16)
        for d in range(1, strips):
            t = lax.rem(s + d, strips)
            start(
                send_to(
                    m.ag.at[mine, pl.ds(pl.multiple_of(t * 64, 64), 64)],
                    m.ai.at[mine, z],
                    m.ai_sem,
                    (n, d),
                    b,
                    t,
                )
            )
        start(send_to(m.ag.at[mine], m.ag.at[mine], m.ag_sem, n, b, sibling))
        m.ai[mine, z] = m.ag[mine, pl.ds(pl.multiple_of(s * 64, 64), 64), :]

    for n in range(chips):
        loads[f"wr{n}"].wait()
    send_to(m.tg.at[c], m.tg.at[1 - c], m.pair_sem, 0, b, sibling).wait_recv()
    chip_tg = m.tg[...].reshape(total, width)
    for h in range(2):
        m.big[h] = dot_nt(chip_tg, m.wr[h * width : h * width + width, :]).reshape(m.big.shape[1:])

    for n in range(3):
        for d in range(1, strips):
            i = lax.rem(s - d + strips, strips)
            spot = lax.rem(i, 2) * 3 + n
            send_to(
                m.ag.at[spot, pl.ds(0, 64)], m.ai.at[spot, i // 2], m.ai_sem, (n, d), b, i
            ).wait_recv()

    gate1 = block_mod(2)
    shift2 = block_mod(3)
    scale2 = 1.0 + block_mod(4)
    loads["wo"].wait()

    v = jnp.concatenate([m.ai[n].reshape(chips * 64, 128) for n in range(6)], axis=-1)
    m.b1[...] = (dot(v, m.wo[...]) + ob).reshape(m.b1.shape)

    def residual_row(i, _):
        rp = 4 * lax.rem(i, rows // 2) + i // (rows // 2)
        u = m.xd[rp // 2, lax.rem(rp, 2)].astype(F32) + gate1 * m.b1[i]
        m.res[rp] = u
        n, _ = ln_parts(u)
        m.sc[c, rp] = (n * scale2 + shift2).astype(BF16)
        return 0

    lax.fori_loop(0, 2 * rows, residual_row, 0, unroll=4)
    start(send_to(m.sc.at[c], m.sc.at[c], m.pair_sem, 1, b, sibling))

    def block_order(i, at_chip=None):
        at_chip = z if at_chip is None else at_chip
        high, low = at_chip // 2, lax.rem(at_chip, 2)
        flip_high, flip_low = 1 - lax.rem(i, 2), 1 - i // 2
        high = high + flip_high - 2 * high * flip_high
        low = low + flip_low - 2 * low * flip_low
        return 2 * high + low

    def halo_sends(buffer, sems, up_block, down_block):
        up_at = pl.ds(pl.multiple_of(up_block * half, 128), half)
        down_at = pl.ds(pl.multiple_of(down_block * half, 128), half)
        first, last = buffer.at[1, :, :, up_at], buffer.at[chip_rows, :, :, down_at]
        above = buffer.at[0, :, :, down_at]
        below = buffer.at[chip_rows + 1, :, :, up_at]
        up = send_to(first, below, sems, (0, up_block), b, s - 2)
        down = send_to(last, above, sems, (1, down_block), b, s + 2)
        return up, down

    def start_halo(buffer, sems, upward, downward, up_block, down_block):
        up, down = halo_sends(buffer, sems, up_block, down_block)

        @pl.when(jnp.logical_and(z > 0, upward))
        def _():
            up.start()

        @pl.when(jnp.logical_and(z < chips - 1, downward))
        def _():
            down.start()

    def halo_sent(buffer, sems, n):
        up, down = halo_sends(buffer, sems, n, n)

        @pl.when(z > 0)
        def _():
            up.wait_send()

        @pl.when(z < chips - 1)
        def _():
            down.wait_send()

    def take_halo(buffer, sems, n):
        at = pl.ds(pl.multiple_of(n * half, 128), half)
        k = n
        above, below = buffer.at[0, :, :, at], buffer.at[chip_rows + 1, :, :, at]

        @pl.when(z > 0)
        def _():
            send_to(above, above, sems, (1, k), b, s - 2).wait_recv()

        @pl.when(z == 0)
        def _():
            above[...] = jnp.zeros(above.shape, BF16)

        @pl.when(z < chips - 1)
        def _():
            send_to(below, below, sems, (0, k), b, s + 2).wait_recv()

        @pl.when(z == chips - 1)
        def _():
            below[...] = jnp.zeros(below.shape, BF16)

    for n in range(chips):
        loads[f"we{n}"].wait()
    hidden = chips * half
    bias = jnp.concatenate(
        [m.ebf[:, pl.ds(pl.multiple_of((2 * n + c) * half, 128), half)] for n in range(chips)],
        axis=-1,
    )

    def expand(core):
        w = dot(m.sc[core].reshape(rows * 32, width), m.we[...]) + bias
        m.ex[pl.ds(1 + core * rows, rows)] = w.astype(BF16).reshape(rows, 2, 16, hidden)

    expand(c)
    def edges_leave(upward, downward):
        for i in range(chips):
            start_halo(
                m.ex, m.ex_sem, upward, downward, block_order(i, z - 1), block_order(i, z + 1)
            )

    edges_leave(c == 0, c == 1)
    send_to(m.sc.at[c], m.sc.at[1 - c], m.pair_sem, 1, b, sibling).wait_recv()
    expand(1 - c)
    edges_leave(c == 1, c == 0)
    first_mate, then_mate = (x_mate, y_mate), (y_mate, x_mate)
    pair_chip = z + 1 - 2 * lax.rem(z, 2)
    far_chip = lax.rem(z + 2, 4)
    last_chip = 3 - z

    sub = width // 12
    upper = pl.ds(0, sub)

    def u_three(k):
        dest = pair_chip if k < 2 else far_chip
        src = m.u3.at[1] if k == 2 else m.rw.at[pair_chip if k == 0 else last_chip, :, :, upper]
        return send_to(src, m.u3.at[k], m.u3_sem, k, b, 2 * dest + c)

    def u_across():
        u_three(1).wait_recv()
        for i in range(2):
            v = m.u3[1, i].astype(F32) + m.rw[far_chip, i, :, upper].astype(F32)
            m.u3[1, i] = v.astype(BF16)
        u_three(2).start()

    def u_one(h):
        at = pl.ds(h * sub // 2, sub // 2)
        src = m.u0.at[:, 1 - x, at] if h == 0 else m.u0.at[1 - y, :, at]
        return send_to(src, m.u1.at[h], m.u1_sem, h, first_mate[h], s)

    def u_two(h):
        src = m.u1.at[h, (1 - y) if h == 0 else (1 - x)]
        return send_to(src, m.u2.at[h], m.u2_sem, h, then_mate[h], s)

    def u_begin():
        for k in (0, 2):
            u_three(k).wait_recv()
        for i in range(2):
            v = m.rw[z, i, :, upper].astype(F32) + m.u3[0, i].astype(F32)
            m.u0[i] = (v + m.u3[2, i].astype(F32)).astype(BF16)
        for h in range(2):
            u_one(h).start()

    def u_half():
        for h in range(2):
            u_one(h).wait_recv()
            at = pl.ds(h * sub // 2, sub // 2)
            kept = m.u0[:, x, at] if h == 0 else m.u0[y, :, at]
            m.u1[h] = (m.u1[h].astype(F32) + kept.astype(F32)).astype(BF16)
            u_two(h).start()

    def u_sum():
        for h in range(2):
            u_two(h).wait_recv()
            kept = m.u1[h, y if h == 0 else x].astype(F32)
            at = pl.ds(h * sub // 2, sub // 2)
            m.r_all[b, 0, at] = (m.u2[h].astype(F32) + kept).astype(BF16)
        r_four(0, 0).start()
        r_four(0, 1).start()

    def r_source(n, h, mine):
        at = pl.ds(sub + h * sub, sub)
        if h == 0:
            return m.rw.at[n, :, x if mine else 1 - x, at]
        return m.rw.at[n, y if mine else 1 - y, :, at]

    def r_one(n, h):
        return send_to(r_source(n, h, False), m.r1.at[n, h], m.r1_sem, (n, h), first_mate[h], s)

    def r_two(n, h):
        src = m.r1.at[n, h, (1 - y) if h == 0 else (1 - x)]
        return send_to(src, m.r2.at[n, h], m.r2_sem, (n, h), then_mate[h], s)

    def r_three(k):
        dest = pair_chip if k < 2 else far_chip
        t = (pair_chip, last_chip, far_chip)[k]
        return send_to(m.r2.at[t], m.r3.at[k], m.r3_sem, k, b, 2 * dest + c)

    def r_four(g, e):
        spot = m.r_all.at[b, g]
        return send_to(spot, spot, m.r4_sem, (g, e), (x_mate, y_mate)[e], s)

    def r_relay(g, wait):
        source, dest = (x_mate, y_mate) if g < 2 else (y_mate, x_mate)
        spot = m.r_all.at[source, g]
        copy = send_to(spot, spot, m.r4_sem, (g, 2), dest, s)
        if wait:
            copy.wait_send()
            return
        send_to(spot, spot, m.r4_sem, (g, 0 if g < 2 else 1), source, s).wait_recv()
        copy.start()

    def r_arrive(g):
        source, e = (y_mate, 1) if g < 2 else (x_mate, 0)
        spot = m.r_all.at[source, g]
        send_to(spot, spot, m.r4_sem, (g, e), source, s).wait_recv()
        spot = m.r_all.at[3 - b, g]
        send_to(spot, spot, m.r4_sem, (g, 2), source, s).wait_recv()

    def r_half(n):
        for h in range(2):
            r_one(n, h).wait_recv()
            kept = r_source(n, h, True)[...].astype(F32)
            m.r1[n, h] = (m.r1[n, h].astype(F32) + kept).astype(BF16)
            r_two(n, h).start()

    def r_quarter(n):
        for h in range(2):
            r_two(n, h).wait_recv()
            kept = m.r1[n, h, y if h == 0 else x].astype(F32)
            m.r2[n, h] = (m.r2[n, h].astype(F32) + kept).astype(BF16)

    def r_spread():
        r_three(1).start()
        r_three(0).start()

    def r_across():
        r_three(1).wait_recv()
        m.r2[far_chip] = (m.r2[far_chip].astype(F32) + m.r3[1].astype(F32)).astype(BF16)
        r_three(2).start()

    def r_sum():
        v = m.r2[z].astype(F32)
        for k in (0, 2):
            r_three(k).wait_recv()
            v = v + m.r3[k].astype(F32)
        m.r_all[b, pl.ds(1, 2)] = v.astype(BF16)
        for g in (1, 2):
            r_four(g, 0).start()
            r_four(g, 1).start()

    def c_source(j, h, mine):
        block = m.ew.at[j] if not isinstance(j, int) or j < 4 else m.jo.at[j - 4]
        at = pl.ds(2 * h, 2)
        if h == 0:
            return block.at[at, :, x if mine else 1 - x]
        return block.at[at, y if mine else 1 - y]

    def c_one(j, h):
        return send_to(c_source(j, h, False), m.c1.at[j, h], m.c1_sem, (j, h), first_mate[h], s)

    def c_two(j, h):
        src = m.c1.at[j, h, :, 1 - y] if h == 0 else m.c1.at[j, h, :, 1 - x]
        return send_to(src, m.c2.at[j, pl.ds(2 * h, 2)], m.c2_sem, (j, h), then_mate[h], s)

    def c_three(j, k):
        dest = pair_chip if k < 2 else far_chip
        t = (pair_chip, last_chip, far_chip)[k]
        return send_to(m.c2.at[j, t], m.c3.at[j, k], m.c3_sem, (j, k), b, 2 * dest + c)

    def c_copy(j, src, xs, cs, kind, batch, strip):
        return pltpu.make_async_remote_copy(
            src_ref=src,
            dst_ref=m.c_all.at[j, xs, cs],
            send_sem=m.c4_sem[0].at[j, kind],
            recv_sem=m.c4_sem[1].at[j, kind, cs],
            device_id=(batch, strip),
            device_id_type=MESH,
        )

    def c_four(j, kind):
        return c_copy(j, m.c_out.at[j], x, c, kind, (b, x_mate, y_mate)[kind], 2 * z + y)

    def c_got(j, kind, cs):
        xs = 1 - x if kind == 1 else x
        c_copy(j, m.c_out.at[j], xs, cs, kind, b, s).wait_recv()

    def c_passing(j, along_y):
        xs, dest = (1 - x, y_mate) if along_y else (x, x_mate)
        return pltpu.make_async_remote_copy(
            src_ref=m.c_all.at[j, xs],
            dst_ref=m.c_all.at[j, xs],
            send_sem=m.c4_sem[0].at[j, 3],
            recv_sem=m.c4_sem[1].at[j, 3, 0],
            device_id=(dest, s),
            device_id_type=MESH,
        )

    def c_relay(j, along_y):
        @pl.when((c == y) if along_y else (c != y))
        def _():
            for cs in range(2):
                c_got(j, 1 if along_y else 2, cs)
            c_passing(j, along_y).start()

    def c_arrive(j, along_y):
        @pl.when(c == y)
        def _():
            c_copy(j, m.c_out.at[j], x, 1 - c, 0, b, sibling).wait_recv()
            if not along_y:
                for cs in range(2):
                    c_got(j, 1, cs)

        @pl.when(c != y)
        def _():
            if along_y:
                for cs in range(2):
                    c_got(j, 2, cs)
            spot = m.c_all.at[j, 1 - x]
            pltpu.make_async_remote_copy(
                src_ref=spot,
                dst_ref=spot,
                send_sem=m.c4_sem[0].at[j, 3],
                recv_sem=m.c4_sem[1].at[j, 3, 0],
                device_id=(b, s),
                device_id_type=MESH,
            ).wait_recv()

    def c_gone(j, along_y):
        c_four(j, 1).wait_send()
        c_four(j, 2).wait_send()

        @pl.when(c != y)
        def _():
            c_four(j, 0).wait_send()

        @pl.when((c == y) if along_y else (c != y))
        def _():
            c_passing(j, along_y).wait_send()

    def c_begin(j):
        for h in range(2):
            c_one(j, h).start()

    def c_half(j):
        for h in range(2):
            c_one(j, h).wait_recv()
            kept = c_source(j, h, True)[...].astype(F32)
            m.c1[j, h] = (m.c1[j, h].astype(F32) + kept).astype(BF16)
            c_two(j, h).start()

    def c_quarter(j):
        for h in range(2):
            c_two(j, h).wait_recv()
            at = pl.ds(2 * h, 2)
            kept = (m.c1[j, h, :, y] if h == 0 else m.c1[j, h, :, x]).astype(F32)
            m.c2[j, at] = (m.c2[j, at].astype(F32) + kept).astype(BF16)

    def c_spread(j):
        c_three(j, 1).start()
        c_three(j, 0).start()

    def c_across(j):
        c_three(j, 1).wait_recv()
        far = m.c2[j, far_chip].astype(F32) + m.c3[j, 1].astype(F32)
        m.c2[j, far_chip] = far.astype(BF16)
        c_three(j, 2).start()

    def c_sum(j):
        v = m.c2[j, z].astype(F32)
        for k in (0, 2):
            c_three(j, k).wait_recv()
            v = v + m.c3[j, k].astype(F32)
        m.c_out[j] = v.astype(BF16)
        c_finished(j)

    def c_finished(j):
        @pl.when(c == y)
        def _():
            m.c_all[j, x, c] = m.c_out[j]

        c_four(j, 1).start()
        c_four(j, 2).start()

        @pl.when(c != y)
        def _():
            c_four(j, 0).start()

    def v_three(k):
        dest = pair_chip if k < 2 else far_chip
        src = m.v3.at[1] if k == 2 else m.ew.at[3, pair_chip if k == 0 else last_chip]
        return send_to(src, m.v3.at[k], m.v3_sem, k, b, 2 * dest + c)

    def v_across():
        v_three(1).wait_recv()
        m.v3[1] = (m.v3[1].astype(F32) + m.ew[3, far_chip].astype(F32)).astype(BF16)
        v_three(2).start()

    v_rows = (pl.ds(0, 32), pl.ds(32, part - 32))

    def v_one(h):
        src = m.v0.at[:, 1 - x, v_rows[0]] if h == 0 else m.v0.at[1 - y, :, v_rows[1]]
        return send_to(src, (m.v1a, m.v1b)[h], m.v1_sem, h, first_mate[h], s)

    def v_two(h):
        src = m.v1a.at[1 - y] if h == 0 else m.v1b.at[1 - x]
        return send_to(src, (m.v2a, m.v2b)[h], m.v2_sem, h, then_mate[h], s)

    def v_begin():
        for k in (0, 2):
            v_three(k).wait_recv()
        v = m.ew[3, z].astype(F32) + m.v3[0].astype(F32) + m.v3[2].astype(F32)
        m.v0[...] = v.astype(BF16)
        for h in range(2):
            v_one(h).start()

    def v_half():
        for h in range(2):
            v_one(h).wait_recv()
            held = (m.v1a, m.v1b)[h]
            kept = m.v0[:, x, v_rows[0]] if h == 0 else m.v0[y, :, v_rows[1]]
            held[...] = (held[...].astype(F32) + kept.astype(F32)).astype(BF16)
            v_two(h).start()

    def v_sum():
        for h in range(2):
            v_two(h).wait_recv()
            kept = m.v1a[y] if h == 0 else m.v1b[x]
            v = (m.v2a, m.v2b)[h][...].astype(F32) + kept.astype(F32)
            m.c_out[3, v_rows[h]] = v.astype(BF16)
        c_finished(3)

    def activate(i, early):
        n = block_order(i)
        for k in range(3):
            lanes = pl.ds(pl.multiple_of(n * half + k * 128, 128), 128)
            inner = pl.ds(k * 128, 128)
            weights = [m.hk[n, t : t + 1, inner] for t in range(9)]
            spot = pl.ds(pl.multiple_of(lax.rem(n, 2) * half + k * 128, 128), 128)

            def line(r, p):
                return m.ex[r, p, :, lanes]

            def rows_of(low, high):
                above, here = window(line, low), window(line, low + 1)
                for r in range(low, high):
                    below = window(line, r + 2)
                    out = conv((above, here, below), weights, False)
                    for p in range(2):
                        value, slope = gelu_both(out[p])
                        rp = 2 * r + p
                        grad = m.big[n // 2, rp // 16, rp % 16, :, spot]
                        m.act[rp, :, lanes] = value.astype(BF16)
                        m.cg[r + 1, p, :, lanes] = (grad * slope).astype(BF16)
                    above, here = here, below

            if early is None:
                rows_of(0, chip_rows)
            elif early:
                rows_of(1, chip_rows - 1)
            else:
                rows_of(0, 1)
                rows_of(chip_rows - 1, chip_rows)

    def activated(i):
        n = block_order(i)
        at = pl.ds(pl.multiple_of(n * half, 128), half)
        start_halo(m.cg, m.cg_sem, True, True, n, n)
        full = m.act[:, :, at].reshape(total, half)
        m.rw[n] = dot_tn(chip_tg, full).astype(BF16).reshape(m.rw.shape[1:])
        for h in range(2):
            r_one(n, h).start()

    activate(0, True)
    take_halo(m.ex, m.ex_sem, block_order(0))
    activate(0, False)
    activated(0)
    u_three(1).start()
    for i in range(1, chips):
        take_halo(m.ex, m.ex_sem, block_order(i))

    def next_block(i, _):
        activate(i, None)
        activated(i)
        return 0

    lax.fori_loop(1, chips, next_block, 0)
    u_three(0).start()
    full = m.act[...].reshape(total, hidden)
    m.big[0] = dot(full, m.wr[...]).reshape(m.big.shape[1:])
    b2_copy = send_to(m.big.at[0, 1 - c], m.b2_in, m.pair_sem, 2, b, sibling)
    b2_copy.start()
    m.hkg[...] = jnp.zeros_like(m.hkg)
    for n in range(chips):
        take_halo(m.cg, m.cg_sem, n)
    u_across()
    chip_sc = m.sc[...].reshape(total, width)

    def backward(n, _):
        for k in range(3):
            lanes = pl.ds(pl.multiple_of(n * half + k * 128, 128), 128)
            inner = pl.ds(k * 128, 128)
            weights = [m.hk[n, t : t + 1, inner] for t in range(9)]

            def line(r, p):
                return m.cg[r, p, :, lanes]

            above, here = window(line, 0), window(line, 1)
            sums = [jnp.zeros((8, 128), F32) for _ in range(9)]
            total_eg = jnp.zeros((8, 128), F32)
            for r in range(chip_rows):
                below = window(line, r + 2)
                three = (above, here, below)
                low = [v.astype(BF16) for v in conv(three, weights, True)]
                for p in range(2):
                    m.act[2 * r + p, :, lanes] = low[p]
                centre = [m.ex[r + 1, p, :, lanes].astype(F32) for p in range(2)]
                sums = taps(three, centre, sums)
                both = low[0].astype(F32) + low[1].astype(F32)
                total_eg = total_eg + (both[0:8] + both[8:16])
                above, here = here, below
            for t, v in enumerate(sums + [total_eg]):
                m.hkg[n, t : t + 1, inner] = jnp.sum(v, axis=0, keepdims=True)
        full = m.act[:, :, pl.ds(pl.multiple_of(n * half, 128), half)].reshape(total, half)
        m.ew[n] = dot_tn(chip_sc, full).astype(BF16).reshape(m.ew.shape[1:])
        @pl.when(n < 3)
        def _():
            c_begin(n)

        r_half(block_order(n))
        return 0

    lax.fori_loop(0, chips, backward, 0)
    v_three(1).start()
    v_three(0).start()
    for core in (1 - c, c):
        v = m.act[pl.ds(core * 2 * rows, 2 * rows)].reshape(rows * 32, hidden)
        m.big[1, core] = dot_nt(v, m.we[...]).reshape(m.big.shape[2:])
        if core is not c:
            sg_copy = send_to(m.big.at[1, 1 - c], m.sg_in, m.pair_sem, 3, b, sibling)
            sg_copy.start()
    send_to(m.big.at[0, c], m.b2_in, m.pair_sem, 2, b, sibling).wait_recv()
    send_to(m.big.at[1, c], m.sg_in, m.pair_sem, 3, b, sibling).wait_recv()

    def finish(r, _):
        for p in range(2):
            rp = 2 * r + p
            grad = m.big[1, c, rp] + m.sg_in[rp]
            v = m.res[rp]
            n, inv = ln_parts(v)
            branch = m.b1[(rows // 2) * lax.rem(rp, 4) + rp // 4]
            up = m.ctd[rp].astype(F32)
            m.acc[1] += grad
            m.acc[2] += grad * n
            back = up + ln_back(grad * scale2, n, inv)
            m.rg[rp] = back
            m.acc[3] += back * branch
            one = (back * gate1).astype(BF16)
            m.og[lax.rem(rp, 4), rp // 4] = one
            m.acc[4] += one.astype(F32)
            branch2 = m.big[0, c, rp] + m.b2_in[rp] + rb
            m.acc[5] += up * branch2
            interleave(m.rowf, r, p, v + gate2 * branch2)
        m.out[r] = joined(m.rowf, r).astype(BF16)
        return 0

    def first_half(g):
        return pl.ds(0, four // 2)

    def second_half(g):
        return pl.ds(four // 2, four // 2)

    both_halves = (first_half, second_half)
    for k, at in enumerate(both_halves):
        lax.fori_loop(k * four, (k + 1) * four, finish, 0, unroll=2)
        to_groups(m.og, m.gg, m.gg_sem, k, at)
    out_copy = pltpu.make_async_copy(m.out, m.out_hbm, m.load_sem.at[13])
    out_copy.start()

    m.gg[s] = m.og[z]

    pack = []
    for v in (m.acc[3], m.acc[1], m.acc[2], m.acc[5]):
        pair = halves(v)
        for h in range(2):
            pack += [pair[h : h + 1, 0:half], pair[h : h + 1, half:]]
    def own_sums(buffer, sems, value):
        buffer[b, c, z] = value.astype(BF16)
        for d in range(1, chips):
            start(send_to(buffer.at[b, c, z], buffer.at[b, c, z], sems, d, b, 2 * chip(d) + c))

    def to_canvases(buffer, sems, sems2):
        for d in range(1, chips):
            i = chip(chips - d)
            send_to(buffer.at[b, c, i], buffer.at[b, c, i], sems, d, b, 2 * i + c).wait_recv()
        for e in range(1, 4):
            start(send_to(buffer.at[b, c], buffer.at[b, c], sems2, e, lax.rem(b + e, 4), s))

    def to_sibling(buffer, sems2, sems3):
        for e in range(1, 4):
            i = lax.rem(b - e + 4, 4)
            send_to(buffer.at[i, c], buffer.at[i, c], sems2, e, i, s).wait_recv()
        start(send_to(buffer.at[:, c], buffer.at[:, c], sems3, 0, b, sibling))

    def from_sibling(buffer, sems3):
        send_to(buffer.at[:, c], buffer.at[:, 1 - c], sems3, 0, b, sibling).wait_recv()

    own_sums(m.late, m.late_sem, jnp.concatenate(pack, axis=0))
    for t in range(chips):
        m.piece[t] = m.hkg[t].astype(BF16)
    for d in range(1, chips):
        t = chip(d)
        start(send_to(m.piece.at[t], m.piece_in.at[d], m.piece_sem, d, b, 2 * t + c))

    pass_on(m.gg, m.gg_sem, m.gg_sem2, 0, both_halves)
    c_half(0)
    u_begin()
    c_half(1)
    pass_on(m.gg, m.gg_sem, m.gg_sem2, 1, both_halves)
    v_across()
    c_half(2)
    pass_on(m.gg, m.gg_sem, m.gg_sem2, 2, both_halves)
    pass_on(m.gg, m.gg_sem, m.gg_sem2, 3, both_halves)
    u_half()
    for n in range(chips):
        r_quarter(n)
    r_spread()
    groups_ready(m.gg, m.gg_sem2)
    wo_own = m.wo[pl.ds(pl.multiple_of(c * half, 128), half), :]
    w = dot_nt(m.gg[...].reshape(total, width), wo_own).astype(BF16)
    for n in range(3):
        m.da[n] = w[:, n * 128 : n * 128 + 128]

    for n in range(3):
        other = (1 - c) * 3 + n
        send_to(m.ag.at[other], m.ag.at[other], m.ag_sem, n, b, sibling).wait_recv()
    columns = m.gg[:, :, :, pl.ds(pl.multiple_of(c * half, 128), half)].reshape(total, half)
    full = jnp.concatenate([m.ag[n] for n in range(6)], axis=-1)
    m.jo[3] = dot_tn(full, columns).astype(BF16).reshape(m.jo.shape[1:])
    c_begin(7)
    for j in range(3):
        c_quarter(j)
        c_spread(j)

    tops = lax.broadcasted_iota(jnp.int32, (128, total), 0) < 64
    group = m.mg[...].reshape(total, width)
    for n in range(3):
        d2 = m.da[n]
        outs = []
        for h in range(2):
            dp = dot_nt(head(d2, h), m.qkv[6 + n])
            probs = m.probs[n, h].astype(F32)
            inner = jnp.sum(probs * dp, axis=-1, keepdims=True)
            m.ds[h] = (probs * (dp - inner)).astype(BF16)
            outs.append(dot(m.ds[h], m.qkv[3 + n]))
        dq = (jnp.where(lane, outs[0], outs[1]) * factor).astype(BF16)
        dk = [dot_tn(m.qkv[n], m.ds[h]) for h in range(2)]
        dk = (jnp.where(tops, dk[0], dk[1]) * factor).T.astype(BF16)
        dv = [dot_tn(d2, m.probs[n, h]) for h in range(2)]
        dv = jnp.where(tops, dv[0], dv[1]).T.astype(BF16)
        m.dqkv[n] = dq
        m.dqkv[3 + n] = dk
        m.dqkv[6 + n] = dv
        w = dot_tn(group, jnp.concatenate([dq, dk, dv], axis=-1))
        m.jo[n] = w.astype(BF16).reshape(m.jo.shape[1:])
        c_begin(4 + n)

    v_begin()
    r_across()

    b2_copy.wait_send()
    sg_copy.wait_send()

    def partial(core):
        strip_rows = [
            jnp.concatenate(
                [
                    m.dqkv[k, pl.ds(pl.multiple_of((2 * i + core) * 64, 64), 64), :]
                    for i in range(chips)
                ],
                axis=0,
            )
            for k in range(9)
        ]
        weights = jnp.concatenate([m.wj[k] for k in range(3)], axis=-1)
        w = dot_nt(jnp.concatenate(strip_rows, axis=-1), weights)
        m.big[0, core] = w.reshape(m.big.shape[2:])

    partial(1 - c)
    start(send_to(m.big.at[0, 1 - c], m.mp_in, m.pair_sem, 4, b, sibling))
    partial(c)
    c_half(7)
    for j in range(3):
        c_across(j)
    send_to(m.big.at[0, c], m.mp_in, m.pair_sem, 4, b, sibling).wait_recv()
    for d in range(chips):
        i = chip(d)
        at = pl.ds(four * i, four)
        low = (m.big[0, c, at] + m.mp_in[at]).astype(BF16)
        if d:
            m.mo[i] = low
            start(send_to(m.mo.at[i], m.mr.at[z], m.mr_sem, d, b, 2 * i + c))
        else:
            m.mr[z] = low

    c_half(4)
    sums = m.piece[z].astype(F32)
    for d in range(1, chips):
        send_to(m.piece.at[0], m.piece_in.at[d], m.piece_sem, d, b, s).wait_recv()
        sums = sums + m.piece_in[d].astype(F32)
    m.small[b] = sums.astype(BF16)
    for e in range(1, 4):
        start(send_to(m.small.at[b], m.small.at[b], m.small_sem, e, lax.rem(b + e, 4), s))
    c_half(5)
    c_half(6)
    v_half()
    u_sum()
    to_canvases(m.late, m.late_sem, m.late_sem2)
    r_sum()
    for j in (7, 4):
        c_quarter(j)
        c_spread(j)
    for j in range(3):
        c_sum(j)
    for j in (5, 6):
        c_quarter(j)
        c_spread(j)

    for d in range(1, chips):
        i = chip(chips - d)
        send_to(m.mo.at[i], m.mr.at[i], m.mr_sem, d, b, 2 * i + c).wait_recv()
    for r in (0, rows - 1):
        for p in range(2):
            m.md[r + 1, p] = m.mr[(r % 2) * 2 + p, r // 2]
    start_edges(m.md, m.md_sem)
    c_across(7)
    for r in range(1, rows - 1):
        for p in range(2):
            m.md[r + 1, p] = m.mr[(r % 2) * 2 + p, r // 2]

    m.acc1[...] = jnp.zeros_like(m.acc1)

    def mixer_rows(low, high):
        for k in range(width // 128):
            lanes = pl.ds(k * 128, 128)
            weights = [m.mk[t : t + 1, k * 128 : k * 128 + 128] for t in range(9)]

            def line(r, p):
                return m.md[r, p, :, lanes]

            def step(r, carry):
                new = window(line, r + 2)
                three = (carry[0], carry[1], new)
                out = conv(three, weights, True)
                for p in range(2):
                    m.fg[2 * r + p, :, lanes] = out[p]
                centre = [m.fp[r + 1, p, :, lanes].astype(F32) for p in range(2)]
                return carry[1], new, tuple(taps(three, centre, carry[2]))

            begin = tuple(m.acc1[t, :, lanes] for t in range(9))
            _, _, sums = lax.fori_loop(
                low, high, step, (window(line, low), window(line, low + 1), begin), unroll=True
            )
            for t in range(9):
                m.acc1[t, :, lanes] = sums[t]

    m.acc[1] = jnp.zeros_like(m.acc[1])
    m.acc[2] = jnp.zeros_like(m.acc[2])

    def token_row(r, _):
        for p in range(2):
            rp = 2 * r + p
            grad = m.fg[rp]
            n, inv = ln_parts(m.xd[r, p].astype(F32))
            m.acc[1] += grad
            m.acc[2] += grad * n
            interleave(m.rowf, r, p, m.rg[rp] + ln_back(grad * scale1, n, inv))
        m.tgo[r] = joined(m.rowf, r)
        return 0

    mixer_rows(1, rows - 1)
    lax.fori_loop(1, rows - 1, token_row, 0, unroll=3)
    c_across(4)
    v_sum()
    c_across(5)
    top_edge(m.md, m.md_sem)
    mixer_rows(0, 1)
    token_row(0, 0)
    bottom_edge(m.md, m.md_sem)
    mixer_rows(rows - 1, rows)
    token_row(rows - 1, 0)
    tg_copy = pltpu.make_async_copy(m.tgo, m.tg_hbm, m.load_sem.at[14])
    tg_copy.start()

    pack = []
    third = width // 3
    for v in (m.acc[1], m.acc[2]):
        pair = halves(v)
        for h in range(2):
            pack += [pair[h : h + 1, k * third : k * third + third] for k in range(3)]
    pack.append(jnp.zeros((4, third), F32))
    own_sums(m.early, m.early_sem, jnp.concatenate(pack, axis=0))
    mixer_sums = [jnp.sum(m.acc1[t], axis=0, keepdims=True) for t in range(9)]
    mixer_sums += [jnp.sum(m.acc[k], axis=0, keepdims=True) for k in (4, 0)]
    mixer_sums = jnp.concatenate(mixer_sums + [jnp.zeros((5, width), F32)], axis=0)
    pad_lanes = jnp.zeros((16, 128 - own), F32)
    for t in range(strips):
        m.mpiece[t] = jnp.concatenate(
            [mixer_sums[:, t * own : t * own + own], pad_lanes], axis=1
        ).astype(BF16)
    for d in range(1, strips):
        t = lax.rem(s + d, strips)
        start(send_to(m.mpiece.at[t], m.mpiece_in.at[d], m.mpiece_sem, d, b, t))

    c_across(6)
    c_sum(7)
    c_sum(4)
    for g in range(3):
        r_relay(g, False)
    for i in range(2):
        c_relay(i, i % 2 == 0)
    c_sum(5)
    to_canvases(m.early, m.early_sem, m.early_sem2)
    c_sum(6)
    sums = m.mpiece[s].astype(F32)
    for d in range(1, strips):
        send_to(m.mpiece.at[0], m.mpiece_in.at[d], m.mpiece_sem, d, b, s).wait_recv()
        sums = sums + m.mpiece_in[d].astype(F32)
    m.msmall[b] = sums.astype(BF16)
    for e in range(1, 4):
        start(send_to(m.msmall.at[b], m.msmall.at[b], m.msmall_sem, e, lax.rem(b + e, 4), s))
    for i in range(2, 4):
        c_relay(i, i % 2 == 0)
    j_order = (7, 4, 5, 6)
    for i in range(4):
        c_relay(j_order[i], i % 2 == 0)
    to_sibling(m.late, m.late_sem2, m.late_sem3)
    to_sibling(m.early, m.early_sem2, m.early_sem3)

    finals = []

    def store(src, dst, index):
        cp = pltpu.make_async_copy(src, dst, m.load_sem.at[index])
        cp.start()
        finals.append(cp)

    for e in range(1, 4):
        i = lax.rem(b - e + 4, 4)
        send_to(m.cond_all.at[i], m.cond_all.at[i], m.cond_sem, e, i, s).wait_recv()
        send_to(m.small.at[i], m.small.at[i], m.small_sem, e, i, s).wait_recv()
        send_to(m.msmall.at[i], m.msmall.at[i], m.msmall_sem, e, i, s).wait_recv()
    for g in range(3):
        r_arrive(g)
    store(m.r_all, m.r_hbm, 15)
    store(m.cond_all, m.cond_hbm, 16)
    store(m.small, m.small_hbm, 17)
    store(m.msmall, m.msmall_hbm, 18)
    from_sibling(m.late, m.late_sem3)
    from_sibling(m.early, m.early_sem3)
    store(m.late, m.late_hbm, 19)
    store(m.early, m.early_hbm, 20)
    for i in range(4):
        c_arrive(i, i % 2 == 0)
    store(m.c_all.at[pl.ds(0, 4)], m.c_hbm.at[pl.ds(0, 4)], 35)
    for i in range(4):
        c_arrive(j_order[i], i % 2 == 0)
    store(m.c_all.at[pl.ds(4, 4)], m.c_hbm.at[pl.ds(4, 4)], 21)
    for cp in sent:
        cp.wait_send()
    edges_sent(m.fp, m.fp_sem)
    edges_sent(m.md, m.md_sem)

    for n in range(chips):
        halo_sent(m.ex, m.ex_sem, n)
        halo_sent(m.cg, m.cg_sem, n)
    for h in range(2):
        u_one(h).wait_send()
        u_two(h).wait_send()
        for n in range(chips):
            r_one(n, h).wait_send()
            r_two(n, h).wait_send()
        v_one(h).wait_send()
        v_two(h).wait_send()
        for j in (0, 1, 2, 4, 5, 6, 7):
            c_one(j, h).wait_send()
            c_two(j, h).wait_send()
    for k in range(3):
        r_three(k).wait_send()
        u_three(k).wait_send()
        r_four(k, 0).wait_send()
        r_four(k, 1).wait_send()
        r_relay(k, True)
        v_three(k).wait_send()
        for j in (0, 1, 2, 4, 5, 6, 7):
            c_three(j, k).wait_send()

    for i in range(4):
        c_gone(i, i % 2 == 0)
        c_gone(j_order[i], i % 2 == 0)
    out_copy.wait()
    tg_copy.wait()
    for cp in finals:
        cp.wait()


def block(
    tokens, mixer, owner, steps, labels, emb, aw, ab, ob, eb, hk, rb, wj, wo, we, wr, cot, strips
):
    rows, cols, width = tokens.shape
    chips = strips // 2
    half = width // 2
    total = strips * 64
    blocks = 2 * rows
    chip_rows = 2 * rows
    part = width // chips // 4
    third = width // 3
    cond = (steps.shape[1], width + 256)
    shape = jax.ShapeDtypeStruct
    vm = pltpu.VMEM

    def dma(*size):
        return pltpu.SemaphoreType.DMA(size)

    ins = dict(
        tok=tokens, mixer=mixer, owner=owner, steps=steps, labels=labels, ab=ab, ob=ob, eb=eb,
        hidden=hk, rb=rb, emb_hbm=emb, aw4_hbm=aw.reshape(2, 2, width // 4, 6 * width),
        aw5_hbm=aw.reshape(chips, 2, 2, part, 6 * width), wj_hbm=wj, wo_hbm=wo, we_hbm=we, wr_hbm=wr, cot_hbm=cot,
    )
    outs = dict(
        out_hbm=shape((rows, cols, width), BF16),
        tg_hbm=shape((rows, cols, width), F32),
        r_hbm=shape((4, 3, width // 12, half), BF16),
        c_hbm=shape((8, 2, 2, part, half), BF16),
        cond_hbm=shape((4,) + cond, F32),
        small_hbm=shape((4, 16, half), BF16),
        msmall_hbm=shape((4, 16, 128), BF16),
        late_hbm=shape((4, 2, chips, 16, half), BF16),
        early_hbm=shape((4, 2, chips, 16, third), BF16),
    )
    scratch = dict(
        emb=vm(emb.shape, BF16),
        mod=vm((2, 6 * width), F32),
        mk=vm((9, width), F32),
        ebf=vm((1, 2 * chips * half), F32),
        hk=vm((chips, 9, half), F32),
        wj=vm((3, width, half), BF16),
        wo=vm((width, width), BF16),
        we=vm((width, chips * half), BF16),
        wr=vm((chips * half, width), BF16),
        cot=vm((rows, cols, width), BF16),
        cond_all=vm((4,) + cond, F32),
        rowf=vm((rows, width // 128, cols, 128), F32),
        xd=vm((rows, 2, 16, width), BF16),
        fp=vm((rows + 2, 2, 16, width), BF16),
        ms=vm((chips, rows // 2, 16, width), BF16),
        mg=vm((strips, rows // 2, 16, width), BF16),
        qkv=vm((9, total, 128), BF16),
        probs=vm((3, 2, total, total), BF16),
        ag=vm((6, total, 128), BF16),
        ai=vm((6, chips, 64, 128), BF16),
        acc=vm((6, 16, width), F32),
        acc1=vm((9, 8, width), F32),
        ctd=vm((blocks, 16, width), BF16),
        tg=vm((2, blocks, 16, width), BF16),
        sc=vm((2, blocks, 16, width), BF16),
        b1=vm((blocks, 16, width), F32),
        res=vm((blocks, 16, width), F32),
        ex=vm((chip_rows + 2, 2, 16, chips * half), BF16),
        cg=vm((chip_rows + 2, 2, 16, chips * half), BF16),
        act=vm((2 * blocks, 16, chips * half), BF16),
        big=vm((2, 2, blocks, 16, width), F32),
        b2_in=vm((blocks, 16, width), F32),
        sg_in=vm((blocks, 16, width), F32),
        hkg=vm((chips, 16, half), F32),
        rg=vm((blocks, 16, width), F32),
        og=vm((chips, rows // 2, 16, width), BF16),
        out=vm((rows, cols, width), BF16),
        gg=vm((strips, rows // 2, 16, width), BF16),
        da=vm((3, total, 128), BF16),
        ds=vm((2, total, total), BF16),
        dqkv=vm((9, total, 128), BF16),
        mp_in=vm((blocks, 16, width), F32),
        mo=vm((chips, rows // 2, 16, width), BF16),
        mr=vm((chips, rows // 2, 16, width), BF16),
        md=vm((rows + 2, 2, 16, width), BF16),
        fg=vm((blocks, 16, width), F32),
        tgo=vm((rows, cols, width), F32),
        rw=vm((chips, 2, 2, width // 4, half), BF16),
        r1=vm((chips, 2, 2, width // 12, half), BF16),
        r2=vm((chips, 2, width // 12, half), BF16),
        r3=vm((3, 2, width // 12, half), BF16),
        u3=vm((3, 2, 2, width // 12, half), BF16),
        u0=vm((2, 2, width // 12, half), BF16),
        u1=vm((2, 2, width // 24, half), BF16),
        u2=vm((2, width // 24, half), BF16),
        r_all=vm((4, 3, width // 12, half), BF16),
        ew=vm((4, chips, 2, 2, part, half), BF16),
        jo=vm((4, chips, 2, 2, part, half), BF16),
        c1=vm((8, 2, 2, 2, part, half), BF16),
        c2=vm((8, chips, part, half), BF16),
        c3=vm((8, 3, part, half), BF16),
        c_out=vm((8, part, half), BF16),
        c_all=vm((8, 2, 2, part, half), BF16),
        v3=vm((3, 2, 2, part, half), BF16),
        v0=vm((2, 2, part, half), BF16),
        v1a=vm((2, 32, half), BF16),
        v1b=vm((2, part - 32, half), BF16),
        v2a=vm((32, half), BF16),
        v2b=vm((part - 32, half), BF16),
        late=vm((4, 2, chips, 16, half), BF16),
        early=vm((4, 2, chips, 16, third), BF16),
        piece=vm((chips, 16, half), BF16),
        piece_in=vm((chips, 16, half), BF16),
        small=vm((4, 16, half), BF16),
        mpiece=vm((strips, 16, 128), BF16),
        mpiece_in=vm((strips, 16, 128), BF16),
        msmall=vm((4, 16, 128), BF16),
        load_sem=dma(36),
    )
    pairs = dict(
        cond_sem=(4,), fp_sem=(2,), md_sem=(2,), mg_sem=(2, chips), mg_sem2=(chips,),
        gg_sem=(2, chips), gg_sem2=(chips,), ai_sem=(3, strips), ag_sem=(3,), pair_sem=(5,),
        ex_sem=(2, chips), cg_sem=(2, chips), mr_sem=(chips,),
        r1_sem=(chips, 2), r2_sem=(chips, 2), r3_sem=(3,), r4_sem=(3, 3), u3_sem=(3,), u1_sem=(2,), u2_sem=(2,),
        v3_sem=(3,), v1_sem=(2,), v2_sem=(2,),
        c1_sem=(8, 2), c2_sem=(8, 2), c3_sem=(8, 3),
        late_sem=(chips,), late_sem2=(4,), late_sem3=(1,),
        early_sem=(chips,), early_sem2=(4,), early_sem3=(1,),
        piece_sem=(chips,), small_sem=(4,), mpiece_sem=(strips,), msmall_sem=(4,),
    )
    names = list(ins) + list(outs) + list(scratch)
    shapes = list(scratch.values())
    for size in list(pairs.values()):
        shapes += [dma(*size), dma(*size)]
    shapes += [dma(8, 4), dma(8, 4, 2)]
    plain = len(names)

    def kernel(*refs):
        named = list(refs[:plain])
        sems = refs[plain:]
        both = [(sems[2 * i], sems[2 * i + 1]) for i in range(len(sems) // 2)]
        block_kernel(names + list(pairs) + ["c4_sem"], *named, *both)

    return pl.pallas_call(
        kernel,
        name="block",
        out_shape=tuple(outs.values()),
        in_specs=[WHOLE] * 2 + [SCALARS] * 3 + [WHOLE] * 5 + [LEFT] * 8,
        out_specs=(LEFT,) * len(outs),
        scratch_shapes=shapes,
        compiler_params=pltpu.CompilerParams(
            collective_id=0, has_side_effects=True, vmem_limit_bytes=VMEM_BYTES
        ),
    )(*ins.values())


def final_kernel(
    out_in, tg_in, r_in, c_in, cond_ref, small_ref, msmall_ref, late_ref, early_ref, aw_hbm,
    out_ref, tg_ref, tab_ref, ad_out, ab_ref, mix_ref, joint_out, output_out, ob_ref,
    expand_out, eb_ref, hidden_ref, reduce_out, rb_ref,
    aw, out_v, tg_v, r_ref, c_ref, ad_ref, joint_ref, output_ref, expand_ref, reduce_ref, sem,
):
    s = lax.axis_index("strip")
    strips = lax.axis_size("strip")
    width = cond_ref.shape[2] - 256
    own = width // strips
    half = width // 2
    loads = [
        (r_in, r_ref),
        (c_in, c_ref),
        (aw_hbm.at[pl.ds(pl.multiple_of(s * own, 16), own)], aw),
        (out_in, out_v),
        (tg_in, tg_v),
    ]
    loads = [pltpu.make_async_copy(a, v, sem.at[i]) for i, (a, v) in enumerate(loads)]
    for cp in loads:
        cp.start()
    stores = []

    def store(src, dst):
        cp = pltpu.make_async_copy(src, dst, sem.at[5 + len(stores)])
        cp.start()
        stores.append(cp)

    small = small_ref[0].astype(F32)
    mixer = msmall_ref[0].astype(F32)
    for i in range(1, 4):
        small = small + small_ref[i].astype(F32)
        mixer = mixer + msmall_ref[i].astype(F32)
    hidden_ref[...] = small[0:9]
    eb_ref[...] = small[9]
    ob_ref[...] = mixer[9, 0:own]
    rb_ref[...] = mixer[10, 0:own]
    mix_ref[...] = mixer[0:9, 0:own]

    n = width // 4
    loads[0].wait()
    for q in range(4):
        reduce_ref[:, q * n : q * n + n] = r_ref[q].reshape(n, half).astype(F32).T
    store(reduce_ref, reduce_out)
    loads[1].wait()
    part = c_ref.shape[3]
    for xs in range(2):
        rows = slice(xs * part, xs * part + part)
        for cs in range(2):
            for k in range(4):
                at = (2 * k + cs) * half
                expand_ref[rows, at : at + half] = c_ref[k, xs, cs].astype(F32)
            for k in range(3):
                for p in range(3):
                    at = p * width + cs * half + k * 128
                    joint_ref[rows, at : at + 128] = c_ref[
                        4 + k, xs, cs, :, p * 128 : p * 128 + 128
                    ].astype(F32)
            output_ref[rows, cs * half : cs * half + half] = c_ref[7, xs, cs].astype(F32)
    store(expand_ref, expand_out)
    store(joint_ref, joint_out)
    store(output_ref, output_out)
    loads[3].wait()
    store(out_v, out_ref)
    loads[4].wait()
    store(tg_v, tg_ref)

    slots = 32
    condition = cond_ref[...].reshape(slots, width + 256)
    labels = condition[:, width : width + 1]
    slot_late = jnp.concatenate([cond_ref[i, 0:1, width + 128 :] for i in range(4)], axis=1)
    slot_early = jnp.concatenate([cond_ref[i, 1:2, width + 128 :] for i in range(4)], axis=1)
    condition = condition[:, 0:width]
    pick = lax.broadcasted_iota(jnp.int32, (width, own), 0) == (
        lax.broadcasted_iota(jnp.int32, (width, own), 1) + s * own
    )
    pick = jnp.where(pick, 1.0, 0.0)
    condition = jnp.dot(
        condition, pick, precision=lax.Precision.HIGHEST, preferred_element_type=F32
    )
    sigmoid = 1.0 / (1.0 + jnp.exp(-condition))
    silu = (condition * sigmoid).astype(BF16)
    slope = sigmoid * (1.0 + condition * (1.0 - sigmoid))

    count = 4 * strips * 16

    def by_slot(source, slot, parts, period):
        groups = parts * (16 // period)
        index = lax.broadcasted_iota(jnp.int32, (groups * slots, count), 0)
        row = lax.rem(lax.broadcasted_iota(jnp.int32, (groups * slots, count), 1), 16)
        group = index // slots
        mine = jnp.logical_and(
            row // period == group // parts, lax.rem(row, parts) == lax.rem(group, parts)
        )
        mine = jnp.logical_and(mine, lax.rem(index, slots) == slot.astype(jnp.int32))
        grad = dot(jnp.where(mine, 1.0, 0.0).astype(BF16), source[...].reshape(count, source.shape[-1]))
        return [grad[k * slots : k * slots + slots] for k in range(groups)]

    pieces = by_slot(early_ref, slot_early, 3, 6) + by_slot(late_ref, slot_late, 2, 4)
    grad = jnp.concatenate(pieces, axis=1)
    sums = jnp.sum(grad, axis=0, keepdims=True)
    low = grad.astype(BF16)
    ad_ref[...] = dot_tn(silu, low)
    loads[2].wait()
    silu_grad = dot_nt(low, aw[...])
    store(ad_ref, ad_out)
    bias = jnp.zeros((1, 6 * own), F32)
    for t in range(strips):
        bias = jnp.where(s == t, sums[:, t * 6 * own : t * 6 * own + 6 * own], bias)
    ab_ref[...] = bias[0]
    classes = tab_ref.shape[1]
    onehot = lax.broadcasted_iota(jnp.int32, (slots, classes), 1) == labels.astype(jnp.int32)
    tab_ref[...] = lax.dot_general(
        silu_grad * slope,
        jnp.where(onehot, 1.0, 0.0),
        TN,
        precision=lax.Precision.HIGHEST,
        preferred_element_type=F32,
    )
    for cp in stores:
        cp.wait()


def final(parts, aw, classes, strips):
    out, tg, r, c = parts[:4]
    width = out.shape[-1]
    own = width // strips
    half = width // 2
    shape = jax.ShapeDtypeStruct
    vm = pltpu.VMEM
    return pl.pallas_call(
        final_kernel,
        name="final",
        out_shape=(
            shape(out.shape, BF16),
            shape(tg.shape, F32),
            shape((own, classes), F32),
            shape((own, 6 * width), F32),
            shape((6 * own,), F32),
            shape((9, own), F32),
            shape((own, 3 * width), F32),
            shape((own, width), F32),
            shape((own,), F32),
            shape((own, 4 * width), F32),
            shape((half,), F32),
            shape((9, half), F32),
            shape((half, width), F32),
            shape((own,), F32),
        ),
        in_specs=[LEFT] * 4 + [WHOLE] * 5 + [LEFT],
        out_specs=(
            LEFT, LEFT, WHOLE, LEFT, WHOLE, WHOLE, LEFT, LEFT, WHOLE, LEFT, WHOLE, WHOLE, LEFT,
            WHOLE,
        ),
        scratch_shapes=[
            vm((own, 6 * width), BF16),
            vm(out.shape, BF16),
            vm(tg.shape, F32),
            vm(r.shape, BF16),
            vm(c.shape, BF16),
            vm((own, 6 * width), F32),
            vm((own, 3 * width), F32),
            vm((own, width), F32),
            vm((own, 4 * width), F32),
            vm((half, width), F32),
            pltpu.SemaphoreType.DMA((12,)),
        ],
        compiler_params=pltpu.CompilerParams(vmem_limit_bytes=VMEM_BYTES),
    )(*parts, aw)


def local_grouped(
    tokens, tile_owner, time_steps, class_labels, class_embedding_matrix, adaptive_weight,
    adaptive_bias, mixer_kernel, joint_weight, output_weight, output_bias, expand_weight,
    expand_bias, hidden_kernel, reduce_weight, reduce_bias, output_cotangent,
):
    strips = lax.axis_size("strip")
    owner = tile_owner.transpose(0, 2, 1)
    parts = block(
        tokens[0], mixer_kernel.T, owner, time_steps, class_labels, class_embedding_matrix.T,
        adaptive_weight, adaptive_bias, output_bias, expand_bias, hidden_kernel.T, reduce_bias,
        joint_weight, output_weight, expand_weight, reduce_weight, output_cotangent[0], strips,
    )
    classes = class_embedding_matrix.shape[1]
    (
        out, tg, table, adaptive, bias, mixer, joint, output, ob, expand, eb, hidden, reduce, rb,
    ) = final(parts, adaptive_weight, classes, strips)
    return (
        out[None], tg[None], table, adaptive, bias, mixer.T, joint, output, ob, expand, eb,
        hidden.T, reduce, rb,
    )


EXACT_PRECISION = lax.Precision.HIGHEST


def padded_2(block, sides, width):
    for axis, dim in sides:
        count = lax.axis_size(axis)
        forward = [(i, i + 1) for i in range(count - 1)]
        backward = [(target, source) for source, target in forward]
        low = lax.ppermute(
            lax.slice_in_dim(block, block.shape[dim] - width, None, axis=dim), axis, forward
        )
        high = lax.ppermute(lax.slice_in_dim(block, 0, width, axis=dim), axis, backward)
        block = jnp.concatenate([low, block, high], axis=dim)
    return block


def normalize(values):
    centre = jnp.mean(values, axis=-1, keepdims=True)
    centred = values - centre
    spread = jnp.mean(centred * centred, axis=-1, keepdims=True)
    return centred * lax.rsqrt(spread + EPSILON)


def modulate(values, shifting, scaling):
    return normalize(values) * (1.0 + scaling) + shifting


def depthwise(padded, kernel):
    row_count = padded.shape[-3] - 2
    column_total = padded.shape[-2]
    widened = jnp.pad(padded, [(0, 0)] * (padded.ndim - 2) + [(1, 1), (0, 0)])
    result = jnp.zeros(
        padded.shape[:-3] + (row_count, column_total, padded.shape[-1]), padded.dtype
    )
    for tapping in range(9):
        row_shift = tapping // 3
        col_shift = tapping % 3
        window = lax.slice_in_dim(widened, row_shift, row_shift + row_count, axis=widened.ndim - 3)
        window = lax.slice_in_dim(
            window, col_shift, col_shift + column_total, axis=widened.ndim - 2
        )
        result = result + kernel[:, tapping] * window
    return result


def kernel_grad(padded, gradient):
    row_count = gradient.shape[1]
    column_total = gradient.shape[2]
    widened = jnp.pad(padded, ((0, 0), (0, 0), (1, 1), (0, 0)))
    columns = []
    for tapping in range(9):
        row_shift = tapping // 3
        col_shift = tapping % 3
        window = widened[
            :, row_shift : row_shift + row_count, col_shift : col_shift + column_total, :
        ]
        columns.append(jnp.sum(window * gradient, axis=(0, 1, 2)))
    return jnp.stack(columns, axis=1)


def timestep_features(time_steps, model_width):
    half_width = model_width // 2
    frequencies = jnp.exp(
        -math.log(10000.0) * jnp.arange(half_width, dtype=jnp.float32) / half_width
    )
    angles = time_steps.astype(jnp.float32)[..., None] * frequencies
    return jnp.concatenate([jnp.cos(angles), jnp.sin(angles)], axis=-1)


def group_owner(owner):
    canvases, row_count, column_total = owner.shape
    shaped = owner.reshape(canvases, row_count // 2, 2, column_total // 2, 2).transpose(
        0, 2, 4, 1, 3
    )
    return shaped.reshape(canvases, 2, 2, row_count // 2 * (column_total // 2))


def to_groups(tensor, head_count):
    canvases, row_count, column_total, features = tensor.shape
    head_size = features // head_count
    shaped = tensor.reshape(
        canvases, row_count // 2, 2, column_total // 2, 2, head_count, head_size
    )
    shaped = shaped.transpose(0, 2, 4, 5, 1, 3, 6)
    return shaped.reshape(
        canvases, 2, 2, head_count, row_count // 2 * (column_total // 2), head_size
    )


def from_groups(tensor, row_count, column_total):
    canvases, head_count, head_size = (tensor.shape[0], tensor.shape[3], tensor.shape[-1])
    shaped = tensor.reshape(
        canvases, 2, 2, head_count, row_count // 2, column_total // 2, head_size
    )
    shaped = shaped.transpose(0, 4, 1, 5, 2, 3, 6)
    return shaped.reshape(canvases, row_count, column_total, head_count * head_size)


def local(
    tokens,
    tile_owner,
    time_steps,
    class_labels,
    class_embedding_matrix,
    adaptive_weight,
    adaptive_bias,
    mixer_kernel,
    joint_weight,
    output_weight,
    output_bias,
    expand_weight,
    expand_bias,
    hidden_kernel,
    reduce_weight,
    reduce_bias,
    output_cotangent,
):
    canvases, row_count, column_total, model_width = tokens.shape
    head_count = HEADS
    head_size = model_width // head_count
    factor = head_size ** (-0.5)
    half_cols = column_total // 2
    strips = lax.axis_size("strip")
    strip_index = lax.axis_index("strip")
    canvas_rows = row_count * strips
    class_count = class_embedding_matrix.shape[1]
    latent_count = time_steps.shape[1]
    tile_rows = canvas_rows // 4
    full_owner = jnp.broadcast_to(
        tile_owner[:, :, None, :, None], (canvases, 4, tile_rows, 2, half_cols)
    ).reshape(canvases, canvas_rows, column_total)
    local_owner = lax.dynamic_slice_in_dim(full_owner, strip_index * row_count, row_count, 1)
    token_hot = (local_owner[..., None] == jnp.arange(latent_count, dtype=jnp.int32)).astype(
        jnp.float32
    )
    class_onehot = (class_labels[..., None] == jnp.arange(class_count, dtype=jnp.int32)).astype(
        jnp.bfloat16
    )
    class_rows = jnp.einsum(
        "ywj,gj->ywg", class_onehot, class_embedding_matrix, preferred_element_type=jnp.float32
    )
    condition = timestep_features(time_steps, model_width) + class_rows
    silu_value, silu_pull = jax.vjp(jax.nn.silu, condition)
    silu_cond = silu_value.astype(jnp.bfloat16)
    modulation = jnp.einsum(
        "cbd,de->cbe", silu_cond, adaptive_weight, preferred_element_type=jnp.float32
    )
    modulation = modulation + adaptive_bias.astype(jnp.float32)
    token_mod = jnp.einsum("crkb,cbe->crke", token_hot, modulation, precision=EXACT_PRECISION)
    shift_one, scale_one, gate_one, shift_two, scale_two, gate_two = jnp.split(
        token_mod, 6, axis=-1
    )
    inputs = tokens.astype(jnp.float32)
    first_value, first_pull = jax.vjp(modulate, inputs, shift_one, scale_one)
    first = first_value.astype(jnp.bfloat16)
    first_padded = padded_2(first, (("strip", 1),), 1)
    mixer_single_float = mixer_kernel.astype(jnp.float32)
    mixed = depthwise(first_padded.astype(jnp.float32), mixer_single_float).astype(jnp.bfloat16)
    joint = jnp.einsum("crkd,de->crke", mixed, joint_weight, preferred_element_type=jnp.float32)
    query_rows = joint[..., :model_width].astype(jnp.bfloat16)
    keys_local = joint[..., model_width : 2 * model_width].astype(jnp.bfloat16)
    values_local = joint[..., 2 * model_width :].astype(jnp.bfloat16)
    keys_canvas, values_canvas = (
        lax.all_gather(keys_local, "strip", axis=1, tiled=True),
        lax.all_gather(values_local, "strip", axis=1, tiled=True),
    )
    query_groups = to_groups(query_rows, head_count)
    key_groups = to_groups(keys_canvas, head_count)
    value_groups = to_groups(values_canvas, head_count)
    query_owner = group_owner(local_owner)
    key_owner = group_owner(full_owner)
    allowed = (query_owner[..., :, None] == key_owner[..., None, :])[:, :, :, None]

    def attention_scores():
        raw = (
            jnp.einsum(
                "cabhnd,cabhmd->cabhnm",
                query_groups,
                key_groups,
                preferred_element_type=jnp.float32,
            )
            * factor
        )
        return jnp.where(allowed, raw, MASKED)

    scores = attention_scores()
    peak = jnp.max(scores, axis=-1, keepdims=True)
    lifted_float = jnp.exp(scores - peak)
    total = jnp.sum(lifted_float, axis=-1, keepdims=True)
    softened = (lifted_float / total).astype(jnp.bfloat16)
    log_total = peak + jnp.log(total)
    attended_groups = jnp.einsum(
        "cabhnm,cabhmd->cabhnd", softened, value_groups, preferred_element_type=jnp.float32
    )
    attended = from_groups(attended_groups, row_count, column_total).astype(jnp.bfloat16)
    branch_one = jnp.einsum(
        "crkd,de->crke", attended, output_weight, preferred_element_type=jnp.float32
    )
    branch_one = branch_one + output_bias.astype(jnp.float32)
    residual = inputs + gate_one * branch_one
    second_value, second_pull = jax.vjp(modulate, residual, shift_two, scale_two)
    second = second_value.astype(jnp.bfloat16)
    expanded = jnp.einsum(
        "crkd,df->crkf", second, expand_weight, preferred_element_type=jnp.float32
    )
    expanded = (expanded + expand_bias.astype(jnp.float32)).astype(jnp.bfloat16)
    expanded_padded = padded_2(expanded, (("strip", 1),), 1)
    hidden_float = hidden_kernel.astype(jnp.float32)
    conv_out = depthwise(expanded_padded.astype(jnp.float32), hidden_float)
    gelu_value, gelu_pull = jax.vjp(jax.nn.gelu, conv_out)
    activated = gelu_value.astype(jnp.bfloat16)
    branch_two = jnp.einsum(
        "crkf,fd->crkd", activated, reduce_weight, preferred_element_type=jnp.float32
    )
    branch_two = branch_two + reduce_bias.astype(jnp.float32)
    outputs = (residual + gate_two * branch_two).astype(jnp.bfloat16)
    upstream = output_cotangent.astype(jnp.float32)
    two_grad = (upstream * gate_two).astype(jnp.bfloat16)
    gate_two_grad = upstream * branch_two
    reduce_bias_grad = jnp.sum(two_grad.astype(jnp.float32), axis=(0, 1, 2))
    reduce_weight_grad = jnp.einsum(
        "crkf,crkd->fd", activated, two_grad, preferred_element_type=jnp.float32
    )
    activated_grad = jnp.einsum(
        "crkd,fd->crkf", two_grad, reduce_weight, preferred_element_type=jnp.float32
    )
    conv_grad = gelu_pull(activated_grad)[0].astype(jnp.bfloat16)
    conv_padded = padded_2(conv_grad, (("strip", 1),), 1)
    expanded_grad = depthwise(conv_padded.astype(jnp.float32), hidden_float[:, ::-1]).astype(
        jnp.bfloat16
    )
    hidden_kernel_grad = kernel_grad(
        expanded_padded.astype(jnp.float32), conv_grad.astype(jnp.float32)
    )
    expand_bias_grad = jnp.sum(expanded_grad.astype(jnp.float32), axis=(0, 1, 2))
    expand_weight_grad = jnp.einsum(
        "crkd,crkf->df", second, expanded_grad, preferred_element_type=jnp.float32
    )
    second_grad = jnp.einsum(
        "crkf,df->crkd", expanded_grad, expand_weight, preferred_element_type=jnp.float32
    )
    residual_part, shift_two_grad, scale_two_grad = second_pull(second_grad)
    residual_grad = upstream + residual_part
    gate_one_grad = residual_grad * branch_one
    one_grad = (residual_grad * gate_one).astype(jnp.bfloat16)
    output_bias_grad = jnp.sum(one_grad.astype(jnp.float32), axis=(0, 1, 2))
    output_weight_grad = jnp.einsum(
        "crkd,crke->de", attended, one_grad, preferred_element_type=jnp.float32
    )
    attended_grad = jnp.einsum(
        "crke,de->crkd", one_grad, output_weight, preferred_element_type=jnp.float32
    ).astype(jnp.bfloat16)
    attended_grad_groups = to_groups(attended_grad, head_count)
    probs = jnp.exp(attention_scores() - log_total)
    prob_grads = jnp.einsum(
        "cabhnd,cabhmd->cabhnm",
        attended_grad_groups,
        value_groups,
        preferred_element_type=jnp.float32,
    )
    spread_sum = jnp.sum(probs * prob_grads, axis=-1, keepdims=True)
    score_grads = (probs * (prob_grads - spread_sum)).astype(jnp.bfloat16)
    query_grad_groups = (
        jnp.einsum(
            "cabhnm,cabhmd->cabhnd", score_grads, key_groups, preferred_element_type=jnp.float32
        )
        * factor
    )
    query_grad = from_groups(query_grad_groups, row_count, column_total).astype(jnp.bfloat16)
    all_queries, all_attended = (
        lax.all_gather(query_groups, "strip", axis=4, tiled=True),
        lax.all_gather(attended_grad_groups, "strip", axis=4, tiled=True),
    )
    all_logs, all_spreads = (
        lax.all_gather(log_total[..., 0], "strip", axis=4, tiled=True),
        lax.all_gather(spread_sum[..., 0], "strip", axis=4, tiled=True),
    )
    own_keys = to_groups(keys_local, head_count)
    own_values = to_groups(values_local, head_count)
    own_allowed = (key_owner[..., :, None] == query_owner[..., None, :])[:, :, :, None]
    own_scores = (
        jnp.einsum(
            "cabhnd,cabhmd->cabhnm", all_queries, own_keys, preferred_element_type=jnp.float32
        )
        * factor
    )
    own_scores = jnp.where(own_allowed, own_scores, MASKED)
    own_probs = jnp.exp(own_scores - all_logs[..., None])
    own_prob_grads = jnp.einsum(
        "cabhnd,cabhmd->cabhnm", all_attended, own_values, preferred_element_type=jnp.float32
    )
    own_score_grads = (own_probs * (own_prob_grads - all_spreads[..., None])).astype(jnp.bfloat16)
    key_grad_groups = (
        jnp.einsum(
            "cabhnm,cabhnd->cabhmd",
            own_score_grads,
            all_queries,
            preferred_element_type=jnp.float32,
        )
        * factor
    )
    value_grad_groups = jnp.einsum(
        "cabhnm,cabhnd->cabhmd",
        own_probs.astype(jnp.bfloat16),
        all_attended,
        preferred_element_type=jnp.float32,
    )
    key_grad = from_groups(key_grad_groups, row_count, column_total).astype(jnp.bfloat16)
    value_grad = from_groups(value_grad_groups, row_count, column_total).astype(jnp.bfloat16)
    joint_grad = jnp.concatenate([query_grad, key_grad, value_grad], axis=-1)
    joint_weight_grad = jnp.einsum(
        "crkd,crke->de", mixed, joint_grad, preferred_element_type=jnp.float32
    )
    mixed_grad = jnp.einsum(
        "crke,de->crkd", joint_grad, joint_weight, preferred_element_type=jnp.float32
    ).astype(jnp.bfloat16)
    mixed_padded = padded_2(mixed_grad, (("strip", 1),), 1)
    first_grad = depthwise(mixed_padded.astype(jnp.float32), mixer_single_float[:, ::-1])
    mixer_kernel_grad = kernel_grad(
        first_padded.astype(jnp.float32), mixed_grad.astype(jnp.float32)
    )
    input_part, shift_one_grad, scale_one_grad = first_pull(first_grad)
    tokens_grad = residual_grad + input_part
    token_grad = jnp.concatenate(
        [
            shift_one_grad,
            scale_one_grad,
            gate_one_grad,
            shift_two_grad,
            scale_two_grad,
            gate_two_grad,
        ],
        axis=-1,
    )
    modulation_grad = jnp.einsum("crkb,crke->cbe", token_hot, token_grad, precision=EXACT_PRECISION)
    silu_grad = jnp.einsum(
        "cbe,de->cbd",
        modulation_grad,
        adaptive_weight.astype(jnp.float32),
        precision=EXACT_PRECISION,
    )
    conditioning_grad = silu_pull(silu_grad)[0]
    table_grad = jnp.einsum(
        "soy,sok->yk",
        conditioning_grad,
        class_onehot.astype(jnp.float32),
        precision=EXACT_PRECISION,
    )
    adaptive_grad = jnp.einsum(
        "cbd,cbe->de", silu_cond.astype(jnp.float32), modulation_grad, precision=EXACT_PRECISION
    )
    adaptive_bias_grad = jnp.sum(modulation_grad, axis=(0, 1))
    (
        table_shard,
        adaptive_shard,
        adaptive_bias_shard,
        mixer_shard,
        joint_shard,
        output_shard,
        output_bias_shard,
        expand_shard,
        expand_bias_shard,
        hidden_shard,
        reduce_shard,
        reduce_bias_shard,
    ) = (
        lax.psum_scatter(
            table_grad.astype(jnp.bfloat16), "strip", scatter_dimension=0, tiled=True
        ).astype(jnp.float32),
        lax.psum_scatter(
            adaptive_grad.astype(jnp.bfloat16), "strip", scatter_dimension=0, tiled=True
        ).astype(jnp.float32),
        lax.psum_scatter(
            adaptive_bias_grad.astype(jnp.bfloat16), "strip", scatter_dimension=0, tiled=True
        ).astype(jnp.float32),
        lax.psum_scatter(
            mixer_kernel_grad.astype(jnp.bfloat16), "strip", scatter_dimension=0, tiled=True
        ).astype(jnp.float32),
        lax.psum_scatter(
            joint_weight_grad.astype(jnp.bfloat16), "strip", scatter_dimension=0, tiled=True
        ).astype(jnp.float32),
        lax.psum_scatter(
            output_weight_grad.astype(jnp.bfloat16), "strip", scatter_dimension=0, tiled=True
        ).astype(jnp.float32),
        lax.psum_scatter(
            output_bias_grad.astype(jnp.bfloat16), "strip", scatter_dimension=0, tiled=True
        ).astype(jnp.float32),
        lax.psum_scatter(
            expand_weight_grad.astype(jnp.bfloat16), "strip", scatter_dimension=0, tiled=True
        ).astype(jnp.float32),
        lax.psum_scatter(
            expand_bias_grad.astype(jnp.bfloat16), "strip", scatter_dimension=0, tiled=True
        ).astype(jnp.float32),
        lax.psum_scatter(
            hidden_kernel_grad.astype(jnp.bfloat16), "strip", scatter_dimension=0, tiled=True
        ).astype(jnp.float32),
        lax.psum_scatter(
            reduce_weight_grad.astype(jnp.bfloat16), "strip", scatter_dimension=0, tiled=True
        ).astype(jnp.float32),
        lax.psum_scatter(
            reduce_bias_grad.astype(jnp.bfloat16), "strip", scatter_dimension=0, tiled=True
        ).astype(jnp.float32),
    )
    summed = (
        lax.psum(table_shard.astype(jnp.bfloat16), "batch").astype(jnp.float32),
        lax.psum(adaptive_shard.astype(jnp.bfloat16), "batch").astype(jnp.float32),
        lax.psum(adaptive_bias_shard.astype(jnp.bfloat16), "batch").astype(jnp.float32),
        lax.psum(mixer_shard.astype(jnp.bfloat16), "batch").astype(jnp.float32),
        lax.psum(joint_shard.astype(jnp.bfloat16), "batch").astype(jnp.float32),
        lax.psum(output_shard.astype(jnp.bfloat16), "batch").astype(jnp.float32),
        lax.psum(output_bias_shard.astype(jnp.bfloat16), "batch").astype(jnp.float32),
        lax.psum(expand_shard.astype(jnp.bfloat16), "batch").astype(jnp.float32),
        lax.psum(expand_bias_shard.astype(jnp.bfloat16), "batch").astype(jnp.float32),
        lax.psum(hidden_shard.astype(jnp.bfloat16), "batch").astype(jnp.float32),
        lax.psum(reduce_shard.astype(jnp.bfloat16), "batch").astype(jnp.float32),
        lax.psum(reduce_bias_shard.astype(jnp.bfloat16), "batch").astype(jnp.float32),
    )
    return (
        outputs,
        tokens_grad,
        summed[0],
        summed[1],
        summed[2],
        summed[3],
        summed[4],
        summed[5],
        summed[6],
        summed[7],
        summed[8],
        summed[9],
        summed[10],
        summed[11],
    )


def solution(mesh):
    grouped = (mesh.shape["batch"], mesh.shape["strip"]) == (4, 8)
    return jax.shard_map(
        local_grouped if grouped else local,
        mesh=mesh,
        in_specs=(
            P("batch", "strip", None, None),
            P("batch", None, None),
            P("batch", None),
            P("batch", None),
            P(),
            P(),
            P(),
            P(),
            P(),
            P(),
            P(),
            P(),
            P(),
            P(),
            P(),
            P(),
            P("batch", "strip", None, None),
        ),
        out_specs=(
            P("batch", "strip", None, None),
            P("batch", "strip", None, None),
            P("strip", None),
            P("strip", None),
            P("strip"),
            P("strip", None),
            P("strip", None),
            P("strip", None),
            P("strip"),
            P("strip", None),
            P("strip"),
            P("strip", None),
            P("strip", None),
            P("strip"),
        ),
        check_vma=False,
    )
```
